32 devices in a mesh: seq: 4 (over z), shard: 8 (over y, x, core).
Axes of the slice: x: 2, y: 2, z: 4, core: 2. Of those that a mesh axis runs over, the one named last changes fastest.
Arguments:
- tokens: bfloat16 [8, 2048, 768], P('shard', 'seq'), may hold values from -6 to 6
- ln1_gain: bfloat16 [768], P('shard'), may hold values from 0.099609375 to 1.8984375
- ln1_shift: bfloat16 [768], P('shard'), may hold values from -3 to 3
- w_qkv: bfloat16 [768, 2304], P('shard'), may hold values from -0.21875 to 0.21875
- q_bias: bfloat16 [768], P('shard'), may hold values from -3 to 3
- v_bias: bfloat16 [768], P('shard'), may hold values from -3 to 3
- w_out: bfloat16 [768, 768], P('shard'), may hold values from -3 to 3
- out_bias: bfloat16 [768], P('shard'), may hold values from -3 to 3
- ln2_gain: bfloat16 [768], P('shard'), may hold values from 0.099609375 to 1.8984375
- ln2_shift: bfloat16 [768], P('shard'), may hold values from -3 to 3
- w_in: bfloat16 [768, 3072], P('shard'), may hold values from -0.21875 to 0.21875
- in_bias: bfloat16 [3072], P('shard'), may hold values from -3 to 3
- w_fin: bfloat16 [3072, 768], P('shard'), may hold values from -0.109375 to 0.109375
- fin_bias: bfloat16 [768], P('shard'), may hold values from -3 to 3
- cotangent: bfloat16 [8, 2048, 768], P('shard', 'seq'), may hold values from -6 to 6
- lengths: int32 [8], P('shard'), may hold values from 512 to 2048, as said below
Outputs:
- output: bfloat16 [8, 2048, 768], P('shard', 'seq')
- grad_tokens: bfloat16 [8, 2048, 768], P('shard', 'seq')
- grad_ln1_gain: float32 [768], P('shard')
- grad_ln1_shift: float32 [768], P('shard')
- grad_w_qkv: float32 [768, 2304], P('shard')
- grad_q_bias: float32 [768], P('shard')
- grad_v_bias: float32 [768], P('shard')
- grad_w_out: float32 [768, 768], P('shard')
- grad_out_bias: float32 [768], P('shard')
- grad_ln2_gain: float32 [768], P('shard')
- grad_ln2_shift: float32 [768], P('shard')
- grad_w_in: float32 [768, 3072], P('shard')
- grad_in_bias: float32 [3072], P('shard')
- grad_w_fin: float32 [3072, 768], P('shard')
- grad_fin_bias: float32 [768], P('shard')
The draws below stay inside these ranges and needn't reach their ends.
Inputs may be any that keep to these rules, and one draw needn't show every extreme that they name: Each slot holds lengths[s] valid tokens at its start; at least one slot is full, with 2048.
All inputs are finite; a program needn't handle non-finite values.
Results may differ from the reference program's by a relative error of at most 0.014.
Values may be sent and summed in bfloat16 or wider, within the bound.
A program may use at most 128 MiB of HBM per device.

```python
import jax
import jax.numpy as jnp
from jax import lax

D = 768
HEADS = 12
HEAD_DIM = 64
FF = 3072
SLOT = 2048
SLOTS = 8


def draw_lengths(key, part):
    key_draw, key_pick = jax.random.split(key)
    drawn = jax.random.randint(key_draw, (SLOTS,), SLOT // 4, SLOT + 1)
    chosen = jax.random.randint(key_pick, (), 0, SLOTS)
    return jnp.where(jnp.arange(SLOTS) == chosen, SLOT, drawn).astype(jnp.int32)


def block_levels(key, dims, pieces, smallest, top_value):
    factor_of = 1.0
    for axis_at, blocks in pieces:
        heights = jax.random.uniform(jax.random.fold_in(jax.random.fold_in(key, 6), axis_at), (blocks,), jnp.float32, smallest / len(pieces), top_value / len(pieces))
        factor_of = factor_of * jnp.repeat(jnp.exp(heights), dims[axis_at] // blocks).reshape((-1,) + (1,) * (len(dims) - 1 - axis_at))
    return factor_of


def noise(stream_key, extent, width, bound, cuts=(), held_as=jnp.bfloat16):
    level = block_levels(stream_key, extent, cuts, -0.22, 0.18) if cuts else 1.0
    entries = jax.random.normal(stream_key, extent, jnp.float32) * width * level
    return jnp.minimum(jnp.maximum(entries, -bound), bound).astype(held_as)


def setup_inputs(seed: int = 0) -> dict:
    key_list = jax.random.split(jax.random.key(seed), 17)
    return {
        "tokens": noise(key_list[0], (SLOTS, SLOT, D), 1.0, 6.0, ((0, 8), (1, 4))),
        "ln1_gain": jnp.clip(1.0 + 0.18 * jax.random.normal(key_list[1], (D,), jnp.float32), 0.099609375, 1.8984375).astype(jnp.bfloat16),
        "ln1_shift": noise(key_list[2], (D,), 0.5, 3.0, ((0, 8),)),
        "w_qkv": noise(key_list[3], (D, 3 * D), D ** -0.5, 0.21875, ((0, 8),)),
        "q_bias": noise(key_list[4], (D,), 0.5, 3.0, ((0, 8),)),
        "v_bias": noise(key_list[5], (D,), 0.5, 3.0, ((0, 8),)),
        "w_out": noise(key_list[6], (D, D), 4 ** -0.5, 3.0, ((0, 8),)),
        "out_bias": noise(key_list[7], (D,), 0.5, 3.0, ((0, 8),)),
        "ln2_gain": jnp.clip(1.0 + 0.18 * jax.random.normal(key_list[8], (D,), jnp.float32), 0.099609375, 1.8984375).astype(jnp.bfloat16),
        "ln2_shift": noise(key_list[9], (D,), 0.5, 3.0, ((0, 8),)),
        "w_in": noise(key_list[10], (D, FF), D ** -0.5, 0.21875, ((0, 8),)),
        "in_bias": noise(key_list[11], (FF,), 0.5, 3.0, ((0, 8),)),
        "w_fin": noise(key_list[12], (FF, D), FF ** -0.5, 0.109375, ((0, 8),)),
        "fin_bias": noise(key_list[13], (D,), 0.5, 3.0, ((0, 8),)),
        "cotangent": noise(key_list[14], (SLOTS, SLOT, D), 1.0, 6.0, ((0, 8), (1, 4))),
        "lengths": draw_lengths(jax.random.fold_in(key_list[16], 71), 0),
    }


EPS = 1e-05

@jax.custom_vjp
def low(v):
    return lax.optimization_barrier(v.astype(jnp.bfloat16)).astype(jnp.float32)

@jax.custom_vjp
def low_back(v):
    return v

def low_keep(v):
    return (low(v), None)

def low_pass(kept, grad):
    return (grad,)

def back_keep(v):
    return (v, None)

def back_low(kept, grad):
    return (low(grad),)
low.defvjp(low_keep, low_pass)
low_back.defvjp(back_keep, back_low)

def matmul(left, right):
    return jnp.dot(left, right, precision=lax.Precision.HIGHEST, preferred_element_type=jnp.float32)

def layer_norm(values, gain, shift):
    average = lax.optimization_barrier(jnp.mean(values, -1, keepdims=True))
    centred = values - average
    spread = lax.optimization_barrier(jnp.mean(centred * centred, -1, keepdims=True))
    return centred * lax.rsqrt(spread + EPS) * gain + shift

def attend_rows(query_rows, keys, values, key_live):
    scores = jnp.einsum('qhd,khd->hqk', query_rows, keys, precision=lax.Precision.HIGHEST) * HEAD_DIM ** (-0.5)
    scores = low_back(scores)
    scores = jnp.where(key_live[None, None, :], scores, -jnp.inf)
    highest = lax.optimization_barrier(jnp.max(scores, -1, keepdims=True))
    raised = jnp.exp(scores - highest)
    weights = low(raised / lax.optimization_barrier(jnp.sum(raised, -1, keepdims=True)))
    context = jnp.einsum('hqk,khd->qhd', weights, values, precision=lax.Precision.HIGHEST)
    return context.reshape(query_rows.shape[0], HEADS * HEAD_DIM)

def layer_slot(inputs, length, params):
    ln1_gain, ln1_shift, w_qkv, q_bias, v_bias, w_out, out_bias, ln2_gain, ln2_shift, w_in, in_bias, w_fin, fin_bias = params
    key_live = jnp.arange(SLOT, dtype=jnp.int32) < length
    normed = low(layer_norm(inputs, ln1_gain, ln1_shift))
    projected = matmul(normed, w_qkv)
    query = low_back(low(projected[:, :D] + q_bias)).reshape(SLOT, HEADS, HEAD_DIM)
    keys = low_back(low(projected[:, D:2 * D])).reshape(SLOT, HEADS, HEAD_DIM)
    values = low_back(low(projected[:, 2 * D:] + v_bias)).reshape(SLOT, HEADS, HEAD_DIM)
    row_block = min(512, SLOT)
    blocked = query.reshape(SLOT // row_block, row_block, HEADS, HEAD_DIM)
    attend_block = jax.checkpoint(lambda query_rows: attend_rows(query_rows, keys, values, key_live))
    context = lax.map(attend_block, blocked).reshape(SLOT, D)
    context = low_back(low(context))
    branch = low_back(matmul(context, w_out) + out_bias)
    middle = inputs + branch
    normed_two = low(layer_norm(middle, ln2_gain, ln2_shift))
    inner = low_back(matmul(normed_two, w_in) + in_bias)
    active = low(jax.nn.gelu(inner, approximate=True))
    outer = low_back(matmul(active, w_fin) + fin_bias)
    return middle + outer

def reference(tokens, ln1_gain, ln1_shift, w_qkv, q_bias, v_bias, w_out, out_bias, ln2_gain, ln2_shift, w_in, in_bias, w_fin, fin_bias, cotangent, lengths):
    params = (ln1_gain.astype(jnp.float32), ln1_shift.astype(jnp.float32), w_qkv.astype(jnp.float32), q_bias.astype(jnp.float32), v_bias.astype(jnp.float32), w_out.astype(jnp.float32), out_bias.astype(jnp.float32), ln2_gain.astype(jnp.float32), ln2_shift.astype(jnp.float32), w_in.astype(jnp.float32), in_bias.astype(jnp.float32), w_fin.astype(jnp.float32), fin_bias.astype(jnp.float32))
    inputs = tokens.astype(jnp.float32)
    slot_layer = jax.checkpoint(layer_slot)

    def forward(slot_inputs, weights):
        return lax.map(lambda slot_pair: slot_layer(slot_pair[0], slot_pair[1], weights), (slot_inputs, lengths))
    output, pullback = jax.vjp(forward, inputs, params)
    live = (jnp.arange(SLOT, dtype=jnp.int32)[None, :] < lengths[:, None]).astype(jnp.float32)
    seeded = cotangent.astype(jnp.float32) * live[:, :, None]
    grad_inputs, grad_params = pullback(seeded)
    g_ln1_gain, g_ln1_shift, g_w_qkv, g_q_bias, g_v_bias, g_w_out, g_out_bias, g_ln2_gain, g_ln2_shift, g_w_in, g_in_bias, g_w_fin, g_fin_bias = grad_params
    return (output.astype(jnp.bfloat16), grad_inputs.astype(jnp.bfloat16), g_ln1_gain, g_ln1_shift, g_w_qkv, g_q_bias, g_v_bias, g_w_out, g_out_bias, g_ln2_gain, g_ln2_shift, g_w_in, g_in_bias, g_w_fin, g_fin_bias)
```

```python
import functools
import math

import jax
import jax.numpy as jnp
from jax import lax
from jax.experimental import pallas as pl
from jax.experimental.pallas import tpu as pltpu
from jax.sharding import PartitionSpec as P

HEAD_DIM = 64
EPS = 1e-05
GELU_C = 0.7978845608028654
GELU_K = 0.044715
MASKED = -1e30

BF = jnp.bfloat16
F32 = jnp.float32
MESH = pl.DeviceIdType.MESH
VMEM = pl.BlockSpec(memory_space=pltpu.VMEM)
ANY = pl.BlockSpec(memory_space=pl.ANY)

LN1G, LN1B, QB, VB, OB, LN2G, LN2B, FB, IB = range(9)
VECS = 12
VROWS = 16


def dot(left, right):
    return jnp.dot(left, right, preferred_element_type=F32)


def dot_t(left, right):
    return lax.dot_general(left, right, (((1,), (1,)), ((), ())), preferred_element_type=F32)


def mean_rows(values):
    return jnp.mean(values, -1, keepdims=True)


def unit_of(values):
    centred = values - mean_rows(values)
    inverse = lax.rsqrt(mean_rows(centred * centred) + EPS)
    return centred * inverse, inverse


def split3(values):
    high = values.astype(BF)
    rest = values - high.astype(F32)
    mid = rest.astype(BF)
    low = (rest - mid.astype(F32)).astype(BF)
    return high, mid, low


class Place:
    def __init__(self, shards):
        self.shards = shards
        per_plane = shards // 4
        q = lax.axis_index("seq")
        s = lax.axis_index("shard")
        self.q, self.s = q, s
        self.core = lax.rem(s, 2)
        plane, member = s // per_plane, lax.rem(s, per_plane)
        side = lax.rem(q + plane + member, 2)
        self.to = (plane, member * 4 + side * 2 + q // 2)
        group, side_here = s // 4, lax.rem(s // 2, 2)
        self.quarter = lax.rem(side_here + q + group, 2) + 2 * self.core
        self.origin = (self.quarter, q * per_plane + group)
        self.stays = (self.to[0] == q) & (self.to[1] == s)
        self.sibling = (q, s + 1 - 2 * self.core)
        self.beside = (q, s + 2 - 4 * side_here)
        self.quarters = [
            lax.rem(side_here + j // 2 + q + group, 2) + 2 * (j % 2) for j in range(4)
        ]


def relocation(n_seq, shards):
    per_plane = shards // 4
    pairs = []
    for q in range(n_seq):
        for s in range(shards):
            plane, member = s // per_plane, s % per_plane
            side = (q + plane + member) % 2
            pairs.append((q * shards + s, plane * shards + member * 4 + side * 2 + q // 2))
    return pairs


def remote(src, dst, send, recv, device):
    return pltpu.make_async_remote_copy(
        src_ref=src, dst_ref=dst, send_sem=send, recv_sem=recv, device_id=device, device_id_type=MESH
    )


def greet(here, devices, mover):
    barrier = pltpu.get_barrier_semaphore()
    for device in devices:
        pl.semaphore_signal(barrier, inc=1, device_id=device, device_id_type=MESH)

    @pl.when(jnp.logical_not(here.stays))
    def _():
        pl.semaphore_signal(barrier, inc=1, device_id=mover, device_id_type=MESH)
        pl.semaphore_wait(barrier, len(devices) + 1)

    @pl.when(here.stays)
    def _():
        pl.semaphore_wait(barrier, len(devices))


def forward_kernel(dims, *refs):
    shards, rows, width, heads, gather = dims
    n_in = 4
    tok, length_in, w_in, vec_in = refs[:n_in]
    (ka_o, va_o, kt_o, qat_o, ctxt_o, ctx_o, h1_o, wf_o, xown_o, len_o, vec_o, inb_o) = refs[
        n_in : n_in + 12
    ]
    (
        xs, wf, vg, lens, h1, ka, va, kt, vt, qat, ctxt, ctx,
        perm_s, perm_r, sib_s, sib_r, side_s, side_r, back_s, back_r,
        len_s, len_r, w_s, w_r, out_s, ctx_s, ctx_r,
    ) = refs[n_in + 12 :]
    here = Place(shards)
    core, s = here.core, here.s
    half = width // 2
    share = width // shards
    chunks = 4
    step = rows // chunks
    partner_y = (here.q, s + 4 - 8 * lax.rem(s // 4, 2))

    partners = [here.sibling, here.beside] + ([partner_y] if gather else [])
    greet(here, partners, here.origin)

    to_core = here.q // 2

    def block(ref, j, i):
        return ref.at[pl.ds(pl.multiple_of(j * rows + i * step, step), step), :]

    def perm_copy(i):
        return remote(
            tok.at[pl.ds(i * step, step), :], block(xs, to_core, i), perm_s.at[i], perm_r.at[i], here.to
        )

    def len_copy():
        return remote(length_in, lens, len_s, len_r, here.to)

    @pl.when(jnp.logical_not(here.stays))
    def _():
        for i in range(chunks):
            perm_copy(i).start()
        len_copy().start()

    @pl.when(here.stays)
    def _():
        for i in range(chunks):
            pltpu.make_async_copy(
                tok.at[pl.ds(i * step, step), :], block(xs, to_core, i), perm_r.at[i]
            ).start()
        pltpu.make_async_copy(length_in, lens, len_r).start()

    w_copies = []
    if gather:
        def columns(j, which):
            return pl.ds(pl.multiple_of(j * width + which * half, 128), half)

        mine = pl.ds(pl.multiple_of(s * share, share), share)
        for j in range(3):
            copy = remote(
                w_in.at[:, columns(j, 1 - core)], wf.at[mine, pl.ds(j * half, half)],
                w_s.at[j], w_r.at[j], here.sibling,
            )
            copy.start()
            w_copies.append(copy)
            copy = pltpu.make_async_copy(
                w_in.at[:, columns(j, core)], wf.at[mine, pl.ds(j * half, half)], w_s.at[4 + j]
            )
            copy.start()
            w_copies.append(copy)
        copy = remote(vec_in, vg.at[s], w_s.at[3], w_r.at[3], here.sibling)
        copy.start()
        w_copies.append(copy)
        copy = pltpu.make_async_copy(vec_in, vg.at[s], w_s.at[7])
        copy.start()
        w_copies.append(copy)
    else:
        copy = pltpu.make_async_copy(w_in, wf, w_s.at[0])
        copy.start()
        w_copies.append(copy)

    def hop(count, device, at):
        first = s // count * count
        rows_of = pl.ds(pl.multiple_of(first * share, share), count * share)
        one = remote(wf.at[rows_of, :], wf.at[rows_of, :], w_s.at[at], w_r.at[at], device)
        two = remote(
            vg.at[pl.ds(first, count)], vg.at[pl.ds(first, count)], w_s.at[at + 1], w_r.at[at + 1], device
        )
        one.start()
        two.start()
        return [one, two]

    def receive(i):
        pltpu.make_async_copy(tok.at[pl.ds(i * step, step), :], block(xs, core, i), perm_r.at[i]).wait()
        sib = remote(block(xs, core, i), block(xs, core, i), sib_s.at[i], sib_r.at[i], here.sibling)
        side = remote(block(xs, core, i), block(xs, 2 + core, i), side_s.at[i], side_r.at[i], here.beside)
        side.start()
        sib.start()
        return [sib, side]

    def relay(i):
        block_in = block(xs, 2 + core, i)
        remote(block_in, block_in, side_s.at[i], side_r.at[i], here.beside).wait_recv()
        copy = remote(block_in, block_in, back_s.at[i], back_r.at[i], here.sibling)
        copy.start()
        return copy

    moved = []
    hops = []
    if gather:
        for copy in w_copies:
            copy.wait()
        hops += hop(2, here.beside, 8)
    moved += receive(0)
    moved += receive(1)
    if gather:
        for copy in hops:
            copy.wait_recv()
        second = hop(4, partner_y, 10)
    moved += receive(2)
    moved += receive(3)

    def norm_one(first, count):
        def body(i, _):
            at = pl.ds(pl.multiple_of(first + i * 256, 256), 256)
            unit, _ = unit_of(xs[at, :].astype(F32))
            h1[at, :] = (unit * vec_o[LN1G : LN1G + 1, :] + vec_o[LN1B : LN1B + 1, :]).astype(BF)
            return 0

        lax.fori_loop(0, count // 256, body, 0)

    if gather:
        for copy in second:
            copy.wait_recv()
        for i in range(shards):
            piece = vg[i].astype(F32)
            vec_o[:, i * share : (i + 1) * share] = piece[:, :share]
            for r in range(4):
                at = (4 * i + r) * share
                inb_o[:, at : at + share] = jnp.broadcast_to(
                    piece[IB + r : IB + r + 1, :share], (8, share)
                )
    else:
        for copy in w_copies:
            copy.wait()
        vec_o[...] = vec_in[...].astype(F32)
        inb_o[...] = jnp.zeros_like(inb_o)

    pltpu.make_async_copy(length_in, lens, len_r).wait()
    length = lens[0:1, 0:1]
    lane = lax.broadcasted_iota(jnp.int32, (rows, 128), 1)
    row_at = lax.broadcasted_iota(jnp.int32, (rows, 128), 0)
    lower = lane < HEAD_DIM
    ones_rows = (lax.broadcasted_iota(jnp.int32, (16, rows), 0) == 0).astype(BF)
    q_rest = (lax.broadcasted_iota(jnp.int32, (64, 2 * rows), 0) == 3).astype(BF)
    for h in range(heads):
        qat[h, HEAD_DIM:, :] = q_rest

    def bias_half(at):
        full = vec_o[at : at + 1, :]
        return jnp.where(core == 0, full[:, :half], full[:, half:])

    def project(j):
        at = slice(j * rows, (j + 1) * rows)
        norm = h1[at, :]
        dead = jnp.where(here.quarters[j] * rows + row_at < length, 0.0, MASKED)
        k_rest = jnp.where(lane == HEAD_DIM + 3, dead, jnp.where(lane < HEAD_DIM + 3, 1.0, 0.0))
        v_rest = jnp.where(lane < HEAD_DIM + 3, -1.0, 0.0)
        if j < 2:
            q = (dot(norm, wf[:, :half]) + bias_half(QB)).astype(BF) * BF(HEAD_DIM**-0.5)
        k = dot(norm, wf[:, half : 2 * half])
        v = dot(norm, wf[:, 2 * half :]) + bias_half(VB)
        for i in range(heads // 2):
            two = slice(i * 128, (i + 1) * 128)
            kp, vp = k[:, two], v[:, two]
            ka[2 * i, at, :] = jnp.where(lower, kp, k_rest).astype(BF)
            ka[2 * i + 1, at, :] = jnp.where(lower, pltpu.roll(kp, 64, 1), k_rest).astype(BF)
            va[2 * i, at, :] = jnp.where(lower, vp, v_rest).astype(BF)
            va[2 * i + 1, at, :] = jnp.where(lower, pltpu.roll(vp, 64, 1), v_rest).astype(BF)
            turned = kp.astype(BF).T
            kt[2 * i, :, at] = turned[:64]
            kt[2 * i + 1, :, at] = turned[64:]
            turned = vp.astype(BF).T
            vt[2 * i, :64, at] = turned[:64]
            vt[2 * i + 1, :64, at] = turned[64:]
            vt[2 * i, 64:, at] = ones_rows
            vt[2 * i + 1, 64:, at] = ones_rows
            if j < 2:
                turned = q[:, two].T
                qat[2 * i, :64, at] = turned[:64]
                qat[2 * i + 1, :64, at] = turned[64:]

    for i in range(chunks):
        remote(block(xs, core, i), block(xs, 1 - core, i), sib_s.at[i], sib_r.at[i], here.sibling).wait_recv()
    norm_one(0, 2 * rows)
    project(0)
    project(1)
    relays = [relay(i) for i in range(chunks)]
    for i in range(chunks):
        pl_block = block(xs, 3 - core, i)
        remote(pl_block, pl_block, back_s.at[i], back_r.at[i], here.sibling).wait_recv()
    norm_one(2 * rows, 2 * rows)
    project(2)
    project(3)

    saves = []
    own = pl.ds(pl.multiple_of(core * rows, rows), rows)
    for at, (src, dst) in enumerate(
        ((ka, ka_o), (va, va_o), (kt, kt_o), (h1, h1_o), (wf, wf_o), (xs.at[own, :], xown_o), (lens, len_o))
    ):
        copy = pltpu.make_async_copy(src, dst, out_s.at[at])
        copy.start()
        saves.append(copy)

    size = 512
    keys = 4 * rows

    def attend(h, _):
        for qb in range(2 * rows // size):
            at = slice(qb * size, (qb + 1) * size)
            query = qat[h, :, at]

            def scores(c):
                return dot(ka[h, c * size : (c + 1) * size, :], query)

            ahead = scores(0)
            highest = total = None
            for c in range(keys // size):
                now = ahead
                if c + 1 < keys // size:
                    ahead = scores(c + 1)
                top = jnp.max(now, axis=0, keepdims=True)
                top = top if highest is None else jnp.maximum(highest, top)
                weights = jnp.exp(now - top).astype(BF)
                part = dot(vt[h, :, c * size : (c + 1) * size], weights)
                total = part if total is None else total * jnp.exp(highest - top) + part
                highest = top
            mass = total[64:65]
            result = (total[:64] / mass).astype(BF)
            ctxt[pl.ds(pl.multiple_of(h * 64, 64), 64), at] = result
            high, mid, low = split3(-(highest + jnp.log(mass)))
            index = lax.broadcasted_iota(jnp.int32, (16, size), 0)
            rest = jnp.where(index == 3, 1.0, 0.0)
            for r, term in enumerate((high, mid, low)):
                rest = jnp.where(index == r, term.astype(F32), rest)
            qat[h, 64:80, at] = rest.astype(BF)
        return 0

    lax.fori_loop(0, heads, attend, 0)

    mine = pl.ds(pl.multiple_of(core * half, 128), half)
    own = pl.ds(pl.multiple_of(core * rows, rows), rows)
    other = pl.ds(pl.multiple_of((1 - core) * rows, rows), rows)
    trade = remote(ctxt.at[:, other], ctx.at[mine, :], ctx_s, ctx_r, here.sibling)
    trade.start()
    local = pltpu.make_async_copy(ctxt.at[:, own], ctx.at[mine, :], out_s.at[7])
    local.start()
    for at, (src, dst) in enumerate(((qat, qat_o), (ctxt, ctxt_o))):
        copy = pltpu.make_async_copy(src, dst, out_s.at[8 + at])
        copy.start()
        saves.append(copy)
    local.wait()
    trade.wait()
    copy = pltpu.make_async_copy(ctx, ctx_o, out_s.at[10])
    copy.start()
    saves.append(copy)
    for copy in saves:
        copy.wait()

    @pl.when(jnp.logical_not(here.stays))
    def _():
        for i in range(chunks):
            perm_copy(i).wait_send()
        len_copy().wait_send()

    for copy in moved + relays:
        copy.wait_send()
    if gather:
        for copy in hops + second:
            copy.wait_send()


def attention_forward(dims, tok, length, w, vec):
    shards, rows, width, heads, gather = dims
    half = width // 2
    keys = 4 * rows
    out = [
        ((heads, keys, 128), BF),
        ((heads, keys, 128), BF),
        ((heads, 64, keys), BF),
        ((heads, 128, 2 * rows), BF),
        ((half, 2 * rows), BF),
        ((width, rows), BF),
        ((keys, width), BF),
        ((width, 3 * half), BF),
        ((rows, width), BF),
        ((8, 128), jnp.int32),
        ((VROWS, width), F32),
        ((8, 4 * width), F32),
    ]
    sems = pltpu.SemaphoreType.DMA
    return pl.pallas_call(
        functools.partial(forward_kernel, dims),
        out_shape=tuple(jax.ShapeDtypeStruct(*o) for o in out),
        in_specs=[ANY, VMEM, ANY, VMEM],
        out_specs=tuple([ANY] * 10 + [VMEM] * 2),
        scratch_shapes=[
            pltpu.VMEM((keys, width), BF),
            pltpu.VMEM((width, 3 * half), BF),
            pltpu.VMEM((shards, VROWS, 128), BF),
            pltpu.VMEM((8, 128), jnp.int32),
            pltpu.VMEM((keys, width), BF),
            pltpu.VMEM((heads, keys, 128), BF),
            pltpu.VMEM((heads, keys, 128), BF),
            pltpu.VMEM((heads, 64, keys), BF),
            pltpu.VMEM((heads, 80, keys), BF),
            pltpu.VMEM((heads, 128, 2 * rows), BF),
            pltpu.VMEM((half, 2 * rows), BF),
            pltpu.VMEM((width, rows), BF),
            sems((4,)), sems((4,)), sems((4,)), sems((4,)), sems((4,)), sems((4,)), sems((4,)), sems((4,)),
            sems, sems, sems((12,)), sems((12,)), sems((12,)), sems, sems,
        ],
        compiler_params=pltpu.CompilerParams(
            collective_id=0, has_side_effects=True, vmem_limit_bytes=56 * 2**20
        ),
        name="attention_forward",
    )(tok, length, w, vec)


def feed_kernel(dims, *refs):
    shards, rows, width, heads, _ = dims
    ctx, x, cot, lens, vec, inb, wo_h, wi_h, wf_h = refs[:9]
    out_o, ect_o, gmid_o, gwi_o, gwf_o, gwo_o, vec_o, gib_o = refs[9:17]
    wo, wi, wf, mid, h2, h2t, eo, eot, gh2, acc, in_s = refs[17:]
    here = Place(shards)
    loads = []
    for at, (src, dst) in enumerate(((wo_h, wo), (wi_h, wi), (wf_h, wf))):
        copy = pltpu.make_async_copy(src, dst, in_s.at[at])
        copy.start()
        loads.append(copy)

    def vector(at):
        return vec[at : at + 1, :]

    row_at = lax.broadcasted_iota(jnp.int32, (rows, 1), 0) + here.quarter * rows
    live = row_at < lens[0:1, 0:1]
    e_outer = jnp.where(live, cot[...].astype(F32), 0.0)
    eo[...] = e_outer.astype(BF)
    eot[...] = eo[...].T
    vec_o[...] = jnp.zeros_like(vec_o)
    vec_o[FB : FB + 1, :] = jnp.sum(e_outer, 0, keepdims=True)

    loads[0].wait()
    middle = x[...].astype(F32) + dot(ctx[...].T, wo[...]) + vector(OB)
    mid[...] = middle
    unit, _ = unit_of(middle)
    h2[...] = (unit * vector(LN2G) + vector(LN2B)).astype(BF)
    h2t[:width, :] = h2[...].T
    h2t[width:, :] = jnp.ones((16, rows), BF)
    acc[...] = middle + vector(FB)
    gh2[...] = jnp.zeros_like(gh2)
    loads[1].wait()
    loads[2].wait()

    size = 512

    def part(c, _):
        at = pl.ds(pl.multiple_of(c * size, size), size)
        wic, wfc = wi[:, at], wf[at, :]
        inner = dot(h2[...], wic) + inb[0:1, at]
        square = inner * inner
        swing = jnp.tanh(GELU_C * inner * (1.0 + GELU_K * square))
        active = (0.5 * inner * (1.0 + swing)).astype(BF)
        slope = 0.5 * (1.0 + swing) + 0.5 * inner * (1.0 - swing * swing) * (
            GELU_C * (1.0 + 3.0 * GELU_K * square)
        )
        e_inner = (dot_t(eo[...], wfc) * slope).astype(BF)
        acc[...] += dot(active, wfc)
        gh2[...] += dot_t(e_inner, wic)
        gwf_o[:, at] = dot(eot[...], active).astype(BF)
        grads = dot(h2t[...], e_inner)
        gwi_o[:, at] = grads[:width].astype(BF)
        gib_o[:, at] = grads[width : width + 8]
        return 0

    lax.fori_loop(0, 4 * width // size, part, 0)
    out_o[...] = acc[...].astype(BF)
    unit, inverse = unit_of(mid[...])
    e_norm = gh2[...]
    vec_o[LN2G : LN2G + 1, :] = jnp.sum(e_norm * unit, 0, keepdims=True)
    vec_o[LN2B : LN2B + 1, :] = jnp.sum(e_norm, 0, keepdims=True)
    e_unit = e_norm * vector(LN2G)
    grad_mid = jnp.where(live, cot[...].astype(F32), 0.0) + inverse * (
        e_unit - mean_rows(e_unit) - unit * mean_rows(e_unit * unit)
    )
    gmid_o[...] = grad_mid
    e_branch = grad_mid.astype(BF)
    vec_o[OB : OB + 1, :] = jnp.sum(e_branch.astype(F32), 0, keepdims=True)
    gwo_o[...] = dot(ctx[...], e_branch).astype(BF)
    ect_o[...] = dot_t(wo[...], e_branch).astype(BF)


def feed_forward(dims, ctx, x, cot, lens, vec, inb, wo, wi, wf):
    shards, rows, width, heads, _ = dims
    out = [
        ((rows, width), BF),
        ((width, rows), BF),
        ((rows, width), F32),
        ((width, 4 * width), BF),
        ((width, 4 * width), BF),
        ((width, width), BF),
        ((VROWS, width), F32),
        ((8, 4 * width), F32),
    ]
    return pl.pallas_call(
        functools.partial(feed_kernel, dims),
        out_shape=tuple(jax.ShapeDtypeStruct(*o) for o in out),
        in_specs=[VMEM] * 6 + [ANY] * 3,
        out_specs=tuple([VMEM] * 8),
        scratch_shapes=[
            pltpu.VMEM((width, width), BF),
            pltpu.VMEM((width, 4 * width), BF),
            pltpu.VMEM((4 * width, width), BF),
            pltpu.VMEM((rows, width), F32),
            pltpu.VMEM((rows, width), BF),
            pltpu.VMEM((width + 16, rows), BF),
            pltpu.VMEM((rows, width), BF),
            pltpu.VMEM((width, rows), BF),
            pltpu.VMEM((rows, width), F32),
            pltpu.VMEM((rows, width), F32),
            pltpu.SemaphoreType.DMA((3,)),
        ],
        compiler_params=pltpu.CompilerParams(vmem_limit_bytes=58 * 2**20),
        name="feed_forward",
    )(ctx, x, cot, lens, vec, inb, wo, wi, wf)


def backward_kernel(dims, *refs):
    shards, rows, width, heads, _ = dims
    ect, ka_h, va_h, kt_h, qat_h, ctxt_h, h1_h, wf_h, x, gmid, vec = refs[:11]
    gtok_o, gw_o, vec_o = refs[11:14]
    (
        ka, va, kt, qat, ctxt, h1, wf, dot_all, doat, grads, dk_sum, dv_sum, sib_out, sib_in, side_out, side_in,
        own_sum, gt, load_s, do_s, do_r, sib_s, sib_r, side_s, side_r, perm_s, perm_r,
    ) = refs[14:]
    here = Place(shards)
    core = here.core
    half = width // 2
    keys = 4 * rows
    chunks = 4
    step = rows // chunks

    loads = []
    for at, (src, dst) in enumerate(
        ((ctxt_h, ctxt), (qat_h, qat), (ka_h, ka), (va_h, va), (kt_h, kt), (wf_h, wf), (h1_h, h1))
    ):
        copy = pltpu.make_async_copy(src, dst, load_s.at[at])
        copy.start()
        loads.append(copy)

    greet(here, [here.sibling, here.beside], here.to)

    mine = pl.ds(pl.multiple_of(core * half, 128), half)
    theirs = pl.ds(pl.multiple_of((1 - core) * half, 128), half)
    own = pl.ds(pl.multiple_of(core * rows, rows), rows)
    trade = remote(ect.at[theirs, :], dot_all.at[:, own], do_s.at[0], do_r, here.sibling)
    trade.start()
    local = pltpu.make_async_copy(ect.at[mine, :], dot_all.at[:, own], do_s.at[1])
    local.start()
    local.wait()
    trade.wait()
    loads[0].wait()
    index = lax.broadcasted_iota(jnp.int32, (16, 2 * rows), 0)
    for h in range(heads):
        at = slice(h * 64, (h + 1) * 64)
        e_ctx = dot_all[at, :]
        delta = jnp.sum(e_ctx.astype(F32) * ctxt[at, :].astype(F32), 0, keepdims=True)
        doat[h, :64, :] = e_ctx
        rest = jnp.zeros((16, 2 * rows), F32)
        for r, term in enumerate(split3(delta)):
            rest = jnp.where(index == r, term.astype(F32), rest)
        doat[h, 64:80, :] = rest.astype(BF)
        doat[h, 80:, :] = jnp.zeros((48, 2 * rows), BF)
    for copy in loads[1:]:
        copy.wait()

    size = 512
    parts = 2 * rows // size

    def attend(h, _):
        head = pl.ds(pl.multiple_of(h * 64, 64), 64)
        for qb in range(parts):
            at = slice(qb * size, (qb + 1) * size)
            query, e_ctx = qat[h, :, at], doat[h, :, at]
            e_query = None
            for c in range(keys // size):
                to = slice(c * size, (c + 1) * size)
                weights = jnp.exp(dot(ka[h, to, :], query))
                e_scores = (weights * dot(va[h, to, :], e_ctx)).astype(BF)
                weights = weights.astype(BF)
                e_value = dot_t(e_ctx[:64], weights)
                e_key = dot_t(query[:64], e_scores)
                part = dot(kt[h, :, to], e_scores)
                e_query = part if e_query is None else e_query + part
                if qb > 0:
                    e_value += dv_sum[:, to]
                    e_key += dk_sum[:, to]
                if qb < parts - 1:
                    dv_sum[:, to] = e_value
                    dk_sum[:, to] = e_key
                else:
                    grads[pl.ds(pl.multiple_of(half + h * 64, 64), 64), to] = e_key.astype(BF)
                    grads[pl.ds(pl.multiple_of(2 * half + h * 64, 64), 64), to] = e_value.astype(BF)
            grads[head, at] = (e_query * HEAD_DIM**-0.5).astype(BF)
        return 0

    lax.fori_loop(0, heads, attend, 0)

    def partial_of(j, own_chip):
        at = pl.ds(pl.multiple_of(j * rows, rows), rows)
        if own_chip:
            return dot(wf[...], grads[:, at])
        return dot(wf[:, half:], grads[half:, at])

    sib_out[0] = partial_of(3 - core, False).astype(BF)
    away = remote(sib_out.at[0], sib_in.at[0], sib_s.at[0], sib_r.at[0], here.sibling)
    away.start()
    beside = partial_of(2 + core, False)
    away.wait_recv()
    side_out[...] = (beside + sib_in[0].astype(F32)).astype(BF)
    sides = []
    for i in range(chunks):
        at = slice(i * step, (i + 1) * step)
        copy = remote(side_out.at[:, at], side_in.at[:, at], side_s.at[i], side_r.at[i], here.beside)
        copy.start()
        sides.append(copy)
    sib_out[1] = partial_of(1 - core, True).astype(BF)
    near = remote(sib_out.at[1], sib_in.at[1], sib_s.at[1], sib_r.at[1], here.sibling)
    near.start()
    own_part = partial_of(core, True)
    near.wait_recv()
    own_sum[...] = own_part + sib_in[1].astype(F32)

    gw_o[:, :half] = dot(grads[:half, : 2 * rows], h1[: 2 * rows, :]).T.astype(BF)
    gw_o[:, half : 2 * half] = dot(grads[half : 2 * half, :], h1[...]).T.astype(BF)
    gw_o[:, 2 * half :] = dot(grads[2 * half :, :], h1[...]).T.astype(BF)
    vec_o[...] = jnp.zeros_like(vec_o)

    def row_sums(values):
        wide = values.shape[1]
        folded = values[:, :128].astype(F32)
        for i in range(1, wide // 128):
            folded += values[:, i * 128 : (i + 1) * 128].astype(F32)
        return jnp.sum(folded.T, 0, keepdims=True)

    vec_o[QB : QB + 1, :half] = row_sums(grads[:half, : 2 * rows])
    vec_o[VB : VB + 1, :half] = row_sums(grads[2 * half :, :])

    gain = vec[LN1G : LN1G + 1, :]

    def perm_copy(i):
        at = pl.ds(i * step, step)
        return remote(gt.at[at, :], gtok_o.at[at, :], perm_s.at[i], perm_r.at[i], here.origin)

    def stay_copy(i):
        at = pl.ds(i * step, step)
        return pltpu.make_async_copy(gt.at[at, :], gtok_o.at[at, :], perm_r.at[i])

    gain_sum = shift_sum = None
    for i in range(chunks):
        at = slice(i * step, (i + 1) * step)
        sides[i].wait_recv()
        e_norm = (own_sum[:, at] + side_in[:, at].astype(F32)).T
        unit, inverse = unit_of(x[at, :].astype(F32))
        e_unit = e_norm * gain
        result = gmid[at, :] + inverse * (
            e_unit - mean_rows(e_unit) - unit * mean_rows(e_unit * unit)
        )
        gt[at, :] = result.astype(BF)

        @pl.when(jnp.logical_not(here.stays))
        def _():
            perm_copy(i).start()

        @pl.when(here.stays)
        def _():
            stay_copy(i).start()

        gains = jnp.sum(e_norm * unit, 0, keepdims=True)
        shifts = jnp.sum(e_norm, 0, keepdims=True)
        gain_sum = gains if i == 0 else gain_sum + gains
        shift_sum = shifts if i == 0 else shift_sum + shifts
    vec_o[LN1G : LN1G + 1, :] = gain_sum
    vec_o[LN1B : LN1B + 1, :] = shift_sum

    for copy in [away, near] + sides:
        copy.wait_send()
    for i in range(chunks):
        stay_copy(i).wait()

    @pl.when(jnp.logical_not(here.stays))
    def _():
        for i in range(chunks):
            perm_copy(i).wait_send()


def attention_backward(dims, *args):
    shards, rows, width, heads, _ = dims
    half = width // 2
    keys = 4 * rows
    out = [((rows, width), BF), ((width, 3 * half), BF), ((VROWS, width), F32)]
    sems = pltpu.SemaphoreType.DMA
    return pl.pallas_call(
        functools.partial(backward_kernel, dims),
        out_shape=tuple(jax.ShapeDtypeStruct(*o) for o in out),
        in_specs=[VMEM] + [ANY] * 7 + [VMEM] * 3,
        out_specs=(ANY, VMEM, VMEM),
        scratch_shapes=[
            pltpu.VMEM((heads, keys, 128), BF),
            pltpu.VMEM((heads, keys, 128), BF),
            pltpu.VMEM((heads, 64, keys), BF),
            pltpu.VMEM((heads, 128, 2 * rows), BF),
            pltpu.VMEM((half, 2 * rows), BF),
            pltpu.VMEM((keys, width), BF),
            pltpu.VMEM((width, 3 * half), BF),
            pltpu.VMEM((half, 2 * rows), BF),
            pltpu.VMEM((heads, 128, 2 * rows), BF),
            pltpu.VMEM((3 * half, keys), BF),
            pltpu.VMEM((64, keys), F32),
            pltpu.VMEM((64, keys), F32),
            pltpu.VMEM((2, width, rows), BF),
            pltpu.VMEM((2, width, rows), BF),
            pltpu.VMEM((width, rows), BF),
            pltpu.VMEM((width, rows), BF),
            pltpu.VMEM((width, rows), F32),
            pltpu.VMEM((rows, width), BF),
            sems((7,)), sems((2,)), sems, sems((2,)), sems((2,)), sems((4,)), sems((4,)), sems((4,)), sems((4,)),
        ],
        compiler_params=pltpu.CompilerParams(
            collective_id=1, has_side_effects=True, vmem_limit_bytes=58 * 2**20
        ),
        name="attention_backward",
    )(*args)


def on_device(
    tokens, ln1_gain, ln1_shift, w_qkv, q_bias, v_bias, w_out, out_bias, ln2_gain, ln2_shift, w_in, in_bias,
    w_fin, fin_bias, cotangent, lengths, n_seq, shards,
):
    _, rows, width = tokens.shape
    heads = width // HEAD_DIM // 2
    half = width // 2
    share = width // shards
    gather = shards == 8
    dims = (shards, rows, width, heads, gather)
    axes = ("seq", "shard")
    there = relocation(n_seq, shards)
    back = [(b, a) for a, b in there]
    core = lax.rem(lax.axis_index("shard"), 2)

    packed = jnp.concatenate(
        [v.reshape(-1, share) for v in (ln1_gain, ln1_shift, q_bias, v_bias, out_bias, ln2_gain, ln2_shift, fin_bias, in_bias)]
    )
    length = jnp.broadcast_to(lengths.reshape(1, 1), (8, 128))
    if gather:
        vec = jnp.pad(packed, ((0, VROWS - VECS), (0, 128 - share)))
        w_here = w_qkv
    else:
        every = lax.all_gather(packed, "shard", axis=1, tiled=True)
        vec = jnp.pad(every, ((0, VROWS - VECS), (0, 0)))
        full_w = lax.all_gather(w_qkv, "shard", axis=0, tiled=True)
        w_here = lax.dynamic_index_in_dim(
            full_w.reshape(width, 3, 2, half), core, 2, keepdims=False
        ).reshape(width, 3 * half)
    (ka, va, kt, qat, ctxt, ctx, h1, wf, x, lens, vecs, inb) = attention_forward(
        dims, tokens.reshape(rows, width), length, w_here, vec
    )
    if not gather:
        inb = jnp.broadcast_to(
            lax.all_gather(in_bias, "shard", axis=0, tiled=True).astype(F32)[None], (8, 4 * width)
        )
    full_wo = lax.all_gather(w_out, "shard", axis=0, tiled=True)
    full_wi = lax.all_gather(w_in, "shard", axis=0, tiled=True)
    full_wf = lax.all_gather(w_fin, "shard", axis=0, tiled=True)
    cot = lax.ppermute(cotangent.reshape(rows, width), axes, there)
    out, ect, gmid, gwi, gwf, gwo, vec_two, gib = feed_forward(
        dims, ctx, x, cot, lens, vecs, inb, full_wo, full_wi, full_wf
    )
    output = lax.ppermute(out, axes, back).reshape(tokens.shape)
    gtok, gw, vec_one = attention_backward(
        dims, ect, ka, va, kt, qat, ctxt, h1, wf, x, gmid, vecs
    )

    def total(grad, dim):
        part = lax.psum_scatter(grad, "shard", scatter_dimension=dim, tiled=True)
        return lax.psum(part, "seq").astype(F32)

    total_wi = total(gwi, 0)
    total_wf = total(gwf, 1).T
    total_wo = total(gwo, 0)
    wide = jnp.zeros((width, 3, 2, half), BF)
    wide = lax.dynamic_update_index_in_dim(wide, gw.reshape(width, 3, half), core, 2)
    total_w = total(wide.reshape(width, 3 * width), 0)

    halves = jnp.zeros((2, 2, half), F32)
    halves = lax.dynamic_update_index_in_dim(halves, vec_one[QB : VB + 1, :half], core, 1).reshape(2, width)
    sums = jnp.concatenate(
        (vec_one[:QB], halves, vec_two[OB:IB], gib[0].reshape(4, width))
    )
    sums = lax.psum(sums, axes)
    s = lax.axis_index("shard")
    mine = lax.dynamic_slice_in_dim(sums[:IB], s * share, share, 1)
    total_ib = lax.dynamic_slice_in_dim(sums[IB:].reshape(-1), s * 4 * share, 4 * share, 0)
    return (
        output,
        gtok.reshape(tokens.shape),
        mine[LN1G],
        mine[LN1B],
        total_w,
        mine[QB],
        mine[VB],
        total_wo,
        mine[OB],
        mine[LN2G],
        mine[LN2B],
        total_wi,
        total_ib,
        total_wf,
        mine[FB],
    )


def solution(mesh):
    vector, matrix, rows = P("shard"), P("shard", None), P("shard", "seq", None)
    return jax.shard_map(
        functools.partial(on_device, n_seq=mesh.shape["seq"], shards=mesh.shape["shard"]),
        mesh=mesh,
        in_specs=(
            rows, vector, vector, matrix, vector, vector, matrix, vector, vector, vector, matrix, vector,
            matrix, vector, rows, vector,
        ),
        out_specs=(
            rows, rows, vector, vector, matrix, vector, vector, matrix, vector, vector, vector, matrix,
            vector, matrix, vector,
        ),
        check_vma=False,
    )
```

```python
import functools
import math

import jax
import jax.numpy as jnp
from jax import lax
from jax.experimental import pallas as pl
from jax.experimental.pallas import tpu as pltpu
from jax.sharding import PartitionSpec as P

HEAD_DIM = 64
EPS = 1e-05
GELU_C = 0.7978845608028654
GELU_K = 0.044715
MASKED = -1e30

BF = jnp.bfloat16
F32 = jnp.float32
MESH = pl.DeviceIdType.MESH
VMEM = pl.BlockSpec(memory_space=pltpu.VMEM)
ANY = pl.BlockSpec(memory_space=pl.ANY)

LN1G, LN1B, QB, VB, OB, LN2G, LN2B, FB, IB = range(9)
VECS = 12
VROWS = 16


def dot(left, right):
    return jnp.dot(left, right, preferred_element_type=F32)


def dot_t(left, right):
    return lax.dot_general(left, right, (((1,), (1,)), ((), ())), preferred_element_type=F32)


def mean_rows(values):
    return jnp.mean(values, -1, keepdims=True)


def unit_of(values):
    centred = values - mean_rows(values)
    inverse = lax.rsqrt(mean_rows(centred * centred) + EPS)
    return centred * inverse, inverse


def split3(values):
    high = values.astype(BF)
    rest = values - high.astype(F32)
    mid = rest.astype(BF)
    low = (rest - mid.astype(F32)).astype(BF)
    return high, mid, low


class Place:
    def __init__(self):
        q = lax.axis_index("seq")
        s = lax.axis_index("shard")
        self.q, self.s = q, s
        self.core = core = lax.rem(s, 2)
        self.to = (2 * core + lax.rem(q, 2), s - core + q // 2)
        side = lax.rem(q, 2)
        self.quarter = side + 2 * core
        self.origin = (self.quarter, s - core + q // 2)
        self.stays = q // 2 == core
        self.sibling = (q, s + 1 - 2 * core)
        self.beside = (q + 1 - 2 * side, s)
        self.quarters = [side, side + 2, 1 - side, 3 - side]


def relocation(n_seq, shards):
    return [
        (q * shards + s, (2 * (s % 2) + q % 2) * shards + s - s % 2 + q // 2)
        for q in range(n_seq)
        for s in range(shards)
    ]


def remote(src, dst, send, recv, device):
    return pltpu.make_async_remote_copy(
        src_ref=src, dst_ref=dst, send_sem=send, recv_sem=recv, device_id=device, device_id_type=MESH
    )


def greet(here, devices, mover):
    barrier = pltpu.get_barrier_semaphore()
    for device in devices:
        pl.semaphore_signal(barrier, inc=1, device_id=device, device_id_type=MESH)

    @pl.when(jnp.logical_not(here.stays))
    def _():
        pl.semaphore_signal(barrier, inc=1, device_id=mover, device_id_type=MESH)
        pl.semaphore_wait(barrier, len(devices) + 1)

    @pl.when(here.stays)
    def _():
        pl.semaphore_wait(barrier, len(devices))


def forward_kernel(dims, *refs):
    shards, rows, width, heads, gather = dims
    n_more = 3 if gather else 0
    tok, length_in, w_in, vec_in = refs[:4]
    shares = refs[4 : 4 + n_more]
    refs = refs[4 + n_more :]
    (ka_o, va_o, kt_o, qat_o, ctxt_o, ctx_o, h1_o, wf_o, xown_o, len_o, vec_o, inb_o) = refs[:12]
    wholes = refs[12 : 12 + n_more]
    refs = refs[12 + n_more :]
    (
        xs, wf, vg, lens, h1, ka, va, kt, vt, qat, ctxt, ctx,
        perm_s, perm_r, sib_s, sib_r, side_s, side_r, back_s, back_r,
        len_s, len_r, w_s, w_r, out_s, ctx_s, ctx_r, all_s, all_r, all_l,
    ) = refs
    here = Place()
    core, s = here.core, here.s
    half = width // 2
    share = width // shards
    chunks = 4
    step = rows // chunks
    x_bit, y_bit = lax.rem(s // 2, 2), lax.rem(s // 4, 2)
    shard_x, shard_y = s + 2 - 4 * x_bit, s + 4 - 8 * y_bit
    shard_d = shard_x + 4 - 8 * y_bit
    partner_x, partner_y = (here.q, shard_x), (here.q, shard_y)

    partners = [here.sibling, here.beside] + ([partner_x, partner_y] if gather else [])
    greet(here, partners, here.origin)

    to_core = here.q // 2

    def block(ref, j, i):
        return ref.at[pl.ds(pl.multiple_of(j * rows + i * step, step), step), :]

    def perm_copy(i):
        return remote(
            tok.at[pl.ds(i * step, step), :], block(xs, to_core, i), perm_s.at[i], perm_r.at[i], here.to
        )

    def len_copy():
        return remote(length_in, lens, len_s, len_r, here.to)

    @pl.when(jnp.logical_not(here.stays))
    def _():
        for i in range(chunks):
            perm_copy(i).start()
        len_copy().start()

    @pl.when(here.stays)
    def _():
        for i in range(chunks):
            pltpu.make_async_copy(
                tok.at[pl.ds(i * step, step), :], block(xs, to_core, i), perm_r.at[i]
            ).start()
        pltpu.make_async_copy(length_in, lens, len_r).start()

    w_copies = []
    if gather:
        def columns(j, which):
            return pl.ds(pl.multiple_of(j * width + which * half, 128), half)

        mine = pl.ds(pl.multiple_of(s * share, share), share)
        for j in range(3):
            copy = remote(
                w_in.at[:, columns(j, 1 - core)], wf.at[mine, pl.ds(j * half, half)],
                w_s.at[j], w_r.at[j], here.sibling,
            )
            copy.start()
            w_copies.append(copy)
            copy = pltpu.make_async_copy(
                w_in.at[:, columns(j, core)], wf.at[mine, pl.ds(j * half, half)], w_s.at[4 + j]
            )
            copy.start()
            w_copies.append(copy)
        copy = remote(vec_in, vg.at[s], w_s.at[3], w_r.at[3], here.sibling)
        copy.start()
        w_copies.append(copy)
        copy = pltpu.make_async_copy(vec_in, vg.at[s], w_s.at[7])
        copy.start()
        w_copies.append(copy)
    else:
        copy = pltpu.make_async_copy(w_in, wf, w_s.at[0])
        copy.start()
        w_copies.append(copy)

    def w_move(at):
        src, count, device = (
            (s - core, 2, partner_x),
            (s - core, 2, partner_y),
            (shard_x - core, 1, partner_y),
            (shard_y - core + 1, 1, partner_x),
        )[at]
        part = wf.at[pl.ds(pl.multiple_of(src * share, share), count * share), :]
        return remote(part, part, w_s.at[8 + at], w_r.at[8 + at], device)

    def v_move(at):
        src, device = ((s, partner_x), (s, partner_y), (shard_x, partner_y))[at]
        part = vg.at[pl.ds(src - core, 2)]
        return remote(part, part, w_s.at[12 + at], w_r.at[12 + at], device)

    def receive(i):
        pltpu.make_async_copy(tok.at[pl.ds(i * step, step), :], block(xs, core, i), perm_r.at[i]).wait()
        sib = remote(block(xs, core, i), block(xs, core, i), sib_s.at[i], sib_r.at[i], here.sibling)
        side = remote(block(xs, core, i), block(xs, 2 + core, i), side_s.at[i], side_r.at[i], here.beside)
        side.start()
        sib.start()
        return [sib, side]

    def relay(i):
        block_in = block(xs, 2 + core, i)
        remote(block_in, block_in, side_s.at[i], side_r.at[i], here.beside).wait_recv()
        copy = remote(block_in, block_in, back_s.at[i], back_r.at[i], here.sibling)
        copy.start()
        return copy

    def rows_of(k, shard):
        count = shares[k].shape[0]
        return pl.ds(pl.multiple_of(shard * count, count), count)

    def piece(k, shard, part=None):
        cut = shares[k].shape[1] // 2
        if part is None:
            return wholes[k].at[rows_of(k, shard), :]
        return wholes[k].at[rows_of(k, shard), part * cut : (part + 1) * cut]

    def pass_on(k, slot, src, dst, device):
        return remote(src, dst, all_s.at[k, slot], all_r.at[k, slot], device)

    def got(k, slot, ref):
        pass_on(k, slot, ref, ref, here.sibling).wait_recv()

    def move(k, slot):
        src, device = (
            (None, partner_x),
            (None, partner_y),
            (None, here.sibling),
            ((shard_x, 0), partner_y),
            ((shard_x,), here.sibling),
            ((shard_y, 1), partner_x),
            ((shard_y,), here.sibling),
            ((shard_d,), here.sibling),
        )[slot]
        if src is None:
            return pass_on(k, slot, shares[k], piece(k, s), device)
        return pass_on(k, slot, piece(k, *src), piece(k, *src), device)

    def share_out(k):
        for slot in range(3):
            move(k, slot).start()
        pltpu.make_async_copy(shares[k], piece(k, s), all_l.at[k]).start()

    def from_x(k):
        got(k, 0, piece(k, shard_x))
        move(k, 3).start()
        move(k, 4).start()

    def from_y(k):
        got(k, 1, piece(k, shard_y))
        move(k, 5).start()
        move(k, 6).start()

    def from_far(k):
        got(k, 3, piece(k, shard_d, 0))
        got(k, 5, piece(k, shard_d, 1))
        move(k, 7).start()

    def all_here(k):
        flip = 1 - 2 * core
        for slot, shard in ((2, s), (4, shard_x), (6, shard_y), (7, shard_d)):
            got(k, slot, piece(k, shard + flip))
        pltpu.make_async_copy(shares[k], piece(k, s), all_l.at[k]).wait()

    moved = []
    if gather:
        for copy in w_copies:
            copy.wait()
        for at in range(2):
            w_move(at).start()
            v_move(at).start()
        for k in range(n_more):
            share_out(k)
    moved += receive(0)
    moved += receive(1)
    if gather:
        w_move(0).wait_recv()
        v_move(0).wait_recv()
        w_move(2).start()
        v_move(2).start()
        w_move(1).wait_recv()
        v_move(1).wait_recv()
        w_move(3).start()
    moved += receive(2)
    moved += receive(3)

    def norm_one(first, count):
        def body(i, _):
            at = pl.ds(pl.multiple_of(first + i * 256, 256), 256)
            unit, _ = unit_of(xs[at, :].astype(F32))
            h1[at, :] = (unit * vec_o[LN1G : LN1G + 1, :] + vec_o[LN1B : LN1B + 1, :]).astype(BF)
            return 0

        lax.fori_loop(0, count // 256, body, 0)

    if gather:
        w_move(2).wait_recv()
        w_move(3).wait_recv()
        v_move(2).wait_recv()
        for i in range(shards):
            part = vg[i].astype(F32)
            vec_o[:, i * share : (i + 1) * share] = part[:, :share]
            for r in range(4):
                at = (4 * i + r) * share
                inb_o[:, at : at + share] = jnp.broadcast_to(
                    part[IB + r : IB + r + 1, :share], (8, share)
                )
    else:
        for copy in w_copies:
            copy.wait()
        vec_o[...] = vec_in[...].astype(F32)
        inb_o[...] = jnp.zeros_like(inb_o)

    pltpu.make_async_copy(length_in, lens, len_r).wait()
    length = lens[0:1, 0:1]
    lane = lax.broadcasted_iota(jnp.int32, (rows, 128), 1)
    row_at = lax.broadcasted_iota(jnp.int32, (rows, 128), 0)
    lower = lane < HEAD_DIM
    ones_rows = (lax.broadcasted_iota(jnp.int32, (16, rows), 0) == 0).astype(BF)
    q_rest = (lax.broadcasted_iota(jnp.int32, (64, 2 * rows), 0) == 3).astype(BF)
    for h in range(heads):
        qat[h, HEAD_DIM:, :] = q_rest

    def bias_half(at):
        full = vec_o[at : at + 1, :]
        return jnp.where(core == 0, full[:, :half], full[:, half:])

    def project(j):
        at = slice(j * rows, (j + 1) * rows)
        norm = h1[at, :]
        dead = jnp.where(here.quarters[j] * rows + row_at < length, 0.0, MASKED)
        k_rest = jnp.where(lane == HEAD_DIM + 3, dead, jnp.where(lane < HEAD_DIM + 3, 1.0, 0.0))
        v_rest = jnp.where(lane < HEAD_DIM + 3, -1.0, 0.0)
        if j < 2:
            q = (dot(norm, wf[:, :half]) + bias_half(QB)).astype(BF) * BF(HEAD_DIM**-0.5)
        k = dot(norm, wf[:, half : 2 * half])
        v = dot(norm, wf[:, 2 * half :]) + bias_half(VB)
        for i in range(heads // 2):
            two = slice(i * 128, (i + 1) * 128)
            kp, vp = k[:, two], v[:, two]
            ka[2 * i, at, :] = jnp.where(lower, kp, k_rest).astype(BF)
            ka[2 * i + 1, at, :] = jnp.where(lower, pltpu.roll(kp, 64, 1), k_rest).astype(BF)
            va[2 * i, at, :] = jnp.where(lower, vp, v_rest).astype(BF)
            va[2 * i + 1, at, :] = jnp.where(lower, pltpu.roll(vp, 64, 1), v_rest).astype(BF)
            turned = kp.astype(BF).T
            kt[2 * i, :, at] = turned[:64]
            kt[2 * i + 1, :, at] = turned[64:]
            turned = vp.astype(BF).T
            vt[2 * i, :64, at] = turned[:64]
            vt[2 * i + 1, :64, at] = turned[64:]
            vt[2 * i, 64:, at] = ones_rows
            vt[2 * i + 1, 64:, at] = ones_rows
            if j < 2:
                turned = q[:, two].T
                qat[2 * i, :64, at] = turned[:64]
                qat[2 * i + 1, :64, at] = turned[64:]

    for i in range(chunks):
        remote(block(xs, core, i), block(xs, 1 - core, i), sib_s.at[i], sib_r.at[i], here.sibling).wait_recv()
    norm_one(0, 2 * rows)
    project(0)
    project(1)
    if gather:
        from_x(0)
        from_y(0)
    relays = [relay(i) for i in range(chunks)]
    for i in range(chunks):
        pl_block = block(xs, 3 - core, i)
        remote(pl_block, pl_block, back_s.at[i], back_r.at[i], here.sibling).wait_recv()
    norm_one(2 * rows, 2 * rows)
    project(2)
    project(3)
    if gather:
        from_x(1)
        from_y(1)

    saves = []
    own = pl.ds(pl.multiple_of(core * rows, rows), rows)
    for at, (src, dst) in enumerate(
        ((ka, ka_o), (va, va_o), (kt, kt_o), (h1, h1_o), (wf, wf_o), (xs.at[own, :], xown_o), (lens, len_o))
    ):
        copy = pltpu.make_async_copy(src, dst, out_s.at[at])
        copy.start()
        saves.append(copy)

    size = 512
    keys = 4 * rows

    def attend(h, _):
        for qb in range(2 * rows // size):
            at = slice(qb * size, (qb + 1) * size)
            query = qat[h, :, at]

            def scores(c):
                return dot(ka[h, c * size : (c + 1) * size, :], query)

            ahead = scores(0)
            highest = total = None
            for c in range(keys // size):
                now = ahead
                if c + 1 < keys // size:
                    ahead = scores(c + 1)
                top = jnp.max(now, axis=0, keepdims=True)
                top = top if highest is None else jnp.maximum(highest, top)
                weights = jnp.exp(now - top).astype(BF)
                part = dot(vt[h, :, c * size : (c + 1) * size], weights)
                total = part if total is None else total * jnp.exp(highest - top) + part
                highest = top
            mass = total[64:65]
            result = (total[:64] / mass).astype(BF)
            ctxt[pl.ds(pl.multiple_of(h * 64, 64), 64), at] = result
            high, mid, low = split3(-(highest + jnp.log(mass)))
            index = lax.broadcasted_iota(jnp.int32, (16, size), 0)
            rest = jnp.where(index == 3, 1.0, 0.0)
            for r, term in enumerate((high, mid, low)):
                rest = jnp.where(index == r, term.astype(F32), rest)
            qat[h, 64:80, at] = rest.astype(BF)

        if gather:
            @pl.when(h == 0)
            def _():
                from_far(0)

            @pl.when(h == heads // 3)
            def _():
                from_x(2)
                from_y(2)

            @pl.when(h == heads - 2)
            def _():
                from_far(1)

            @pl.when(h == heads - 1)
            def _():
                from_far(2)

        return 0

    lax.fori_loop(0, heads, attend, 0)

    mine = pl.ds(pl.multiple_of(core * half, 128), half)
    own = pl.ds(pl.multiple_of(core * rows, rows), rows)
    other = pl.ds(pl.multiple_of((1 - core) * rows, rows), rows)
    trade = remote(ctxt.at[:, other], ctx.at[mine, :], ctx_s, ctx_r, here.sibling)
    trade.start()
    local = pltpu.make_async_copy(ctxt.at[:, own], ctx.at[mine, :], out_s.at[7])
    local.start()
    for at, (src, dst) in enumerate(((qat, qat_o), (ctxt, ctxt_o))):
        copy = pltpu.make_async_copy(src, dst, out_s.at[8 + at])
        copy.start()
        saves.append(copy)
    local.wait()
    trade.wait()
    copy = pltpu.make_async_copy(ctx, ctx_o, out_s.at[10])
    copy.start()
    saves.append(copy)
    for copy in saves:
        copy.wait()

    @pl.when(jnp.logical_not(here.stays))
    def _():
        for i in range(chunks):
            perm_copy(i).wait_send()
        len_copy().wait_send()

    for copy in moved + relays:
        copy.wait_send()
    if gather:
        for k in range(n_more):
            all_here(k)
            for slot in range(8):
                move(k, slot).wait_send()
        for at in range(4):
            w_move(at).wait_send()
        for at in range(3):
            v_move(at).wait_send()


def attention_forward(dims, tok, length, w, vec, *shares):
    shards, rows, width, heads, gather = dims
    half = width // 2
    keys = 4 * rows
    out = [
        ((heads, keys, 128), BF),
        ((heads, keys, 128), BF),
        ((heads, 64, keys), BF),
        ((heads, 128, 2 * rows), BF),
        ((half, 2 * rows), BF),
        ((width, rows), BF),
        ((keys, width), BF),
        ((width, 3 * half), BF),
        ((rows, width), BF),
        ((8, 128), jnp.int32),
        ((VROWS, width), F32),
        ((8, 4 * width), F32),
    ] + [((shards * share.shape[0], share.shape[1]), BF) for share in shares]
    sems = pltpu.SemaphoreType.DMA
    return pl.pallas_call(
        functools.partial(forward_kernel, dims),
        out_shape=tuple(jax.ShapeDtypeStruct(*o) for o in out),
        in_specs=[ANY, VMEM, ANY, VMEM] + [ANY] * len(shares),
        out_specs=tuple([ANY] * 10 + [VMEM] * 2 + [ANY] * len(shares)),
        scratch_shapes=[
            pltpu.VMEM((keys, width), BF),
            pltpu.VMEM((width, 3 * half), BF),
            pltpu.VMEM((shards, VROWS, 128), BF),
            pltpu.VMEM((8, 128), jnp.int32),
            pltpu.VMEM((keys, width), BF),
            pltpu.VMEM((heads, keys, 128), BF),
            pltpu.VMEM((heads, keys, 128), BF),
            pltpu.VMEM((heads, 64, keys), BF),
            pltpu.VMEM((heads, 80, keys), BF),
            pltpu.VMEM((heads, 128, 2 * rows), BF),
            pltpu.VMEM((half, 2 * rows), BF),
            pltpu.VMEM((width, rows), BF),
            sems((4,)), sems((4,)), sems((4,)), sems((4,)), sems((4,)), sems((4,)), sems((4,)), sems((4,)),
            sems, sems, sems((16,)), sems((16,)), sems((12,)), sems, sems,
            sems((3, 8)), sems((3, 8)), sems((3,)),
        ],
        compiler_params=pltpu.CompilerParams(
            collective_id=0, has_side_effects=True, vmem_limit_bytes=56 * 2**20
        ),
        name="attention_forward",
    )(tok, length, w, vec, *shares)


def feed_kernel(dims, *refs):
    shards, rows, width, heads, blocked = dims
    ctx, x, cot, lens, vec, inb, wo_h, wi_h, wf_h = refs[:9]
    out_o, ect_o, gmid_o, gwi_o, gwf_o, gwo_o, vec_o, gib_o = refs[9:17]
    wo, wi, wf, mid, h2, h2t, eo, eot, gh2, acc, in_s = refs[17:]
    here = Place()
    loads = []
    for at, (src, dst) in enumerate(((wo_h, wo), (wi_h, wi), (wf_h, wf))):
        copy = pltpu.make_async_copy(src, dst, in_s.at[at])
        copy.start()
        loads.append(copy)

    def vector(at):
        return vec[at : at + 1, :]

    row_at = lax.broadcasted_iota(jnp.int32, (rows, 1), 0) + here.quarter * rows
    live = row_at < lens[0:1, 0:1]
    e_outer = jnp.where(live, cot[...].astype(F32), 0.0)
    eo[...] = e_outer.astype(BF)
    eot[...] = eo[...].T
    vec_o[...] = jnp.zeros_like(vec_o)
    vec_o[FB : FB + 1, :] = jnp.sum(e_outer, 0, keepdims=True)

    loads[0].wait()
    middle = x[...].astype(F32) + dot(ctx[...].T, wo[...]) + vector(OB)
    mid[...] = middle
    unit, _ = unit_of(middle)
    h2[...] = (unit * vector(LN2G) + vector(LN2B)).astype(BF)
    h2t[:width, :] = h2[...].T
    h2t[width:, :] = jnp.ones((16, rows), BF)
    acc[...] = middle + vector(FB)
    gh2[...] = jnp.zeros_like(gh2)
    loads[1].wait()
    loads[2].wait()

    size = width
    share, half = width // shards, width // 2

    def part(c, _):
        at = pl.ds(pl.multiple_of(c * size, size), size)
        wic, wfc = wi[:, at], wf[at, :]
        inner = dot(h2[...], wic) + inb[0:1, at]
        square = inner * inner
        swing = jnp.tanh(GELU_C * inner * (1.0 + GELU_K * square))
        active = (0.5 * inner * (1.0 + swing)).astype(BF)
        slope = 0.5 * (1.0 + swing) + 0.5 * inner * (1.0 - swing * swing) * (
            GELU_C * (1.0 + 3.0 * GELU_K * square)
        )
        e_inner = (dot_t(eo[...], wfc) * slope).astype(BF)
        acc[...] += dot(active, wfc)
        gh2[...] += dot_t(e_inner, wic)
        grads = dot(eot[...], active).astype(BF)
        if blocked:
            for core in range(2):
                for ab in range(2):
                    gwf_o[c // 2, lax.rem(c, 2), core, ab] = grads[
                        ab * half : (ab + 1) * half, core * half : (core + 1) * half
                    ]
        else:
            gwf_o[:, at] = grads
        grads = dot(h2t[...], e_inner)
        if blocked:
            to = pl.ds(pl.multiple_of(lax.rem(c, 2) * size, size), size)
            for i in range(shards):
                gwi_o[i // 4, i // 2 % 2, i % 2, c // 2, :, to] = grads[i * share : (i + 1) * share].astype(BF)
        else:
            gwi_o[:, at] = grads[:width].astype(BF)
        gib_o[:, at] = grads[width : width + 8]
        return 0

    lax.fori_loop(0, 4 * width // size, part, 0)
    out_o[...] = acc[...].astype(BF)
    unit, inverse = unit_of(mid[...])
    e_norm = gh2[...]
    vec_o[LN2G : LN2G + 1, :] = jnp.sum(e_norm * unit, 0, keepdims=True)
    vec_o[LN2B : LN2B + 1, :] = jnp.sum(e_norm, 0, keepdims=True)
    e_unit = e_norm * vector(LN2G)
    grad_mid = jnp.where(live, cot[...].astype(F32), 0.0) + inverse * (
        e_unit - mean_rows(e_unit) - unit * mean_rows(e_unit * unit)
    )
    gmid_o[...] = grad_mid
    e_branch = grad_mid.astype(BF)
    vec_o[OB : OB + 1, :] = jnp.sum(e_branch.astype(F32), 0, keepdims=True)
    grads = dot(ctx[...], e_branch).astype(BF)
    if blocked:
        for i in range(shards):
            for ab in range(2):
                gwo_o[i // 4, i // 2 % 2, i % 2, ab] = grads[
                    i * share : (i + 1) * share, ab * half : (ab + 1) * half
                ]
    else:
        gwo_o[...] = grads
    ect_o[...] = dot_t(wo[...], e_branch).astype(BF)


def grad_blocks(dims):
    shards, rows, width, heads, blocked = dims
    if not blocked:
        return [(width, 4 * width), (width, 4 * width), (width, width)]
    share, half = width // shards, width // 2
    return [(2, 2, 2, 2) + part for part in ((half, 4 * share), (share, 2 * width), (share, half))]


def feed_forward(dims, ctx, x, cot, lens, vec, inb, wo, wi, wf):
    shards, rows, width, heads, _ = dims
    blocks = grad_blocks(dims)
    out = [
        ((rows, width), BF),
        ((width, rows), BF),
        ((rows, width), F32),
        (blocks[1], BF),
        (blocks[0], BF),
        (blocks[2], BF),
        ((VROWS, width), F32),
        ((8, 4 * width), F32),
    ]
    return pl.pallas_call(
        functools.partial(feed_kernel, dims),
        out_shape=tuple(jax.ShapeDtypeStruct(*o) for o in out),
        in_specs=[VMEM] * 6 + [ANY] * 3,
        out_specs=tuple([VMEM] * 8),
        scratch_shapes=[
            pltpu.VMEM((width, width), BF),
            pltpu.VMEM((width, 4 * width), BF),
            pltpu.VMEM((4 * width, width), BF),
            pltpu.VMEM((rows, width), F32),
            pltpu.VMEM((rows, width), BF),
            pltpu.VMEM((width + 16, rows), BF),
            pltpu.VMEM((rows, width), BF),
            pltpu.VMEM((width, rows), BF),
            pltpu.VMEM((rows, width), F32),
            pltpu.VMEM((rows, width), F32),
            pltpu.SemaphoreType.DMA((3,)),
        ],
        compiler_params=pltpu.CompilerParams(vmem_limit_bytes=58 * 2**20),
        name="feed_forward",
    )(ctx, x, cot, lens, vec, inb, wo, wi, wf)


class Reduction:
    def __init__(self, here, refs, whole=None):
        self.mine, self.near, self.got, self.last, self.seq_in, self.done, self.send, self.recv = refs
        self.here, self.whole = here, whole
        s, q, core = here.s, here.q, here.core
        self.x, self.y = lax.rem(s // 2, 2), lax.rem(s // 4, 2)
        self.side, self.high = lax.rem(q, 2), q // 2
        self.to_x = (q, s + 2 - 4 * self.x)
        self.to_y = (q, s + 4 - 8 * self.y)
        self.to_far = (q + 2 - 4 * self.high, s)
        self.own = self.mine.at[self.y, self.x]

    @staticmethod
    def scratch(r, c, core):
        sems = pltpu.SemaphoreType.DMA
        return [
            pltpu.VMEM((2, 2, 2, r, c), BF),
            pltpu.VMEM((2, 2, 2, r, c) if core else (16, 128), BF),
            pltpu.VMEM((2, 2, r, c), BF),
            pltpu.VMEM((2, r, c), BF),
            pltpu.VMEM((r + r // 2, c), BF),
            pltpu.VMEM((2, r, c), BF),
            sems((10,)),
            sems((9,)),
        ]

    def quarter(self, ref, which):
        r = ref.shape[0] // 2
        return ref.at[pl.ds(pl.multiple_of(which * r, r), r), :]

    def copy(self, at):
        x, y, side, high, own, done = self.x, self.y, self.side, self.high, self.own, self.done
        mine, got, last = self.mine, self.got, self.last
        r = own.shape[1]
        if at == 0:
            src, dst, device = self.whole.at[:, :, 1 - self.here.core], self.near, self.here.sibling
        elif at == 1:
            src, dst, device = mine.at[:, 1 - x, 0], got.at[0], self.to_x
        elif at == 2:
            src, dst, device = mine.at[1 - y, :, 1], got.at[1], self.to_y
        elif at == 3:
            src, dst, device = mine.at[1 - y, x, 0], last.at[0], self.to_y
        elif at == 4:
            src, dst, device = mine.at[y, 1 - x, 1], last.at[1], self.to_x
        elif at == 5:
            src, dst, device = own.at[1 - side], self.seq_in.at[:r, :], self.here.beside
        elif at == 6:
            src, dst, device = self.quarter(own.at[side], 1 - high), self.seq_in.at[r:, :], self.to_far
        elif at == 7:
            src = dst = self.quarter(done.at[side], high)
            device = self.to_far
        else:
            src = dst = done.at[side]
            device = self.here.beside
        return remote(src, dst, self.send.at[at], self.recv.at[at], device)

    def load(self):
        return pltpu.make_async_copy(self.whole.at[:, :, self.here.core], self.mine, self.send.at[9])

    def arrived(self, at):
        done, side, high = self.done, self.side, self.high
        if at == 7:
            ref = self.quarter(done.at[side], 1 - high)
        elif at == 8:
            ref = done.at[1 - side]
        else:
            self.copy(at).wait_recv()
            return
        remote(ref, ref, self.send.at[at], self.recv.at[at], self.here.beside).wait_recv()

    def add(self, into, other, out=None):
        r = into.shape[-2]
        step = 96 if into.shape[-1] > 512 and r % 96 == 0 else r
        out = into if out is None else out

        def body(i, _):
            at = pl.ds(pl.multiple_of(i * step, step), step)
            out[at, :] = into[at, :] + other[at, :]
            return 0

        lax.fori_loop(0, r // step, body, 0)

    def phase(self, number):
        x, y = self.x, self.y
        if number == 0:
            self.load().start()
            self.copy(0).start()
        elif number == 1:
            if self.whole is not None:
                self.load().wait()
                self.arrived(0)
                for j in range(2):
                    for i in range(2):
                        for ab in range(2):
                            self.add(self.mine.at[j, i, ab], self.near.at[j, i, ab])
            self.copy(1).start()
            self.copy(2).start()
        elif number == 2:
            self.arrived(1)
            self.arrived(2)
            for i in range(2):
                self.add(self.mine.at[i, x, 0], self.got.at[0, i])
                self.add(self.mine.at[y, i, 1], self.got.at[1, i])
            self.copy(3).start()
            self.copy(4).start()
        elif number == 3:
            self.arrived(3)
            self.arrived(4)
            for ab in range(2):
                self.add(self.own.at[ab], self.last.at[ab])
            self.copy(5).start()
        elif number == 4:
            self.arrived(5)
            self.add(self.own.at[self.side], self.seq_in)
            self.copy(6).start()
        elif number == 5:
            self.arrived(6)
            r = self.own.shape[1]
            self.add(
                self.quarter(self.own.at[self.side], self.high),
                self.seq_in.at[r:, :],
                self.quarter(self.done.at[self.side], self.high),
            )
            self.copy(7).start()
        elif number == 6:
            self.arrived(7)
            self.copy(8).start()
        elif number == 7:
            self.arrived(8)

    def finish(self):
        for at in range(0 if self.whole is not None else 1, 9):
            self.copy(at).wait_send()


def backward_kernel(dims, *refs):
    shards, rows, width, heads, gather = dims
    ect, ka_h, va_h, kt_h, qat_h, ctxt_h, h1_h, wf_h, x, gmid, vec = refs[:11]
    refs = refs[11:]
    if gather:
        vec_two, gib = refs[:2]
        wholes = refs[2:5]
        gtok_o, vec_o = refs[5:7]
        sums_o = refs[7:11]
        refs = refs[11:]
    else:
        gtok_o, gw_o, vec_o = refs[:3]
        refs = refs[3:]
    (
        ka, va, kt, qat, ctxt, h1, wf, dot_all, doat, grads, dk_sum, dv_sum, sib_out, sib_in, side_out, side_in,
        own_sum, gt, load_s, do_s, do_r, sib_s, sib_r, side_s, side_r, perm_s, perm_r,
    ) = refs[:27]
    refs = refs[27:]
    here = Place()
    if gather:
        sums = [Reduction(here, refs[8 * i : 8 * i + 8], wholes[i]) for i in range(3)]
        sums.append(Reduction(here, refs[24:32]))
        gw_o, trade_in, trade_s, trade_r, vec_in, vec_s, vec_r, final_s = refs[32:]
    core = here.core
    half = width // 2
    keys = 4 * rows
    chunks = 4
    step = rows // chunks

    loads = []
    for at, (src, dst) in enumerate(
        ((ctxt_h, ctxt), (qat_h, qat), (ka_h, ka), (va_h, va), (kt_h, kt), (wf_h, wf), (h1_h, h1))
    ):
        copy = pltpu.make_async_copy(src, dst, load_s.at[at])
        copy.start()
        loads.append(copy)

    partners = [here.sibling, here.beside]
    if gather:
        partners += [sums[0].to_x, sums[0].to_y, sums[0].to_far]
    greet(here, partners, here.to)

    def run(*steps):
        if gather:
            for which, number in steps:
                sums[which].phase(number)

    run((0, 0), (1, 0), (2, 0))

    mine = pl.ds(pl.multiple_of(core * half, 128), half)
    theirs = pl.ds(pl.multiple_of((1 - core) * half, 128), half)
    own = pl.ds(pl.multiple_of(core * rows, rows), rows)
    trade = remote(ect.at[theirs, :], dot_all.at[:, own], do_s.at[0], do_r, here.sibling)
    trade.start()
    local = pltpu.make_async_copy(ect.at[mine, :], dot_all.at[:, own], do_s.at[1])
    local.start()
    local.wait()
    trade.wait()
    loads[0].wait()
    index = lax.broadcasted_iota(jnp.int32, (16, 2 * rows), 0)
    for h in range(heads):
        at = slice(h * 64, (h + 1) * 64)
        e_ctx = dot_all[at, :]
        delta = jnp.sum(e_ctx.astype(F32) * ctxt[at, :].astype(F32), 0, keepdims=True)
        doat[h, :64, :] = e_ctx
        rest = jnp.zeros((16, 2 * rows), F32)
        for r, term in enumerate(split3(delta)):
            rest = jnp.where(index == r, term.astype(F32), rest)
        doat[h, 64:80, :] = rest.astype(BF)
        doat[h, 80:, :] = jnp.zeros((48, 2 * rows), BF)
    for copy in loads[1:]:
        copy.wait()

    size = 512
    parts = 2 * rows // size

    def attend(h, _):
        head = pl.ds(pl.multiple_of(h * 64, 64), 64)
        for qb in range(parts):
            at = slice(qb * size, (qb + 1) * size)
            query, e_ctx = qat[h, :, at], doat[h, :, at]
            e_query = None
            for c in range(keys // size):
                to = slice(c * size, (c + 1) * size)
                weights = jnp.exp(dot(ka[h, to, :], query))
                e_scores = (weights * dot(va[h, to, :], e_ctx)).astype(BF)
                weights = weights.astype(BF)
                e_value = dot_t(e_ctx[:64], weights)
                e_key = dot_t(query[:64], e_scores)
                part = dot(kt[h, :, to], e_scores)
                e_query = part if e_query is None else e_query + part
                if qb > 0:
                    e_value += dv_sum[:, to]
                    e_key += dk_sum[:, to]
                if qb < parts - 1:
                    dv_sum[:, to] = e_value
                    dk_sum[:, to] = e_key
                else:
                    grads[pl.ds(pl.multiple_of(half + h * 64, 64), 64), to] = e_key.astype(BF)
                    grads[pl.ds(pl.multiple_of(2 * half + h * 64, 64), 64), to] = e_value.astype(BF)
            grads[head, at] = (e_query * HEAD_DIM**-0.5).astype(BF)

        for when, steps in IN_HEADS:
            @pl.when(h == when)
            def _():
                run(*steps)

        return 0

    lax.fori_loop(0, heads, attend, 0)

    def partial_of(j, own_chip):
        at = pl.ds(pl.multiple_of(j * rows, rows), rows)
        if own_chip:
            return dot(wf[...], grads[:, at])
        return dot(wf[:, half:], grads[half:, at])

    sib_out[0] = partial_of(3 - core, False).astype(BF)
    away = remote(sib_out.at[0], sib_in.at[0], sib_s.at[0], sib_r.at[0], here.sibling)
    away.start()
    beside = partial_of(2 + core, False)
    away.wait_recv()
    side_out[...] = (beside + sib_in[0].astype(F32)).astype(BF)
    sides = []
    for i in range(chunks):
        at = slice(i * step, (i + 1) * step)
        copy = remote(side_out.at[:, at], side_in.at[:, at], side_s.at[i], side_r.at[i], here.beside)
        copy.start()
        sides.append(copy)
    run(*TAIL[0])
    sib_out[1] = partial_of(1 - core, True).astype(BF)
    near = remote(sib_out.at[1], sib_in.at[1], sib_s.at[1], sib_r.at[1], here.sibling)
    near.start()
    own_part = partial_of(core, True)
    near.wait_recv()
    own_sum[...] = own_part + sib_in[1].astype(F32)

    for i, (left, right) in enumerate(
        ((grads[:half, : 2 * rows], h1[: 2 * rows, :]), (grads[half : 2 * half, :], h1[...]), (grads[2 * half :, :], h1[...]))
    ):
        result = dot(left, right).T.astype(BF)
        at = slice(i * half, (i + 1) * half)
        if gather:
            share = width // shards
            for j in range(shards):
                sums[3].mine[j // 4, j // 2 % 2, j % 2, :, at] = result[j * share : (j + 1) * share]
        else:
            gw_o[:, at] = result
    run(*TAIL[1])
    vec_o[...] = jnp.zeros_like(vec_o)

    def row_sums(values):
        wide = values.shape[1]
        folded = values[:, :128].astype(F32)
        for i in range(1, wide // 128):
            folded += values[:, i * 128 : (i + 1) * 128].astype(F32)
        return jnp.sum(folded.T, 0, keepdims=True)

    for at, part in ((QB, grads[:half, : 2 * rows]), (VB, grads[2 * half :, :])):
        total = row_sums(part)
        for i in range(2):
            vec_o[at : at + 1, i * half : (i + 1) * half] = jnp.where(core == i, total, 0.0)

    gain = vec[LN1G : LN1G + 1, :]

    def perm_copy(i):
        at = pl.ds(i * step, step)
        return remote(gt.at[at, :], gtok_o.at[at, :], perm_s.at[i], perm_r.at[i], here.origin)

    def stay_copy(i):
        at = pl.ds(i * step, step)
        return pltpu.make_async_copy(gt.at[at, :], gtok_o.at[at, :], perm_r.at[i])

    gain_sum = shift_sum = None
    for i in range(chunks):
        at = slice(i * step, (i + 1) * step)
        sides[i].wait_recv()
        e_norm = (own_sum[:, at] + side_in[:, at].astype(F32)).T
        unit, inverse = unit_of(x[at, :].astype(F32))
        e_unit = e_norm * gain
        result = gmid[at, :] + inverse * (
            e_unit - mean_rows(e_unit) - unit * mean_rows(e_unit * unit)
        )
        gt[at, :] = result.astype(BF)

        @pl.when(jnp.logical_not(here.stays))
        def _():
            perm_copy(i).start()

        @pl.when(here.stays)
        def _():
            stay_copy(i).start()

        gains = jnp.sum(e_norm * unit, 0, keepdims=True)
        shifts = jnp.sum(e_norm, 0, keepdims=True)
        gain_sum = gains if i == 0 else gain_sum + gains
        shift_sum = shifts if i == 0 else shift_sum + shifts
    vec_o[LN1G : LN1G + 1, :] = gain_sum
    vec_o[LN1B : LN1B + 1, :] = shift_sum

    if gather:
        vec_o[OB:IB, :] = vec_two[OB:IB, :]
        for r in range(4):
            vec_o[IB + r : IB + r + 1, :] = gib[0:1, r * width : (r + 1) * width]
        steps = [here.sibling, here.beside, sums[0].to_x, sums[0].to_y, sums[0].to_far]
        vec_copies = []
        for i, device in enumerate(steps):
            src = vec_o if i == 0 else vec_in.at[2 * i - 1]
            copy = remote(src, vec_in.at[2 * i], vec_s.at[i], vec_r.at[i], device)
            copy.start()
            vec_copies.append(copy)
            run(*TAIL[2 + i])
            copy.wait_recv()
            if i < 4:
                vec_in[2 * i + 1] = src[...] + vec_in[2 * i]
            else:
                for last in vec_copies:
                    last.wait_send()
                vec_o[...] = src[...] + vec_in[2 * i]
        run(*TAIL[7])
        trade_w = remote(sums[3].done.at[1 - core], trade_in, trade_s, trade_r, here.sibling)
        trade_w.start()
        finals = []
        for i in range(3):
            copy = pltpu.make_async_copy(sums[i].done, sums_o[i], final_s.at[i])
            copy.start()
            finals.append(copy)
        trade_w.wait()
        for i, src in enumerate((sums[3].done.at[core], trade_in)):
            which = core if i == 0 else 1 - core
            copy = pltpu.make_async_copy(src, sums_o[3].at[which], final_s.at[3 + i])
            copy.start()
            finals.append(copy)
        for copy in finals:
            copy.wait()
        for each in sums:
            each.finish()

    for copy in [away, near] + sides:
        copy.wait_send()
    for i in range(chunks):
        stay_copy(i).wait()

    @pl.when(jnp.logical_not(here.stays))
    def _():
        for i in range(chunks):
            perm_copy(i).wait_send()


IN_HEADS = (
    (0, ((0, 1),)),
    (2, ((1, 1),)),
    (3, ((0, 2),)),
    (4, ((0, 3), (2, 1))),
    (5, ((1, 2), (0, 4))),
)
TAIL = (
    ((0, 5),),
    ((3, 1), (1, 3), (2, 2), (0, 6)),
    ((2, 3), (1, 4)),
    ((3, 2), (1, 5)),
    ((3, 3), (2, 4), (1, 6)),
    ((3, 4), (2, 5)),
    ((3, 5), (2, 6), (0, 7), (1, 7)),
    ((3, 6), (2, 7), (3, 7)),
)


def attention_backward(dims, *args):
    shards, rows, width, heads, gather = dims
    half = width // 2
    keys = 4 * rows
    share = width // shards
    sems = pltpu.SemaphoreType.DMA
    if gather:
        parts = [block[4:] for block in grad_blocks(dims)]
        out = [((rows, width), BF), ((VROWS, width), F32)]
        out += [((2,) + part, BF) for part in parts] + [((2, share, 3 * half), BF)]
        in_specs = [VMEM] + [ANY] * 7 + [VMEM] * 5 + [ANY] * 3
        out_specs = (ANY, VMEM) + (ANY,) * 4
        more = sum((Reduction.scratch(*part, True) for part in parts), [])
        more += Reduction.scratch(share, 3 * half, False)
        more += [
            pltpu.VMEM((16, 128), BF), pltpu.VMEM((share, 3 * half), BF), sems, sems,
            pltpu.VMEM((9, VROWS, width), F32), sems((5,)), sems((5,)), sems((5,)),
        ]
    else:
        out = [((rows, width), BF), ((width, 3 * half), BF), ((VROWS, width), F32)]
        in_specs = [VMEM] + [ANY] * 7 + [VMEM] * 3
        out_specs = (ANY, VMEM, VMEM)
        more = []
    return pl.pallas_call(
        functools.partial(backward_kernel, dims),
        out_shape=tuple(jax.ShapeDtypeStruct(*o) for o in out),
        in_specs=in_specs,
        out_specs=out_specs,
        scratch_shapes=[
            pltpu.VMEM((heads, keys, 128), BF),
            pltpu.VMEM((heads, keys, 128), BF),
            pltpu.VMEM((heads, 64, keys), BF),
            pltpu.VMEM((heads, 128, 2 * rows), BF),
            pltpu.VMEM((half, 2 * rows), BF),
            pltpu.VMEM((keys, width), BF),
            pltpu.VMEM((width, 3 * half), BF),
            pltpu.VMEM((half, 2 * rows), BF),
            pltpu.VMEM((heads, 128, 2 * rows), BF),
            pltpu.VMEM((3 * half, keys), BF),
            pltpu.VMEM((64, keys), F32),
            pltpu.VMEM((64, keys), F32),
            pltpu.VMEM((2, width, rows), BF),
            pltpu.VMEM((2, width, rows), BF),
            pltpu.VMEM((width, rows), BF),
            pltpu.VMEM((width, rows), BF),
            pltpu.VMEM((width, rows), F32),
            pltpu.VMEM((rows, width), BF),
            sems((7,)), sems((2,)), sems, sems((2,)), sems((2,)), sems((4,)), sems((4,)), sems((4,)), sems((4,)),
        ] + more,
        compiler_params=pltpu.CompilerParams(
            collective_id=1, has_side_effects=True, vmem_limit_bytes=60 * 2**20
        ),
        name="attention_backward",
    )(*args)


def on_device(
    tokens, ln1_gain, ln1_shift, w_qkv, q_bias, v_bias, w_out, out_bias, ln2_gain, ln2_shift, w_in, in_bias,
    w_fin, fin_bias, cotangent, lengths, n_seq, shards,
):
    _, rows, width = tokens.shape
    heads = width // HEAD_DIM // 2
    half = width // 2
    share = width // shards
    gather = shards == 8
    dims = (shards, rows, width, heads, gather)
    axes = ("seq", "shard")
    there = relocation(n_seq, shards)
    back = [(b, a) for a, b in there]
    core = lax.rem(lax.axis_index("shard"), 2)

    packed = jnp.concatenate(
        [v.reshape(-1, share) for v in (ln1_gain, ln1_shift, q_bias, v_bias, out_bias, ln2_gain, ln2_shift, fin_bias, in_bias)]
    )
    length = jnp.broadcast_to(lengths.reshape(1, 1), (8, 128))
    if gather:
        vec = jnp.pad(packed, ((0, VROWS - VECS), (0, 128 - share)))
        w_here = w_qkv
    else:
        every = lax.all_gather(packed, "shard", axis=1, tiled=True)
        vec = jnp.pad(every, ((0, VROWS - VECS), (0, 0)))
        full_w = lax.all_gather(w_qkv, "shard", axis=0, tiled=True)
        w_here = lax.dynamic_index_in_dim(
            full_w.reshape(width, 3, 2, half), core, 2, keepdims=False
        ).reshape(width, 3 * half)
    shares = (w_out, w_in, w_fin) if gather else ()
    (ka, va, kt, qat, ctxt, ctx, h1, wf, x, lens, vecs, inb, *wholes) = attention_forward(
        dims, tokens.reshape(rows, width), length, w_here, vec, *shares
    )
    if not gather:
        inb = jnp.broadcast_to(
            lax.all_gather(in_bias, "shard", axis=0, tiled=True).astype(F32)[None], (8, 4 * width)
        )
        wholes = [lax.all_gather(w, "shard", axis=0, tiled=True) for w in (w_out, w_in, w_fin)]
    cot = lax.ppermute(cotangent.reshape(rows, width), axes, there)
    out, ect, gmid, gwi, gwf, gwo, vec_two, gib = feed_forward(
        dims, ctx, x, cot, lens, vecs, inb, *wholes
    )
    output = lax.ppermute(out, axes, back).reshape(tokens.shape)
    args = (ect, ka, va, kt, qat, ctxt, h1, wf, x, gmid, vecs)
    s = lax.axis_index("shard")
    if gather:
        gtok, sums, t_wf, t_wi, t_wo, t_w = attention_backward(dims, *args, vec_two, gib, gwf, gwi, gwo)
        total_wf = t_wf.reshape(width, 4 * share).T.astype(F32)
        total_wi = t_wi.transpose(1, 0, 2).reshape(share, 4 * width).astype(F32)
        total_wo = t_wo.transpose(1, 0, 2).reshape(share, width).astype(F32)
        total_w = t_w.reshape(2, share, 3, half).transpose(1, 2, 0, 3).reshape(share, 3 * width).astype(F32)
    else:
        gtok, gw, vec_one = attention_backward(dims, *args)

        def total(grad, dim):
            part = lax.psum_scatter(grad, "shard", scatter_dimension=dim, tiled=True)
            return lax.psum(part, "seq").astype(F32)

        total_wi = total(gwi, 0)
        total_wf = total(gwf, 1).T
        total_wo = total(gwo, 0)
        wide = jnp.zeros((width, 3, 2, half), BF)
        wide = lax.dynamic_update_index_in_dim(wide, gw.reshape(width, 3, half), core, 2)
        total_w = total(wide.reshape(width, 3 * width), 0)
        sums = jnp.concatenate((vec_one[:OB], vec_two[OB:IB], gib[0].reshape(4, width)))
        sums = lax.psum(sums, axes)
    mine = lax.dynamic_slice_in_dim(sums[:IB], s * share, share, 1)
    total_ib = lax.dynamic_slice_in_dim(sums[IB:VECS].reshape(-1), s * 4 * share, 4 * share, 0)
    return (
        output,
        gtok.reshape(tokens.shape),
        mine[LN1G],
        mine[LN1B],
        total_w,
        mine[QB],
        mine[VB],
        total_wo,
        mine[OB],
        mine[LN2G],
        mine[LN2B],
        total_wi,
        total_ib,
        total_wf,
        mine[FB],
    )


def solution(mesh):
    vector, matrix, rows = P("shard"), P("shard", None), P("shard", "seq", None)
    return jax.shard_map(
        functools.partial(on_device, n_seq=mesh.shape["seq"], shards=mesh.shape["shard"]),
        mesh=mesh,
        in_specs=(
            rows, vector, vector, matrix, vector, vector, matrix, vector, vector, vector, matrix, vector,
            matrix, vector, rows, vector,
        ),
        out_specs=(
            rows, rows, vector, vector, matrix, vector, vector, matrix, vector, vector, vector, matrix,
            vector, matrix, vector,
        ),
        check_vma=False,
    )
```

```python
import functools
import math

import jax
import jax.numpy as jnp
from jax import lax
from jax.experimental import pallas as pl
from jax.experimental.pallas import tpu as pltpu
from jax.sharding import PartitionSpec as P

HEAD_DIM = 64
EPS = 1e-05
GELU_C = 0.7978845608028654
GELU_K = 0.044715
MASKED = -1e30

BF = jnp.bfloat16
F32 = jnp.float32
MESH = pl.DeviceIdType.MESH
VMEM = pl.BlockSpec(memory_space=pltpu.VMEM)
ANY = pl.BlockSpec(memory_space=pl.ANY)

LN1G, LN1B, QB, VB, OB, LN2G, LN2B, FB, IB = range(9)
VECS = 12
VROWS = 16


def dot(left, right):
    return jnp.dot(left, right, preferred_element_type=F32)


def dot_t(left, right):
    return lax.dot_general(left, right, (((1,), (1,)), ((), ())), preferred_element_type=F32)


def mean_rows(values):
    return jnp.mean(values, -1, keepdims=True)


def unit_of(values):
    centred = values - mean_rows(values)
    inverse = lax.rsqrt(mean_rows(centred * centred) + EPS)
    return centred * inverse, inverse


def split3(values):
    high = values.astype(BF)
    rest = values - high.astype(F32)
    mid = rest.astype(BF)
    low = (rest - mid.astype(F32)).astype(BF)
    return high, mid, low


class Place:
    def __init__(self):
        q = lax.axis_index("seq")
        s = lax.axis_index("shard")
        self.q, self.s = q, s
        self.core = core = lax.rem(s, 2)
        self.to = (2 * core + lax.rem(q, 2), s - core + q // 2)
        side = lax.rem(q, 2)
        self.quarter = side + 2 * core
        self.origin = (self.quarter, s - core + q // 2)
        self.stays = q // 2 == core
        self.sibling = (q, s + 1 - 2 * core)
        self.beside = (q + 1 - 2 * side, s)
        self.quarters = [side, side + 2, 1 - side, 3 - side]


def relocation(n_seq, shards):
    return [
        (q * shards + s, (2 * (s % 2) + q % 2) * shards + s - s % 2 + q // 2)
        for q in range(n_seq)
        for s in range(shards)
    ]


def remote(src, dst, send, recv, device):
    return pltpu.make_async_remote_copy(
        src_ref=src, dst_ref=dst, send_sem=send, recv_sem=recv, device_id=device, device_id_type=MESH
    )


class Named:
    def __init__(self, specs, refs):
        for (name, _), ref in zip(specs, refs, strict=True):
            setattr(self, name, ref)


def greet_all(devices):
    barrier = pltpu.get_barrier_semaphore()
    for device in devices:
        pl.semaphore_signal(barrier, inc=1, device_id=device, device_id_type=MESH)
    pl.semaphore_wait(barrier, len(devices))


def greet(here, devices, mover):
    barrier = pltpu.get_barrier_semaphore()
    for device in devices:
        pl.semaphore_signal(barrier, inc=1, device_id=device, device_id_type=MESH)

    @pl.when(jnp.logical_not(here.stays))
    def _():
        pl.semaphore_signal(barrier, inc=1, device_id=mover, device_id_type=MESH)
        pl.semaphore_wait(barrier, len(devices) + 1)

    @pl.when(here.stays)
    def _():
        pl.semaphore_wait(barrier, len(devices))


def forward_kernel(dims, *refs):
    shards, rows, width, heads, gather = dims
    n_more = 3 if gather else 0
    tok, length_in, w_in, vec_in = refs[:4]
    shares = refs[4 : 4 + n_more]
    refs = refs[4 + n_more :]
    (ka_o, va_o, kt_o, qat_o, ctxt_o, ctx_o, h1_o, wf_o, xown_o, len_o, vec_o, inb_o) = refs[:12]
    wholes = refs[12 : 12 + n_more]
    refs = refs[12 + n_more :]
    (
        xs, wf, vg, lens, h1, ka, va, kt, vt, qat, ctxt, ctx, exact,
        perm_s, perm_r, sib_s, sib_r, side_s, side_r, back_s, back_r,
        len_s, len_r, w_s, w_r, out_s, ctx_s, ctx_r, all_s, all_r, all_l,
    ) = refs
    here = Place()
    core, s = here.core, here.s
    half = width // 2
    share = width // shards
    chunks = 4
    step = rows // chunks
    x_bit, y_bit = lax.rem(s // 2, 2), lax.rem(s // 4, 2)
    shard_x, shard_y = s + 2 - 4 * x_bit, s + 4 - 8 * y_bit
    shard_d = shard_x + 4 - 8 * y_bit
    partner_x, partner_y = (here.q, shard_x), (here.q, shard_y)

    partners = [here.sibling, here.beside] + ([partner_x, partner_y] if gather else [])
    greet(here, partners, here.origin)

    to_core = here.q // 2

    def block(ref, j, i):
        return ref.at[pl.ds(pl.multiple_of(j * rows + i * step, step), step), :]

    def perm_copy(i):
        return remote(
            tok.at[pl.ds(i * step, step), :], block(xs, to_core, i), perm_s.at[i], perm_r.at[i], here.to
        )

    def len_copy():
        return remote(length_in, lens, len_s, len_r, here.to)

    @pl.when(jnp.logical_not(here.stays))
    def _():
        for i in range(chunks):
            perm_copy(i).start()
        len_copy().start()

    @pl.when(here.stays)
    def _():
        for i in range(chunks):
            pltpu.make_async_copy(
                tok.at[pl.ds(i * step, step), :], block(xs, to_core, i), perm_r.at[i]
            ).start()
        pltpu.make_async_copy(length_in, lens, len_r).start()

    w_copies = []
    if gather:
        def columns(j, which):
            return pl.ds(pl.multiple_of(j * width + which * half, 128), half)

        mine = pl.ds(pl.multiple_of(s * share, share), share)
        for j in range(3):
            copy = remote(
                w_in.at[:, columns(j, 1 - core)], wf.at[mine, pl.ds(j * half, half)],
                w_s.at[j], w_r.at[j], here.sibling,
            )
            copy.start()
            w_copies.append(copy)
            copy = pltpu.make_async_copy(
                w_in.at[:, columns(j, core)], wf.at[mine, pl.ds(j * half, half)], w_s.at[4 + j]
            )
            copy.start()
            w_copies.append(copy)
        copy = remote(vec_in, vg.at[s], w_s.at[3], w_r.at[3], here.sibling)
        copy.start()
        w_copies.append(copy)
        copy = pltpu.make_async_copy(vec_in, vg.at[s], w_s.at[7])
        copy.start()
        w_copies.append(copy)
    else:
        copy = pltpu.make_async_copy(w_in, wf, w_s.at[0])
        copy.start()
        w_copies.append(copy)

    def w_move(at):
        src, count, device = (
            (s - core, 2, partner_x),
            (s - core, 2, partner_y),
            (shard_x - core, 1, partner_y),
            (shard_y - core + 1, 1, partner_x),
        )[at]
        part = wf.at[pl.ds(pl.multiple_of(src * share, share), count * share), :]
        return remote(part, part, w_s.at[8 + at], w_r.at[8 + at], device)

    def v_move(at):
        src, device = ((s, partner_x), (s, partner_y), (shard_x, partner_y))[at]
        part = vg.at[pl.ds(src - core, 2)]
        return remote(part, part, w_s.at[12 + at], w_r.at[12 + at], device)

    def receive(i):
        pltpu.make_async_copy(tok.at[pl.ds(i * step, step), :], block(xs, core, i), perm_r.at[i]).wait()
        sib = remote(block(xs, core, i), block(xs, core, i), sib_s.at[i], sib_r.at[i], here.sibling)
        side = remote(block(xs, core, i), block(xs, 2 + core, i), side_s.at[i], side_r.at[i], here.beside)
        side.start()
        sib.start()
        return [sib, side]

    def relay(i):
        block_in = block(xs, 2 + core, i)
        remote(block_in, block_in, side_s.at[i], side_r.at[i], here.beside).wait_recv()
        copy = remote(block_in, block_in, back_s.at[i], back_r.at[i], here.sibling)
        copy.start()
        return copy

    def rows_of(k, shard):
        count = shares[k].shape[0]
        return pl.ds(pl.multiple_of(shard * count, count), count)

    def piece(k, shard, part=None):
        cut = shares[k].shape[1] // 2
        if part is None:
            return wholes[k].at[rows_of(k, shard), :]
        return wholes[k].at[rows_of(k, shard), part * cut : (part + 1) * cut]

    def pass_on(k, slot, src, dst, device):
        return remote(src, dst, all_s.at[k, slot], all_r.at[k, slot], device)

    def got(k, slot, ref):
        pass_on(k, slot, ref, ref, here.sibling).wait_recv()

    def move(k, slot):
        src, device = (
            (None, partner_x),
            (None, partner_y),
            (None, here.sibling),
            ((shard_x, 0), partner_y),
            ((shard_x,), here.sibling),
            ((shard_y, 1), partner_x),
            ((shard_y,), here.sibling),
            ((shard_d,), here.sibling),
        )[slot]
        if src is None:
            return pass_on(k, slot, shares[k], piece(k, s), device)
        return pass_on(k, slot, piece(k, *src), piece(k, *src), device)

    def share_out(k):
        for slot in range(3):
            move(k, slot).start()
        pltpu.make_async_copy(shares[k], piece(k, s), all_l.at[k]).start()

    def from_x(k):
        got(k, 0, piece(k, shard_x))
        move(k, 3).start()
        move(k, 4).start()

    def from_y(k):
        got(k, 1, piece(k, shard_y))
        move(k, 5).start()
        move(k, 6).start()

    def from_far(k):
        got(k, 3, piece(k, shard_d, 0))
        got(k, 5, piece(k, shard_d, 1))
        move(k, 7).start()

    def all_here(k):
        flip = 1 - 2 * core
        for slot, shard in ((2, s), (4, shard_x), (6, shard_y), (7, shard_d)):
            got(k, slot, piece(k, shard + flip))
        pltpu.make_async_copy(shares[k], piece(k, s), all_l.at[k]).wait()

    moved = []
    if gather:
        for copy in w_copies:
            copy.wait()
        for at in range(2):
            w_move(at).start()
            v_move(at).start()
        for k in range(n_more):
            share_out(k)
    moved += receive(0)
    moved += receive(1)
    if gather:
        w_move(0).wait_recv()
        v_move(0).wait_recv()
        w_move(2).start()
        v_move(2).start()
        w_move(1).wait_recv()
        v_move(1).wait_recv()
        w_move(3).start()
    moved += receive(2)
    moved += receive(3)

    def norm_one(first, count):
        def body(i, _):
            at = pl.ds(pl.multiple_of(first + i * 256, 256), 256)
            unit, _ = unit_of(xs[at, :].astype(F32))
            h1[at, :] = (unit * vec_o[LN1G : LN1G + 1, :] + vec_o[LN1B : LN1B + 1, :]).astype(BF)
            return 0

        lax.fori_loop(0, count // 256, body, 0)

    if gather:
        w_move(2).wait_recv()
        w_move(3).wait_recv()
        v_move(2).wait_recv()
        for i in range(shards):
            part = vg[i].astype(F32)
            vec_o[:, i * share : (i + 1) * share] = part[:, :share]
            for r in range(4):
                at = (4 * i + r) * share
                inb_o[:, at : at + share] = jnp.broadcast_to(
                    part[IB + r : IB + r + 1, :share], (8, share)
                )
    else:
        for copy in w_copies:
            copy.wait()
        vec_o[...] = vec_in[...].astype(F32)
        inb_o[...] = jnp.zeros_like(inb_o)

    pltpu.make_async_copy(length_in, lens, len_r).wait()
    length = lens[0:1, 0:1]
    lane = lax.broadcasted_iota(jnp.int32, (rows, 128), 1)
    row_at = lax.broadcasted_iota(jnp.int32, (rows, 128), 0)
    lower = lane < HEAD_DIM
    ones_rows = (lax.broadcasted_iota(jnp.int32, (16, rows), 0) == 0).astype(BF)
    q_rest = (lax.broadcasted_iota(jnp.int32, (64, 2 * rows), 0) == 3).astype(BF)
    for h in range(heads):
        qat[h, HEAD_DIM:, :] = q_rest

    def bias_half(at):
        full = vec_o[at : at + 1, :]
        return jnp.where(core == 0, full[:, :half], full[:, half:])

    def project(j):
        at = slice(j * rows, (j + 1) * rows)
        norm = h1[at, :]
        dead = jnp.where(here.quarters[j] * rows + row_at < length, 0.0, MASKED)
        k_rest = jnp.where(lane == HEAD_DIM + 3, dead, jnp.where(lane < HEAD_DIM + 3, 1.0, 0.0))
        v_rest = jnp.where(lane < HEAD_DIM + 3, -1.0, 0.0)
        if j < 2:
            q = (dot(norm, wf[:, :half]) + bias_half(QB)).astype(BF) * BF(HEAD_DIM**-0.5)
        k = dot(norm, wf[:, half : 2 * half])
        v = dot(norm, wf[:, 2 * half :]) + bias_half(VB)
        for i in range(heads // 2):
            two = slice(i * 128, (i + 1) * 128)
            kp, vp = k[:, two], v[:, two]
            ka[2 * i, at, :] = jnp.where(lower, kp, k_rest).astype(BF)
            ka[2 * i + 1, at, :] = jnp.where(lower, pltpu.roll(kp, 64, 1), k_rest).astype(BF)
            va[2 * i, at, :] = jnp.where(lower, vp, v_rest).astype(BF)
            va[2 * i + 1, at, :] = jnp.where(lower, pltpu.roll(vp, 64, 1), v_rest).astype(BF)
            turned = kp.astype(BF).T
            kt[2 * i, :, at] = turned[:64]
            kt[2 * i + 1, :, at] = turned[64:]
            turned = vp.astype(BF).T
            vt[2 * i, :64, at] = turned[:64]
            vt[2 * i + 1, :64, at] = turned[64:]
            vt[2 * i, 64:, at] = ones_rows
            vt[2 * i + 1, 64:, at] = ones_rows
            if j < 2:
                turned = q[:, two].T
                qat[2 * i, :64, at] = turned[:64]
                qat[2 * i + 1, :64, at] = turned[64:]

    for i in range(chunks):
        remote(block(xs, core, i), block(xs, 1 - core, i), sib_s.at[i], sib_r.at[i], here.sibling).wait_recv()
    norm_one(0, 2 * rows)
    project(0)
    project(1)
    if gather:
        from_x(0)
        from_y(0)
    relays = [relay(i) for i in range(chunks)]
    for i in range(chunks):
        pl_block = block(xs, 3 - core, i)
        remote(pl_block, pl_block, back_s.at[i], back_r.at[i], here.sibling).wait_recv()
    norm_one(2 * rows, 2 * rows)
    project(2)
    project(3)
    if gather:
        from_x(1)
        from_y(1)

    saves = []
    own = pl.ds(pl.multiple_of(core * rows, rows), rows)
    for at, (src, dst) in enumerate(
        ((ka, ka_o), (va, va_o), (kt, kt_o), (h1, h1_o), (wf, wf_o), (xs.at[own, :], xown_o), (lens, len_o))
    ):
        copy = pltpu.make_async_copy(src, dst, out_s.at[at])
        copy.start()
        saves.append(copy)

    size = 512
    keys = 4 * rows

    def attend(h, _):
        for qb in range(2 * rows // size):
            at = slice(qb * size, (qb + 1) * size)
            query = qat[h, :, at]

            def scores(c):
                return dot(ka[h, c * size : (c + 1) * size, :], query)

            ahead = scores(0)
            highest = total = None
            for c in range(keys // size):
                now = ahead
                if c + 1 < keys // size:
                    ahead = scores(c + 1)
                top = jnp.max(now, axis=0, keepdims=True)
                top = top if highest is None else jnp.maximum(highest, top)
                weights = jnp.exp(now - top).astype(BF)
                part = dot(vt[h, :, c * size : (c + 1) * size], weights)
                total = part if total is None else total * jnp.exp(highest - top) + part
                highest = top
            mass = total[64:65]
            result = total[:64] / mass
            head = pl.ds(pl.multiple_of(h * 64, 64), 64)
            exact[head, at] = result
            ctxt[head, at] = result.astype(BF)
            high, mid, low = split3(-(highest + jnp.log(mass)))
            index = lax.broadcasted_iota(jnp.int32, (16, size), 0)
            rest = jnp.where(index == 3, 1.0, 0.0)
            for r, term in enumerate((high, mid, low)):
                rest = jnp.where(index == r, term.astype(F32), rest)
            qat[h, 64:80, at] = rest.astype(BF)

        if gather:
            @pl.when(h == 0)
            def _():
                from_far(0)

            @pl.when(h == heads // 3)
            def _():
                from_x(2)
                from_y(2)

            @pl.when(h == heads - 2)
            def _():
                from_far(1)

            @pl.when(h == heads - 1)
            def _():
                from_far(2)

        return 0

    lax.fori_loop(0, heads, attend, 0)

    mine = pl.ds(pl.multiple_of(core * half, 128), half)
    own = pl.ds(pl.multiple_of(core * rows, rows), rows)
    other = pl.ds(pl.multiple_of((1 - core) * rows, rows), rows)
    trade = remote(ctxt.at[:, other], ctx.at[mine, :], ctx_s, ctx_r, here.sibling)
    trade.start()
    local = pltpu.make_async_copy(ctxt.at[:, own], ctx.at[mine, :], out_s.at[7])
    local.start()
    for at, (src, dst) in enumerate(((qat, qat_o), (exact, ctxt_o))):
        copy = pltpu.make_async_copy(src, dst, out_s.at[8 + at])
        copy.start()
        saves.append(copy)
    local.wait()
    trade.wait()
    copy = pltpu.make_async_copy(ctx, ctx_o, out_s.at[10])
    copy.start()
    saves.append(copy)
    for copy in saves:
        copy.wait()

    @pl.when(jnp.logical_not(here.stays))
    def _():
        for i in range(chunks):
            perm_copy(i).wait_send()
        len_copy().wait_send()

    for copy in moved + relays:
        copy.wait_send()
    if gather:
        for k in range(n_more):
            all_here(k)
            for slot in range(8):
                move(k, slot).wait_send()
        for at in range(4):
            w_move(at).wait_send()
        for at in range(3):
            v_move(at).wait_send()


def attention_forward(dims, tok, length, w, vec, *shares):
    shards, rows, width, heads, gather = dims
    half = width // 2
    keys = 4 * rows
    out = [
        ((heads, keys, 128), BF),
        ((heads, keys, 128), BF),
        ((heads, 64, keys), BF),
        ((heads, 128, 2 * rows), BF),
        ((half, 2 * rows), F32),
        ((width, rows), BF),
        ((keys, width), BF),
        ((width, 3 * half), BF),
        ((rows, width), BF),
        ((8, 128), jnp.int32),
        ((VROWS, width), F32),
        ((8, 4 * width), F32),
    ] + [((shards * share.shape[0], share.shape[1]), BF) for share in shares]
    sems = pltpu.SemaphoreType.DMA
    return pl.pallas_call(
        functools.partial(forward_kernel, dims),
        out_shape=tuple(jax.ShapeDtypeStruct(*o) for o in out),
        in_specs=[ANY, VMEM, ANY, VMEM] + [ANY] * len(shares),
        out_specs=tuple([ANY] * 10 + [VMEM] * 2 + [ANY] * len(shares)),
        scratch_shapes=[
            pltpu.VMEM((keys, width), BF),
            pltpu.VMEM((width, 3 * half), BF),
            pltpu.VMEM((shards, VROWS, 128), BF),
            pltpu.VMEM((8, 128), jnp.int32),
            pltpu.VMEM((keys, width), BF),
            pltpu.VMEM((heads, keys, 128), BF),
            pltpu.VMEM((heads, keys, 128), BF),
            pltpu.VMEM((heads, 64, keys), BF),
            pltpu.VMEM((heads, 80, keys), BF),
            pltpu.VMEM((heads, 128, 2 * rows), BF),
            pltpu.VMEM((half, 2 * rows), BF),
            pltpu.VMEM((width, rows), BF),
            pltpu.VMEM((half, 2 * rows), F32),
            sems((4,)), sems((4,)), sems((4,)), sems((4,)), sems((4,)), sems((4,)), sems((4,)), sems((4,)),
            sems, sems, sems((16,)), sems((16,)), sems((12,)), sems, sems,
            sems((3, 8)), sems((3, 8)), sems((3,)),
        ],
        compiler_params=pltpu.CompilerParams(
            collective_id=0, has_side_effects=True, vmem_limit_bytes=56 * 2**20
        ),
        name="attention_forward",
    )(tok, length, w, vec, *shares)


FAR_HEADS = (
    (0, ((2, 1),)),
    (1, ((0, 2),)),
    (2, ((1, 2),)),
    (3, ((2, 2),)),
    (4, ((0, 3),)),
    (5, ((1, 3), (2, 3))),
)
NEAR_HEADS = (
    (2, ((0, 4),)),
    (4, ((1, 4), (3, 2))),
    (5, ((2, 4), (0, 5), (3, 3))),
)
TAIL = (
    ((4, 2), (1, 5), (2, 5), (5, 2)),
    ((3, 4), (4, 3), (0, 6), (5, 3)),
    ((3, 5), (4, 4), (5, 4), (1, 6), (2, 6), (3, 6), (4, 5), (5, 5), (4, 6), (5, 6)),
)


class Links:
    def __init__(self, here):
        s, q = here.s, here.q
        self.x, self.y = lax.rem(s // 2, 2), lax.rem(s // 4, 2)
        self.to_x = (q, s + 2 - 4 * self.x)
        self.to_y = (q, s + 4 - 8 * self.y)
        self.inner = (q == 1) | (q == 2)
        self.to_inner = (3 - q, s)


class Reduction:
    NAMES = ("got", "last", "seq_in", "inner_in", "done", "send", "recv")

    def __init__(self, here, links, v, name, mine, first_hops=None, core=None):
        for each in self.NAMES:
            setattr(self, each, getattr(v, f"{each}_{name}"))
        self.here, self.links, self.mine = here, links, mine
        self.first_hops, self.core = first_hops, core
        self.own = mine.at[links.y, links.x]

    @staticmethod
    def scratch(name, r, c):
        sems = pltpu.SemaphoreType.DMA
        specs = [pltpu.VMEM((2, 2, r, c), BF)] + [pltpu.VMEM((2, r, c), BF)] * 4 + [sems((8,)), sems((8,))]
        return [(f"{each}_{name}", spec) for each, spec in zip(Reduction.NAMES, specs, strict=True)]

    def copy(self, at):
        here, links, mine, own = self.here, self.links, self.mine, self.own
        x, y = links.x, links.y
        src, dst, device = (
            lambda: self.core + (here.sibling,),
            lambda: (mine.at[:, 1 - x, 0], self.got.at[0], links.to_x),
            lambda: (mine.at[1 - y, :, 1], self.got.at[1], links.to_y),
            lambda: (mine.at[1 - y, x, 0], self.last.at[0], links.to_y),
            lambda: (mine.at[y, 1 - x, 1], self.last.at[1], links.to_x),
            lambda: (own, self.seq_in, here.beside),
            lambda: (own, self.inner_in, links.to_inner),
            lambda: (self.done, self.done, here.beside),
        )[at]()
        return remote(src, dst, self.send.at[at], self.recv.at[at], device)

    def add(self, left, right, out=None):
        r = left.shape[-2]
        step = 96 if left.shape[-1] > 512 else r
        out = left if out is None else out

        def body(n, _):
            at = pl.ds(pl.multiple_of(n * step, step), step)
            out[at, :] = left[at, :] + right[at, :]
            return 0

        lax.fori_loop(0, r // step, body, 0)

    def phase(self, number):
        links, mine = self.links, self.mine
        x, y, outer = links.x, links.y, jnp.logical_not(links.inner)
        if number == 1:
            if self.core is not None:
                self.copy(0).wait_recv()
                for j in range(2):
                    for i in range(2):
                        for ab in range(2):
                            self.add(mine.at[j, i, ab], self.core[1].at[j, i, ab])
            self.copy(1).start()
            self.copy(2).start()
        elif number == 2:
            for copy in self.first_hops or (self.copy(1), self.copy(2)):
                copy.wait_recv()
            for i in range(2):
                self.add(mine.at[i, x, 0], self.got.at[0, i])
                self.add(mine.at[y, i, 1], self.got.at[1, i])
            self.copy(3).start()
            self.copy(4).start()
        elif number == 3:
            self.copy(3).wait_recv()
            self.copy(4).wait_recv()
            for ab in range(2):
                self.add(self.own.at[ab], self.last.at[ab])
            pl.when(outer)(lambda: self.copy(5).start())
        elif number == 4:
            @pl.when(links.inner)
            def _():
                self.copy(5).wait_recv()
                for ab in range(2):
                    self.add(self.own.at[ab], self.seq_in.at[ab])
                self.copy(6).start()
        elif number == 5:
            @pl.when(links.inner)
            def _():
                self.copy(6).wait_recv()
                for ab in range(2):
                    self.add(self.own.at[ab], self.inner_in.at[ab], self.done.at[ab])
                self.copy(7).start()
        else:
            pl.when(outer)(lambda: self.copy(7).wait_recv())

    def finish(self):
        if self.core is not None:
            self.copy(0).wait_send()
        for copy in self.first_hops or (self.copy(1), self.copy(2)):
            copy.wait_send()
        self.copy(3).wait_send()
        self.copy(4).wait_send()
        pl.when(jnp.logical_not(self.links.inner))(lambda: self.copy(5).wait_send())

        @pl.when(self.links.inner)
        def _():
            self.copy(6).wait_send()
            self.copy(7).wait_send()


class FirstHop:
    def __init__(self, make, sends=None, receives=None):
        self.make, self.sends, self.receives = make, sends, receives

    @staticmethod
    def on(condition, action):
        if condition is None:
            action()
        else:
            pl.when(condition)(action)

    def start(self):
        self.on(self.sends, lambda: self.make().start())

    def wait_send(self):
        self.on(self.sends, lambda: self.make().wait_send())

    def wait_recv(self):
        self.on(self.receives, lambda: self.make().wait_recv())


def grad_parts(dims):
    shards, rows, width, heads, _ = dims
    share, half = width // shards, width // 2
    return (half, 4 * share), (share, 2 * width), (share, half)


def middle_specs(dims):
    shards, rows, width, heads, _ = dims
    half, keys, share = width // 2, 4 * rows, width // shards
    groups = heads // 2
    sems = pltpu.SemaphoreType.DMA
    part_f, part_i, part_o = grad_parts(dims)
    ins = [(name, VMEM) for name in ("ctx", "x", "cot", "lens", "vec", "inb")]
    ins += [
        (name, ANY)
        for name in ("wo_h", "wi_h", "wf_h", "ka_h", "va_h", "kt_h", "qat_h", "ctxt_h", "h1_h", "wq_h")
    ]
    outs = [
        ("gtok_o", ((rows, width), BF), ANY),
        ("out_o", ((rows, width), BF), ANY),
        ("vec_o", ((VROWS, 128), F32), VMEM),
        ("sum_f", ((2,) + part_f, BF), ANY),
        ("sum_i", ((2,) + part_i, BF), ANY),
        ("sum_o", ((2,) + part_o, BF), ANY),
        ("sum_w", ((groups, 2, share, half), BF), ANY),
    ]
    scratch = []
    for name, part in (("f", part_f), ("i", part_i), ("o", part_o)):
        scratch += Reduction.scratch(name, *part)
        scratch += [(f"near_{name}", pltpu.VMEM((2, 2, 2) + part, BF))]
    for g in range(groups):
        scratch += Reduction.scratch(g, share, half) + [(f"mine_{g}", pltpu.VMEM((2, 2, 2, share, half), BF))]
    for name in "fi":
        for each in ("core_s", "core_r", "x_s", "x_r", "y_s", "y_r"):
            scratch.append((f"{each}{name}", sems((4,))))
    scratch += [
        ("mine_f", pltpu.VMEM((2, 2, 2) + part_f, BF)),
        ("mine_i", pltpu.VMEM((2, 2, 2) + part_i, BF)),
        ("both_o", pltpu.VMEM((2, 2, 2, 2) + part_o, BF)),
        ("gmid", pltpu.VMEM((rows, width), F32)),
        ("vecs", pltpu.VMEM((VROWS, width), F32)),
        ("gib", pltpu.VMEM((8, 4 * width), F32)),
        ("gt", pltpu.VMEM((rows, width), BF)),
        ("e_ctx", pltpu.VMEM((half, 2 * rows), BF)),
        ("sib_in", pltpu.VMEM((2, width, rows), BF)),
        ("side_in", pltpu.VMEM((width, rows), BF)),
        ("vec_out", pltpu.VMEM((shards, VROWS, 128), F32)),
        ("vec_in", pltpu.VMEM((shards, VROWS, 128), F32)),
        ("vec_all", pltpu.VMEM((4, VROWS, 128), F32)),
        ("w_in", pltpu.VMEM((groups, share, half), BF)),
        ("load_s", sems((8,))),
        ("head_s", sems((2, 4))),
        ("trade_s", sems((2,))),
        ("trade_r", sems),
        ("sib_s", sems((2,))),
        ("sib_r", sems((2,))),
        ("side_s", sems((4,))),
        ("side_r", sems((4,))),
        ("perm_s", sems((5,))),
        ("perm_r", sems((5,))),
        ("vec_s", sems((shards + 4,))),
        ("vec_r", sems((shards + 4,))),
        ("w_s", sems((groups,))),
        ("w_r", sems((groups,))),
        ("final_s", sems((3 + 2 * groups,))),
    ]
    feed = [
        ("wo", pltpu.VMEM((width, width), BF)),
        ("wi", pltpu.VMEM((2, width, width), BF)),
        ("wf", pltpu.VMEM((2, width, width), BF)),
        ("mid", pltpu.VMEM((rows, width), F32)),
        ("h2", pltpu.VMEM((rows, width), BF)),
        ("h2t", pltpu.VMEM((width + 16, rows), BF)),
        ("eo", pltpu.VMEM((rows, width), BF)),
        ("eot", pltpu.VMEM((width, rows), BF)),
        ("gh2", pltpu.VMEM((rows, width), F32)),
        ("acc", pltpu.VMEM((rows, width), F32)),
        ("ect", pltpu.VMEM((width, rows), BF)),
        ("both_f", pltpu.VMEM((2, 2, 2) + part_f, BF)),
        ("both_i", pltpu.VMEM((2, 2, 2, 2, share, width), BF)),
    ]
    attend = [
        ("ka", pltpu.VMEM((2, 2 * rows, 128), BF)),
        ("va", pltpu.VMEM((2, 2 * rows, 128), BF)),
        ("kt", pltpu.VMEM((2, 64, 2 * rows), BF)),
        ("qat", pltpu.VMEM((2, 128, 2 * rows), BF)),
        ("h1", pltpu.VMEM((keys, width), BF)),
        ("wq", pltpu.VMEM((width, 3 * half), BF)),
        ("eat", pltpu.VMEM((heads, 128, 2 * rows), BF)),
        ("grads", pltpu.VMEM((3 * half, keys), BF)),
        ("sums", pltpu.VMEM((width, rows), F32)),
        ("sib_out", pltpu.VMEM((2, width, rows), BF)),
        ("side_out", pltpu.VMEM((width, rows), BF)),
    ]
    return ins, outs, scratch, feed, attend


def middle_kernel(dims, *refs):
    shards, rows, width, heads, _ = dims
    ins, outs, scratch, feed, attend = middle_specs(dims)
    at_ins, at_outs = len(ins), len(ins) + len(outs)
    i = Named(ins, refs[:at_ins])
    o = Named([out[:2] for out in outs], refs[at_ins:at_outs])
    v = Named(scratch, refs[at_outs:])
    here = Place()
    links = Links(here)
    core, x, y = here.core, links.x, links.y
    half, keys, share, size = width // 2, 4 * rows, width // shards, width
    groups, parts, chunks = heads // 2, 4, 4
    step = rows // chunks

    in_plane = [(here.q, lax.rem(here.s + n, shards)) for n in range(1, shards)]
    along = [(lax.rem(here.q + n, 4), here.s) for n in range(1, 4)]
    greet(here, in_plane + along, here.to)

    def columns(c):
        return slice(c // 2 * size, (c // 2 + 1) * size)

    def x_f(c):
        return remote(v.mine_f.at[c // 2, c % 2, 0], v.got_f.at[0, c // 2], v.x_sf.at[c], v.x_rf.at[c], links.to_x)

    def y_f(c):
        return remote(v.mine_f.at[c // 2, c % 2, 1], v.got_f.at[1, c % 2], v.y_sf.at[c], v.y_rf.at[c], links.to_y)

    def on_i(c):
        to = columns(c)
        if c % 2 == 0:
            return remote(
                v.mine_i.at[:, 1 - x, 0, :, to], v.got_i.at[0, :, :, to], v.x_si.at[c], v.x_ri.at[c], links.to_x
            )
        return remote(
            v.mine_i.at[1 - y, :, 1, :, to], v.got_i.at[1, :, :, to], v.y_si.at[c], v.y_ri.at[c], links.to_y
        )

    hops_f, hops_i = [], []
    for c in range(parts):
        hops_f.append(FirstHop(functools.partial(x_f, c), x != c % 2, x == c % 2))
        hops_f.append(FirstHop(functools.partial(y_f, c), y != c // 2, y == c // 2))
        hops_i.append(FirstHop(functools.partial(on_i, c)))
    sums = [
        Reduction(here, links, v, "f", v.mine_f, hops_f),
        Reduction(here, links, v, "i", v.mine_i, hops_i),
        Reduction(here, links, v, "o", v.both_o.at[core], None, (v.both_o.at[1 - core], v.near_o)),
    ]
    sums += [Reduction(here, links, v, g, getattr(v, f"mine_{g}")) for g in range(groups)]

    def run(*steps):
        for which, number in steps:
            sums[which].phase(number)

    def home(src, dst, at):
        return remote(src, dst, v.perm_s.at[at], v.perm_r.at[at], here.origin)

    def home_start(src, dst, at):
        @pl.when(jnp.logical_not(here.stays))
        def _():
            home(src, dst, at).start()

        @pl.when(here.stays)
        def _():
            pltpu.make_async_copy(src, dst, v.perm_s.at[at]).start()

    def home_sent(src, dst, at):
        @pl.when(jnp.logical_not(here.stays))
        def _():
            home(src, dst, at).wait_send()

        @pl.when(here.stays)
        def _():
            pltpu.make_async_copy(src, dst, v.perm_s.at[at]).wait()

    def home_came(src, dst, at):
        @pl.when(jnp.logical_not(here.stays))
        def _():
            home(src, dst, at).wait_recv()

    def vector(at):
        return i.vec[at : at + 1, :]

    def feed_part(*buffers):
        b = Named(feed, buffers)

        def load(at):
            if at == 0:
                return pltpu.make_async_copy(i.wo_h, b.wo, v.load_s.at[0])
            c, slot = (at - 1) // 2, (at - 1) // 2 % 2
            to = slice(c * size, (c + 1) * size)
            if at % 2:
                return pltpu.make_async_copy(i.wi_h.at[:, to], b.wi.at[slot], v.load_s.at[1 + 2 * slot])
            return pltpu.make_async_copy(i.wf_h.at[to, :], b.wf.at[slot], v.load_s.at[2 + 2 * slot])

        for at in range(5):
            load(at).start()

        row_at = lax.broadcasted_iota(jnp.int32, (rows, 1), 0) + here.quarter * rows
        live = row_at < i.lens[0:1, 0:1]
        e_outer = jnp.where(live, i.cot[...].astype(F32), 0.0)
        b.eo[...] = e_outer.astype(BF)
        b.eot[...] = b.eo[...].T
        v.vecs[...] = jnp.zeros_like(v.vecs)
        v.vecs[FB : FB + 1, :] = jnp.sum(e_outer, 0, keepdims=True)

        load(0).wait()
        middle = i.x[...].astype(F32) + dot(i.ctx[...].T, b.wo[...]) + vector(OB)
        b.mid[...] = middle
        unit, _ = unit_of(middle)
        b.h2[...] = (unit * vector(LN2G) + vector(LN2B)).astype(BF)
        b.h2t[:width, :] = b.h2[...].T
        b.h2t[width:, :] = jnp.ones((16, rows), BF)
        b.acc[...] = middle + vector(FB)

        def near_f(c):
            return remote(
                b.both_f.at[c % 2, 1 - core], v.near_f.at[c // 2, c % 2], v.core_sf.at[c], v.core_rf.at[c],
                here.sibling,
            )

        def near_i(c):
            return remote(
                b.both_i.at[c % 2, 1 - core], v.near_i.at[:, :, c % 2, :, columns(c)], v.core_si.at[c],
                v.core_ri.at[c], here.sibling,
            )

        def store(c, grad_f, grad_i):
            if c >= 2:
                near_f(c - 2).wait_send()
                near_i(c - 2).wait_send()
            for k in range(2):
                for ab in range(2):
                    b.both_f[c % 2, k, ab] = grad_f[ab * half : (ab + 1) * half, k * half : (k + 1) * half]
                for n in range(4):
                    at = (2 * n + k) * share
                    b.both_i[c % 2, k, n // 2, n % 2] = grad_i[at : at + share]
            near_f(c).start()
            near_i(c).start()

        def send(c):
            to = columns(c)
            near_f(c).wait_recv()
            near_i(c).wait_recv()
            for ab in range(2):
                v.mine_f[c // 2, c % 2, ab] = b.both_f[c % 2, core, ab] + v.near_f[c // 2, c % 2, ab]
            hops_f[2 * c].start()
            hops_f[2 * c + 1].start()
            for n in range(4):
                v.mine_i[n // 2, n % 2, c % 2, :, to] = (
                    b.both_i[c % 2, core, n // 2, n % 2] + v.near_i[n // 2, n % 2, c % 2, :, to]
                )
            hops_i[c].start()

        for c in range(parts):
            at = slice(c * size, (c + 1) * size)
            load(1 + 2 * c).wait()
            load(2 + 2 * c).wait()
            wic, wfc = b.wi[c % 2], b.wf[c % 2]
            inner = dot(b.h2[...], wic) + i.inb[0:1, at]
            square = inner * inner
            swing = jnp.tanh(GELU_C * inner * (1.0 + GELU_K * square))
            active = (0.5 * inner * (1.0 + swing)).astype(BF)
            slope = 0.5 * (1.0 + swing) + 0.5 * inner * (1.0 - swing * swing) * (
                GELU_C * (1.0 + 3.0 * GELU_K * square)
            )
            e_inner = (dot_t(b.eo[...], wfc) * slope).astype(BF)
            grad_f = dot(b.eot[...], active).astype(BF)
            grad_i = dot(b.h2t[...], e_inner)
            v.gib[:, at] = grad_i[width : width + 8]
            store(c, grad_f, grad_i[:width].astype(BF))
            b.acc[...] += dot(active, wfc)
            part = dot_t(e_inner, wic)
            b.gh2[...] = part if c == 0 else b.gh2[...] + part
            if c + 2 < parts:
                load(5 + 2 * c).start()
                load(6 + 2 * c).start()
            if c > 0:
                send(c - 1)
        v.gt[...] = b.acc[...].astype(BF)
        home_start(v.gt, o.out_o, 4)
        unit, inverse = unit_of(b.mid[...])
        e_norm = b.gh2[...]
        v.vecs[LN2G : LN2G + 1, :] = jnp.sum(e_norm * unit, 0, keepdims=True)
        v.vecs[LN2B : LN2B + 1, :] = jnp.sum(e_norm, 0, keepdims=True)
        e_unit = e_norm * vector(LN2G)
        grad_mid = jnp.where(live, i.cot[...].astype(F32), 0.0) + inverse * (
            e_unit - mean_rows(e_unit) - unit * mean_rows(e_unit * unit)
        )
        v.gmid[...] = grad_mid
        e_branch = grad_mid.astype(BF)
        v.vecs[OB : OB + 1, :] = jnp.sum(e_branch.astype(F32), 0, keepdims=True)
        b.ect[...] = dot_t(b.wo[...], e_branch).astype(BF)
        mine = pl.ds(pl.multiple_of(core * half, 128), half)
        theirs = pl.ds(pl.multiple_of((1 - core) * half, 128), half)
        own = pl.ds(pl.multiple_of(core * rows, rows), rows)
        trade = remote(b.ect.at[theirs, :], v.e_ctx.at[:, own], v.trade_s.at[0], v.trade_r, here.sibling)
        trade.start()
        local = pltpu.make_async_copy(b.ect.at[mine, :], v.e_ctx.at[:, own], v.trade_s.at[1])
        local.start()
        send(parts - 1)
        grads = dot(i.ctx[...], e_branch).astype(BF)
        for n in range(shards):
            for ab in range(2):
                v.both_o[n % 2, n // 4, n // 2 % 2, ab] = grads[
                    n * share : (n + 1) * share, ab * half : (ab + 1) * half
                ]
        sums[2].copy(0).start()
        local.wait()
        trade.wait()
        for c in range(2, parts):
            near_f(c).wait_send()
            near_i(c).wait_send()

    pl.run_scoped(feed_part, *[spec for _, spec in feed])

    def attend_part(*buffers):
        b = Named(attend, buffers)

        def fetch(far, h, slot):
            rows_of = slice(2 * rows, keys) if far else slice(0, 2 * rows)
            return [
                pltpu.make_async_copy(src, dst, v.head_s.at[slot, n])
                for n, (src, dst) in enumerate(
                    (
                        (i.qat_h.at[h], b.qat.at[slot]),
                        (i.ka_h.at[h, rows_of, :], b.ka.at[slot]),
                        (i.va_h.at[h, rows_of, :], b.va.at[slot]),
                        (i.kt_h.at[h, :, rows_of], b.kt.at[slot]),
                    )
                )
            ]

        for copy in fetch(True, 0, 0):
            copy.start()

        def with_delta(ctxt, sem):
            load = pltpu.make_async_copy(i.ctxt_h, ctxt, sem)
            load.start()
            load.wait()
            index = lax.broadcasted_iota(jnp.int32, (16, 2 * rows), 0)
            for h in range(heads):
                at = slice(h * 64, (h + 1) * 64)
                e_ctx = v.e_ctx[at, :]
                delta = jnp.sum(e_ctx.astype(F32) * ctxt[at, :], 0, keepdims=True)
                rest = jnp.zeros((16, 2 * rows), F32)
                for r, term in enumerate(split3(delta)):
                    rest = jnp.where(index == r, term.astype(F32), rest)
                b.eat[h, :64, :] = e_ctx
                b.eat[h, 64:80, :] = rest.astype(BF)
                b.eat[h, 80:, :] = jnp.zeros((48, 2 * rows), BF)

        pl.run_scoped(with_delta, pltpu.VMEM((half, 2 * rows), F32), pltpu.SemaphoreType.DMA)
        loads = [
            pltpu.make_async_copy(i.wq_h, b.wq, v.load_s.at[5]),
            pltpu.make_async_copy(i.h1_h, b.h1, v.load_s.at[6]),
        ]
        for copy in loads:
            copy.start()
        block = 256

        def attend_half(far, polls):
            first = 2 * rows if far else 0

            def body(h, _):
                slot = lax.rem(h, 2)
                for copy in fetch(far, h, slot):
                    copy.wait()

                @pl.when(h < heads - 1)
                def _():
                    for copy in fetch(far, h + 1, 1 - slot):
                        copy.start()

                if far:
                    @pl.when(h == heads - 1)
                    def _():
                        for copy in fetch(False, 0, 1 - slot):
                            copy.start()

                query, e_ctx = b.qat[slot], b.eat[h]
                e_query = None
                for c in range(2 * rows // block):
                    of = slice(c * block, (c + 1) * block)
                    to = slice(first + c * block, first + (c + 1) * block)
                    weights = jnp.exp(dot(b.ka[slot, of, :], query))
                    e_scores = (weights * dot(b.va[slot, of, :], e_ctx)).astype(BF)
                    e_value = dot_t(e_ctx[:64], weights.astype(BF))
                    e_key = dot_t(query[:64], e_scores)
                    part = dot(b.kt[slot, :, of], e_scores)
                    e_query = part if e_query is None else e_query + part
                    b.grads[pl.ds(pl.multiple_of(half + h * 64, 64), 64), to] = e_key.astype(BF)
                    b.grads[pl.ds(pl.multiple_of(2 * half + h * 64, 64), 64), to] = e_value.astype(BF)
                head = pl.ds(pl.multiple_of(h * 64, 64), 64)
                lower = pl.ds(pl.multiple_of(half + h * 64, 64), 64)
                if far:
                    b.sums[head, :] = e_query[:, :rows]
                    b.sums[lower, :] = e_query[:, rows:]
                else:
                    b.grads[head, :rows] = ((b.sums[head, :] + e_query[:, :rows]) * HEAD_DIM**-0.5).astype(BF)
                    b.grads[head, rows : 2 * rows] = (
                        (b.sums[lower, :] + e_query[:, rows:]) * HEAD_DIM**-0.5
                    ).astype(BF)
                for when, action in polls:
                    pl.when(h == when)(action)
                return 0

            lax.fori_loop(0, heads, body, 0)

        def steps_of(table):
            return [(when, functools.partial(run, *steps)) for when, steps in table]

        def partial_of(j, near):
            at = pl.ds(pl.multiple_of(j * rows, rows), rows)
            if near:
                return dot(b.wq[...], b.grads[:, at])
            return dot(b.wq[:, half:], b.grads[half:, at])

        def sib_copy(at):
            return remote(b.sib_out.at[at], v.sib_in.at[at], v.sib_s.at[at], v.sib_r.at[at], here.sibling)

        def side_copy(at):
            to = slice(at * step, (at + 1) * step)
            return remote(
                b.side_out.at[:, to], v.side_in.at[:, to], v.side_s.at[at], v.side_r.at[at], here.beside
            )

        def to_side():
            sib_copy(0).wait_recv()
            b.side_out[...] = (partial_of(2 + core, False) + v.sib_in[0].astype(F32)).astype(BF)
            for at in range(chunks):
                side_copy(at).start()

        def weight_grad(g):
            for part, count in ((0, 2 * rows), (1, keys), (2, keys)):
                at = part * half + g * 128
                result = dot(b.grads[at : at + 128, :count], b.h1[:count, :]).T.astype(BF)
                to = slice(part * 128, (part + 1) * 128)
                for j in range(shards):
                    sums[3 + g].mine[j // 4, j // 2 % 2, j % 2, :, to] = result[j * share : (j + 1) * share]
            run((3 + g, 1))

        attend_half(True, steps_of(FAR_HEADS))
        for copy in loads:
            copy.wait()
        b.sib_out[0] = partial_of(3 - core, False).astype(BF)
        sib_copy(0).start()
        attend_half(
            False,
            [(0, to_side)]
            + [(2 * g + 1, functools.partial(weight_grad, g)) for g in range(groups - 1)]
            + steps_of(NEAR_HEADS),
        )
        b.sib_out[1] = partial_of(1 - core, True).astype(BF)
        sib_copy(1).start()
        weight_grad(groups - 1)
        own_part = partial_of(core, True)
        home_sent(v.gt, o.out_o, 4)
        sib_copy(1).wait_recv()
        b.sums[...] = own_part + v.sib_in[1].astype(F32)

        gain = vector(LN1G)
        gain_sum = shift_sum = None
        for at in range(chunks):
            to = slice(at * step, (at + 1) * step)
            side_copy(at).wait_recv()
            e_norm = (b.sums[:, to] + v.side_in[:, to].astype(F32)).T
            unit, inverse = unit_of(i.x[to, :].astype(F32))
            e_unit = e_norm * gain
            result = v.gmid[to, :] + inverse * (
                e_unit - mean_rows(e_unit) - unit * mean_rows(e_unit * unit)
            )
            v.gt[to, :] = result.astype(BF)
            home_start(v.gt.at[to, :], o.gtok_o.at[to, :], at)
            gains = jnp.sum(e_norm * unit, 0, keepdims=True)
            shifts = jnp.sum(e_norm, 0, keepdims=True)
            gain_sum = gains if at == 0 else gain_sum + gains
            shift_sum = shifts if at == 0 else shift_sum + shifts
        v.vecs[LN1G : LN1G + 1, :] = gain_sum
        v.vecs[LN1B : LN1B + 1, :] = shift_sum

        def row_sums(values):
            folded = values[:, :128].astype(F32)
            for n in range(1, values.shape[1] // 128):
                folded += values[:, n * 128 : (n + 1) * 128].astype(F32)
            return jnp.sum(folded.T, 0, keepdims=True)

        for at, part in ((QB, b.grads[:half, : 2 * rows]), (VB, b.grads[2 * half :, :])):
            total = row_sums(part)
            for n in range(2):
                v.vecs[at : at + 1, n * half : (n + 1) * half] = jnp.where(core == n, total, 0.0)

        for n in range(shards):
            v.vec_out[n, :, :share] = v.vecs[:, n * share : (n + 1) * share]
            for r in range(4):
                to = (4 * n + r) * share
                v.vec_out[n, IB + r : IB + r + 1, :share] = v.gib[0:1, to : to + share]

        def vec_plane(n):
            to = lax.rem(here.s + n, shards)
            return remote(
                v.vec_out.at[to], v.vec_in.at[here.s], v.vec_s.at[n], v.vec_r.at[n], (here.q, to)
            )

        def vec_along(n):
            to, at = lax.rem(here.q + n, 4), shards + n
            return remote(
                v.vec_all.at[here.q], v.vec_all.at[here.q], v.vec_s.at[at], v.vec_r.at[at], (to, here.s)
            )

        for n in range(1, shards):
            vec_plane(n).start()
        v.vec_in[here.s] = v.vec_out[here.s]
        run(*TAIL[0])
        for n in range(1, shards):
            vec_plane(n).wait_recv()
        total = v.vec_in[0]
        for n in range(1, shards):
            total += v.vec_in[n]
        v.vec_all[here.q] = total
        for n in range(1, 4):
            vec_along(n).start()
        run(*TAIL[1])
        for n in range(1, 4):
            vec_along(n).wait_recv()
        o.vec_o[...] = (v.vec_all[0] + v.vec_all[1]) + (v.vec_all[2] + v.vec_all[3])
        run(*TAIL[2])
        finals = []

        def final(src, dst, at):
            copy = pltpu.make_async_copy(src, dst, v.final_s.at[at])
            copy.start()
            finals.append(copy)

        def w_trade(g):
            return remote(sums[3 + g].done.at[1 - core], v.w_in.at[g], v.w_s.at[g], v.w_r.at[g], here.sibling)

        for g in range(groups):
            w_trade(g).start()
        for n, dst in enumerate((o.sum_f, o.sum_i, o.sum_o)):
            final(sums[n].done, dst, n)
        for g in range(groups):
            final(sums[3 + g].done.at[core], o.sum_w.at[g, core], 3 + 2 * g)
            w_trade(g).wait()
            final(v.w_in.at[g], o.sum_w.at[g, 1 - core], 4 + 2 * g)
        for copy in finals:
            copy.wait()
        for each in sums:
            each.finish()
        for n in range(1, shards):
            vec_plane(n).wait_send()
        for n in range(1, 4):
            vec_along(n).wait_send()
        for at in range(2):
            sib_copy(at).wait_send()
        for at in range(chunks):
            side_copy(at).wait_send()
            to = slice(at * step, (at + 1) * step)
            home_sent(v.gt.at[to, :], o.gtok_o.at[to, :], at)
            home_came(v.gt.at[to, :], o.gtok_o.at[to, :], at)
        home_came(v.gt, o.out_o, 4)

    pl.run_scoped(attend_part, *[spec for _, spec in attend])


def middle(dims, *args):
    ins, outs, scratch, _, _ = middle_specs(dims)
    return pl.pallas_call(
        functools.partial(middle_kernel, dims),
        out_shape=tuple(jax.ShapeDtypeStruct(*out[1]) for out in outs),
        in_specs=[spec for _, spec in ins],
        out_specs=tuple(out[2] for out in outs),
        scratch_shapes=[spec for _, spec in scratch],
        compiler_params=pltpu.CompilerParams(
            collective_id=1, has_side_effects=True, vmem_limit_bytes=62 * 2**20
        ),
        name="feed_forward_and_attention_backward",
    )(*args)


def feed_specs(dims):
    shards, rows, width, heads, gather = dims
    half, share = width // 2, width // shards
    sems = pltpu.SemaphoreType.DMA
    ins = [(name, VMEM) for name in ("ctx", "x", "cot", "lens", "vec", "inb")]
    ins += [(name, ANY) for name in ("wo_h", "wi_h", "wf_h")]
    outs = [
        ("out_o", ((rows, width), BF)),
        ("ect_o", ((width, rows), BF)),
        ("gmid_o", ((rows, width), F32)),
        ("vec_o", ((VROWS, width), F32)),
        ("gib_o", ((8, 4 * width), F32)),
    ]
    scratch = [
        ("wo", pltpu.VMEM((width, width), BF)),
        ("wi", pltpu.VMEM((width, 4 * width), BF)),
        ("wf", pltpu.VMEM((4 * width, width), BF)),
        ("mid", pltpu.VMEM((rows, width), F32)),
        ("h2", pltpu.VMEM((rows, width), BF)),
        ("h2t", pltpu.VMEM((width + 16, rows), BF)),
        ("eo", pltpu.VMEM((rows, width), BF)),
        ("eot", pltpu.VMEM((width, rows), BF)),
        ("gh2", pltpu.VMEM((rows, width), F32)),
        ("acc", pltpu.VMEM((rows, width), F32)),
        ("in_s", sems((9,))),
    ]
    if gather:
        part_f, part_i, part_o = grad_parts(dims)
        outs += [
            ("pair_f", ((2, 2) + part_f, BF)),
            ("pair_i", ((2, 2) + part_i, BF)),
            ("gwo_o", ((2, 2, 2, 2) + part_o, BF)),
        ]
        for name, part, away in (("f", part_f, (2, 2) + part_f), ("i", part_i, (2, 2, 2, share, width))):
            scratch += [
                ("mine_" + name, pltpu.VMEM((2, 2, 2) + part, BF)),
                ("near_" + name, pltpu.VMEM((2, 2, 2) + part, BF)),
                ("got_" + name, pltpu.VMEM((2, 2) + part, BF)),
                ("away_" + name, pltpu.VMEM(away, BF)),
                ("core_s" + name, sems((4,))),
                ("core_r" + name, sems((4,))),
                ("x_s" + name, sems((4,))),
                ("x_r" + name, sems((4,))),
                ("y_s" + name, sems((4,))),
                ("y_r" + name, sems((4,))),
            ]
    else:
        outs += [
            ("gwf_o", ((width, 4 * width), BF)),
            ("gwi_o", ((width, 4 * width), BF)),
            ("gwo_o", ((width, width), BF)),
        ]
    return ins, outs, scratch


def feed_kernel(dims, *refs):
    shards, rows, width, heads, gather = dims
    ins, outs, scratch = feed_specs(dims)
    at_ins, at_outs = len(ins), len(ins) + len(outs)
    i = Named(ins, refs[:at_ins])
    o = Named(outs, refs[at_ins:at_outs])
    v = Named(scratch, refs[at_outs:])
    here = Place()
    size = width
    share, half = width // shards, width // 2
    parts = 4

    def load(at):
        if at == 0:
            return pltpu.make_async_copy(i.wo_h, v.wo, v.in_s.at[0])
        to = slice((at - 1) // 2 * size, ((at - 1) // 2 + 1) * size)
        if at % 2:
            return pltpu.make_async_copy(i.wi_h.at[:, to], v.wi.at[:, to], v.in_s.at[at])
        return pltpu.make_async_copy(i.wf_h.at[to, :], v.wf.at[to, :], v.in_s.at[at])

    for at in range(9):
        load(at).start()
    if gather:
        links = Links(here)
        greet_all([here.sibling, links.to_x, links.to_y])

    def vector(at):
        return i.vec[at : at + 1, :]

    row_at = lax.broadcasted_iota(jnp.int32, (rows, 1), 0) + here.quarter * rows
    live = row_at < i.lens[0:1, 0:1]
    e_outer = jnp.where(live, i.cot[...].astype(F32), 0.0)
    v.eo[...] = e_outer.astype(BF)
    v.eot[...] = v.eo[...].T
    o.vec_o[...] = jnp.zeros_like(o.vec_o)
    o.vec_o[FB : FB + 1, :] = jnp.sum(e_outer, 0, keepdims=True)

    load(0).wait()
    middle = i.x[...].astype(F32) + dot(i.ctx[...].T, v.wo[...]) + vector(OB)
    v.mid[...] = middle
    unit, _ = unit_of(middle)
    v.h2[...] = (unit * vector(LN2G) + vector(LN2B)).astype(BF)
    v.h2t[:width, :] = v.h2[...].T
    v.h2t[width:, :] = jnp.ones((16, rows), BF)
    v.acc[...] = middle + vector(FB)

    def near_f(c):
        y, x = c // 2, c % 2
        return remote(
            v.away_f.at[c % 2], v.near_f.at[y, x], v.core_sf.at[c], v.core_rf.at[c], here.sibling
        )

    def near_i(c):
        to = slice(c // 2 * size, (c // 2 + 1) * size)
        return remote(
            v.away_i.at[c % 2], v.near_i.at[:, :, c % 2, :, to], v.core_si.at[c], v.core_ri.at[c], here.sibling
        )

    def x_f(c):
        return remote(v.mine_f.at[c // 2, c % 2, 0], v.got_f.at[0, c // 2], v.x_sf.at[c], v.x_rf.at[c], links.to_x)

    def y_f(c):
        return remote(v.mine_f.at[c // 2, c % 2, 1], v.got_f.at[1, c % 2], v.y_sf.at[c], v.y_rf.at[c], links.to_y)

    def on_i(c):
        to = slice(c // 2 * size, (c // 2 + 1) * size)
        if c % 2 == 0:
            return remote(
                v.mine_i.at[:, 1 - links.x, 0, :, to], v.got_i.at[0, :, :, to], v.x_si.at[c], v.x_ri.at[c], links.to_x
            )
        return remote(
            v.mine_i.at[1 - links.y, :, 1, :, to], v.got_i.at[1, :, :, to], v.y_si.at[c], v.y_ri.at[c], links.to_y
        )

    def store(c, grad_f, grad_i):
        y, x, to = c // 2, c % 2, slice(c // 2 * size, (c // 2 + 1) * size)
        if c >= 2:
            near_f(c - 2).wait_send()
            near_i(c - 2).wait_send()

        def keep(core):
            for ab in range(2):
                rows_of = slice(ab * half, (ab + 1) * half)
                v.mine_f[y, x, ab] = grad_f[rows_of, core * half : (core + 1) * half]
                v.away_f[c % 2, ab] = grad_f[rows_of, (1 - core) * half : (2 - core) * half]
            for n in range(4):
                one, two = 2 * n + core, 2 * n + 1 - core
                v.mine_i[n // 2, n % 2, c % 2, :, to] = grad_i[one * share : (one + 1) * share]
                v.away_i[c % 2, n // 2, n % 2] = grad_i[two * share : (two + 1) * share]

        for core in range(2):
            pl.when(here.core == core)(functools.partial(keep, core))
        near_f(c).start()
        near_i(c).start()

    def send(c):
        y, x, to = c // 2, c % 2, slice(c // 2 * size, (c // 2 + 1) * size)
        near_f(c).wait_recv()
        near_i(c).wait_recv()
        for ab in range(2):
            v.mine_f[y, x, ab] += v.near_f[y, x, ab]
        for n in range(4):
            v.mine_i[n // 2, n % 2, c % 2, :, to] += v.near_i[n // 2, n % 2, c % 2, :, to]
        pl.when(links.x != x)(lambda: x_f(c).start())
        pl.when(links.y != y)(lambda: y_f(c).start())
        on_i(c).start()

    for c in range(parts):
        at = slice(c * size, (c + 1) * size)
        load(1 + 2 * c).wait()
        load(2 + 2 * c).wait()
        wic, wfc = v.wi[:, at], v.wf[at, :]
        inner = dot(v.h2[...], wic) + i.inb[0:1, at]
        square = inner * inner
        swing = jnp.tanh(GELU_C * inner * (1.0 + GELU_K * square))
        active = (0.5 * inner * (1.0 + swing)).astype(BF)
        slope = 0.5 * (1.0 + swing) + 0.5 * inner * (1.0 - swing * swing) * (
            GELU_C * (1.0 + 3.0 * GELU_K * square)
        )
        e_inner = (dot_t(v.eo[...], wfc) * slope).astype(BF)
        grad_f = dot(v.eot[...], active).astype(BF)
        grad_i = dot(v.h2t[...], e_inner)
        o.gib_o[:, at] = grad_i[width : width + 8]
        grad_i = grad_i[:width].astype(BF)
        if gather:
            store(c, grad_f, grad_i)
        else:
            o.gwf_o[:, at] = grad_f
            o.gwi_o[:, at] = grad_i
        v.acc[...] += dot(active, wfc)
        part = dot_t(e_inner, wic)
        v.gh2[...] = part if c == 0 else v.gh2[...] + part
        if gather and c > 0:
            send(c - 1)
    o.out_o[...] = v.acc[...].astype(BF)
    unit, inverse = unit_of(v.mid[...])
    e_norm = v.gh2[...]
    o.vec_o[LN2G : LN2G + 1, :] = jnp.sum(e_norm * unit, 0, keepdims=True)
    o.vec_o[LN2B : LN2B + 1, :] = jnp.sum(e_norm, 0, keepdims=True)
    if gather:
        send(parts - 1)
    e_unit = e_norm * vector(LN2G)
    grad_mid = jnp.where(live, i.cot[...].astype(F32), 0.0) + inverse * (
        e_unit - mean_rows(e_unit) - unit * mean_rows(e_unit * unit)
    )
    o.gmid_o[...] = grad_mid
    e_branch = grad_mid.astype(BF)
    o.vec_o[OB : OB + 1, :] = jnp.sum(e_branch.astype(F32), 0, keepdims=True)
    o.ect_o[...] = dot_t(v.wo[...], e_branch).astype(BF)
    grads = dot(i.ctx[...], e_branch).astype(BF)
    if not gather:
        o.gwo_o[...] = grads
        return
    for n in range(shards):
        for ab in range(2):
            o.gwo_o[n // 4, n // 2 % 2, n % 2, ab] = grads[
                n * share : (n + 1) * share, ab * half : (ab + 1) * half
            ]
    y, x = links.y, links.x
    for c in range(parts):
        pl.when(x == c % 2)(lambda: x_f(c).wait_recv())
        pl.when(y == c // 2)(lambda: y_f(c).wait_recv())
        on_i(c).wait_recv()
    for mine, got, pair in ((v.mine_f, v.got_f, o.pair_f), (v.mine_i, v.got_i, o.pair_i)):
        pair[0, 0] = mine[y, x, 0] + got[0, y]
        pair[0, 1] = mine[1 - y, x, 0] + got[0, 1 - y]
        pair[1, 0] = mine[y, x, 1] + got[1, x]
        pair[1, 1] = mine[y, 1 - x, 1] + got[1, 1 - x]
    for c in range(parts):
        if c >= 2:
            near_f(c).wait_send()
            near_i(c).wait_send()
        pl.when(x != c % 2)(lambda: x_f(c).wait_send())
        pl.when(y != c // 2)(lambda: y_f(c).wait_send())
        on_i(c).wait_send()


def feed_forward(dims, *args):
    ins, outs, scratch = feed_specs(dims)
    gather = dims[-1]
    return pl.pallas_call(
        functools.partial(feed_kernel, dims),
        out_shape=tuple(jax.ShapeDtypeStruct(*out[1]) for out in outs),
        in_specs=[spec for _, spec in ins],
        out_specs=tuple([VMEM] * len(outs)),
        scratch_shapes=[spec for _, spec in scratch],
        compiler_params=pltpu.CompilerParams(
            collective_id=2 if gather else None, has_side_effects=gather, vmem_limit_bytes=60 * 2**20
        ),
        name="feed_forward",
    )(*args)


def backward_specs(dims):
    shards, rows, width, heads, gather = dims
    half, keys, share = width // 2, 4 * rows, width // shards
    groups = heads // 2
    sems = pltpu.SemaphoreType.DMA
    ins = [("ect", VMEM)]
    ins += [(name, ANY) for name in ("ka_h", "va_h", "kt_h", "qat_h", "ctxt_h", "h1_h", "wq_h", "out_h")]
    ins += [(name, VMEM) for name in ("x", "gmid", "vec")]
    outs = [
        ("gtok_o", ((rows, width), BF), ANY),
        ("out_o", ((rows, width), BF), ANY),
        ("vec_o", ((VROWS, 128 if gather else width), F32), VMEM),
    ]
    scratch = [
        ("vecs", pltpu.VMEM((VROWS, width), F32)),
        ("ka", pltpu.VMEM((heads, keys, 128), BF)),
        ("va", pltpu.VMEM((heads, keys, 128), BF)),
        ("kt", pltpu.VMEM((heads, 64, keys), BF)),
        ("qat", pltpu.VMEM((heads, 128, 2 * rows), BF)),
        ("h1", pltpu.VMEM((keys, width), BF)),
        ("wq", pltpu.VMEM((width, 3 * half), BF)),
        ("e_ctx", pltpu.VMEM((half, 2 * rows), BF)),
        ("eat", pltpu.VMEM((heads, 128, 2 * rows), BF)),
        ("grads", pltpu.VMEM((3 * half, keys), BF)),
        ("sums", pltpu.VMEM((width, rows), F32)),
        ("sib_out", pltpu.VMEM((2, width, rows), BF)),
        ("sib_in", pltpu.VMEM((2, width, rows), BF)),
        ("side_out", pltpu.VMEM((width, rows), BF)),
        ("side_in", pltpu.VMEM((width, rows), BF)),
        ("gt", pltpu.VMEM((rows, width), BF)),
        ("load_s", sems((7,))),
        ("trade_s", sems((2,))),
        ("trade_r", sems),
        ("sib_s", sems((2,))),
        ("sib_r", sems((2,))),
        ("side_s", sems((4,))),
        ("side_r", sems((4,))),
        ("perm_s", sems((5,))),
        ("perm_r", sems((5,))),
    ]
    if gather:
        parts = grad_parts(dims)
        ins += [("vec_two", VMEM), ("gib", VMEM)] + [(f"whole{i}", ANY) for i in range(3)]
        outs += [(f"sum{i}", ((2,) + part, BF), ANY) for i, part in enumerate(parts)]
        outs += [("sum_w", ((groups, 2, share, half), BF), ANY)]
        for i in range(3 + groups):
            shape = parts[i] if i < 3 else (share, half)
            scratch += [(f"r{i}_{j}", spec) for j, spec in enumerate(Reduction.scratch(*shape, i == 2, i < 2))]
        scratch += [
            ("vec_out", pltpu.VMEM((shards, VROWS, 128), F32)),
            ("vec_in", pltpu.VMEM((shards, VROWS, 128), F32)),
            ("vec_all", pltpu.VMEM((4, VROWS, 128), F32)),
            ("vec_s", sems((shards + 4,))),
            ("vec_r", sems((shards + 4,))),
            ("w_in", pltpu.VMEM((groups, share, half), BF)),
            ("w_s", sems((groups,))),
            ("w_r", sems((groups,))),
            ("final_s", sems((3 + 2 * groups,))),
        ]
    else:
        outs += [("gw_o", ((groups, width, half), BF), VMEM)]
    return ins, outs, scratch


def backward_kernel(dims, *refs):
    shards, rows, width, heads, gather = dims
    ins, outs, scratch = backward_specs(dims)
    at_ins, at_outs = len(ins), len(ins) + len(outs)
    i = Named(ins, refs[:at_ins])
    o = Named([out[:2] for out in outs], refs[at_ins:at_outs])
    v = Named(scratch, refs[at_outs:])
    here = Place()
    core = here.core
    half, keys, share = width // 2, 4 * rows, width // shards
    groups = heads // 2
    chunks = 4
    step = rows // chunks
    sums = []
    if gather:
        links = Links(here)
        for n in range(3 + groups):
            buffers = [getattr(v, f"r{n}_{j}") for j in range(Reduction.REFS)]
            source = getattr(i, f"whole{n}") if n < 3 else None
            sums.append(Reduction(here, links, buffers, source if n == 2 else None, source if n < 2 else None))

    loads = []
    for at, (src, dst) in enumerate(
        ((i.qat_h, v.qat), (i.ka_h, v.ka), (i.va_h, v.va), (i.kt_h, v.kt), (i.wq_h, v.wq), (i.h1_h, v.h1))
    ):
        copy = pltpu.make_async_copy(src, dst, v.load_s.at[at])
        copy.start()
        loads.append(copy)

    partners = [here.sibling, here.beside]
    if gather:
        in_plane = [(here.q, lax.rem(here.s + n, shards)) for n in range(1, shards)]
        along = [(lax.rem(here.q + n, 4), here.s) for n in range(1, 4)]
        partners = in_plane + along
    greet(here, partners, here.to)

    def run(*steps):
        if gather:
            for which, number in steps:
                sums[which].phase(number)

    mine = pl.ds(pl.multiple_of(core * half, 128), half)
    theirs = pl.ds(pl.multiple_of((1 - core) * half, 128), half)
    own = pl.ds(pl.multiple_of(core * rows, rows), rows)
    trade = remote(i.ect.at[theirs, :], v.e_ctx.at[:, own], v.trade_s.at[0], v.trade_r, here.sibling)
    trade.start()
    local = pltpu.make_async_copy(i.ect.at[mine, :], v.e_ctx.at[:, own], v.trade_s.at[1])
    local.start()
    run((0, 0), (1, 0), (2, 0))
    run((0, 2), (1, 2))

    def home(src, dst, at):
        return remote(src, dst, v.perm_s.at[at], v.perm_r.at[at], here.origin)

    def home_start(src, dst, at):
        @pl.when(jnp.logical_not(here.stays))
        def _():
            home(src, dst, at).start()

        @pl.when(here.stays)
        def _():
            pltpu.make_async_copy(src, dst, v.perm_r.at[at]).start()

    def home_wait(src, dst, at):
        pltpu.make_async_copy(src, dst, v.perm_r.at[at]).wait()

        @pl.when(jnp.logical_not(here.stays))
        def _():
            home(src, dst, at).wait_send()

    home_start(i.out_h, o.out_o, 4)
    local.wait()
    trade.wait()

    def with_delta(ctxt, sem):
        load = pltpu.make_async_copy(i.ctxt_h, ctxt, sem)
        load.start()
        load.wait()
        index = lax.broadcasted_iota(jnp.int32, (16, 2 * rows), 0)
        for h in range(heads):
            at = slice(h * 64, (h + 1) * 64)
            e_ctx = v.e_ctx[at, :]
            delta = jnp.sum(e_ctx.astype(F32) * ctxt[at, :], 0, keepdims=True)
            rest = jnp.zeros((16, 2 * rows), F32)
            for r, term in enumerate(split3(delta)):
                rest = jnp.where(index == r, term.astype(F32), rest)
            v.eat[h, :64, :] = e_ctx
            v.eat[h, 64:80, :] = rest.astype(BF)
            v.eat[h, 80:, :] = jnp.zeros((48, 2 * rows), BF)

    pl.run_scoped(with_delta, pltpu.VMEM((half, 2 * rows), F32), pltpu.SemaphoreType.DMA)
    for copy in loads:
        copy.wait()

    size = 256

    def attend(far, polls):
        first = 2 * rows if far else 0

        def body(h, _):
            query, e_ctx = v.qat[h], v.eat[h]
            e_query = None
            for c in range(2 * rows // size):
                to = slice(first + c * size, first + (c + 1) * size)
                weights = jnp.exp(dot(v.ka[h, to, :], query))
                e_scores = (weights * dot(v.va[h, to, :], e_ctx)).astype(BF)
                e_value = dot_t(e_ctx[:64], weights.astype(BF))
                e_key = dot_t(query[:64], e_scores)
                part = dot(v.kt[h, :, to], e_scores)
                e_query = part if e_query is None else e_query + part
                v.grads[pl.ds(pl.multiple_of(half + h * 64, 64), 64), to] = e_key.astype(BF)
                v.grads[pl.ds(pl.multiple_of(2 * half + h * 64, 64), 64), to] = e_value.astype(BF)
            head = pl.ds(pl.multiple_of(h * 64, 64), 64)
            lower = pl.ds(pl.multiple_of(half + h * 64, 64), 64)
            if far:
                v.sums[head, :] = e_query[:, :rows]
                v.sums[lower, :] = e_query[:, rows:]
            else:
                v.grads[head, :rows] = ((v.sums[head, :] + e_query[:, :rows]) * HEAD_DIM**-0.5).astype(BF)
                v.grads[head, rows : 2 * rows] = (
                    (v.sums[lower, :] + e_query[:, rows:]) * HEAD_DIM**-0.5
                ).astype(BF)
            for when, action in polls:
                pl.when(h == when)(action)
            return 0

        lax.fori_loop(0, heads, body, 0)

    def steps_of(table):
        return [(when, functools.partial(run, *steps)) for when, steps in table]

    def partial_of(j, near):
        at = pl.ds(pl.multiple_of(j * rows, rows), rows)
        if near:
            return dot(v.wq[...], v.grads[:, at])
        return dot(v.wq[:, half:], v.grads[half:, at])

    def sib_copy(at):
        return remote(v.sib_out.at[at], v.sib_in.at[at], v.sib_s.at[at], v.sib_r.at[at], here.sibling)

    def side_copy(at):
        to = slice(at * step, (at + 1) * step)
        return remote(
            v.side_out.at[:, to], v.side_in.at[:, to], v.side_s.at[at], v.side_r.at[at], here.beside
        )

    def to_side():
        sib_copy(0).wait_recv()
        v.side_out[...] = (partial_of(2 + core, False) + v.sib_in[0].astype(F32)).astype(BF)
        for at in range(chunks):
            side_copy(at).start()

    def weight_grad(g):
        for part, count in ((0, 2 * rows), (1, keys), (2, keys)):
            at = part * half + g * 128
            result = dot(v.grads[at : at + 128, :count], v.h1[:count, :]).T.astype(BF)
            to = slice(part * 128, (part + 1) * 128)
            if gather:
                for j in range(shards):
                    sums[3 + g].mine[j // 4, j // 2 % 2, j % 2, :, to] = result[j * share : (j + 1) * share]
            else:
                o.gw_o[g, :, to] = result
        run((3 + g, 1))

    attend(True, steps_of(FAR_HEADS))
    v.sib_out[0] = partial_of(3 - core, False).astype(BF)
    sib_copy(0).start()
    attend(
        False,
        [(0, to_side)]
        + [(2 * g + 1, functools.partial(weight_grad, g)) for g in range(groups - 1)]
        + steps_of(NEAR_HEADS),
    )
    v.sib_out[1] = partial_of(1 - core, True).astype(BF)
    sib_copy(1).start()
    weight_grad(groups - 1)
    own_part = partial_of(core, True)
    sib_copy(1).wait_recv()
    v.sums[...] = own_part + v.sib_in[1].astype(F32)

    def row_sums(values):
        folded = values[:, :128].astype(F32)
        for n in range(1, values.shape[1] // 128):
            folded += values[:, n * 128 : (n + 1) * 128].astype(F32)
        return jnp.sum(folded.T, 0, keepdims=True)

    v.vecs[...] = jnp.zeros_like(v.vecs)
    for at, part in ((QB, v.grads[:half, : 2 * rows]), (VB, v.grads[2 * half :, :])):
        total = row_sums(part)
        for n in range(2):
            v.vecs[at : at + 1, n * half : (n + 1) * half] = jnp.where(core == n, total, 0.0)
    if gather:
        v.vecs[OB:IB, :] = i.vec_two[OB:IB, :]

    gain = i.vec[LN1G : LN1G + 1, :]
    gain_sum = shift_sum = None
    for at in range(chunks):
        to = slice(at * step, (at + 1) * step)
        side_copy(at).wait_recv()
        e_norm = (v.sums[:, to] + v.side_in[:, to].astype(F32)).T
        unit, inverse = unit_of(i.x[to, :].astype(F32))
        e_unit = e_norm * gain
        result = i.gmid[to, :] + inverse * (
            e_unit - mean_rows(e_unit) - unit * mean_rows(e_unit * unit)
        )
        v.gt[to, :] = result.astype(BF)
        home_start(v.gt.at[to, :], o.gtok_o.at[to, :], at)
        gains = jnp.sum(e_norm * unit, 0, keepdims=True)
        shifts = jnp.sum(e_norm, 0, keepdims=True)
        gain_sum = gains if at == 0 else gain_sum + gains
        shift_sum = shifts if at == 0 else shift_sum + shifts
    v.vecs[LN1G : LN1G + 1, :] = gain_sum
    v.vecs[LN1B : LN1B + 1, :] = shift_sum
    if not gather:
        o.vec_o[...] = v.vecs[...]

    if gather:
        for n in range(shards):
            v.vec_out[n, :, :share] = v.vecs[:, n * share : (n + 1) * share]
            for r in range(4):
                to = (4 * n + r) * share
                v.vec_out[n, IB + r : IB + r + 1, :share] = i.gib[0:1, to : to + share]

        def vec_plane(n):
            to = lax.rem(here.s + n, shards)
            return remote(
                v.vec_out.at[to], v.vec_in.at[here.s], v.vec_s.at[n], v.vec_r.at[n], (here.q, to)
            )

        def vec_along(n):
            to = lax.rem(here.q + n, 4)
            at = shards + n
            return remote(
                v.vec_all.at[here.q], v.vec_all.at[here.q], v.vec_s.at[at], v.vec_r.at[at], (to, here.s)
            )

        for n in range(1, shards):
            vec_plane(n).start()
        v.vec_in[here.s] = v.vec_out[here.s]
        run(*TAIL[0])
        for n in range(1, shards):
            vec_plane(n).wait_recv()
        total = v.vec_in[0]
        for n in range(1, shards):
            total += v.vec_in[n]
        v.vec_all[here.q] = total
        for n in range(1, 4):
            vec_along(n).start()
        run(*TAIL[1])
        for n in range(1, 4):
            vec_along(n).wait_recv()
        o.vec_o[...] = (v.vec_all[0] + v.vec_all[1]) + (v.vec_all[2] + v.vec_all[3])
        run(*TAIL[2])
        finals = []

        def final(src, dst, at):
            copy = pltpu.make_async_copy(src, dst, v.final_s.at[at])
            copy.start()
            finals.append(copy)

        def w_trade(g):
            return remote(sums[3 + g].done.at[1 - core], v.w_in.at[g], v.w_s.at[g], v.w_r.at[g], here.sibling)

        for g in range(groups):
            w_trade(g).start()
        for n in range(3):
            final(sums[n].done, getattr(o, f"sum{n}"), n)
        for g in range(groups):
            final(sums[3 + g].done.at[core], o.sum_w.at[g, core], 3 + 2 * g)
            w_trade(g).wait()
            final(v.w_in.at[g], o.sum_w.at[g, 1 - core], 4 + 2 * g)
        for copy in finals:
            copy.wait()
        for each in sums:
            each.finish()
        for n in range(1, shards):
            vec_plane(n).wait_send()
        for n in range(1, 4):
            vec_along(n).wait_send()

    for at in range(2):
        sib_copy(at).wait_send()
    for at in range(chunks):
        side_copy(at).wait_send()
        to = slice(at * step, (at + 1) * step)
        home_wait(v.gt.at[to, :], o.gtok_o.at[to, :], at)
    home_wait(i.out_h, o.out_o, 4)


def attention_backward(dims, *args):
    ins, outs, scratch = backward_specs(dims)
    return pl.pallas_call(
        functools.partial(backward_kernel, dims),
        out_shape=tuple(jax.ShapeDtypeStruct(*out[1]) for out in outs),
        in_specs=[spec for _, spec in ins],
        out_specs=tuple(out[2] for out in outs),
        scratch_shapes=[spec for _, spec in scratch],
        compiler_params=pltpu.CompilerParams(
            collective_id=1, has_side_effects=True, vmem_limit_bytes=61 * 2**20
        ),
        name="attention_backward",
    )(*args)


def final_kernel(vec, d_f, d_i, d_o, d_w, t_f, t_i, t_o, t_w, *vectors):
    half, share = d_f.shape[1], d_i.shape[1]
    width = 2 * half
    for ab in range(2):
        t_f[:, ab * half : (ab + 1) * half] = d_f[ab].astype(F32).T
        t_o[:, ab * half : (ab + 1) * half] = d_o[ab].astype(F32)
        for sub in range(2):
            to = (2 * sub + ab) * width
            t_i[:, to : to + width] = d_i[ab, :, sub * width : (sub + 1) * width].astype(F32)
    for g in range(d_w.shape[0]):
        for core in range(2):
            for part in range(3):
                to = part * width + core * half + g * 128
                t_w[:, to : to + 128] = d_w[g, core, :, part * 128 : (part + 1) * 128].astype(F32)
    for n, out in enumerate(vectors[:-1]):
        out[...] = vec[n : n + 1, :share]
    for r in range(4):
        vectors[-1][:, r * share : (r + 1) * share] = vec[IB + r : IB + r + 1, :share]


def final_layout(dims, vec, *sums):
    shards, rows, width, heads, _ = dims
    share = width // shards
    out = [(4 * share, width), (share, 4 * width), (share, width), (share, 3 * width)]
    out += [(1, share)] * IB + [(1, 4 * share)]
    return pl.pallas_call(
        final_kernel,
        out_shape=tuple(jax.ShapeDtypeStruct(o, F32) for o in out),
        in_specs=[VMEM] * 5,
        out_specs=tuple([VMEM] * len(out)),
        compiler_params=pltpu.CompilerParams(vmem_limit_bytes=32 * 2**20),
        name="final_layout",
    )(vec, *sums)


def on_device(
    tokens, ln1_gain, ln1_shift, w_qkv, q_bias, v_bias, w_out, out_bias, ln2_gain, ln2_shift, w_in, in_bias,
    w_fin, fin_bias, cotangent, lengths, n_seq, shards,
):
    _, rows, width = tokens.shape
    heads = width // HEAD_DIM // 2
    half = width // 2
    share = width // shards
    gather = shards == 8
    dims = (shards, rows, width, heads, gather)
    axes = ("seq", "shard")
    there = relocation(n_seq, shards)
    core = lax.rem(lax.axis_index("shard"), 2)

    packed = jnp.concatenate(
        [v.reshape(-1, share) for v in (ln1_gain, ln1_shift, q_bias, v_bias, out_bias, ln2_gain, ln2_shift, fin_bias, in_bias)]
    )
    length = jnp.broadcast_to(lengths.reshape(1, 1), (8, 128))
    if gather:
        vec = jnp.pad(packed, ((0, VROWS - VECS), (0, 128 - share)))
        w_here = w_qkv
    else:
        every = lax.all_gather(packed, "shard", axis=1, tiled=True)
        vec = jnp.pad(every, ((0, VROWS - VECS), (0, 0)))
        full_w = lax.all_gather(w_qkv, "shard", axis=0, tiled=True)
        w_here = lax.dynamic_index_in_dim(
            full_w.reshape(width, 3, 2, half), core, 2, keepdims=False
        ).reshape(width, 3 * half)
    shares = (w_out, w_in, w_fin) if gather else ()
    (ka, va, kt, qat, ctxt, ctx, h1, wf, x, lens, vecs, inb, *wholes) = attention_forward(
        dims, tokens.reshape(rows, width), length, w_here, vec, *shares
    )
    if not gather:
        inb = jnp.broadcast_to(
            lax.all_gather(in_bias, "shard", axis=0, tiled=True).astype(F32)[None], (8, 4 * width)
        )
        wholes = [lax.all_gather(w, "shard", axis=0, tiled=True) for w in (w_out, w_in, w_fin)]
    cot = lax.ppermute(cotangent.reshape(rows, width), axes, there)
    if gather:
        gtok, output, *sums = middle(
            dims, ctx, x, cot, lens, vecs, inb, *wholes, ka, va, kt, qat, ctxt, h1, wf
        )
        total_wf, total_wi, total_wo, total_w, *vectors = final_layout(dims, *sums)
        vectors = [v.reshape(-1) for v in vectors]
    else:
        out, ect, gmid, vec_two, gib, *grads = feed_forward(dims, ctx, x, cot, lens, vecs, inb, *wholes)
        gtok, output, vec_one, gw = attention_backward(
            dims, ect, ka, va, kt, qat, ctxt, h1, wf, out, x, gmid, vecs
        )

        def total(grad, dim):
            part = lax.psum_scatter(grad, "shard", scatter_dimension=dim, tiled=True)
            return lax.psum(part, "seq").astype(F32)

        groups = heads // 2
        total_wf = total(grads[0], 1).T
        total_wi = total(grads[1], 0)
        total_wo = total(grads[2], 0)
        gw = gw.reshape(groups, width, 3, 128).transpose(1, 2, 0, 3).reshape(width, 3, half)
        wide = jnp.zeros((width, 3, 2, half), BF)
        wide = lax.dynamic_update_index_in_dim(wide, gw, core, 2)
        total_w = total(wide.reshape(width, 3 * width), 0)
        sums = jnp.concatenate((vec_one[:OB], vec_two[OB:IB], gib[0].reshape(4, width)))
        sums = lax.psum(sums, axes)
        s = lax.axis_index("shard")
        mine = lax.dynamic_slice_in_dim(sums[:IB], s * share, share, 1)
        vectors = [mine[n] for n in range(IB)]
        vectors.append(lax.dynamic_slice_in_dim(sums[IB:VECS].reshape(-1), s * 4 * share, 4 * share, 0))
    return (
        output.reshape(tokens.shape),
        gtok.reshape(tokens.shape),
        vectors[LN1G],
        vectors[LN1B],
        total_w,
        vectors[QB],
        vectors[VB],
        total_wo,
        vectors[OB],
        vectors[LN2G],
        vectors[LN2B],
        total_wi,
        vectors[IB],
        total_wf,
        vectors[FB],
    )


def solution(mesh):
    vector, matrix, rows = P("shard"), P("shard", None), P("shard", "seq", None)
    return jax.shard_map(
        functools.partial(on_device, n_seq=mesh.shape["seq"], shards=mesh.shape["shard"]),
        mesh=mesh,
        in_specs=(
            rows, vector, vector, matrix, vector, vector, matrix, vector, vector, vector, matrix, vector,
            matrix, vector, rows, vector,
        ),
        out_specs=(
            rows, rows, vector, vector, matrix, vector, vector, matrix, vector, vector, vector, matrix,
            vector, matrix, vector,
        ),
        check_vma=False,
    )
```

```python
import functools
import math

import jax
import jax.numpy as jnp
from jax import lax
from jax.experimental import pallas as pl
from jax.experimental.pallas import tpu as pltpu
from jax.sharding import PartitionSpec as P

HEAD_DIM = 64
EPS = 1e-05
GELU_C = 0.7978845608028654
GELU_K = 0.044715
MASKED = -1e30

BF = jnp.bfloat16
F32 = jnp.float32
MESH = pl.DeviceIdType.MESH
VMEM = pl.BlockSpec(memory_space=pltpu.VMEM)
ANY = pl.BlockSpec(memory_space=pl.ANY)

LN1G, LN1B, QB, VB, OB, LN2G, LN2B, FB, IB = range(9)
VECS = 12
VROWS = 16


def dot(left, right):
    return jnp.dot(left, right, preferred_element_type=F32)


def dot_t(left, right):
    return lax.dot_general(left, right, (((1,), (1,)), ((), ())), preferred_element_type=F32)


def mean_rows(values):
    return jnp.mean(values, -1, keepdims=True)


def length_of(packed):
    numbers = packed[VECS : VECS + 2, 0:1].astype(F32)
    return (numbers[0:1] * 256.0 + numbers[1:2]).astype(jnp.int32)


def unit_of(values):
    centred = values - mean_rows(values)
    inverse = lax.rsqrt(mean_rows(centred * centred) + EPS)
    return centred * inverse, inverse


def split3(values):
    high = values.astype(BF)
    rest = values - high.astype(F32)
    mid = rest.astype(BF)
    low = (rest - mid.astype(F32)).astype(BF)
    return high, mid, low


class Place:
    def __init__(self):
        q = lax.axis_index("seq")
        s = lax.axis_index("shard")
        self.q, self.s = q, s
        self.core = core = lax.rem(s, 2)
        self.to = (2 * core + lax.rem(q, 2), s - core + q // 2)
        side = lax.rem(q, 2)
        self.quarter = side + 2 * core
        self.origin = (self.quarter, s - core + q // 2)
        self.stays = q // 2 == core
        self.sibling = (q, s + 1 - 2 * core)
        self.beside = (q + 1 - 2 * side, s)
        self.quarters = [side, side + 2, 1 - side, 3 - side]


def remote(src, dst, send, recv, device):
    return pltpu.make_async_remote_copy(
        src_ref=src, dst_ref=dst, send_sem=send, recv_sem=recv, device_id=device, device_id_type=MESH
    )


class Named:
    def __init__(self, specs, refs):
        refs = iter(refs)
        for name, spec in specs.items():
            setattr(self, name, [next(refs) for _ in spec] if isinstance(spec, list) else next(refs))


def flat(specs):
    return [one for spec in specs.values() for one in (spec if isinstance(spec, list) else [spec])]


def greet(here, devices, mover):
    barrier = pltpu.get_barrier_semaphore()
    for device in devices:
        pl.semaphore_signal(barrier, inc=1, device_id=device, device_id_type=MESH)

    @pl.when(jnp.logical_not(here.stays))
    def _():
        pl.semaphore_signal(barrier, inc=1, device_id=mover, device_id_type=MESH)
        pl.semaphore_wait(barrier, len(devices) + 1)

    @pl.when(here.stays)
    def _():
        pl.semaphore_wait(barrier, len(devices))


def forward_kernel(dims, *refs):
    shards, rows, width, heads, gather = dims
    n_more = 3 if gather else 0
    tok, cot, length_in, w_in, vec_in = refs[:5]
    shares = refs[5 : 5 + n_more]
    refs = refs[5 + n_more :]
    (ka_o, va_o, kt_o, qat_o, ctxt_o, ctx_o, h1_o, wf_o, xown_o, cot_o, len_o, vec_o, inb_o) = refs[:13]
    wholes = refs[13 : 13 + n_more]
    refs = refs[13 + n_more :]
    (
        xs, wf, vg, lens, h1, ka, va, kt, vt, qat, ctxt, ctx, exact,
        perm_s, perm_r, sib_s, sib_r, side_s, side_r, back_s, back_r,
        len_s, len_r, w_s, w_r, out_s, ctx_s, ctx_r, cot_s, cot_r, all_s, all_r, all_l,
    ) = refs
    here = Place()
    core, s = here.core, here.s
    half = width // 2
    share = width // shards
    chunks = 4
    step = rows // chunks
    x_bit, y_bit = lax.rem(s // 2, 2), lax.rem(s // 4, 2)
    shard_x, shard_y = s + 2 - 4 * x_bit, s + 4 - 8 * y_bit
    shard_d = shard_x + 4 - 8 * y_bit
    partner_x, partner_y = (here.q, shard_x), (here.q, shard_y)

    partners = [here.sibling, here.beside] + ([partner_x, partner_y] if gather else [])
    greet(here, partners, here.origin)

    to_core = here.q // 2

    def block(ref, j, i):
        return ref.at[pl.ds(pl.multiple_of(j * rows + i * step, step), step), :]

    def perm_copy(i):
        return remote(
            tok.at[pl.ds(i * step, step), :], block(xs, to_core, i), perm_s.at[i], perm_r.at[i], here.to
        )

    def len_copy():
        return remote(length_in, lens, len_s, len_r, here.to)

    @pl.when(jnp.logical_not(here.stays))
    def _():
        for i in range(chunks):
            perm_copy(i).start()
        len_copy().start()

    @pl.when(here.stays)
    def _():
        for i in range(chunks):
            pltpu.make_async_copy(
                tok.at[pl.ds(i * step, step), :], block(xs, to_core, i), perm_r.at[i]
            ).start()
        pltpu.make_async_copy(length_in, lens, len_r).start()

    w_copies = []
    if gather:
        def columns(j, which):
            return pl.ds(pl.multiple_of(j * width + which * half, 128), half)

        mine = pl.ds(pl.multiple_of(s * share, share), share)
        for j in range(3):
            copy = remote(
                w_in.at[:, columns(j, 1 - core)], wf.at[mine, pl.ds(j * half, half)],
                w_s.at[j], w_r.at[j], here.sibling,
            )
            copy.start()
            w_copies.append(copy)
            copy = pltpu.make_async_copy(
                w_in.at[:, columns(j, core)], wf.at[mine, pl.ds(j * half, half)], w_s.at[4 + j]
            )
            copy.start()
            w_copies.append(copy)
        copy = remote(vec_in, vg.at[s], w_s.at[3], w_r.at[3], here.sibling)
        copy.start()
        w_copies.append(copy)
        copy = pltpu.make_async_copy(vec_in, vg.at[s], w_s.at[7])
        copy.start()
        w_copies.append(copy)
    else:
        copy = pltpu.make_async_copy(w_in, wf, w_s.at[0])
        copy.start()
        w_copies.append(copy)

    def w_move(at):
        src, count, device = (
            (s - core, 2, partner_x),
            (s - core, 2, partner_y),
            (shard_x - core, 1, partner_y),
            (shard_y - core + 1, 1, partner_x),
        )[at]
        part = wf.at[pl.ds(pl.multiple_of(src * share, share), count * share), :]
        return remote(part, part, w_s.at[8 + at], w_r.at[8 + at], device)

    def v_move(at):
        src, device = ((s, partner_x), (s, partner_y), (shard_x, partner_y))[at]
        part = vg.at[pl.ds(src - core, 2)]
        return remote(part, part, w_s.at[12 + at], w_r.at[12 + at], device)

    def receive(i):
        pltpu.make_async_copy(tok.at[pl.ds(i * step, step), :], block(xs, core, i), perm_r.at[i]).wait()
        sib = remote(block(xs, core, i), block(xs, core, i), sib_s.at[i], sib_r.at[i], here.sibling)
        side = remote(block(xs, core, i), block(xs, 2 + core, i), side_s.at[i], side_r.at[i], here.beside)
        side.start()
        sib.start()
        return [sib, side]

    def relay(i):
        block_in = block(xs, 2 + core, i)
        remote(block_in, block_in, side_s.at[i], side_r.at[i], here.beside).wait_recv()
        copy = remote(block_in, block_in, back_s.at[i], back_r.at[i], here.sibling)
        copy.start()
        return copy

    def rows_of(k, shard):
        count = shares[k].shape[0]
        return pl.ds(pl.multiple_of(shard * count, count), count)

    def piece(k, shard, part=None):
        cut = shares[k].shape[1] // 2
        if part is None:
            return wholes[k].at[rows_of(k, shard), :]
        return wholes[k].at[rows_of(k, shard), part * cut : (part + 1) * cut]

    def pass_on(k, slot, src, dst, device):
        return remote(src, dst, all_s.at[k, slot], all_r.at[k, slot], device)

    def got(k, slot, ref):
        pass_on(k, slot, ref, ref, here.sibling).wait_recv()

    def move(k, slot):
        src, device = (
            (None, partner_x),
            (None, partner_y),
            (None, here.sibling),
            ((shard_x, 0), partner_y),
            ((shard_x,), here.sibling),
            ((shard_y, 1), partner_x),
            ((shard_y,), here.sibling),
            ((shard_d,), here.sibling),
        )[slot]
        if src is None:
            return pass_on(k, slot, shares[k], piece(k, s), device)
        return pass_on(k, slot, piece(k, *src), piece(k, *src), device)

    def share_out(k):
        for slot in range(3):
            move(k, slot).start()
        pltpu.make_async_copy(shares[k], piece(k, s), all_l.at[k]).start()

    def from_x(k):
        got(k, 0, piece(k, shard_x))
        move(k, 3).start()
        move(k, 4).start()

    def from_y(k):
        got(k, 1, piece(k, shard_y))
        move(k, 5).start()
        move(k, 6).start()

    def from_far(k):
        got(k, 3, piece(k, shard_d, 0))
        got(k, 5, piece(k, shard_d, 1))
        move(k, 7).start()

    def all_here(k):
        flip = 1 - 2 * core
        for slot, shard in ((2, s), (4, shard_x), (6, shard_y), (7, shard_d)):
            got(k, slot, piece(k, shard + flip))
        pltpu.make_async_copy(shares[k], piece(k, s), all_l.at[k]).wait()

    moved = []
    if gather:
        for copy in w_copies:
            copy.wait()
        for at in range(2):
            w_move(at).start()
            v_move(at).start()
        share_out(0)
        share_out(1)
    moved += receive(0)
    moved += receive(1)
    if gather:
        w_move(0).wait_recv()
        v_move(0).wait_recv()
        w_move(2).start()
        v_move(2).start()
        w_move(1).wait_recv()
        v_move(1).wait_recv()
        w_move(3).start()
    moved += receive(2)
    moved += receive(3)

    def cot_copy():
        return remote(cot, cot_o, cot_s, cot_r, here.to)

    @pl.when(jnp.logical_not(here.stays))
    def _():
        cot_copy().start()

    @pl.when(here.stays)
    def _():
        pltpu.make_async_copy(cot, cot_o, cot_r).start()

    def norm_one(first, count):
        def body(i, _):
            at = pl.ds(pl.multiple_of(first + i * 256, 256), 256)
            unit, _ = unit_of(xs[at, :].astype(F32))
            h1[at, :] = (unit * vec_o[LN1G : LN1G + 1, :] + vec_o[LN1B : LN1B + 1, :]).astype(BF)
            return 0

        lax.fori_loop(0, count // 256, body, 0)

    if gather:
        w_move(2).wait_recv()
        w_move(3).wait_recv()
        v_move(2).wait_recv()
        for i in range(shards):
            part = vg[i].astype(F32)
            vec_o[:, i * share : (i + 1) * share] = part[:, :share]
            for r in range(4):
                at = (4 * i + r) * share
                inb_o[:, at : at + share] = jnp.broadcast_to(
                    part[IB + r : IB + r + 1, :share], (8, share)
                )
    else:
        for copy in w_copies:
            copy.wait()
        vec_o[...] = vec_in[...].astype(F32)
        inb_o[...] = jnp.zeros_like(inb_o)

    pltpu.make_async_copy(length_in, lens, len_r).wait()
    length = length_of(lens)
    lane = lax.broadcasted_iota(jnp.int32, (rows, 128), 1)
    row_at = lax.broadcasted_iota(jnp.int32, (rows, 128), 0)
    lower = lane < HEAD_DIM
    ones_rows = (lax.broadcasted_iota(jnp.int32, (16, rows), 0) == 0).astype(BF)
    q_rest = (lax.broadcasted_iota(jnp.int32, (64, 2 * rows), 0) == 3).astype(BF)
    for h in range(heads):
        qat[h, HEAD_DIM:, :] = q_rest

    def bias_half(at):
        full = vec_o[at : at + 1, :]
        return jnp.where(core == 0, full[:, :half], full[:, half:])

    def project(j):
        at = slice(j * rows, (j + 1) * rows)
        norm = h1[at, :]
        dead = jnp.where(here.quarters[j] * rows + row_at < length, 0.0, MASKED)
        k_rest = jnp.where(lane == HEAD_DIM + 3, dead, jnp.where(lane < HEAD_DIM + 3, 1.0, 0.0))
        v_rest = jnp.where(lane < HEAD_DIM + 3, -1.0, 0.0)
        if j < 2:
            q = (dot(norm, wf[:, :half]) + bias_half(QB)).astype(BF) * BF(HEAD_DIM**-0.5)
        k = dot(norm, wf[:, half : 2 * half])
        v = dot(norm, wf[:, 2 * half :]) + bias_half(VB)
        for i in range(heads // 2):
            two = slice(i * 128, (i + 1) * 128)
            kp, vp = k[:, two], v[:, two]
            ka[2 * i, at, :] = jnp.where(lower, kp, k_rest).astype(BF)
            ka[2 * i + 1, at, :] = jnp.where(lower, pltpu.roll(kp, 64, 1), k_rest).astype(BF)
            va[2 * i, at, :] = jnp.where(lower, vp, v_rest).astype(BF)
            va[2 * i + 1, at, :] = jnp.where(lower, pltpu.roll(vp, 64, 1), v_rest).astype(BF)
            turned = kp.astype(BF).T
            kt[2 * i, :, at] = turned[:64]
            kt[2 * i + 1, :, at] = turned[64:]
            turned = vp.astype(BF).T
            vt[2 * i, :64, at] = turned[:64]
            vt[2 * i + 1, :64, at] = turned[64:]
            vt[2 * i, 64:, at] = ones_rows
            vt[2 * i + 1, 64:, at] = ones_rows
            if j < 2:
                turned = q[:, two].T
                qat[2 * i, :64, at] = turned[:64]
                qat[2 * i + 1, :64, at] = turned[64:]

    for i in range(chunks):
        remote(block(xs, core, i), block(xs, 1 - core, i), sib_s.at[i], sib_r.at[i], here.sibling).wait_recv()
    norm_one(0, 2 * rows)
    project(0)
    project(1)
    if gather:
        from_x(0)
        from_y(0)
    relays = [relay(i) for i in range(chunks)]
    for i in range(chunks):
        pl_block = block(xs, 3 - core, i)
        remote(pl_block, pl_block, back_s.at[i], back_r.at[i], here.sibling).wait_recv()
    norm_one(2 * rows, 2 * rows)
    project(2)
    project(3)
    if gather:
        from_x(1)
        from_y(1)
        share_out(2)

    saves = []
    own = pl.ds(pl.multiple_of(core * rows, rows), rows)
    for at, (src, dst) in enumerate(
        ((ka, ka_o), (va, va_o), (kt, kt_o), (h1, h1_o), (wf, wf_o), (xs.at[own, :], xown_o), (lens, len_o))
    ):
        copy = pltpu.make_async_copy(src, dst, out_s.at[at])
        copy.start()
        saves.append(copy)

    size = 512
    keys = 4 * rows

    def attend(h, _):
        for qb in range(2 * rows // size):
            at = slice(qb * size, (qb + 1) * size)
            query = qat[h, :, at]

            def scores(c):
                return dot(ka[h, c * size : (c + 1) * size, :], query)

            ahead = scores(0)
            highest = total = None
            for c in range(keys // size):
                now = ahead
                if c + 1 < keys // size:
                    ahead = scores(c + 1)
                top = jnp.max(now, axis=0, keepdims=True)
                top = top if highest is None else jnp.maximum(highest, top)
                weights = jnp.exp(now - top).astype(BF)
                part = dot(vt[h, :, c * size : (c + 1) * size], weights)
                total = part if total is None else total * jnp.exp(highest - top) + part
                highest = top
            mass = total[64:65]
            result = total[:64] / mass
            head = pl.ds(pl.multiple_of(h * 64, 64), 64)
            exact[head, at] = result
            ctxt[head, at] = result.astype(BF)
            high, mid, low = split3(-(highest + jnp.log(mass)))
            index = lax.broadcasted_iota(jnp.int32, (16, size), 0)
            rest = jnp.where(index == 3, 1.0, 0.0)
            for r, term in enumerate((high, mid, low)):
                rest = jnp.where(index == r, term.astype(F32), rest)
            qat[h, 64:80, at] = rest.astype(BF)

        if gather:
            @pl.when(h == 0)
            def _():
                from_far(0)

            @pl.when(h == heads // 2)
            def _():
                from_far(1)

        return 0

    lax.fori_loop(0, heads, attend, 0)

    mine = pl.ds(pl.multiple_of(core * half, 128), half)
    own = pl.ds(pl.multiple_of(core * rows, rows), rows)
    other = pl.ds(pl.multiple_of((1 - core) * rows, rows), rows)
    trade = remote(ctxt.at[:, other], ctx.at[mine, :], ctx_s, ctx_r, here.sibling)
    trade.start()
    local = pltpu.make_async_copy(ctxt.at[:, own], ctx.at[mine, :], out_s.at[7])
    local.start()
    for at, (src, dst) in enumerate(((qat, qat_o), (exact, ctxt_o))):
        copy = pltpu.make_async_copy(src, dst, out_s.at[8 + at])
        copy.start()
        saves.append(copy)
    local.wait()
    trade.wait()
    copy = pltpu.make_async_copy(ctx, ctx_o, out_s.at[10])
    copy.start()
    saves.append(copy)
    for copy in saves:
        copy.wait()

    @pl.when(jnp.logical_not(here.stays))
    def _():
        for i in range(chunks):
            perm_copy(i).wait_send()
        len_copy().wait_send()
        cot_copy().wait_send()

    pltpu.make_async_copy(cot, cot_o, cot_r).wait()
    for copy in moved + relays:
        copy.wait_send()
    if gather:
        for k in range(2):
            all_here(k)
            for slot in range(8):
                move(k, slot).wait_send()
        got(2, 0, piece(2, shard_x))
        got(2, 1, piece(2, shard_y))
        got(2, 2, piece(2, s + 1 - 2 * core))
        pltpu.make_async_copy(shares[2], piece(2, s), all_l.at[2]).wait()
        for slot in range(3):
            move(2, slot).wait_send()
        for at in range(4):
            w_move(at).wait_send()
        for at in range(3):
            v_move(at).wait_send()


def attention_forward(dims, tok, cot, length, w, vec, *shares):
    shards, rows, width, heads, gather = dims
    half = width // 2
    keys = 4 * rows
    out = [
        ((heads, keys, 128), BF),
        ((heads, keys, 128), BF),
        ((heads, 64, keys), BF),
        ((heads, 128, 2 * rows), BF),
        ((half, 2 * rows), F32),
        ((width, rows), BF),
        ((keys, width), BF),
        ((width, 3 * half), BF),
        ((rows, width), BF),
        ((rows, width), BF),
        ((VROWS, 128), BF),
        ((VROWS, width), F32),
        ((8, 4 * width), F32),
    ] + [((shards * share.shape[0], share.shape[1]), BF) for share in shares]
    sems = pltpu.SemaphoreType.DMA
    return pl.pallas_call(
        functools.partial(forward_kernel, dims),
        out_shape=tuple(jax.ShapeDtypeStruct(*o) for o in out),
        in_specs=[ANY, ANY, VMEM, ANY, VMEM] + [ANY] * len(shares),
        out_specs=tuple([ANY] * 11 + [VMEM] * 2 + [ANY] * len(shares)),
        scratch_shapes=[
            pltpu.VMEM((keys, width), BF),
            pltpu.VMEM((width, 3 * half), BF),
            pltpu.VMEM((shards, VROWS, 128), BF),
            pltpu.VMEM((VROWS, 128), BF),
            pltpu.VMEM((keys, width), BF),
            pltpu.VMEM((heads, keys, 128), BF),
            pltpu.VMEM((heads, keys, 128), BF),
            pltpu.VMEM((heads, 64, keys), BF),
            pltpu.VMEM((heads, 80, keys), BF),
            pltpu.VMEM((heads, 128, 2 * rows), BF),
            pltpu.VMEM((half, 2 * rows), BF),
            pltpu.VMEM((width, rows), BF),
            pltpu.VMEM((half, 2 * rows), F32),
            sems((4,)), sems((4,)), sems((4,)), sems((4,)), sems((4,)), sems((4,)), sems((4,)), sems((4,)),
            sems, sems, sems((16,)), sems((16,)), sems((12,)), sems, sems,
            sems, sems, sems((3, 8)), sems((3, 8)), sems((3,)),
        ],
        compiler_params=pltpu.CompilerParams(
            collective_id=0, has_side_effects=True, vmem_limit_bytes=56 * 2**20
        ),
        name=forward_kernel.__name__,
    )(tok, cot, length, w, vec, *shares)


FAR_HEADS = (
    (0, ((2, 1),)),
    (1, ((0, 2),)),
    (2, ((1, 2),)),
    (3, ((2, 2),)),
    (4, ((0, 3),)),
    (5, ((1, 3), (2, 3))),
)
NEAR_HEADS = (
    (2, ((0, 4),)),
    (4, ((1, 4), (3, 2))),
    (5, ((2, 4), (0, 5), (3, 3))),
)
TAIL = (
    ((4, 2), (1, 5), (2, 5), (5, 2)),
    ((3, 4), (4, 3), (0, 6), (5, 3)),
    ((3, 5), (4, 4), (5, 4), (1, 6), (2, 6), (3, 6), (4, 5), (5, 5), (4, 6), (5, 6)),
)


class Links:
    def __init__(self, here):
        s, q = here.s, here.q
        self.x, self.y = lax.rem(s // 2, 2), lax.rem(s // 4, 2)
        self.to_x = (q, s + 2 - 4 * self.x)
        self.to_y = (q, s + 4 - 8 * self.y)
        self.inner = (q == 1) | (q == 2)
        self.to_inner = (3 - q, s)


class Reduction:
    def __init__(self, here, links, refs, mine, first_hops=None, core=None):
        self.got, self.last, self.seq_in, self.inner_in, self.done, self.send, self.recv = refs
        self.here, self.links, self.mine = here, links, mine
        self.first_hops, self.core = first_hops, core
        self.own = mine.at[links.y, links.x]

    @staticmethod
    def scratch(r, c):
        sems = pltpu.SemaphoreType.DMA
        return [pltpu.VMEM((2, 2, r, c), BF)] + [pltpu.VMEM((2, r, c), BF)] * 4 + [sems((8,)), sems((8,))]

    def copy(self, at):
        here, links, mine, own = self.here, self.links, self.mine, self.own
        x, y = links.x, links.y
        src, dst, device = (
            lambda: self.core + (here.sibling,),
            lambda: (mine.at[:, 1 - x, 0], self.got.at[0], links.to_x),
            lambda: (mine.at[1 - y, :, 1], self.got.at[1], links.to_y),
            lambda: (mine.at[1 - y, x, 0], self.last.at[0], links.to_y),
            lambda: (mine.at[y, 1 - x, 1], self.last.at[1], links.to_x),
            lambda: (own, self.seq_in, here.beside),
            lambda: (own, self.inner_in, links.to_inner),
            lambda: (self.done, self.done, here.beside),
        )[at]()
        return remote(src, dst, self.send.at[at], self.recv.at[at], device)

    def add(self, left, right, out=None):
        r = left.shape[-2]
        step = 96 if left.shape[-1] > 512 else r
        out = left if out is None else out

        def body(n, _):
            at = pl.ds(pl.multiple_of(n * step, step), step)
            out[at, :] = left[at, :] + right[at, :]
            return 0

        lax.fori_loop(0, r // step, body, 0)

    def phase(self, number):
        links, mine = self.links, self.mine
        x, y, outer = links.x, links.y, jnp.logical_not(links.inner)
        if number == 1:
            if self.core is not None:
                self.copy(0).wait_recv()
                for j in range(2):
                    for i in range(2):
                        for ab in range(2):
                            self.add(mine.at[j, i, ab], self.core[1].at[j, i, ab])
            self.copy(1).start()
            self.copy(2).start()
        elif number == 2:
            for copy in self.first_hops or (self.copy(1), self.copy(2)):
                copy.wait_recv()
            for i in range(2):
                self.add(mine.at[i, x, 0], self.got.at[0, i])
                self.add(mine.at[y, i, 1], self.got.at[1, i])
            self.copy(3).start()
            self.copy(4).start()
        elif number == 3:
            self.copy(3).wait_recv()
            self.copy(4).wait_recv()
            for ab in range(2):
                self.add(self.own.at[ab], self.last.at[ab])
            pl.when(outer)(lambda: self.copy(5).start())
        elif number == 4:
            @pl.when(links.inner)
            def _():
                self.copy(5).wait_recv()
                for ab in range(2):
                    self.add(self.own.at[ab], self.seq_in.at[ab])
                self.copy(6).start()
        elif number == 5:
            @pl.when(links.inner)
            def _():
                self.copy(6).wait_recv()
                for ab in range(2):
                    self.add(self.own.at[ab], self.inner_in.at[ab], self.done.at[ab])
                self.copy(7).start()
        else:
            pl.when(outer)(lambda: self.copy(7).wait_recv())

    def finish(self):
        if self.core is not None:
            self.copy(0).wait_send()
        for copy in self.first_hops or (self.copy(1), self.copy(2)):
            copy.wait_send()
        self.copy(3).wait_send()
        self.copy(4).wait_send()
        pl.when(jnp.logical_not(self.links.inner))(lambda: self.copy(5).wait_send())

        @pl.when(self.links.inner)
        def _():
            self.copy(6).wait_send()
            self.copy(7).wait_send()


class FirstHop:
    def __init__(self, make, sends=None, receives=None):
        self.make, self.sends, self.receives = make, sends, receives

    @staticmethod
    def on(condition, action):
        if condition is None:
            action()
        else:
            pl.when(condition)(action)

    def start(self):
        self.on(self.sends, lambda: self.make().start())

    def wait_send(self):
        self.on(self.sends, lambda: self.make().wait_send())

    def wait_recv(self):
        self.on(self.receives, lambda: self.make().wait_recv())


def grad_parts(dims):
    shards, rows, width, heads, _ = dims
    share, half = width // shards, width // 2
    return (half, 4 * share), (share, 2 * width), (share, half)


def middle_specs(dims):
    shards, rows, width, heads, _ = dims
    half, keys, share = width // 2, 4 * rows, width // shards
    groups = heads // 2
    sems = pltpu.SemaphoreType.DMA
    part_f, part_i, part_o = grad_parts(dims)
    ins = dict(ctx=VMEM, x=VMEM, cot=VMEM, lens=VMEM, vec=VMEM, inb=VMEM)
    ins |= dict(wo_h=ANY, wi_h=ANY, wf_h=ANY, ka_h=ANY, va_h=ANY, kt_h=ANY, qat_h=ANY, ctxt_h=ANY, h1_h=ANY, wq_h=ANY)
    outs = dict(
        gtok_o=((rows, width), BF, ANY),
        out_o=((rows, width), BF, ANY),
        vec_o=((VROWS, 128), F32, VMEM),
        sum_f=((2,) + part_f, BF, ANY),
        sum_i=((2,) + part_i, BF, ANY),
        sum_o=((2,) + part_o, BF, ANY),
        sum_w=((groups, 2, share, half), BF, ANY),
        far_f=((4 * width, width), BF, ANY),
    )
    scratch = dict(
        sum_refs=sum((Reduction.scratch(*part) for part in (part_f, part_i, part_o)), [])
        + Reduction.scratch(share, half) * groups,
        mine_w=[pltpu.VMEM((2, 2, 2, share, half), BF)] * groups,
        near_f=pltpu.VMEM((2, 2, 2) + part_f, BF),
        near_i=pltpu.VMEM((2, 2, 2) + part_i, BF),
        near_o=pltpu.VMEM((2, 2, 2) + part_o, BF),
        mine_f=pltpu.VMEM((2, 2, 2) + part_f, BF),
        mine_i=pltpu.VMEM((2, 2, 2) + part_i, BF),
        both_o=pltpu.VMEM((2, 2, 2, 2) + part_o, BF),
        gmid=pltpu.VMEM((rows, width), F32),
        vecs=pltpu.VMEM((VROWS, width), F32),
        gib=pltpu.VMEM((8, 4 * width), F32),
        gt=pltpu.VMEM((rows, width), BF),
        e_ctx=pltpu.VMEM((half, 2 * rows), BF),
        sib_in=pltpu.VMEM((2, width, rows), BF),
        side_in=pltpu.VMEM((width, rows), BF),
        vec_out=pltpu.VMEM((shards, VROWS, 128), F32),
        vec_in=pltpu.VMEM((shards, VROWS, 128), F32),
        vec_all=pltpu.VMEM((4, VROWS, 128), F32),
        w_in=pltpu.VMEM((groups, share, half), BF),
        core_sf=sems((4,)),
        core_rf=sems((4,)),
        core_si=sems((4,)),
        core_ri=sems((4,)),
        x_sf=sems((4,)),
        x_rf=sems((4,)),
        y_sf=sems((4,)),
        y_rf=sems((4,)),
        x_si=sems((4,)),
        x_ri=sems((4,)),
        y_si=sems((4,)),
        y_ri=sems((4,)),
        far_s=sems((8,)),
        far_r=sems((8,)),
        load_s=sems((9,)),
        head_s=sems((2, 4)),
        trade_s=sems((2,)),
        trade_r=sems,
        sib_s=sems((2,)),
        sib_r=sems((2,)),
        side_s=sems((4,)),
        side_r=sems((4,)),
        perm_s=sems((5,)),
        perm_r=sems((5,)),
        vec_s=sems((shards + 4,)),
        vec_r=sems((shards + 4,)),
        w_s=sems((groups,)),
        w_r=sems((groups,)),
        final_s=sems((3 + 2 * groups,)),
    )
    feed = dict(
        wo=pltpu.VMEM((width, width), BF),
        wi=pltpu.VMEM((2, width, width), BF),
        wf=pltpu.VMEM((2, width, width), BF),
        mid=pltpu.VMEM((rows, width), F32),
        h2=pltpu.VMEM((rows, width), BF),
        h2t=pltpu.VMEM((width + 16, rows), BF),
        eo=pltpu.VMEM((rows, width), BF),
        eot=pltpu.VMEM((width, rows), BF),
        gh2=pltpu.VMEM((rows, width), F32),
        acc=pltpu.VMEM((rows, width), F32),
        ect=pltpu.VMEM((width, rows), BF),
        both_f=pltpu.VMEM((2, 2, 2) + part_f, BF),
        both_i=pltpu.VMEM((2, 2, 2, 2, share, width), BF),
    )
    attend = dict(
        ka=pltpu.VMEM((2, 2 * rows, 128), BF),
        va=pltpu.VMEM((2, 2 * rows, 128), BF),
        kt=pltpu.VMEM((2, 64, 2 * rows), BF),
        qat=pltpu.VMEM((2, 128, 2 * rows), BF),
        h1=pltpu.VMEM((keys, width), BF),
        wq=pltpu.VMEM((width, 3 * half), BF),
        eat=pltpu.VMEM((heads, 128, 2 * rows), BF),
        grads=pltpu.VMEM((3 * half, keys), BF),
        sums=pltpu.VMEM((width, rows), F32),
        sib_out=pltpu.VMEM((2, width, rows), BF),
        side_out=pltpu.VMEM((width, rows), BF),
    )
    return ins, outs, scratch, feed, attend


def middle_kernel(dims, *refs):
    shards, rows, width, heads, _ = dims
    ins, outs, scratch, feed, attend = middle_specs(dims)
    at_ins, at_outs = len(ins), len(ins) + len(outs)
    i = Named(ins, refs[:at_ins])
    o = Named(outs, refs[at_ins:at_outs])
    v = Named(scratch, refs[at_outs:])
    here = Place()
    links = Links(here)
    core, x, y = here.core, links.x, links.y
    half, keys, share, size = width // 2, 4 * rows, width // shards, width
    groups, parts, chunks = heads // 2, 4, 4
    step = rows // chunks

    in_plane = [(here.q, lax.rem(here.s + n, shards)) for n in range(1, shards)]
    along = [(lax.rem(here.q + n, 4), here.s) for n in range(1, 4)]
    greet(here, in_plane + along, here.to)

    flip = 1 - 2 * core
    shard_x, shard_y = here.s + 2 - 4 * x, here.s + 4 - 8 * y
    shard_d = shard_x + 4 - 8 * y

    def share_of(ref, shard, part=None):
        count = 4 * share
        rows_of = pl.ds(pl.multiple_of(shard * count, count), count)
        return ref.at[rows_of, :] if part is None else ref.at[rows_of, part * half : (part + 1) * half]

    def far_move(at):
        shard, part, device = (
            (shard_x, 0, links.to_y),
            (shard_y, 1, links.to_x),
            (shard_x, None, here.sibling),
            (shard_y, None, here.sibling),
            (shard_d, None, here.sibling),
        )[at]
        src = share_of(o.far_f if at == 4 else i.wf_h, shard, part)
        return remote(src, share_of(o.far_f, shard, part), v.far_s.at[at], v.far_r.at[at], device)

    def far_came(at):
        shard, part = ((shard_d, 0), (shard_d, 1), (shard_x + flip, None), (shard_y + flip, None), (shard_d + flip, None))[at]
        ref = share_of(o.far_f, shard, part)
        remote(ref, ref, v.far_s.at[at], v.far_r.at[at], here.sibling).wait_recv()

    for at in range(4):
        far_move(at).start()

    def chip_of(k):
        return (1 - y if k // 2 else y), (1 - x if k % 2 else x)

    def columns(k):
        return pl.ds(pl.multiple_of(chip_of(k)[0] * size, size), size)

    def x_f(k):
        cy, cx = chip_of(k)
        return remote(v.mine_f.at[cy, cx, 0], v.got_f.at[0, cy], v.x_sf.at[k], v.x_rf.at[k], links.to_x)

    def y_f(k):
        cy, cx = chip_of(k)
        return remote(v.mine_f.at[cy, cx, 1], v.got_f.at[1, cx], v.y_sf.at[k], v.y_rf.at[k], links.to_y)

    def x_i(k):
        to = columns(k)
        return remote(
            v.mine_i.at[:, 1 - x, 0, :, to], v.got_i.at[0, :, :, to], v.x_si.at[k], v.x_ri.at[k], links.to_x
        )

    def y_i(k):
        to = columns(k)
        return remote(
            v.mine_i.at[1 - y, :, 1, :, to], v.got_i.at[1, :, :, to], v.y_si.at[k], v.y_ri.at[k], links.to_y
        )

    refs = [v.sum_refs[7 * n : 7 * n + 7] for n in range(3 + groups)]
    v.got_f, v.got_i = refs[0][0], refs[1][0]
    hops_f, hops_i = [], []
    for k in range(parts):
        cx = chip_of(k)[1]
        hops_f.append(([FirstHop(functools.partial(x_f, k))] if k % 2 else []) + ([FirstHop(functools.partial(y_f, k))] if k // 2 else []))
        hops_i.append(
            [FirstHop(functools.partial(x_i, k), cx == 0, cx == 1), FirstHop(functools.partial(y_i, k), cx == 1, cx == 1)]
        )
    sums = [
        Reduction(here, links, refs[0], v.mine_f, sum(hops_f, [])),
        Reduction(here, links, refs[1], v.mine_i, sum(hops_i, [])),
        Reduction(here, links, refs[2], v.both_o.at[core], None, (v.both_o.at[1 - core], v.near_o)),
    ]
    sums += [Reduction(here, links, refs[3 + g], v.mine_w[g]) for g in range(groups)]

    def run(*steps):
        for which, number in steps:
            sums[which].phase(number)

    def home(src, dst, at):
        return remote(src, dst, v.perm_s.at[at], v.perm_r.at[at], here.origin)

    def home_start(src, dst, at):
        @pl.when(jnp.logical_not(here.stays))
        def _():
            home(src, dst, at).start()

        @pl.when(here.stays)
        def _():
            pltpu.make_async_copy(src, dst, v.perm_s.at[at]).start()

    def home_sent(src, dst, at):
        @pl.when(jnp.logical_not(here.stays))
        def _():
            home(src, dst, at).wait_send()

        @pl.when(here.stays)
        def _():
            pltpu.make_async_copy(src, dst, v.perm_s.at[at]).wait()

    def home_came(src, dst, at):
        @pl.when(jnp.logical_not(here.stays))
        def _():
            home(src, dst, at).wait_recv()

    def vector(at):
        return i.vec[at : at + 1, :]

    def feed_part(*buffers):
        b = Named(feed, buffers)

        load_o = pltpu.make_async_copy(i.wo_h, b.wo, v.load_s.at[0])
        load_o.start()

        def load_i(k):
            cy, cx = chip_of(k)
            to = pl.ds(pl.multiple_of((2 * cy + cx) * size, size), size)
            return pltpu.make_async_copy(i.wi_h.at[:, to], b.wi.at[k % 2], v.load_s.at[1 + k % 2])

        def load_f(k):
            shard = (here.s, shard_x, shard_y, shard_d)[k]
            count = 4 * share
            return [
                pltpu.make_async_copy(
                    share_of(o.far_f if n or k == 3 else i.wf_h, each) if k else share_of(i.wf_h, each),
                    b.wf.at[k % 2, pl.ds(pl.multiple_of(lax.rem(each, 2) * count, count), count), :],
                    v.load_s.at[3 + 2 * (k % 2) + n],
                )
                for n, each in enumerate((shard, shard + flip))
            ]

        load_i(0).start()
        load_i(1).start()
        for copy in load_f(0):
            copy.start()

        row_at = lax.broadcasted_iota(jnp.int32, (rows, 1), 0) + here.quarter * rows
        live = row_at < length_of(i.lens)
        e_outer = jnp.where(live, i.cot[...].astype(F32), 0.0)
        b.eo[...] = e_outer.astype(BF)
        b.eot[...] = b.eo[...].T
        v.vecs[...] = jnp.zeros_like(v.vecs)
        v.vecs[FB : FB + 1, :] = jnp.sum(e_outer, 0, keepdims=True)

        load_o.wait()
        middle = i.x[...].astype(F32) + dot(i.ctx[...].T, b.wo[...]) + vector(OB)
        b.mid[...] = middle
        unit, _ = unit_of(middle)
        b.h2[...] = (unit * vector(LN2G) + vector(LN2B)).astype(BF)
        b.h2t[:width, :] = b.h2[...].T
        b.h2t[width:, :] = jnp.ones((16, rows), BF)
        b.acc[...] = middle + vector(FB)

        def near_f(k):
            cy, cx = chip_of(k)
            return remote(
                b.both_f.at[k % 2, 1 - core], v.near_f.at[cy, cx], v.core_sf.at[k], v.core_rf.at[k], here.sibling
            )

        def near_i(k):
            return remote(
                b.both_i.at[k % 2, 1 - core], v.near_i.at[:, :, chip_of(k)[1], :, columns(k)], v.core_si.at[k],
                v.core_ri.at[k], here.sibling,
            )

        def store(k, grad_f, grad_i):
            if k >= 2:
                near_f(k - 2).wait_send()
                near_i(k - 2).wait_send()
            for c in range(2):
                for ab in range(2):
                    b.both_f[k % 2, c, ab] = grad_f[ab * half : (ab + 1) * half, c * half : (c + 1) * half]
                for n in range(4):
                    at = (2 * n + c) * share
                    b.both_i[k % 2, c, n // 2, n % 2] = grad_i[at : at + share]
            near_f(k).start()
            near_i(k).start()

        def send(k):
            (cy, cx), to = chip_of(k), columns(k)
            near_f(k).wait_recv()
            near_i(k).wait_recv()
            for ab in range(2):
                v.mine_f[cy, cx, ab] = b.both_f[k % 2, core, ab] + v.near_f[cy, cx, ab]
            for hop in hops_f[k]:
                hop.start()
            for n in range(4):
                v.mine_i[n // 2, n % 2, cx, :, to] = (
                    b.both_i[k % 2, core, n // 2, n % 2] + v.near_i[n // 2, n % 2, cx, :, to]
                )
            for hop in hops_i[k]:
                hop.start()

        for k in range(parts):
            cy, cx = chip_of(k)
            at = pl.ds(pl.multiple_of((2 * cy + cx) * size, size), size)
            load_i(k).wait()
            for copy in load_f(k):
                copy.wait()
            if k == 0:
                far_came(2)
                far_came(3)
            if k == 1:
                far_came(0)
                far_came(1)
                far_move(4).start()
            if k == 2:
                far_came(4)
            if k + 1 < parts:
                for copy in load_f(k + 1):
                    copy.start()
            wic, wfc = b.wi[k % 2], b.wf[k % 2]
            inner = dot(b.h2[...], wic) + i.inb[0:1, at]
            square = inner * inner
            swing = jnp.tanh(GELU_C * inner * (1.0 + GELU_K * square))
            active = (0.5 * inner * (1.0 + swing)).astype(BF)
            slope = 0.5 * (1.0 + swing) + 0.5 * inner * (1.0 - swing * swing) * (
                GELU_C * (1.0 + 3.0 * GELU_K * square)
            )
            e_inner = (dot_t(b.eo[...], wfc) * slope).astype(BF)
            grad_f = dot(b.eot[...], active).astype(BF)
            grad_i = dot(b.h2t[...], e_inner)
            v.gib[:, at] = grad_i[width : width + 8]
            store(k, grad_f, grad_i[:width].astype(BF))
            b.acc[...] += dot(active, wfc)
            part = dot_t(e_inner, wic)
            b.gh2[...] = part if k == 0 else b.gh2[...] + part
            if k + 2 < parts:
                load_i(k + 2).start()
            if k > 0:
                send(k - 1)
        v.gt[...] = b.acc[...].astype(BF)
        home_start(v.gt, o.out_o, 4)
        unit, inverse = unit_of(b.mid[...])
        e_norm = b.gh2[...]
        v.vecs[LN2G : LN2G + 1, :] = jnp.sum(e_norm * unit, 0, keepdims=True)
        v.vecs[LN2B : LN2B + 1, :] = jnp.sum(e_norm, 0, keepdims=True)
        e_unit = e_norm * vector(LN2G)
        grad_mid = jnp.where(live, i.cot[...].astype(F32), 0.0) + inverse * (
            e_unit - mean_rows(e_unit) - unit * mean_rows(e_unit * unit)
        )
        v.gmid[...] = grad_mid
        e_branch = grad_mid.astype(BF)
        v.vecs[OB : OB + 1, :] = jnp.sum(e_branch.astype(F32), 0, keepdims=True)
        b.ect[...] = dot_t(b.wo[...], e_branch).astype(BF)
        mine = pl.ds(pl.multiple_of(core * half, 128), half)
        theirs = pl.ds(pl.multiple_of((1 - core) * half, 128), half)
        own = pl.ds(pl.multiple_of(core * rows, rows), rows)
        trade = remote(b.ect.at[theirs, :], v.e_ctx.at[:, own], v.trade_s.at[0], v.trade_r, here.sibling)
        trade.start()
        local = pltpu.make_async_copy(b.ect.at[mine, :], v.e_ctx.at[:, own], v.trade_s.at[1])
        local.start()
        send(parts - 1)
        grads = dot(i.ctx[...], e_branch).astype(BF)
        for n in range(shards):
            for ab in range(2):
                v.both_o[n % 2, n // 4, n // 2 % 2, ab] = grads[
                    n * share : (n + 1) * share, ab * half : (ab + 1) * half
                ]
        sums[2].copy(0).start()
        local.wait()
        trade.wait()
        for k in range(2, parts):
            near_f(k).wait_send()
            near_i(k).wait_send()
        for at in range(5):
            far_move(at).wait_send()

    pl.run_scoped(feed_part, *flat(feed))

    def attend_part(*buffers):
        b = Named(attend, buffers)

        def fetch(far, h, slot):
            rows_of = slice(2 * rows, keys) if far else slice(0, 2 * rows)
            return [
                pltpu.make_async_copy(src, dst, v.head_s.at[slot, n])
                for n, (src, dst) in enumerate(
                    (
                        (i.qat_h.at[h], b.qat.at[slot]),
                        (i.ka_h.at[h, rows_of, :], b.ka.at[slot]),
                        (i.va_h.at[h, rows_of, :], b.va.at[slot]),
                        (i.kt_h.at[h, :, rows_of], b.kt.at[slot]),
                    )
                )
            ]

        for copy in fetch(True, 0, 0):
            copy.start()

        def with_delta(ctxt, sem):
            load = pltpu.make_async_copy(i.ctxt_h, ctxt, sem)
            load.start()
            load.wait()
            index = lax.broadcasted_iota(jnp.int32, (16, 2 * rows), 0)
            for h in range(heads):
                at = slice(h * 64, (h + 1) * 64)
                e_ctx = v.e_ctx[at, :]
                delta = jnp.sum(e_ctx.astype(F32) * ctxt[at, :], 0, keepdims=True)
                rest = jnp.zeros((16, 2 * rows), F32)
                for r, term in enumerate(split3(delta)):
                    rest = jnp.where(index == r, term.astype(F32), rest)
                b.eat[h, :64, :] = e_ctx
                b.eat[h, 64:80, :] = rest.astype(BF)
                b.eat[h, 80:, :] = jnp.zeros((48, 2 * rows), BF)

        pl.run_scoped(with_delta, pltpu.VMEM((half, 2 * rows), F32), pltpu.SemaphoreType.DMA)
        loads = [
            pltpu.make_async_copy(i.wq_h, b.wq, v.load_s.at[7]),
            pltpu.make_async_copy(i.h1_h, b.h1, v.load_s.at[8]),
        ]
        for copy in loads:
            copy.start()
        block = 256

        def attend_half(far, polls):
            first = 2 * rows if far else 0

            def body(h, _):
                slot = lax.rem(h, 2)
                for copy in fetch(far, h, slot):
                    copy.wait()

                @pl.when(h < heads - 1)
                def _():
                    for copy in fetch(far, h + 1, 1 - slot):
                        copy.start()

                if far:
                    @pl.when(h == heads - 1)
                    def _():
                        for copy in fetch(False, 0, 1 - slot):
                            copy.start()

                query, e_ctx = b.qat[slot], b.eat[h]
                e_query = None
                for c in range(2 * rows // block):
                    of = slice(c * block, (c + 1) * block)
                    to = slice(first + c * block, first + (c + 1) * block)
                    weights = jnp.exp(dot(b.ka[slot, of, :], query))
                    e_scores = (weights * dot(b.va[slot, of, :], e_ctx)).astype(BF)
                    e_value = dot_t(e_ctx[:64], weights.astype(BF))
                    e_key = dot_t(query[:64], e_scores)
                    part = dot(b.kt[slot, :, of], e_scores)
                    e_query = part if e_query is None else e_query + part
                    b.grads[pl.ds(pl.multiple_of(half + h * 64, 64), 64), to] = e_key.astype(BF)
                    b.grads[pl.ds(pl.multiple_of(2 * half + h * 64, 64), 64), to] = e_value.astype(BF)
                head = pl.ds(pl.multiple_of(h * 64, 64), 64)
                lower = pl.ds(pl.multiple_of(half + h * 64, 64), 64)
                if far:
                    b.sums[head, :] = e_query[:, :rows]
                    b.sums[lower, :] = e_query[:, rows:]
                else:
                    b.grads[head, :rows] = ((b.sums[head, :] + e_query[:, :rows]) * HEAD_DIM**-0.5).astype(BF)
                    b.grads[head, rows : 2 * rows] = (
                        (b.sums[lower, :] + e_query[:, rows:]) * HEAD_DIM**-0.5
                    ).astype(BF)
                for when, action in polls:
                    pl.when(h == when)(action)
                return 0

            lax.fori_loop(0, heads, body, 0)

        def steps_of(table):
            return [(when, functools.partial(run, *steps)) for when, steps in table]

        def partial_of(j, near):
            at = pl.ds(pl.multiple_of(j * rows, rows), rows)
            if near:
                return dot(b.wq[...], b.grads[:, at])
            return dot(b.wq[:, half:], b.grads[half:, at])

        def sib_copy(at):
            return remote(b.sib_out.at[at], v.sib_in.at[at], v.sib_s.at[at], v.sib_r.at[at], here.sibling)

        def side_copy(at):
            to = slice(at * step, (at + 1) * step)
            return remote(
                b.side_out.at[:, to], v.side_in.at[:, to], v.side_s.at[at], v.side_r.at[at], here.beside
            )

        def to_side():
            sib_copy(0).wait_recv()
            b.side_out[...] = (partial_of(2 + core, False) + v.sib_in[0].astype(F32)).astype(BF)
            for at in range(chunks):
                side_copy(at).start()

        def weight_grad(g):
            for part, count in ((0, 2 * rows), (1, keys), (2, keys)):
                at = part * half + g * 128
                result = dot(b.grads[at : at + 128, :count], b.h1[:count, :]).T.astype(BF)
                to = slice(part * 128, (part + 1) * 128)
                for j in range(shards):
                    sums[3 + g].mine[j // 4, j // 2 % 2, j % 2, :, to] = result[j * share : (j + 1) * share]
            run((3 + g, 1))

        attend_half(True, steps_of(FAR_HEADS))
        for copy in loads:
            copy.wait()
        b.sib_out[0] = partial_of(3 - core, False).astype(BF)
        sib_copy(0).start()
        attend_half(
            False,
            [(0, to_side)]
            + [(2 * g + 1, functools.partial(weight_grad, g)) for g in range(groups - 1)]
            + steps_of(NEAR_HEADS),
        )
        b.sib_out[1] = partial_of(1 - core, True).astype(BF)
        sib_copy(1).start()
        weight_grad(groups - 1)
        own_part = partial_of(core, True)
        home_sent(v.gt, o.out_o, 4)
        sib_copy(1).wait_recv()
        b.sums[...] = own_part + v.sib_in[1].astype(F32)

        gain = vector(LN1G)
        gain_sum = shift_sum = None
        for at in range(chunks):
            to = slice(at * step, (at + 1) * step)
            side_copy(at).wait_recv()
            e_norm = (b.sums[:, to] + v.side_in[:, to].astype(F32)).T
            unit, inverse = unit_of(i.x[to, :].astype(F32))
            e_unit = e_norm * gain
            result = v.gmid[to, :] + inverse * (
                e_unit - mean_rows(e_unit) - unit * mean_rows(e_unit * unit)
            )
            v.gt[to, :] = result.astype(BF)
            home_start(v.gt.at[to, :], o.gtok_o.at[to, :], at)
            gains = jnp.sum(e_norm * unit, 0, keepdims=True)
            shifts = jnp.sum(e_norm, 0, keepdims=True)
            gain_sum = gains if at == 0 else gain_sum + gains
            shift_sum = shifts if at == 0 else shift_sum + shifts
        v.vecs[LN1G : LN1G + 1, :] = gain_sum
        v.vecs[LN1B : LN1B + 1, :] = shift_sum

        def row_sums(values):
            folded = values[:, :128].astype(F32)
            for n in range(1, values.shape[1] // 128):
                folded += values[:, n * 128 : (n + 1) * 128].astype(F32)
            return jnp.sum(folded.T, 0, keepdims=True)

        for at, part in ((QB, b.grads[:half, : 2 * rows]), (VB, b.grads[2 * half :, :])):
            total = row_sums(part)
            for n in range(2):
                v.vecs[at : at + 1, n * half : (n + 1) * half] = jnp.where(core == n, total, 0.0)

        for n in range(shards):
            v.vec_out[n, :, :share] = v.vecs[:, n * share : (n + 1) * share]
            for r in range(4):
                to = (4 * n + r) * share
                v.vec_out[n, IB + r : IB + r + 1, :share] = v.gib[0:1, to : to + share]

        def vec_plane(n):
            to = lax.rem(here.s + n, shards)
            return remote(
                v.vec_out.at[to], v.vec_in.at[here.s], v.vec_s.at[n], v.vec_r.at[n], (here.q, to)
            )

        def vec_along(n):
            to, at = lax.rem(here.q + n, 4), shards + n
            return remote(
                v.vec_all.at[here.q], v.vec_all.at[here.q], v.vec_s.at[at], v.vec_r.at[at], (to, here.s)
            )

        for n in range(1, shards):
            vec_plane(n).start()
        v.vec_in[here.s] = v.vec_out[here.s]
        run(*TAIL[0])
        for n in range(1, shards):
            vec_plane(n).wait_recv()
        total = v.vec_in[0]
        for n in range(1, shards):
            total += v.vec_in[n]
        v.vec_all[here.q] = total
        for n in range(1, 4):
            vec_along(n).start()
        run(*TAIL[1])
        for n in range(1, 4):
            vec_along(n).wait_recv()
        o.vec_o[...] = (v.vec_all[0] + v.vec_all[1]) + (v.vec_all[2] + v.vec_all[3])
        run(*TAIL[2])
        finals = []

        def final(src, dst, at):
            copy = pltpu.make_async_copy(src, dst, v.final_s.at[at])
            copy.start()
            finals.append(copy)

        def w_trade(g):
            return remote(sums[3 + g].done.at[1 - core], v.w_in.at[g], v.w_s.at[g], v.w_r.at[g], here.sibling)

        for g in range(groups):
            w_trade(g).start()
        for n, dst in enumerate((o.sum_f, o.sum_i, o.sum_o)):
            final(sums[n].done, dst, n)
        for g in range(groups):
            final(sums[3 + g].done.at[core], o.sum_w.at[g, core], 3 + 2 * g)
            w_trade(g).wait()
            final(v.w_in.at[g], o.sum_w.at[g, 1 - core], 4 + 2 * g)
        for copy in finals:
            copy.wait()
        for each in sums:
            each.finish()
        for n in range(1, shards):
            vec_plane(n).wait_send()
        for n in range(1, 4):
            vec_along(n).wait_send()
        for at in range(2):
            sib_copy(at).wait_send()
        for at in range(chunks):
            side_copy(at).wait_send()
            to = slice(at * step, (at + 1) * step)
            home_sent(v.gt.at[to, :], o.gtok_o.at[to, :], at)
            home_came(v.gt.at[to, :], o.gtok_o.at[to, :], at)
        home_came(v.gt, o.out_o, 4)

    pl.run_scoped(attend_part, *flat(attend))


def call(kernel, dims, specs, args, **params):
    ins, outs, scratch = specs[:3]
    return pl.pallas_call(
        functools.partial(kernel, dims),
        out_shape=tuple(jax.ShapeDtypeStruct(*out[:2]) for out in outs.values()),
        in_specs=flat(ins),
        out_specs=tuple(out[2] for out in outs.values()),
        scratch_shapes=flat(scratch),
        compiler_params=pltpu.CompilerParams(**params),
        name=kernel.__name__,
    )(*args)


def middle(dims, *args):
    return call(
        middle_kernel, dims, middle_specs(dims), args, collective_id=1, has_side_effects=True,
        vmem_limit_bytes=62 * 2**20,
    )[:-1]


def feed_plain(ctx, x, cot, length, vec, in_bias, wo, wi, wf):
    here = Place()
    rows = x.shape[0]
    row_at = lax.broadcasted_iota(jnp.int32, (rows, 1), 0) + here.quarter * rows
    e_outer = jnp.where(row_at < length, cot.astype(F32), 0.0)
    mid = x.astype(F32) + dot(ctx.T, wo) + vec[OB]
    unit, inverse = unit_of(mid)
    h2 = (unit * vec[LN2G] + vec[LN2B]).astype(BF)
    inner = dot(h2, wi) + in_bias
    square = inner * inner
    swing = jnp.tanh(GELU_C * inner * (1.0 + GELU_K * square))
    active = (0.5 * inner * (1.0 + swing)).astype(BF)
    slope = 0.5 * (1.0 + swing) + 0.5 * inner * (1.0 - swing * swing) * (
        GELU_C * (1.0 + 3.0 * GELU_K * square)
    )
    out = (mid + dot(active, wf) + vec[FB]).astype(BF)
    e_low = e_outer.astype(BF)
    e_inner = (dot_t(e_low, wf) * slope).astype(BF)
    e_norm = dot_t(e_inner, wi)
    e_unit = e_norm * vec[LN2G]
    grad_mid = e_outer + inverse * (e_unit - mean_rows(e_unit) - unit * mean_rows(e_unit * unit))
    e_branch = grad_mid.astype(BF)
    grads = dot(active.T, e_low), dot(h2.T, e_inner), dot(ctx, e_branch)
    vectors = (
        jnp.sum(e_branch.astype(F32), 0),
        jnp.sum(e_norm * unit, 0),
        jnp.sum(e_norm, 0),
        jnp.sum(e_outer, 0),
    )
    in_sums = jnp.sum(e_inner.astype(F32), 0).reshape(4, -1)
    vectors = jnp.concatenate((jnp.stack(vectors), in_sums))
    return out, dot_t(wo, e_branch).astype(BF), grad_mid, vectors, [g.astype(BF) for g in grads]


def backward_specs(dims):
    shards, rows, width, heads, _ = dims
    half, keys = width // 2, 4 * rows
    sems = pltpu.SemaphoreType.DMA
    ins = dict(
        ect=VMEM, ka_h=ANY, va_h=ANY, kt_h=ANY, qat_h=ANY, ctxt_h=ANY, h1_h=ANY, wq_h=ANY, out_h=ANY, x=VMEM,
        gmid=VMEM, vec=VMEM,
    )
    outs = dict(
        gtok_o=((rows, width), BF, ANY),
        out_o=((rows, width), BF, ANY),
        vec_o=((VROWS, width), F32, VMEM),
        gw_o=((width, 3 * half), BF, VMEM),
    )
    scratch = dict(
        vecs=pltpu.VMEM((VROWS, width), F32),
        ka=pltpu.VMEM((heads, keys, 128), BF),
        va=pltpu.VMEM((heads, keys, 128), BF),
        kt=pltpu.VMEM((heads, 64, keys), BF),
        qat=pltpu.VMEM((heads, 128, 2 * rows), BF),
        h1=pltpu.VMEM((keys, width), BF),
        wq=pltpu.VMEM((width, 3 * half), BF),
        e_ctx=pltpu.VMEM((half, 2 * rows), BF),
        eat=pltpu.VMEM((heads, 128, 2 * rows), BF),
        grads=pltpu.VMEM((3 * half, keys), BF),
        sums=pltpu.VMEM((width, rows), F32),
        sib_out=pltpu.VMEM((2, width, rows), BF),
        sib_in=pltpu.VMEM((2, width, rows), BF),
        side_out=pltpu.VMEM((width, rows), BF),
        side_in=pltpu.VMEM((width, rows), BF),
        gt=pltpu.VMEM((rows, width), BF),
        load_s=sems((7,)),
        trade_s=sems((2,)),
        trade_r=sems,
        sib_s=sems((2,)),
        sib_r=sems((2,)),
        side_s=sems((4,)),
        side_r=sems((4,)),
        perm_s=sems((5,)),
        perm_r=sems((5,)),
    )
    return ins, outs, scratch


def backward_kernel(dims, *refs):
    shards, rows, width, heads, _ = dims
    ins, outs, scratch = backward_specs(dims)
    at_ins, at_outs = len(ins), len(ins) + len(outs)
    i = Named(ins, refs[:at_ins])
    o = Named(outs, refs[at_ins:at_outs])
    v = Named(scratch, refs[at_outs:])
    here = Place()
    core = here.core
    half, keys = width // 2, 4 * rows
    chunks = 4
    step = rows // chunks
    loads = []
    for at, (src, dst) in enumerate(
        ((i.qat_h, v.qat), (i.ka_h, v.ka), (i.va_h, v.va), (i.kt_h, v.kt), (i.wq_h, v.wq), (i.h1_h, v.h1))
    ):
        copy = pltpu.make_async_copy(src, dst, v.load_s.at[at])
        copy.start()
        loads.append(copy)

    greet(here, [here.sibling, here.beside], here.to)

    mine = pl.ds(pl.multiple_of(core * half, 128), half)
    theirs = pl.ds(pl.multiple_of((1 - core) * half, 128), half)
    own = pl.ds(pl.multiple_of(core * rows, rows), rows)
    trade = remote(i.ect.at[theirs, :], v.e_ctx.at[:, own], v.trade_s.at[0], v.trade_r, here.sibling)
    trade.start()
    local = pltpu.make_async_copy(i.ect.at[mine, :], v.e_ctx.at[:, own], v.trade_s.at[1])
    local.start()

    def home(src, dst, at):
        return remote(src, dst, v.perm_s.at[at], v.perm_r.at[at], here.origin)

    def home_start(src, dst, at):
        @pl.when(jnp.logical_not(here.stays))
        def _():
            home(src, dst, at).start()

        @pl.when(here.stays)
        def _():
            pltpu.make_async_copy(src, dst, v.perm_r.at[at]).start()

    def home_wait(src, dst, at):
        pltpu.make_async_copy(src, dst, v.perm_r.at[at]).wait()

        @pl.when(jnp.logical_not(here.stays))
        def _():
            home(src, dst, at).wait_send()

    home_start(i.out_h, o.out_o, 4)
    local.wait()
    trade.wait()

    def with_delta(ctxt, sem):
        load = pltpu.make_async_copy(i.ctxt_h, ctxt, sem)
        load.start()
        load.wait()
        index = lax.broadcasted_iota(jnp.int32, (16, 2 * rows), 0)
        for h in range(heads):
            at = slice(h * 64, (h + 1) * 64)
            e_ctx = v.e_ctx[at, :]
            delta = jnp.sum(e_ctx.astype(F32) * ctxt[at, :], 0, keepdims=True)
            rest = jnp.zeros((16, 2 * rows), F32)
            for r, term in enumerate(split3(delta)):
                rest = jnp.where(index == r, term.astype(F32), rest)
            v.eat[h, :64, :] = e_ctx
            v.eat[h, 64:80, :] = rest.astype(BF)
            v.eat[h, 80:, :] = jnp.zeros((48, 2 * rows), BF)

    pl.run_scoped(with_delta, pltpu.VMEM((half, 2 * rows), F32), pltpu.SemaphoreType.DMA)
    for copy in loads:
        copy.wait()

    size = 256

    def attend(far):
        first = 2 * rows if far else 0

        def body(h, _):
            query, e_ctx = v.qat[h], v.eat[h]
            e_query = None
            for c in range(2 * rows // size):
                to = slice(first + c * size, first + (c + 1) * size)
                weights = jnp.exp(dot(v.ka[h, to, :], query))
                e_scores = (weights * dot(v.va[h, to, :], e_ctx)).astype(BF)
                e_value = dot_t(e_ctx[:64], weights.astype(BF))
                e_key = dot_t(query[:64], e_scores)
                part = dot(v.kt[h, :, to], e_scores)
                e_query = part if e_query is None else e_query + part
                v.grads[pl.ds(pl.multiple_of(half + h * 64, 64), 64), to] = e_key.astype(BF)
                v.grads[pl.ds(pl.multiple_of(2 * half + h * 64, 64), 64), to] = e_value.astype(BF)
            head = pl.ds(pl.multiple_of(h * 64, 64), 64)
            lower = pl.ds(pl.multiple_of(half + h * 64, 64), 64)
            if far:
                v.sums[head, :] = e_query[:, :rows]
                v.sums[lower, :] = e_query[:, rows:]
            else:
                v.grads[head, :rows] = ((v.sums[head, :] + e_query[:, :rows]) * HEAD_DIM**-0.5).astype(BF)
                v.grads[head, rows : 2 * rows] = (
                    (v.sums[lower, :] + e_query[:, rows:]) * HEAD_DIM**-0.5
                ).astype(BF)
            return 0

        lax.fori_loop(0, heads, body, 0)

    def partial_of(j, near):
        at = pl.ds(pl.multiple_of(j * rows, rows), rows)
        if near:
            return dot(v.wq[...], v.grads[:, at])
        return dot(v.wq[:, half:], v.grads[half:, at])

    def sib_copy(at):
        return remote(v.sib_out.at[at], v.sib_in.at[at], v.sib_s.at[at], v.sib_r.at[at], here.sibling)

    def side_copy(at):
        to = slice(at * step, (at + 1) * step)
        return remote(
            v.side_out.at[:, to], v.side_in.at[:, to], v.side_s.at[at], v.side_r.at[at], here.beside
        )

    def to_side():
        sib_copy(0).wait_recv()
        v.side_out[...] = (partial_of(2 + core, False) + v.sib_in[0].astype(F32)).astype(BF)
        for at in range(chunks):
            side_copy(at).start()

    attend(True)
    v.sib_out[0] = partial_of(3 - core, False).astype(BF)
    sib_copy(0).start()
    attend(False)
    to_side()
    v.sib_out[1] = partial_of(1 - core, True).astype(BF)
    sib_copy(1).start()
    for part, count in ((0, 2 * rows), (1, keys), (2, keys)):
        at = slice(part * half, (part + 1) * half)
        o.gw_o[:, at] = dot(v.grads[at, :count], v.h1[:count, :]).T.astype(BF)
    own_part = partial_of(core, True)
    sib_copy(1).wait_recv()
    v.sums[...] = own_part + v.sib_in[1].astype(F32)

    def row_sums(values):
        folded = values[:, :128].astype(F32)
        for n in range(1, values.shape[1] // 128):
            folded += values[:, n * 128 : (n + 1) * 128].astype(F32)
        return jnp.sum(folded.T, 0, keepdims=True)

    v.vecs[...] = jnp.zeros_like(v.vecs)
    for at, part in ((QB, v.grads[:half, : 2 * rows]), (VB, v.grads[2 * half :, :])):
        total = row_sums(part)
        for n in range(2):
            v.vecs[at : at + 1, n * half : (n + 1) * half] = jnp.where(core == n, total, 0.0)

    gain = i.vec[LN1G : LN1G + 1, :]
    gain_sum = shift_sum = None
    for at in range(chunks):
        to = slice(at * step, (at + 1) * step)
        side_copy(at).wait_recv()
        e_norm = (v.sums[:, to] + v.side_in[:, to].astype(F32)).T
        unit, inverse = unit_of(i.x[to, :].astype(F32))
        e_unit = e_norm * gain
        result = i.gmid[to, :] + inverse * (
            e_unit - mean_rows(e_unit) - unit * mean_rows(e_unit * unit)
        )
        v.gt[to, :] = result.astype(BF)
        home_start(v.gt.at[to, :], o.gtok_o.at[to, :], at)
        gains = jnp.sum(e_norm * unit, 0, keepdims=True)
        shifts = jnp.sum(e_norm, 0, keepdims=True)
        gain_sum = gains if at == 0 else gain_sum + gains
        shift_sum = shifts if at == 0 else shift_sum + shifts
    v.vecs[LN1G : LN1G + 1, :] = gain_sum
    v.vecs[LN1B : LN1B + 1, :] = shift_sum
    o.vec_o[...] = v.vecs[...]

    for at in range(2):
        sib_copy(at).wait_send()
    for at in range(chunks):
        side_copy(at).wait_send()
        to = slice(at * step, (at + 1) * step)
        home_wait(v.gt.at[to, :], o.gtok_o.at[to, :], at)
    home_wait(i.out_h, o.out_o, 4)


def attention_backward(dims, *args):
    return call(
        backward_kernel, dims, backward_specs(dims), args, collective_id=2, has_side_effects=True,
        vmem_limit_bytes=60 * 2**20,
    )


def final_specs(dims):
    shards, rows, width, heads, _ = dims
    share, half = width // shards, width // 2
    ins = dict(vec=VMEM, sums=[ANY] * 4)
    outs = [(4 * share, width), (share, 4 * width), (share, width), (share, 3 * width)]
    outs += [(1, share)] * IB + [(1, 4 * share)]
    outs = {n: (shape, F32, VMEM) for n, shape in enumerate(outs)}
    shapes = [(2,) + part for part in grad_parts(dims)] + [(heads // 2, 2, share, half)]
    scratch = dict(held=[pltpu.VMEM(shape, BF) for shape in shapes], sem=pltpu.SemaphoreType.DMA((4,)))
    return ins, outs, scratch


def final_kernel(dims, *refs):
    vec, sums, out, held, sem = refs[0], refs[1:5], refs[5:-5], refs[-5:-1], refs[-1]
    copies = [pltpu.make_async_copy(src, dst, sem.at[n]) for n, (src, dst) in enumerate(zip(sums, held))]
    for copy in copies:
        copy.start()
    t_f, t_i, t_o, t_w, *vectors = out
    d_f, d_i, d_o, d_w = held
    half, share = d_f.shape[1], d_i.shape[1]
    width = 2 * half
    for n, result in enumerate(vectors[:-1]):
        result[...] = vec[n : n + 1, :share]
    for r in range(4):
        vectors[-1][:, r * share : (r + 1) * share] = vec[IB + r : IB + r + 1, :share]
    for copy in copies:
        copy.wait()
    for ab in range(2):
        t_f[:, ab * half : (ab + 1) * half] = d_f[ab].astype(F32).T
        t_o[:, ab * half : (ab + 1) * half] = d_o[ab].astype(F32)
        for sub in range(2):
            to = (2 * sub + ab) * width
            t_i[:, to : to + width] = d_i[ab, :, sub * width : (sub + 1) * width].astype(F32)
    for g in range(d_w.shape[0]):
        for core in range(2):
            for part in range(3):
                to = part * width + core * half + g * 128
                t_w[:, to : to + 128] = d_w[g, core, :, part * 128 : (part + 1) * 128].astype(F32)


def on_device(
    tokens, ln1_gain, ln1_shift, w_qkv, q_bias, v_bias, w_out, out_bias, ln2_gain, ln2_shift, w_in, in_bias,
    w_fin, fin_bias, cotangent, lengths, shards,
):
    _, rows, width = tokens.shape
    heads = width // HEAD_DIM // 2
    half = width // 2
    share = width // shards
    gather = shards == 8
    dims = (shards, rows, width, heads, gather)
    core = lax.rem(lax.axis_index("shard"), 2)

    vectors = (ln1_gain, ln1_shift, q_bias, v_bias, out_bias, ln2_gain, ln2_shift, fin_bias, in_bias)
    lanes = 128 if gather else max(128, share)
    packed = jnp.zeros((VROWS, lanes), BF)
    for at, one in enumerate(vectors):
        one = one.reshape(-1, share)
        packed += jnp.pad(one, ((at, VROWS - at - one.shape[0]), (0, lanes - share)))
    numbers = jnp.stack((lengths // 256, lengths % 256)).astype(BF)
    packed += jnp.pad(numbers, ((VECS, VROWS - VECS - 2), (0, lanes - 1)))
    if gather:
        vec, w_here, shares = packed, w_qkv, (w_out, w_in, w_fin)
    else:
        vec = lax.all_gather(packed[:, :share], "shard", axis=1, tiled=True)
        full_w = lax.all_gather(w_qkv, "shard", axis=0, tiled=True)
        w_here = lax.dynamic_index_in_dim(
            full_w.reshape(width, 3, 2, half), core, 2, keepdims=False
        ).reshape(width, 3 * half)
        shares = ()
    (ka, va, kt, qat, ctxt, ctx, h1, wq, x, cot, lens, vecs, inb, *wholes) = attention_forward(
        dims, tokens.reshape(rows, width), cotangent.reshape(rows, width), packed, w_here, vec, *shares
    )
    if gather:
        gtok, output, *sums = middle(
            dims, ctx, x, cot, lens, vecs, inb, *wholes, ka, va, kt, qat, ctxt, h1, wq
        )
        total_wf, total_wi, total_wo, total_w, *vectors = call(
            final_kernel, dims, final_specs(dims), sums, vmem_limit_bytes=60 * 2**20
        )
        vectors = [v.reshape(-1) for v in vectors]
    else:
        wholes = [lax.all_gather(w, "shard", axis=0, tiled=True) for w in (w_out, w_in, w_fin)]
        full_ib = lax.all_gather(in_bias, "shard", axis=0, tiled=True).astype(F32)
        out, ect, gmid, vec_two, grads = feed_plain(ctx, x, cot, length_of(lens), vecs, full_ib, *wholes)
        gtok, output, vec_one, gw = attention_backward(
            dims, ect, ka, va, kt, qat, ctxt, h1, wq, out, x, gmid, vecs
        )

        def total(grad):
            part = lax.psum_scatter(grad, "shard", scatter_dimension=0, tiled=True)
            return lax.psum(part, "seq").astype(F32)

        total_wf, total_wi, total_wo = [total(grad) for grad in grads]
        wide = jnp.zeros((width, 3, 2, half), BF)
        wide = lax.dynamic_update_index_in_dim(wide, gw.reshape(width, 3, half), core, 2)
        total_w = total(wide.reshape(width, 3 * width))
        sums = lax.psum(jnp.concatenate((vec_one[:OB], vec_two)), ("seq", "shard"))
        s = lax.axis_index("shard")
        mine = lax.dynamic_slice_in_dim(sums[:IB], s * share, share, 1)
        vectors = [mine[n] for n in range(IB)]
        vectors.append(lax.dynamic_slice_in_dim(sums[IB:].reshape(-1), s * 4 * share, 4 * share, 0))
    return (
        output.reshape(tokens.shape),
        gtok.reshape(tokens.shape),
        vectors[LN1G],
        vectors[LN1B],
        total_w,
        vectors[QB],
        vectors[VB],
        total_wo,
        vectors[OB],
        vectors[LN2G],
        vectors[LN2B],
        total_wi,
        vectors[IB],
        total_wf,
        vectors[FB],
    )


def solution(mesh):
    vector, matrix, rows = P("shard"), P("shard", None), P("shard", "seq", None)
    return jax.shard_map(
        functools.partial(on_device, shards=mesh.shape["shard"]),
        mesh=mesh,
        in_specs=(
            rows, vector, vector, matrix, vector, vector, matrix, vector, vector, vector, matrix, vector,
            matrix, vector, rows, vector,
        ),
        out_specs=(
            rows, rows, vector, vector, matrix, vector, vector, matrix, vector, vector, vector, matrix,
            vector, matrix, vector,
        ),
        check_vma=False,
    )
```

```python
import functools
import math

import jax
import jax.numpy as jnp
from jax import lax
from jax.experimental import pallas as pl
from jax.experimental.pallas import tpu as pltpu
from jax.sharding import PartitionSpec as P

HEAD_DIM = 64
EPS = 1e-05
GELU_C = 0.7978845608028654
GELU_K = 0.044715
MASKED = -1e30

BF = jnp.bfloat16
F32 = jnp.float32
MESH = pl.DeviceIdType.MESH
VMEM = pl.BlockSpec(memory_space=pltpu.VMEM)
ANY = pl.BlockSpec(memory_space=pl.ANY)

LN1G, LN1B, QB, VB, OB, LN2G, LN2B, FB, IB = range(9)
VECS = 12
VROWS = 16


def dot(left, right):
    return jnp.dot(left, right, preferred_element_type=F32)


def dot_t(left, right):
    return lax.dot_general(left, right, (((1,), (1,)), ((), ())), preferred_element_type=F32)


def mean_rows(values):
    return jnp.mean(values, -1, keepdims=True)


def length_of(packed):
    numbers = packed[VECS : VECS + 2, 0:1].astype(F32)
    return (numbers[0:1] * 256.0 + numbers[1:2]).astype(jnp.int32)


def unit_of(values):
    centred = values - mean_rows(values)
    inverse = lax.rsqrt(mean_rows(centred * centred) + EPS)
    return centred * inverse, inverse


def split3(values):
    high = values.astype(BF)
    rest = values - high.astype(F32)
    mid = rest.astype(BF)
    low = (rest - mid.astype(F32)).astype(BF)
    return high, mid, low


class Place:
    def __init__(self):
        q = lax.axis_index("seq")
        s = lax.axis_index("shard")
        self.q, self.s = q, s
        self.core = core = lax.rem(s, 2)
        self.to = (2 * core + lax.rem(q, 2), s - core + q // 2)
        side = lax.rem(q, 2)
        self.quarter = side + 2 * core
        self.origin = (self.quarter, s - core + q // 2)
        self.stays = q // 2 == core
        self.sibling = (q, s + 1 - 2 * core)
        self.beside = (q + 1 - 2 * side, s)
        self.quarters = [side, side + 2, 1 - side, 3 - side]


def remote(src, dst, send, recv, device):
    return pltpu.make_async_remote_copy(
        src_ref=src, dst_ref=dst, send_sem=send, recv_sem=recv, device_id=device, device_id_type=MESH
    )


class Named:
    def __init__(self, specs, refs):
        refs = iter(refs)
        for name, spec in specs.items():
            setattr(self, name, [next(refs) for _ in spec] if isinstance(spec, list) else next(refs))


def flat(specs):
    return [one for spec in specs.values() for one in (spec if isinstance(spec, list) else [spec])]


def greet(here, devices, mover):
    barrier = pltpu.get_barrier_semaphore()
    for device in devices:
        pl.semaphore_signal(barrier, inc=1, device_id=device, device_id_type=MESH)

    @pl.when(jnp.logical_not(here.stays))
    def _():
        pl.semaphore_signal(barrier, inc=1, device_id=mover, device_id_type=MESH)
        pl.semaphore_wait(barrier, len(devices) + 1)

    @pl.when(here.stays)
    def _():
        pl.semaphore_wait(barrier, len(devices))


def forward_kernel(dims, *refs):
    shards, rows, width, heads, gather = dims
    n_more = 3 if gather else 0
    tok, cot, length_in, w_in, vec_in = refs[:5]
    shares = refs[5 : 5 + n_more]
    refs = refs[5 + n_more :]
    (ka_o, va_o, kt_o, qat_o, ctxt_o, ctx_o, h1_o, wf_o, xown_o, cot_o, len_o, vec_o, inb_o) = refs[:13]
    wholes = refs[13 : 13 + n_more]
    refs = refs[13 + n_more :]
    (
        xs, wf, vg, lens, h1, ka, va, kt, vt, qat, ctxt, ctx, exact,
        perm_s, perm_r, sib_s, sib_r, side_s, side_r, back_s, back_r,
        len_s, len_r, w_s, w_r, out_s, ctx_s, ctx_r, cot_s, cot_r, all_s, all_r, all_l,
    ) = refs
    here = Place()
    core, s = here.core, here.s
    half = width // 2
    share = width // shards
    chunks = 4
    step = rows // chunks
    x_bit, y_bit = lax.rem(s // 2, 2), lax.rem(s // 4, 2)
    shard_x, shard_y = s + 2 - 4 * x_bit, s + 4 - 8 * y_bit
    shard_d = shard_x + 4 - 8 * y_bit
    partner_x, partner_y = (here.q, shard_x), (here.q, shard_y)

    partners = [here.sibling, here.beside] + ([partner_x, partner_y] if gather else [])
    greet(here, partners, here.origin)

    to_core = here.q // 2

    def block(ref, j, i):
        return ref.at[pl.ds(pl.multiple_of(j * rows + i * step, step), step), :]

    def perm_copy(i):
        return remote(
            tok.at[pl.ds(i * step, step), :], block(xs, to_core, i), perm_s.at[i], perm_r.at[i], here.to
        )

    def len_copy():
        return remote(length_in, lens, len_s, len_r, here.to)

    @pl.when(jnp.logical_not(here.stays))
    def _():
        for i in range(chunks):
            perm_copy(i).start()
        len_copy().start()

    @pl.when(here.stays)
    def _():
        for i in range(chunks):
            pltpu.make_async_copy(
                tok.at[pl.ds(i * step, step), :], block(xs, to_core, i), perm_r.at[i]
            ).start()
        pltpu.make_async_copy(length_in, lens, len_r).start()

    w_copies = []
    if gather:
        def columns(j, which):
            return pl.ds(pl.multiple_of(j * width + which * half, 128), half)

        mine = pl.ds(pl.multiple_of(s * share, share), share)
        for j in range(3):
            copy = remote(
                w_in.at[:, columns(j, 1 - core)], wf.at[mine, pl.ds(j * half, half)],
                w_s.at[j], w_r.at[j], here.sibling,
            )
            copy.start()
            w_copies.append(copy)
            copy = pltpu.make_async_copy(
                w_in.at[:, columns(j, core)], wf.at[mine, pl.ds(j * half, half)], w_s.at[4 + j]
            )
            copy.start()
            w_copies.append(copy)
        copy = remote(vec_in, vg.at[s], w_s.at[3], w_r.at[3], here.sibling)
        copy.start()
        w_copies.append(copy)
        copy = pltpu.make_async_copy(vec_in, vg.at[s], w_s.at[7])
        copy.start()
        w_copies.append(copy)
    else:
        copy = pltpu.make_async_copy(w_in, wf, w_s.at[0])
        copy.start()
        w_copies.append(copy)

    def w_move(at):
        src, count, device = (
            (s - core, 2, partner_x),
            (s - core, 2, partner_y),
            (shard_x - core, 1, partner_y),
            (shard_y - core + 1, 1, partner_x),
        )[at]
        part = wf.at[pl.ds(pl.multiple_of(src * share, share), count * share), :]
        return remote(part, part, w_s.at[8 + at], w_r.at[8 + at], device)

    def v_move(at):
        src, device = ((s, partner_x), (s, partner_y), (shard_x, partner_y))[at]
        part = vg.at[pl.ds(src - core, 2)]
        return remote(part, part, w_s.at[12 + at], w_r.at[12 + at], device)

    def receive(i):
        pltpu.make_async_copy(tok.at[pl.ds(i * step, step), :], block(xs, core, i), perm_r.at[i]).wait()
        sib = remote(block(xs, core, i), block(xs, core, i), sib_s.at[i], sib_r.at[i], here.sibling)
        side = remote(block(xs, core, i), block(xs, 2 + core, i), side_s.at[i], side_r.at[i], here.beside)
        side.start()
        sib.start()
        return [sib, side]

    def relay(i):
        block_in = block(xs, 2 + core, i)
        remote(block_in, block_in, side_s.at[i], side_r.at[i], here.beside).wait_recv()
        copy = remote(block_in, block_in, back_s.at[i], back_r.at[i], here.sibling)
        copy.start()
        return copy

    def rows_of(k, shard):
        count = shares[k].shape[0]
        return pl.ds(pl.multiple_of(shard * count, count), count)

    def piece(k, shard, part=None):
        cut = shares[k].shape[1] // 2
        if part is None:
            return wholes[k].at[rows_of(k, shard), :]
        return wholes[k].at[rows_of(k, shard), part * cut : (part + 1) * cut]

    def pass_on(k, slot, src, dst, device):
        return remote(src, dst, all_s.at[k, slot], all_r.at[k, slot], device)

    def got(k, slot, ref):
        pass_on(k, slot, ref, ref, here.sibling).wait_recv()

    def move(k, slot):
        src, device = (
            (None, partner_x),
            (None, partner_y),
            (None, here.sibling),
            ((shard_x, 0), partner_y),
            ((shard_x,), here.sibling),
            ((shard_y, 1), partner_x),
            ((shard_y,), here.sibling),
            ((shard_d,), here.sibling),
        )[slot]
        if src is None:
            return pass_on(k, slot, shares[k], piece(k, s), device)
        return pass_on(k, slot, piece(k, *src), piece(k, *src), device)

    def share_out(k):
        for slot in range(3):
            move(k, slot).start()
        pltpu.make_async_copy(shares[k], piece(k, s), all_l.at[k]).start()

    def from_x(k):
        got(k, 0, piece(k, shard_x))
        move(k, 3).start()
        move(k, 4).start()

    def from_y(k):
        got(k, 1, piece(k, shard_y))
        move(k, 5).start()
        move(k, 6).start()

    def from_far(k):
        got(k, 3, piece(k, shard_d, 0))
        got(k, 5, piece(k, shard_d, 1))
        move(k, 7).start()

    def all_here(k):
        flip = 1 - 2 * core
        for slot, shard in ((2, s), (4, shard_x), (6, shard_y), (7, shard_d)):
            got(k, slot, piece(k, shard + flip))
        pltpu.make_async_copy(shares[k], piece(k, s), all_l.at[k]).wait()

    moved = []
    if gather:
        for copy in w_copies:
            copy.wait()
        for at in range(2):
            w_move(at).start()
            v_move(at).start()
        share_out(0)
        share_out(1)
    moved += receive(0)
    moved += receive(1)
    if gather:
        w_move(0).wait_recv()
        v_move(0).wait_recv()
        w_move(2).start()
        v_move(2).start()
        w_move(1).wait_recv()
        v_move(1).wait_recv()
        w_move(3).start()
    moved += receive(2)
    moved += receive(3)
    if gather:
        share_out(2)

    def cot_copy():
        return remote(cot, cot_o, cot_s, cot_r, here.to)

    @pl.when(jnp.logical_not(here.stays))
    def _():
        cot_copy().start()

    @pl.when(here.stays)
    def _():
        pltpu.make_async_copy(cot, cot_o, cot_r).start()

    def norm_one(first, count):
        def body(i, _):
            at = pl.ds(pl.multiple_of(first + i * 256, 256), 256)
            unit, _ = unit_of(xs[at, :].astype(F32))
            h1[at, :] = (unit * vec_o[LN1G : LN1G + 1, :] + vec_o[LN1B : LN1B + 1, :]).astype(BF)
            return 0

        lax.fori_loop(0, count // 256, body, 0)

    if gather:
        w_move(2).wait_recv()
        w_move(3).wait_recv()
        v_move(2).wait_recv()
        for i in range(shards):
            part = vg[i].astype(F32)
            vec_o[:, i * share : (i + 1) * share] = part[:, :share]
            for r in range(4):
                at = (4 * i + r) * share
                inb_o[:, at : at + share] = jnp.broadcast_to(
                    part[IB + r : IB + r + 1, :share], (8, share)
                )
    else:
        for copy in w_copies:
            copy.wait()
        vec_o[...] = vec_in[...].astype(F32)
        inb_o[...] = jnp.zeros_like(inb_o)

    pltpu.make_async_copy(length_in, lens, len_r).wait()
    length = length_of(lens)
    lane = lax.broadcasted_iota(jnp.int32, (rows, 128), 1)
    row_at = lax.broadcasted_iota(jnp.int32, (rows, 128), 0)
    lower = lane < HEAD_DIM
    ones_rows = (lax.broadcasted_iota(jnp.int32, (16, rows), 0) == 0).astype(BF)
    q_rest = (lax.broadcasted_iota(jnp.int32, (64, 2 * rows), 0) == 3).astype(BF)
    for h in range(heads):
        qat[h, HEAD_DIM:, :] = q_rest

    def bias_half(at):
        full = vec_o[at : at + 1, :]
        return jnp.where(core == 0, full[:, :half], full[:, half:])

    def project(j):
        at = slice(j * rows, (j + 1) * rows)
        norm = h1[at, :]
        dead = jnp.where(here.quarters[j] * rows + row_at < length, 0.0, MASKED)
        k_rest = jnp.where(lane == HEAD_DIM + 3, dead, jnp.where(lane < HEAD_DIM + 3, 1.0, 0.0))
        v_rest = jnp.where(lane < HEAD_DIM + 3, -1.0, 0.0)
        if j < 2:
            q = (dot(norm, wf[:, :half]) + bias_half(QB)).astype(BF) * BF(HEAD_DIM**-0.5)
        k = dot(norm, wf[:, half : 2 * half])
        v = dot(norm, wf[:, 2 * half :]) + bias_half(VB)
        for i in range(heads // 2):
            two = slice(i * 128, (i + 1) * 128)
            kp, vp = k[:, two], v[:, two]
            ka[2 * i, at, :] = jnp.where(lower, kp, k_rest).astype(BF)
            ka[2 * i + 1, at, :] = jnp.where(lower, pltpu.roll(kp, 64, 1), k_rest).astype(BF)
            va[2 * i, at, :] = jnp.where(lower, vp, v_rest).astype(BF)
            va[2 * i + 1, at, :] = jnp.where(lower, pltpu.roll(vp, 64, 1), v_rest).astype(BF)
            turned = kp.astype(BF).T
            kt[2 * i, :, at] = turned[:64]
            kt[2 * i + 1, :, at] = turned[64:]
            turned = vp.astype(BF).T
            vt[2 * i, :64, at] = turned[:64]
            vt[2 * i + 1, :64, at] = turned[64:]
            vt[2 * i, 64:, at] = ones_rows
            vt[2 * i + 1, 64:, at] = ones_rows
            if j < 2:
                turned = q[:, two].T
                qat[2 * i, :64, at] = turned[:64]
                qat[2 * i + 1, :64, at] = turned[64:]

    for i in range(chunks):
        remote(block(xs, core, i), block(xs, 1 - core, i), sib_s.at[i], sib_r.at[i], here.sibling).wait_recv()
    norm_one(0, 2 * rows)
    project(0)
    project(1)
    if gather:
        from_x(0)
        from_y(0)
    relays = [relay(i) for i in range(chunks)]
    for i in range(chunks):
        pl_block = block(xs, 3 - core, i)
        remote(pl_block, pl_block, back_s.at[i], back_r.at[i], here.sibling).wait_recv()
    norm_one(2 * rows, 2 * rows)
    project(2)
    project(3)
    if gather:
        from_x(1)
        from_y(1)

    saves = []
    own = pl.ds(pl.multiple_of(core * rows, rows), rows)
    for at, (src, dst) in enumerate(
        ((ka, ka_o), (va, va_o), (kt, kt_o), (h1, h1_o), (wf, wf_o), (xs.at[own, :], xown_o), (lens, len_o))
    ):
        copy = pltpu.make_async_copy(src, dst, out_s.at[at])
        copy.start()
        saves.append(copy)

    size = 512
    keys = 4 * rows

    def attend(h, _):
        for qb in range(2 * rows // size):
            at = slice(qb * size, (qb + 1) * size)
            query = qat[h, :, at]

            def scores(c):
                return dot(ka[h, c * size : (c + 1) * size, :], query)

            ahead = scores(0)
            highest = total = None
            for c in range(keys // size):
                now = ahead
                if c + 1 < keys // size:
                    ahead = scores(c + 1)
                top = jnp.max(now, axis=0, keepdims=True)
                top = top if highest is None else jnp.maximum(highest, top)
                weights = jnp.exp(now - top).astype(BF)
                part = dot(vt[h, :, c * size : (c + 1) * size], weights)
                total = part if total is None else total * jnp.exp(highest - top) + part
                highest = top
            mass = total[64:65]
            result = total[:64] / mass
            head = pl.ds(pl.multiple_of(h * 64, 64), 64)
            exact[head, at] = result
            ctxt[head, at] = result.astype(BF)
            high, mid, low = split3(-(highest + jnp.log(mass)))
            index = lax.broadcasted_iota(jnp.int32, (16, size), 0)
            rest = jnp.where(index == 3, 1.0, 0.0)
            for r, term in enumerate((high, mid, low)):
                rest = jnp.where(index == r, term.astype(F32), rest)
            qat[h, 64:80, at] = rest.astype(BF)

        if gather:
            @pl.when(h == 0)
            def _():
                from_far(0)

            @pl.when(h == heads // 2)
            def _():
                from_far(1)

        return 0

    lax.fori_loop(0, heads, attend, 0)

    mine = pl.ds(pl.multiple_of(core * half, 128), half)
    own = pl.ds(pl.multiple_of(core * rows, rows), rows)
    other = pl.ds(pl.multiple_of((1 - core) * rows, rows), rows)
    trade = remote(ctxt.at[:, other], ctx.at[mine, :], ctx_s, ctx_r, here.sibling)
    trade.start()
    local = pltpu.make_async_copy(ctxt.at[:, own], ctx.at[mine, :], out_s.at[7])
    local.start()
    for at, (src, dst) in enumerate(((qat, qat_o), (exact, ctxt_o))):
        copy = pltpu.make_async_copy(src, dst, out_s.at[8 + at])
        copy.start()
        saves.append(copy)
    local.wait()
    trade.wait()
    copy = pltpu.make_async_copy(ctx, ctx_o, out_s.at[10])
    copy.start()
    saves.append(copy)
    for copy in saves:
        copy.wait()

    @pl.when(jnp.logical_not(here.stays))
    def _():
        for i in range(chunks):
            perm_copy(i).wait_send()
        len_copy().wait_send()
        cot_copy().wait_send()

    pltpu.make_async_copy(cot, cot_o, cot_r).wait()
    for copy in moved + relays:
        copy.wait_send()
    if gather:
        for k in range(2):
            all_here(k)
            for slot in range(8):
                move(k, slot).wait_send()
        got(2, 0, piece(2, shard_x))
        got(2, 1, piece(2, shard_y))
        got(2, 2, piece(2, s + 1 - 2 * core))
        pltpu.make_async_copy(shares[2], piece(2, s), all_l.at[2]).wait()
        for slot in range(3):
            move(2, slot).wait_send()
        for at in range(4):
            w_move(at).wait_send()
        for at in range(3):
            v_move(at).wait_send()


def attention_forward(dims, tok, cot, length, w, vec, *shares):
    shards, rows, width, heads, gather = dims
    half = width // 2
    keys = 4 * rows
    out = [
        ((heads, keys, 128), BF),
        ((heads, keys, 128), BF),
        ((heads, 64, keys), BF),
        ((heads, 128, 2 * rows), BF),
        ((half, 2 * rows), F32),
        ((width, rows), BF),
        ((keys, width), BF),
        ((width, 3 * half), BF),
        ((rows, width), BF),
        ((rows, width), BF),
        ((VROWS, 128), BF),
        ((VROWS, width), F32),
        ((8, 4 * width), F32),
    ] + [((shards * share.shape[0], share.shape[1]), BF) for share in shares]
    sems = pltpu.SemaphoreType.DMA
    return pl.pallas_call(
        functools.partial(forward_kernel, dims),
        out_shape=tuple(jax.ShapeDtypeStruct(*o) for o in out),
        in_specs=[ANY, ANY, VMEM, ANY, VMEM] + [ANY] * len(shares),
        out_specs=tuple([ANY] * 11 + [VMEM] * 2 + [ANY] * len(shares)),
        scratch_shapes=[
            pltpu.VMEM((keys, width), BF),
            pltpu.VMEM((width, 3 * half), BF),
            pltpu.VMEM((shards, VROWS, 128), BF),
            pltpu.VMEM((VROWS, 128), BF),
            pltpu.VMEM((keys, width), BF),
            pltpu.VMEM((heads, keys, 128), BF),
            pltpu.VMEM((heads, keys, 128), BF),
            pltpu.VMEM((heads, 64, keys), BF),
            pltpu.VMEM((heads, 80, keys), BF),
            pltpu.VMEM((heads, 128, 2 * rows), BF),
            pltpu.VMEM((half, 2 * rows), BF),
            pltpu.VMEM((width, rows), BF),
            pltpu.VMEM((half, 2 * rows), F32),
            sems((4,)), sems((4,)), sems((4,)), sems((4,)), sems((4,)), sems((4,)), sems((4,)), sems((4,)),
            sems, sems, sems((16,)), sems((16,)), sems((12,)), sems, sems,
            sems, sems, sems((3, 8)), sems((3, 8)), sems((3,)),
        ],
        compiler_params=pltpu.CompilerParams(
            collective_id=0, has_side_effects=True, vmem_limit_bytes=56 * 2**20
        ),
        name=forward_kernel.__name__,
    )(tok, cot, length, w, vec, *shares)


IN_PARTS = ((2, ((0, 2),)),)
FAR_HEADS = (
    (0, ((0, 3),)),
    (1, ((2, 1),)),
    (2, ((1, 2),)),
    (3, ((2, 2),)),
    (5, ((0, 4), (1, 3), (2, 3))),
)
NEAR_HEADS = (
    (2, ((2, 4),)),
    (3, ((0, 5), (1, 4), (3, 2))),
    (4, ((3, 3),)),
    (5, ((2, 5), (4, 2))),
)
TAIL = (
    ((1, 5), (5, 2), (4, 3), (3, 4)),
    ((5, 3), (4, 4), (3, 5), (0, 6), (2, 6)),
    ((1, 6), (5, 4), (4, 5), (5, 5), (3, 6), (4, 6), (5, 6)),
)


class Links:
    def __init__(self, here):
        s, q = here.s, here.q
        self.x, self.y = lax.rem(s // 2, 2), lax.rem(s // 4, 2)
        self.to_x = (q, s + 2 - 4 * self.x)
        self.to_y = (q, s + 4 - 8 * self.y)
        self.inner = (q == 1) | (q == 2)
        self.to_inner = (3 - q, s)


class Reduction:
    def __init__(self, here, links, refs, mine, first_hops=None, core=None):
        self.got, self.last, self.seq_in, self.inner_in, self.done, self.send, self.recv = refs
        self.here, self.links, self.mine = here, links, mine
        self.first_hops, self.core = first_hops, core
        self.own = mine.at[links.y, links.x]

    @staticmethod
    def scratch(r, c):
        sems = pltpu.SemaphoreType.DMA
        return [pltpu.VMEM((2, 2, r, c), BF)] + [pltpu.VMEM((2, r, c), BF)] * 4 + [sems((11,)), sems((11,))]

    def copy(self, at):
        here, links, mine, own = self.here, self.links, self.mine, self.own
        x, y = links.x, links.y
        src, dst, device = (
            lambda: self.core + (here.sibling,),
            lambda: (mine.at[:, 1 - x, 0], self.got.at[0], links.to_x),
            lambda: (mine.at[1 - y, :, 1], self.got.at[1], links.to_y),
            lambda: (mine.at[1 - y, x, 0], self.last.at[0], links.to_y),
            lambda: (mine.at[y, 1 - x, 1], self.last.at[1], links.to_x),
        )[at]()
        return remote(src, dst, self.send.at[at], self.recv.at[at], device)

    def along(self, hop, ab):
        src, dst, device = (
            (self.own, self.seq_in, self.here.beside),
            (self.own, self.inner_in, self.links.to_inner),
            (self.done, self.done, self.here.beside),
        )[hop]
        at = 5 + 2 * hop + ab
        return remote(src.at[ab], dst.at[ab], self.send.at[at], self.recv.at[at], device)

    def add(self, left, right, out=None):
        r = left.shape[-2]
        step = 96 if left.shape[-1] > 512 else r
        out = left if out is None else out

        def body(n, _):
            at = pl.ds(pl.multiple_of(n * step, step), step)
            out[at, :] = left[at, :] + right[at, :]
            return 0

        lax.fori_loop(0, r // step, body, 0)

    def phase(self, number):
        links, mine = self.links, self.mine
        x, y, outer = links.x, links.y, jnp.logical_not(links.inner)
        if number == 1:
            if self.core is not None:
                self.copy(0).wait_recv()
                for j in range(2):
                    for i in range(2):
                        for ab in range(2):
                            self.add(mine.at[j, i, ab], self.core[1].at[j, i, ab])
            self.copy(1).start()
            self.copy(2).start()
        elif number == 2:
            for copy in self.first_hops or (self.copy(1), self.copy(2)):
                copy.wait_recv()
            for i in range(2):
                self.add(mine.at[i, x, 0], self.got.at[0, i])
                self.add(mine.at[y, i, 1], self.got.at[1, i])
            self.copy(3).start()
            self.copy(4).start()
        elif number == 3:
            self.copy(3).wait_recv()
            self.copy(4).wait_recv()
            for ab in range(2):
                self.add(self.own.at[ab], self.last.at[ab])
                pl.when(outer)(lambda: self.along(0, ab).start())
        elif number == 4:
            @pl.when(links.inner)
            def _():
                for ab in range(2):
                    self.along(0, ab).wait_recv()
                    self.add(self.own.at[ab], self.seq_in.at[ab])
                    self.along(1, ab).start()
        elif number == 5:
            @pl.when(links.inner)
            def _():
                for ab in range(2):
                    self.along(1, ab).wait_recv()
                    self.add(self.own.at[ab], self.inner_in.at[ab], self.done.at[ab])
                    self.along(2, ab).start()
        else:
            @pl.when(outer)
            def _():
                for ab in range(2):
                    self.along(2, ab).wait_recv()

    def finish(self):
        if self.core is not None:
            self.copy(0).wait_send()
        for copy in self.first_hops or (self.copy(1), self.copy(2)):
            copy.wait_send()
        self.copy(3).wait_send()
        self.copy(4).wait_send()

        @pl.when(jnp.logical_not(self.links.inner))
        def _():
            for ab in range(2):
                self.along(0, ab).wait_send()

        @pl.when(self.links.inner)
        def _():
            for ab in range(2):
                self.along(1, ab).wait_send()
                self.along(2, ab).wait_send()


class FirstHop:
    def __init__(self, make, sends=None, receives=None):
        self.make, self.sends, self.receives = make, sends, receives

    @staticmethod
    def on(condition, action):
        if condition is None:
            action()
        else:
            pl.when(condition)(action)

    def start(self):
        self.on(self.sends, lambda: self.make().start())

    def wait_send(self):
        self.on(self.sends, lambda: self.make().wait_send())

    def wait_recv(self):
        self.on(self.receives, lambda: self.make().wait_recv())


def grad_parts(dims):
    shards, rows, width, heads, _ = dims
    share, half = width // shards, width // 2
    return (half, 4 * share), (share, 2 * width), (share, half)


def middle_specs(dims):
    shards, rows, width, heads, _ = dims
    half, keys, share = width // 2, 4 * rows, width // shards
    groups = heads // 2
    sems = pltpu.SemaphoreType.DMA
    part_f, part_i, part_o = grad_parts(dims)
    ins = dict(ctx=VMEM, x=VMEM, cot=VMEM, lens=VMEM, vec=VMEM, inb=VMEM)
    ins |= dict(wo_h=ANY, wi_h=ANY, wf_h=ANY, ka_h=ANY, va_h=ANY, kt_h=ANY, qat_h=ANY, ctxt_h=ANY, h1_h=ANY, wq_h=ANY)
    outs = dict(
        gtok_o=((rows, width), BF, ANY),
        out_o=((rows, width), BF, ANY),
        vec_o=((VROWS, 128), F32, VMEM),
        sum_f=((2,) + part_f, BF, ANY),
        sum_i=((2,) + part_i, BF, ANY),
        sum_o=((2,) + part_o, BF, ANY),
        sum_w=((groups, 2, share, half), BF, ANY),
        far_f=((4 * width, width), BF, ANY),
    )
    scratch = dict(
        sum_refs=sum((Reduction.scratch(*part) for part in (part_f, part_i, part_o)), [])
        + Reduction.scratch(share, half) * groups,
        mine_w=[pltpu.VMEM((2, 2, 2, share, half), BF)] * groups,
        near_f=pltpu.VMEM((2, 2, 2) + part_f, BF),
        near_i=pltpu.VMEM((2, 2, 2) + part_i, BF),
        near_o=pltpu.VMEM((2, 2, 2) + part_o, BF),
        mine_f=pltpu.VMEM((2, 2, 2) + part_f, BF),
        mine_i=pltpu.VMEM((2, 2, 2) + part_i, BF),
        both_o=pltpu.VMEM((2, 2, 2, 2) + part_o, BF),
        gmid=pltpu.VMEM((rows, width), F32),
        vecs=pltpu.VMEM((VROWS, width), F32),
        gib=pltpu.VMEM((8, 4 * width), F32),
        gt=pltpu.VMEM((rows, width), BF),
        e_ctx=pltpu.VMEM((half, 2 * rows), BF),
        sib_in=pltpu.VMEM((2, width, rows), BF),
        side_in=pltpu.VMEM((width, rows), BF),
        vec_out=pltpu.VMEM((shards, VROWS, 128), F32),
        vec_in=pltpu.VMEM((shards, VROWS, 128), F32),
        vec_all=pltpu.VMEM((4, VROWS, 128), F32),
        w_in=pltpu.VMEM((groups, share, half), BF),
        core_sf=sems((4,)),
        core_rf=sems((4,)),
        core_si=sems((4,)),
        core_ri=sems((4,)),
        x_sf=sems((4,)),
        x_rf=sems((4,)),
        y_sf=sems((4,)),
        y_rf=sems((4,)),
        x_si=sems((4,)),
        x_ri=sems((4,)),
        y_si=sems((4,)),
        y_ri=sems((4,)),
        far_s=sems((8,)),
        far_r=sems((8,)),
        load_s=sems((9,)),
        head_s=sems((2, 4)),
        trade_s=sems((2,)),
        trade_r=sems,
        sib_s=sems((2,)),
        sib_r=sems((2,)),
        side_s=sems((4,)),
        side_r=sems((4,)),
        perm_s=sems((5,)),
        perm_r=sems((5,)),
        vec_s=sems((shards + 4,)),
        vec_r=sems((shards + 4,)),
        w_s=sems((groups,)),
        w_r=sems((groups,)),
        final_s=sems((3 + 2 * groups,)),
    )
    feed = dict(
        wo=pltpu.VMEM((width, width), BF),
        wi=pltpu.VMEM((2, width, width), BF),
        wf=pltpu.VMEM((2, width, width), BF),
        mid=pltpu.VMEM((rows, width), F32),
        h2=pltpu.VMEM((rows, width), BF),
        h2t=pltpu.VMEM((width + 16, rows), BF),
        eo=pltpu.VMEM((rows, width), BF),
        active=pltpu.VMEM((4, rows, width), BF),
        slope=pltpu.VMEM((4, rows, width), BF),
    )
    attend = dict(
        ka=pltpu.VMEM((2, 2 * rows, 128), BF),
        va=pltpu.VMEM((2, 2 * rows, 128), BF),
        kt=pltpu.VMEM((2, 64, 2 * rows), BF),
        qat=pltpu.VMEM((2, 128, 2 * rows), BF),
        h1=pltpu.VMEM((keys, width), BF),
        wq=pltpu.VMEM((width, 3 * half), BF),
        eat=pltpu.VMEM((heads, 128, 2 * rows), BF),
        grads=pltpu.VMEM((3 * half, keys), BF),
        sums=pltpu.VMEM((width, rows), F32),
        sib_out=pltpu.VMEM((2, width, rows), BF),
        side_out=pltpu.VMEM((width, rows), BF),
    )
    return ins, outs, scratch, feed, attend


def middle_kernel(dims, *refs):
    shards, rows, width, heads, _ = dims
    ins, outs, scratch, feed, attend = middle_specs(dims)
    at_ins, at_outs = len(ins), len(ins) + len(outs)
    i = Named(ins, refs[:at_ins])
    o = Named(outs, refs[at_ins:at_outs])
    v = Named(scratch, refs[at_outs:])
    here = Place()
    links = Links(here)
    core, x, y = here.core, links.x, links.y
    half, keys, share, size = width // 2, 4 * rows, width // shards, width
    groups, parts, chunks = heads // 2, 4, 4
    step = rows // chunks

    in_plane = [(here.q, lax.rem(here.s + n, shards)) for n in range(1, shards)]
    along = [(lax.rem(here.q + n, 4), here.s) for n in range(1, 4)]
    greet(here, in_plane + along, here.to)

    flip = 1 - 2 * core
    shard_x, shard_y = here.s + 2 - 4 * x, here.s + 4 - 8 * y
    shard_d = shard_x + 4 - 8 * y

    def share_of(ref, shard, part=None):
        count = 4 * share
        rows_of = pl.ds(pl.multiple_of(shard * count, count), count)
        return ref.at[rows_of, :] if part is None else ref.at[rows_of, part * half : (part + 1) * half]

    def far_move(at):
        shard, part, device = (
            (shard_x, 0, links.to_y),
            (shard_y, 1, links.to_x),
            (shard_x, None, here.sibling),
            (shard_y, None, here.sibling),
            (shard_d, None, here.sibling),
        )[at]
        src = share_of(o.far_f if at == 4 else i.wf_h, shard, part)
        return remote(src, share_of(o.far_f, shard, part), v.far_s.at[at], v.far_r.at[at], device)

    def far_came(at):
        shard, part = ((shard_d, 0), (shard_d, 1), (shard_x + flip, None), (shard_y + flip, None), (shard_d + flip, None))[at]
        ref = share_of(o.far_f, shard, part)
        remote(ref, ref, v.far_s.at[at], v.far_r.at[at], here.sibling).wait_recv()

    for at in range(4):
        far_move(at).start()

    def chip_of(k):
        return (1 - y if k // 2 else y), (1 - x if k % 2 else x)

    def columns(k):
        return pl.ds(pl.multiple_of(chip_of(k)[0] * size, size), size)

    def x_f(k):
        cy, cx = chip_of(k)
        return remote(v.mine_f.at[cy, cx, 0], v.got_f.at[0, cy], v.x_sf.at[k], v.x_rf.at[k], links.to_x)

    def y_f(k):
        cy, cx = chip_of(k)
        return remote(v.mine_f.at[cy, cx, 1], v.got_f.at[1, cx], v.y_sf.at[k], v.y_rf.at[k], links.to_y)

    def x_i(k):
        to = columns(k)
        return remote(
            v.mine_i.at[:, 1 - x, 0, :, to], v.got_i.at[0, :, :, to], v.x_si.at[k], v.x_ri.at[k], links.to_x
        )

    def y_i(k):
        to = columns(k)
        return remote(
            v.mine_i.at[1 - y, :, 1, :, to], v.got_i.at[1, :, :, to], v.y_si.at[k], v.y_ri.at[k], links.to_y
        )

    refs = [v.sum_refs[7 * n : 7 * n + 7] for n in range(3 + groups)]
    v.got_f, v.got_i = refs[0][0], refs[1][0]
    hops_f, hops_i = [], []
    for k in range(parts):
        cx = chip_of(k)[1]
        hops_f.append(([FirstHop(functools.partial(x_f, k))] if k % 2 else []) + ([FirstHop(functools.partial(y_f, k))] if k // 2 else []))
        hops_i.append(
            [FirstHop(functools.partial(x_i, k), cx == 0, cx == 1), FirstHop(functools.partial(y_i, k), cx == 1, cx == 1)]
        )
    sums = [
        Reduction(here, links, refs[0], v.mine_f, sum(hops_f, [])),
        Reduction(here, links, refs[1], v.mine_i, sum(hops_i, [])),
        Reduction(here, links, refs[2], v.both_o.at[core], None, (v.both_o.at[1 - core], v.near_o)),
    ]
    sums += [Reduction(here, links, refs[3 + g], v.mine_w[g]) for g in range(groups)]

    def run(*steps):
        for which, number in steps:
            sums[which].phase(number)

    def home(src, dst, at):
        return remote(src, dst, v.perm_s.at[at], v.perm_r.at[at], here.origin)

    def home_start(src, dst, at):
        @pl.when(jnp.logical_not(here.stays))
        def _():
            home(src, dst, at).start()

        @pl.when(here.stays)
        def _():
            pltpu.make_async_copy(src, dst, v.perm_s.at[at]).start()

    def home_sent(src, dst, at):
        @pl.when(jnp.logical_not(here.stays))
        def _():
            home(src, dst, at).wait_send()

        @pl.when(here.stays)
        def _():
            pltpu.make_async_copy(src, dst, v.perm_s.at[at]).wait()

    def home_came(src, dst, at):
        @pl.when(jnp.logical_not(here.stays))
        def _():
            home(src, dst, at).wait_recv()

    def vector(at):
        return i.vec[at : at + 1, :]

    def feed_part(*buffers):
        b = Named(feed, buffers)

        load_o = pltpu.make_async_copy(i.wo_h, b.wo, v.load_s.at[0])
        load_o.start()

        def load_i(k):
            cy, cx = chip_of(k)
            to = pl.ds(pl.multiple_of((2 * cy + cx) * size, size), size)
            return pltpu.make_async_copy(i.wi_h.at[:, to], b.wi.at[k % 2], v.load_s.at[1 + k % 2])

        def load_f(k):
            shard = (here.s, shard_x, shard_y, shard_d)[k]
            count = 4 * share
            return [
                pltpu.make_async_copy(
                    share_of(o.far_f if n or k == 3 else i.wf_h, each) if k else share_of(i.wf_h, each),
                    b.wf.at[k % 2, pl.ds(pl.multiple_of(lax.rem(each, 2) * count, count), count), :],
                    v.load_s.at[3 + 2 * (k % 2) + n],
                )
                for n, each in enumerate((shard, shard + flip))
            ]

        load_i(3).start()
        load_i(2).start()
        for copy in load_f(0):
            copy.start()

        row_at = lax.broadcasted_iota(jnp.int32, (rows, 1), 0) + here.quarter * rows
        live = row_at < length_of(i.lens)
        e_outer = jnp.where(live, i.cot[...].astype(F32), 0.0)
        b.eo[...] = e_outer.astype(BF)
        v.vecs[...] = jnp.zeros_like(v.vecs)
        v.vecs[FB : FB + 1, :] = jnp.sum(e_outer, 0, keepdims=True)

        load_o.wait()
        middle = i.x[...].astype(F32) + dot(i.ctx[...].T, b.wo[...]) + vector(OB)
        b.mid[...] = middle
        unit, _ = unit_of(middle)
        b.h2[...] = (unit * vector(LN2G) + vector(LN2B)).astype(BF)
        b.h2t[:width, :] = b.h2[...].T
        b.h2t[width:, :] = jnp.ones((16, rows), BF)

        def hidden_part(eot, both_f):
            def near_f(k):
                cy, cx = chip_of(k)
                return remote(
                    both_f.at[k % 2, 1 - core], v.near_f.at[cy, cx], v.core_sf.at[k], v.core_rf.at[k], here.sibling
                )

            def send_f(k):
                cy, cx = chip_of(k)
                near_f(k).wait_recv()
                for ab in range(2):
                    v.mine_f[cy, cx, ab] = both_f[k % 2, core, ab] + v.near_f[cy, cx, ab]
                for hop in hops_f[k]:
                    hop.start()

            eot[...] = b.eo[...].T
            order = (3, 2, 1, 0)
            for n, k in enumerate(order):
                cy, cx = chip_of(k)
                at = pl.ds(pl.multiple_of((2 * cy + cx) * size, size), size)
                load_i(k).wait()
                inner = dot(b.h2[...], b.wi[k % 2]) + i.inb[0:1, at]
                if n + 2 < parts:
                    load_i(order[n + 2]).start()
                square = inner * inner
                swing = jnp.tanh(GELU_C * inner * (1.0 + GELU_K * square))
                active = (0.5 * inner * (1.0 + swing)).astype(BF)
                b.active[k] = active
                b.slope[k] = (
                    0.5 * (1.0 + swing)
                    + 0.5 * inner * (1.0 - swing * swing) * (GELU_C * (1.0 + 3.0 * GELU_K * square))
                ).astype(BF)
                grad = dot(eot[...], active).astype(BF)
                if n >= 2:
                    near_f(order[n - 2]).wait_send()
                for c in range(2):
                    for ab in range(2):
                        both_f[k % 2, c, ab] = grad[ab * half : (ab + 1) * half, c * half : (c + 1) * half]
                near_f(k).start()
                if n > 0:
                    send_f(order[n - 1])
            load_i(0).start()
            load_i(1).start()
            send_f(order[-1])
            for k in order[-2:]:
                near_f(k).wait_send()

        part_f = grad_parts(dims)[0]
        pl.run_scoped(hidden_part, pltpu.VMEM((width, rows), BF), pltpu.VMEM((2, 2, 2) + part_f, BF))

        def back_part(gh2, acc, ect, both_i):
            def near_i(k):
                return remote(
                    both_i.at[k % 2, 1 - core], v.near_i.at[:, :, chip_of(k)[1], :, columns(k)], v.core_si.at[k],
                    v.core_ri.at[k], here.sibling,
                )

            def send_i(k):
                (cy, cx), to = chip_of(k), columns(k)
                near_i(k).wait_recv()
                for n in range(4):
                    v.mine_i[n // 2, n % 2, cx, :, to] = (
                        both_i[k % 2, core, n // 2, n % 2] + v.near_i[n // 2, n % 2, cx, :, to]
                    )
                for hop in hops_i[k]:
                    hop.start()

            acc[...] = b.mid[...] + vector(FB)
            for k in range(parts):
                cy, cx = chip_of(k)
                at = pl.ds(pl.multiple_of((2 * cy + cx) * size, size), size)
                load_i(k).wait()
                for copy in load_f(k):
                    copy.wait()
                if k == 0:
                    far_came(2)
                    far_came(3)
                if k == 1:
                    far_came(0)
                    far_came(1)
                    far_move(4).start()
                if k == 2:
                    far_came(4)
                if k + 1 < parts:
                    for copy in load_f(k + 1):
                        copy.start()
                wic, wfc = b.wi[k % 2], b.wf[k % 2]
                e_inner = (dot_t(b.eo[...], wfc) * b.slope[k].astype(F32)).astype(BF)
                grad = dot(b.h2t[...], e_inner)
                v.gib[:, at] = grad[width : width + 8]
                if k >= 2:
                    near_i(k - 2).wait_send()
                for c in range(2):
                    for n in range(4):
                        to = (2 * n + c) * share
                        both_i[k % 2, c, n // 2, n % 2] = grad[to : to + share].astype(BF)
                near_i(k).start()
                acc[...] += dot(b.active[k], wfc)
                part = dot_t(e_inner, wic)
                gh2[...] = part if k == 0 else gh2[...] + part
                if k + 2 < parts:
                    load_i(k + 2).start()
                if k > 0:
                    send_i(k - 1)
                for when, steps in IN_PARTS:
                    if when == k:
                        run(*steps)
            v.gt[...] = acc[...].astype(BF)
            home_start(v.gt, o.out_o, 4)
            unit, inverse = unit_of(b.mid[...])
            e_norm = gh2[...]
            v.vecs[LN2G : LN2G + 1, :] = jnp.sum(e_norm * unit, 0, keepdims=True)
            v.vecs[LN2B : LN2B + 1, :] = jnp.sum(e_norm, 0, keepdims=True)
            e_unit = e_norm * vector(LN2G)
            grad_mid = jnp.where(live, i.cot[...].astype(F32), 0.0) + inverse * (
                e_unit - mean_rows(e_unit) - unit * mean_rows(e_unit * unit)
            )
            v.gmid[...] = grad_mid
            e_branch = grad_mid.astype(BF)
            v.vecs[OB : OB + 1, :] = jnp.sum(e_branch.astype(F32), 0, keepdims=True)
            ect[...] = dot_t(b.wo[...], e_branch).astype(BF)
            mine = pl.ds(pl.multiple_of(core * half, 128), half)
            theirs = pl.ds(pl.multiple_of((1 - core) * half, 128), half)
            own = pl.ds(pl.multiple_of(core * rows, rows), rows)
            trade = remote(ect.at[theirs, :], v.e_ctx.at[:, own], v.trade_s.at[0], v.trade_r, here.sibling)
            trade.start()
            local = pltpu.make_async_copy(ect.at[mine, :], v.e_ctx.at[:, own], v.trade_s.at[1])
            local.start()
            send_i(parts - 1)
            grads = dot(i.ctx[...], e_branch).astype(BF)
            for n in range(shards):
                for ab in range(2):
                    v.both_o[n % 2, n // 4, n // 2 % 2, ab] = grads[
                        n * share : (n + 1) * share, ab * half : (ab + 1) * half
                    ]
            sums[2].copy(0).start()
            local.wait()
            trade.wait()
            for k in range(2, parts):
                near_i(k).wait_send()

        pl.run_scoped(
            back_part,
            pltpu.VMEM((rows, width), F32),
            pltpu.VMEM((rows, width), F32),
            pltpu.VMEM((width, rows), BF),
            pltpu.VMEM((2, 2, 2, 2, share, width), BF),
        )
        for at in range(5):
            far_move(at).wait_send()

    pl.run_scoped(feed_part, *flat(feed))

    def attend_part(*buffers):
        b = Named(attend, buffers)

        def fetch(far, h, slot):
            rows_of = slice(2 * rows, keys) if far else slice(0, 2 * rows)
            return [
                pltpu.make_async_copy(src, dst, v.head_s.at[slot, n])
                for n, (src, dst) in enumerate(
                    (
                        (i.qat_h.at[h], b.qat.at[slot]),
                        (i.ka_h.at[h, rows_of, :], b.ka.at[slot]),
                        (i.va_h.at[h, rows_of, :], b.va.at[slot]),
                        (i.kt_h.at[h, :, rows_of], b.kt.at[slot]),
                    )
                )
            ]

        for copy in fetch(True, 0, 0):
            copy.start()

        def with_delta(ctxt, sem):
            load = pltpu.make_async_copy(i.ctxt_h, ctxt, sem)
            load.start()
            load.wait()
            index = lax.broadcasted_iota(jnp.int32, (16, 2 * rows), 0)
            for h in range(heads):
                at = slice(h * 64, (h + 1) * 64)
                e_ctx = v.e_ctx[at, :]
                delta = jnp.sum(e_ctx.astype(F32) * ctxt[at, :], 0, keepdims=True)
                rest = jnp.zeros((16, 2 * rows), F32)
                for r, term in enumerate(split3(delta)):
                    rest = jnp.where(index == r, term.astype(F32), rest)
                b.eat[h, :64, :] = e_ctx
                b.eat[h, 64:80, :] = rest.astype(BF)
                b.eat[h, 80:, :] = jnp.zeros((48, 2 * rows), BF)

        pl.run_scoped(with_delta, pltpu.VMEM((half, 2 * rows), F32), pltpu.SemaphoreType.DMA)
        loads = [
            pltpu.make_async_copy(i.wq_h, b.wq, v.load_s.at[7]),
            pltpu.make_async_copy(i.h1_h, b.h1, v.load_s.at[8]),
        ]
        for copy in loads:
            copy.start()
        block = 256

        def attend_half(far, polls):
            first = 2 * rows if far else 0

            def body(h, _):
                slot = lax.rem(h, 2)
                for copy in fetch(far, h, slot):
                    copy.wait()

                @pl.when(h < heads - 1)
                def _():
                    for copy in fetch(far, h + 1, 1 - slot):
                        copy.start()

                if far:
                    @pl.when(h == heads - 1)
                    def _():
                        for copy in fetch(False, 0, 1 - slot):
                            copy.start()

                query, e_ctx = b.qat[slot], b.eat[h]
                e_query = None
                for c in range(2 * rows // block):
                    of = slice(c * block, (c + 1) * block)
                    to = slice(first + c * block, first + (c + 1) * block)
                    weights = jnp.exp(dot(b.ka[slot, of, :], query))
                    e_scores = (weights * dot(b.va[slot, of, :], e_ctx)).astype(BF)
                    e_value = dot_t(e_ctx[:64], weights.astype(BF))
                    e_key = dot_t(query[:64], e_scores)
                    part = dot(b.kt[slot, :, of], e_scores)
                    e_query = part if e_query is None else e_query + part
                    b.grads[pl.ds(pl.multiple_of(half + h * 64, 64), 64), to] = e_key.astype(BF)
                    b.grads[pl.ds(pl.multiple_of(2 * half + h * 64, 64), 64), to] = e_value.astype(BF)
                head = pl.ds(pl.multiple_of(h * 64, 64), 64)
                lower = pl.ds(pl.multiple_of(half + h * 64, 64), 64)
                if far:
                    b.sums[head, :] = e_query[:, :rows]
                    b.sums[lower, :] = e_query[:, rows:]
                else:
                    b.grads[head, :rows] = ((b.sums[head, :] + e_query[:, :rows]) * HEAD_DIM**-0.5).astype(BF)
                    b.grads[head, rows : 2 * rows] = (
                        (b.sums[lower, :] + e_query[:, rows:]) * HEAD_DIM**-0.5
                    ).astype(BF)
                for when, action in polls:
                    pl.when(h == when)(action)
                return 0

            lax.fori_loop(0, heads, body, 0)

        def steps_of(table):
            return [(when, functools.partial(run, *steps)) for when, steps in table]

        def partial_of(j, near):
            at = pl.ds(pl.multiple_of(j * rows, rows), rows)
            if near:
                return dot(b.wq[...], b.grads[:, at])
            return dot(b.wq[:, half:], b.grads[half:, at])

        def sib_copy(at):
            return remote(b.sib_out.at[at], v.sib_in.at[at], v.sib_s.at[at], v.sib_r.at[at], here.sibling)

        def side_copy(at):
            to = slice(at * step, (at + 1) * step)
            return remote(
                b.side_out.at[:, to], v.side_in.at[:, to], v.side_s.at[at], v.side_r.at[at], here.beside
            )

        def to_side():
            sib_copy(0).wait_recv()
            b.side_out[...] = (partial_of(2 + core, False) + v.sib_in[0].astype(F32)).astype(BF)
            for at in range(chunks):
                side_copy(at).start()

        def weight_grad(g):
            for part, count in ((0, 2 * rows), (1, keys), (2, keys)):
                at = part * half + g * 128
                result = dot(b.grads[at : at + 128, :count], b.h1[:count, :]).T.astype(BF)
                to = slice(part * 128, (part + 1) * 128)
                for j in range(shards):
                    sums[3 + g].mine[j // 4, j // 2 % 2, j % 2, :, to] = result[j * share : (j + 1) * share]
            run((3 + g, 1))

        attend_half(True, steps_of(FAR_HEADS))
        for copy in loads:
            copy.wait()
        b.sib_out[0] = partial_of(3 - core, False).astype(BF)
        sib_copy(0).start()
        attend_half(
            False,
            [(0, to_side)]
            + [(2 * g + 1, functools.partial(weight_grad, g)) for g in range(groups - 1)]
            + steps_of(NEAR_HEADS),
        )
        b.sib_out[1] = partial_of(1 - core, True).astype(BF)
        sib_copy(1).start()
        weight_grad(groups - 1)
        own_part = partial_of(core, True)
        home_sent(v.gt, o.out_o, 4)
        sib_copy(1).wait_recv()
        b.sums[...] = own_part + v.sib_in[1].astype(F32)

        gain = vector(LN1G)
        gain_sum = shift_sum = None
        for at in range(chunks):
            to = slice(at * step, (at + 1) * step)
            side_copy(at).wait_recv()
            e_norm = (b.sums[:, to] + v.side_in[:, to].astype(F32)).T
            unit, inverse = unit_of(i.x[to, :].astype(F32))
            e_unit = e_norm * gain
            result = v.gmid[to, :] + inverse * (
                e_unit - mean_rows(e_unit) - unit * mean_rows(e_unit * unit)
            )
            v.gt[to, :] = result.astype(BF)
            home_start(v.gt.at[to, :], o.gtok_o.at[to, :], at)
            gains = jnp.sum(e_norm * unit, 0, keepdims=True)
            shifts = jnp.sum(e_norm, 0, keepdims=True)
            gain_sum = gains if at == 0 else gain_sum + gains
            shift_sum = shifts if at == 0 else shift_sum + shifts
        v.vecs[LN1G : LN1G + 1, :] = gain_sum
        v.vecs[LN1B : LN1B + 1, :] = shift_sum

        def row_sums(values):
            folded = values[:, :128].astype(F32)
            for n in range(1, values.shape[1] // 128):
                folded += values[:, n * 128 : (n + 1) * 128].astype(F32)
            return jnp.sum(folded.T, 0, keepdims=True)

        for at, part in ((QB, b.grads[:half, : 2 * rows]), (VB, b.grads[2 * half :, :])):
            total = row_sums(part)
            for n in range(2):
                v.vecs[at : at + 1, n * half : (n + 1) * half] = jnp.where(core == n, total, 0.0)

        for n in range(shards):
            v.vec_out[n, :, :share] = v.vecs[:, n * share : (n + 1) * share]
            for r in range(4):
                to = (4 * n + r) * share
                v.vec_out[n, IB + r : IB + r + 1, :share] = v.gib[0:1, to : to + share]

        def vec_plane(n):
            to = lax.rem(here.s + n, shards)
            return remote(
                v.vec_out.at[to], v.vec_in.at[here.s], v.vec_s.at[n], v.vec_r.at[n], (here.q, to)
            )

        def vec_along(n):
            to, at = lax.rem(here.q + n, 4), shards + n
            return remote(
                v.vec_all.at[here.q], v.vec_all.at[here.q], v.vec_s.at[at], v.vec_r.at[at], (to, here.s)
            )

        for n in range(1, shards):
            vec_plane(n).start()
        v.vec_in[here.s] = v.vec_out[here.s]
        run(*TAIL[0])
        for n in range(1, shards):
            vec_plane(n).wait_recv()
        total = v.vec_in[0]
        for n in range(1, shards):
            total += v.vec_in[n]
        v.vec_all[here.q] = total
        for n in range(1, 4):
            vec_along(n).start()
        run(*TAIL[1])
        for n in range(1, 4):
            vec_along(n).wait_recv()
        o.vec_o[...] = (v.vec_all[0] + v.vec_all[1]) + (v.vec_all[2] + v.vec_all[3])
        run(*TAIL[2])
        finals = []

        def final(src, dst, at):
            copy = pltpu.make_async_copy(src, dst, v.final_s.at[at])
            copy.start()
            finals.append(copy)

        def w_trade(g):
            return remote(sums[3 + g].done.at[1 - core], v.w_in.at[g], v.w_s.at[g], v.w_r.at[g], here.sibling)

        for g in range(groups):
            w_trade(g).start()
        for n, dst in enumerate((o.sum_f, o.sum_i, o.sum_o)):
            final(sums[n].done, dst, n)
        for g in range(groups):
            final(sums[3 + g].done.at[core], o.sum_w.at[g, core], 3 + 2 * g)
            w_trade(g).wait()
            final(v.w_in.at[g], o.sum_w.at[g, 1 - core], 4 + 2 * g)
        for copy in finals:
            copy.wait()
        for each in sums:
            each.finish()
        for n in range(1, shards):
            vec_plane(n).wait_send()
        for n in range(1, 4):
            vec_along(n).wait_send()
        for at in range(2):
            sib_copy(at).wait_send()
        for at in range(chunks):
            side_copy(at).wait_send()
            to = slice(at * step, (at + 1) * step)
            home_sent(v.gt.at[to, :], o.gtok_o.at[to, :], at)
            home_came(v.gt.at[to, :], o.gtok_o.at[to, :], at)
        home_came(v.gt, o.out_o, 4)

    pl.run_scoped(attend_part, *flat(attend))


def call(kernel, dims, specs, args, **params):
    ins, outs, scratch = specs[:3]
    return pl.pallas_call(
        functools.partial(kernel, dims),
        out_shape=tuple(jax.ShapeDtypeStruct(*out[:2]) for out in outs.values()),
        in_specs=flat(ins),
        out_specs=tuple(out[2] for out in outs.values()),
        scratch_shapes=flat(scratch),
        compiler_params=pltpu.CompilerParams(**params),
        name=kernel.__name__,
    )(*args)


def middle(dims, *args):
    return call(
        middle_kernel, dims, middle_specs(dims), args, collective_id=1, has_side_effects=True,
        vmem_limit_bytes=62 * 2**20,
    )[:-1]


def feed_plain(ctx, x, cot, length, vec, in_bias, wo, wi, wf):
    here = Place()
    rows = x.shape[0]
    row_at = lax.broadcasted_iota(jnp.int32, (rows, 1), 0) + here.quarter * rows
    e_outer = jnp.where(row_at < length, cot.astype(F32), 0.0)
    mid = x.astype(F32) + dot(ctx.T, wo) + vec[OB]
    unit, inverse = unit_of(mid)
    h2 = (unit * vec[LN2G] + vec[LN2B]).astype(BF)
    inner = dot(h2, wi) + in_bias
    square = inner * inner
    swing = jnp.tanh(GELU_C * inner * (1.0 + GELU_K * square))
    active = (0.5 * inner * (1.0 + swing)).astype(BF)
    slope = 0.5 * (1.0 + swing) + 0.5 * inner * (1.0 - swing * swing) * (
        GELU_C * (1.0 + 3.0 * GELU_K * square)
    )
    out = (mid + dot(active, wf) + vec[FB]).astype(BF)
    e_low = e_outer.astype(BF)
    e_inner = (dot_t(e_low, wf) * slope).astype(BF)
    e_norm = dot_t(e_inner, wi)
    e_unit = e_norm * vec[LN2G]
    grad_mid = e_outer + inverse * (e_unit - mean_rows(e_unit) - unit * mean_rows(e_unit * unit))
    e_branch = grad_mid.astype(BF)
    grads = dot(active.T, e_low), dot(h2.T, e_inner), dot(ctx, e_branch)
    vectors = (
        jnp.sum(e_branch.astype(F32), 0),
        jnp.sum(e_norm * unit, 0),
        jnp.sum(e_norm, 0),
        jnp.sum(e_outer, 0),
    )
    in_sums = jnp.sum(e_inner.astype(F32), 0).reshape(4, -1)
    vectors = jnp.concatenate((jnp.stack(vectors), in_sums))
    return out, dot_t(wo, e_branch).astype(BF), grad_mid, vectors, [g.astype(BF) for g in grads]


def backward_specs(dims):
    shards, rows, width, heads, _ = dims
    half, keys = width // 2, 4 * rows
    sems = pltpu.SemaphoreType.DMA
    ins = dict(
        ect=VMEM, ka_h=ANY, va_h=ANY, kt_h=ANY, qat_h=ANY, ctxt_h=ANY, h1_h=ANY, wq_h=ANY, out_h=ANY, x=VMEM,
        gmid=VMEM, vec=VMEM,
    )
    outs = dict(
        gtok_o=((rows, width), BF, ANY),
        out_o=((rows, width), BF, ANY),
        vec_o=((VROWS, width), F32, VMEM),
        gw_o=((width, 3 * half), BF, VMEM),
    )
    scratch = dict(
        vecs=pltpu.VMEM((VROWS, width), F32),
        ka=pltpu.VMEM((heads, keys, 128), BF),
        va=pltpu.VMEM((heads, keys, 128), BF),
        kt=pltpu.VMEM((heads, 64, keys), BF),
        qat=pltpu.VMEM((heads, 128, 2 * rows), BF),
        h1=pltpu.VMEM((keys, width), BF),
        wq=pltpu.VMEM((width, 3 * half), BF),
        e_ctx=pltpu.VMEM((half, 2 * rows), BF),
        eat=pltpu.VMEM((heads, 128, 2 * rows), BF),
        grads=pltpu.VMEM((3 * half, keys), BF),
        sums=pltpu.VMEM((width, rows), F32),
        sib_out=pltpu.VMEM((2, width, rows), BF),
        sib_in=pltpu.VMEM((2, width, rows), BF),
        side_out=pltpu.VMEM((width, rows), BF),
        side_in=pltpu.VMEM((width, rows), BF),
        gt=pltpu.VMEM((rows, width), BF),
        load_s=sems((7,)),
        trade_s=sems((2,)),
        trade_r=sems,
        sib_s=sems((2,)),
        sib_r=sems((2,)),
        side_s=sems((4,)),
        side_r=sems((4,)),
        perm_s=sems((5,)),
        perm_r=sems((5,)),
    )
    return ins, outs, scratch


def backward_kernel(dims, *refs):
    shards, rows, width, heads, _ = dims
    ins, outs, scratch = backward_specs(dims)
    at_ins, at_outs = len(ins), len(ins) + len(outs)
    i = Named(ins, refs[:at_ins])
    o = Named(outs, refs[at_ins:at_outs])
    v = Named(scratch, refs[at_outs:])
    here = Place()
    core = here.core
    half, keys = width // 2, 4 * rows
    chunks = 4
    step = rows // chunks
    loads = []
    for at, (src, dst) in enumerate(
        ((i.qat_h, v.qat), (i.ka_h, v.ka), (i.va_h, v.va), (i.kt_h, v.kt), (i.wq_h, v.wq), (i.h1_h, v.h1))
    ):
        copy = pltpu.make_async_copy(src, dst, v.load_s.at[at])
        copy.start()
        loads.append(copy)

    greet(here, [here.sibling, here.beside], here.to)

    mine = pl.ds(pl.multiple_of(core * half, 128), half)
    theirs = pl.ds(pl.multiple_of((1 - core) * half, 128), half)
    own = pl.ds(pl.multiple_of(core * rows, rows), rows)
    trade = remote(i.ect.at[theirs, :], v.e_ctx.at[:, own], v.trade_s.at[0], v.trade_r, here.sibling)
    trade.start()
    local = pltpu.make_async_copy(i.ect.at[mine, :], v.e_ctx.at[:, own], v.trade_s.at[1])
    local.start()

    def home(src, dst, at):
        return remote(src, dst, v.perm_s.at[at], v.perm_r.at[at], here.origin)

    def home_start(src, dst, at):
        @pl.when(jnp.logical_not(here.stays))
        def _():
            home(src, dst, at).start()

        @pl.when(here.stays)
        def _():
            pltpu.make_async_copy(src, dst, v.perm_r.at[at]).start()

    def home_wait(src, dst, at):
        pltpu.make_async_copy(src, dst, v.perm_r.at[at]).wait()

        @pl.when(jnp.logical_not(here.stays))
        def _():
            home(src, dst, at).wait_send()

    home_start(i.out_h, o.out_o, 4)
    local.wait()
    trade.wait()

    def with_delta(ctxt, sem):
        load = pltpu.make_async_copy(i.ctxt_h, ctxt, sem)
        load.start()
        load.wait()
        index = lax.broadcasted_iota(jnp.int32, (16, 2 * rows), 0)
        for h in range(heads):
            at = slice(h * 64, (h + 1) * 64)
            e_ctx = v.e_ctx[at, :]
            delta = jnp.sum(e_ctx.astype(F32) * ctxt[at, :], 0, keepdims=True)
            rest = jnp.zeros((16, 2 * rows), F32)
            for r, term in enumerate(split3(delta)):
                rest = jnp.where(index == r, term.astype(F32), rest)
            v.eat[h, :64, :] = e_ctx
            v.eat[h, 64:80, :] = rest.astype(BF)
            v.eat[h, 80:, :] = jnp.zeros((48, 2 * rows), BF)

    pl.run_scoped(with_delta, pltpu.VMEM((half, 2 * rows), F32), pltpu.SemaphoreType.DMA)
    for copy in loads:
        copy.wait()

    size = 256

    def attend(far):
        first = 2 * rows if far else 0

        def body(h, _):
            query, e_ctx = v.qat[h], v.eat[h]
            e_query = None
            for c in range(2 * rows // size):
                to = slice(first + c * size, first + (c + 1) * size)
                weights = jnp.exp(dot(v.ka[h, to, :], query))
                e_scores = (weights * dot(v.va[h, to, :], e_ctx)).astype(BF)
                e_value = dot_t(e_ctx[:64], weights.astype(BF))
                e_key = dot_t(query[:64], e_scores)
                part = dot(v.kt[h, :, to], e_scores)
                e_query = part if e_query is None else e_query + part
                v.grads[pl.ds(pl.multiple_of(half + h * 64, 64), 64), to] = e_key.astype(BF)
                v.grads[pl.ds(pl.multiple_of(2 * half + h * 64, 64), 64), to] = e_value.astype(BF)
            head = pl.ds(pl.multiple_of(h * 64, 64), 64)
            lower = pl.ds(pl.multiple_of(half + h * 64, 64), 64)
            if far:
                v.sums[head, :] = e_query[:, :rows]
                v.sums[lower, :] = e_query[:, rows:]
            else:
                v.grads[head, :rows] = ((v.sums[head, :] + e_query[:, :rows]) * HEAD_DIM**-0.5).astype(BF)
                v.grads[head, rows : 2 * rows] = (
                    (v.sums[lower, :] + e_query[:, rows:]) * HEAD_DIM**-0.5
                ).astype(BF)
            return 0

        lax.fori_loop(0, heads, body, 0)

    def partial_of(j, near):
        at = pl.ds(pl.multiple_of(j * rows, rows), rows)
        if near:
            return dot(v.wq[...], v.grads[:, at])
        return dot(v.wq[:, half:], v.grads[half:, at])

    def sib_copy(at):
        return remote(v.sib_out.at[at], v.sib_in.at[at], v.sib_s.at[at], v.sib_r.at[at], here.sibling)

    def side_copy(at):
        to = slice(at * step, (at + 1) * step)
        return remote(
            v.side_out.at[:, to], v.side_in.at[:, to], v.side_s.at[at], v.side_r.at[at], here.beside
        )

    def to_side():
        sib_copy(0).wait_recv()
        v.side_out[...] = (partial_of(2 + core, False) + v.sib_in[0].astype(F32)).astype(BF)
        for at in range(chunks):
            side_copy(at).start()

    attend(True)
    v.sib_out[0] = partial_of(3 - core, False).astype(BF)
    sib_copy(0).start()
    attend(False)
    to_side()
    v.sib_out[1] = partial_of(1 - core, True).astype(BF)
    sib_copy(1).start()
    for part, count in ((0, 2 * rows), (1, keys), (2, keys)):
        at = slice(part * half, (part + 1) * half)
        o.gw_o[:, at] = dot(v.grads[at, :count], v.h1[:count, :]).T.astype(BF)
    own_part = partial_of(core, True)
    sib_copy(1).wait_recv()
    v.sums[...] = own_part + v.sib_in[1].astype(F32)

    def row_sums(values):
        folded = values[:, :128].astype(F32)
        for n in range(1, values.shape[1] // 128):
            folded += values[:, n * 128 : (n + 1) * 128].astype(F32)
        return jnp.sum(folded.T, 0, keepdims=True)

    v.vecs[...] = jnp.zeros_like(v.vecs)
    for at, part in ((QB, v.grads[:half, : 2 * rows]), (VB, v.grads[2 * half :, :])):
        total = row_sums(part)
        for n in range(2):
            v.vecs[at : at + 1, n * half : (n + 1) * half] = jnp.where(core == n, total, 0.0)

    gain = i.vec[LN1G : LN1G + 1, :]
    gain_sum = shift_sum = None
    for at in range(chunks):
        to = slice(at * step, (at + 1) * step)
        side_copy(at).wait_recv()
        e_norm = (v.sums[:, to] + v.side_in[:, to].astype(F32)).T
        unit, inverse = unit_of(i.x[to, :].astype(F32))
        e_unit = e_norm * gain
        result = i.gmid[to, :] + inverse * (
            e_unit - mean_rows(e_unit) - unit * mean_rows(e_unit * unit)
        )
        v.gt[to, :] = result.astype(BF)
        home_start(v.gt.at[to, :], o.gtok_o.at[to, :], at)
        gains = jnp.sum(e_norm * unit, 0, keepdims=True)
        shifts = jnp.sum(e_norm, 0, keepdims=True)
        gain_sum = gains if at == 0 else gain_sum + gains
        shift_sum = shifts if at == 0 else shift_sum + shifts
    v.vecs[LN1G : LN1G + 1, :] = gain_sum
    v.vecs[LN1B : LN1B + 1, :] = shift_sum
    o.vec_o[...] = v.vecs[...]

    for at in range(2):
        sib_copy(at).wait_send()
    for at in range(chunks):
        side_copy(at).wait_send()
        to = slice(at * step, (at + 1) * step)
        home_wait(v.gt.at[to, :], o.gtok_o.at[to, :], at)
    home_wait(i.out_h, o.out_o, 4)


def attention_backward(dims, *args):
    return call(
        backward_kernel, dims, backward_specs(dims), args, collective_id=2, has_side_effects=True,
        vmem_limit_bytes=60 * 2**20,
    )


def final_specs(dims):
    shards, rows, width, heads, _ = dims
    share, half = width // shards, width // 2
    ins = dict(vec=VMEM, sums=[ANY] * 4)
    outs = [(4 * share, width), (share, 4 * width), (share, width), (share, 3 * width)]
    outs += [(1, share)] * IB + [(1, 4 * share)]
    outs = {n: (shape, F32, VMEM) for n, shape in enumerate(outs)}
    shapes = [(2,) + part for part in grad_parts(dims)] + [(heads // 2, 2, share, half)]
    scratch = dict(held=[pltpu.VMEM(shape, BF) for shape in shapes], sem=pltpu.SemaphoreType.DMA((4,)))
    return ins, outs, scratch


def final_kernel(dims, *refs):
    vec, sums, out, held, sem = refs[0], refs[1:5], refs[5:-5], refs[-5:-1], refs[-1]
    copies = [pltpu.make_async_copy(src, dst, sem.at[n]) for n, (src, dst) in enumerate(zip(sums, held))]
    for copy in copies:
        copy.start()
    t_f, t_i, t_o, t_w, *vectors = out
    d_f, d_i, d_o, d_w = held
    half, share = d_f.shape[1], d_i.shape[1]
    width = 2 * half
    for n, result in enumerate(vectors[:-1]):
        result[...] = vec[n : n + 1, :share]
    for r in range(4):
        vectors[-1][:, r * share : (r + 1) * share] = vec[IB + r : IB + r + 1, :share]
    for copy in copies:
        copy.wait()
    for ab in range(2):
        t_f[:, ab * half : (ab + 1) * half] = d_f[ab].astype(F32).T
        t_o[:, ab * half : (ab + 1) * half] = d_o[ab].astype(F32)
        for sub in range(2):
            to = (2 * sub + ab) * width
            t_i[:, to : to + width] = d_i[ab, :, sub * width : (sub + 1) * width].astype(F32)
    for g in range(d_w.shape[0]):
        for core in range(2):
            for part in range(3):
                to = part * width + core * half + g * 128
                t_w[:, to : to + 128] = d_w[g, core, :, part * 128 : (part + 1) * 128].astype(F32)


def on_device(
    tokens, ln1_gain, ln1_shift, w_qkv, q_bias, v_bias, w_out, out_bias, ln2_gain, ln2_shift, w_in, in_bias,
    w_fin, fin_bias, cotangent, lengths, shards,
):
    _, rows, width = tokens.shape
    heads = width // HEAD_DIM // 2
    half = width // 2
    share = width // shards
    gather = shards == 8
    dims = (shards, rows, width, heads, gather)
    core = lax.rem(lax.axis_index("shard"), 2)

    vectors = (ln1_gain, ln1_shift, q_bias, v_bias, out_bias, ln2_gain, ln2_shift, fin_bias, in_bias)
    lanes = 128 if gather else max(128, share)
    packed = jnp.zeros((VROWS, lanes), BF)
    for at, one in enumerate(vectors):
        one = one.reshape(-1, share)
        packed += jnp.pad(one, ((at, VROWS - at - one.shape[0]), (0, lanes - share)))
    numbers = jnp.stack((lengths // 256, lengths % 256)).astype(BF)
    packed += jnp.pad(numbers, ((VECS, VROWS - VECS - 2), (0, lanes - 1)))
    if gather:
        vec, w_here, shares = packed, w_qkv, (w_out, w_in, w_fin)
    else:
        vec = lax.all_gather(packed[:, :share], "shard", axis=1, tiled=True)
        full_w = lax.all_gather(w_qkv, "shard", axis=0, tiled=True)
        w_here = lax.dynamic_index_in_dim(
            full_w.reshape(width, 3, 2, half), core, 2, keepdims=False
        ).reshape(width, 3 * half)
        shares = ()
    (ka, va, kt, qat, ctxt, ctx, h1, wq, x, cot, lens, vecs, inb, *wholes) = attention_forward(
        dims, tokens.reshape(rows, width), cotangent.reshape(rows, width), packed, w_here, vec, *shares
    )
    if gather:
        gtok, output, *sums = middle(
            dims, ctx, x, cot, lens, vecs, inb, *wholes, ka, va, kt, qat, ctxt, h1, wq
        )
        total_wf, total_wi, total_wo, total_w, *vectors = call(
            final_kernel, dims, final_specs(dims), sums, vmem_limit_bytes=60 * 2**20
        )
        vectors = [v.reshape(-1) for v in vectors]
    else:
        wholes = [lax.all_gather(w, "shard", axis=0, tiled=True) for w in (w_out, w_in, w_fin)]
        full_ib = lax.all_gather(in_bias, "shard", axis=0, tiled=True).astype(F32)
        out, ect, gmid, vec_two, grads = feed_plain(ctx, x, cot, length_of(lens), vecs, full_ib, *wholes)
        gtok, output, vec_one, gw = attention_backward(
            dims, ect, ka, va, kt, qat, ctxt, h1, wq, out, x, gmid, vecs
        )

        def total(grad):
            part = lax.psum_scatter(grad, "shard", scatter_dimension=0, tiled=True)
            return lax.psum(part, "seq").astype(F32)

        total_wf, total_wi, total_wo = [total(grad) for grad in grads]
        wide = jnp.zeros((width, 3, 2, half), BF)
        wide = lax.dynamic_update_index_in_dim(wide, gw.reshape(width, 3, half), core, 2)
        total_w = total(wide.reshape(width, 3 * width))
        sums = lax.psum(jnp.concatenate((vec_one[:OB], vec_two)), ("seq", "shard"))
        s = lax.axis_index("shard")
        mine = lax.dynamic_slice_in_dim(sums[:IB], s * share, share, 1)
        vectors = [mine[n] for n in range(IB)]
        vectors.append(lax.dynamic_slice_in_dim(sums[IB:].reshape(-1), s * 4 * share, 4 * share, 0))
    return (
        output.reshape(tokens.shape),
        gtok.reshape(tokens.shape),
        vectors[LN1G],
        vectors[LN1B],
        total_w,
        vectors[QB],
        vectors[VB],
        total_wo,
        vectors[OB],
        vectors[LN2G],
        vectors[LN2B],
        total_wi,
        vectors[IB],
        total_wf,
        vectors[FB],
    )


def solution(mesh):
    vector, matrix, rows = P("shard"), P("shard", None), P("shard", "seq", None)
    return jax.shard_map(
        functools.partial(on_device, shards=mesh.shape["shard"]),
        mesh=mesh,
        in_specs=(
            rows, vector, vector, matrix, vector, vector, matrix, vector, vector, vector, matrix, vector,
            matrix, vector, rows, vector,
        ),
        out_specs=(
            rows, rows, vector, vector, matrix, vector, vector, matrix, vector, vector, vector, matrix,
            vector, matrix, vector,
        ),
        check_vma=False,
    )
```

```python
import functools
import math

import jax
import jax.numpy as jnp
from jax import lax
from jax.experimental import pallas as pl
from jax.experimental.pallas import tpu as pltpu
from jax.sharding import PartitionSpec as P

HEAD_DIM = 64
EPS = 1e-05
GELU_C = 0.7978845608028654
GELU_K = 0.044715
MASKED = -1e30

BF = jnp.bfloat16
F32 = jnp.float32
MESH = pl.DeviceIdType.MESH
VMEM = pl.BlockSpec(memory_space=pltpu.VMEM)
ANY = pl.BlockSpec(memory_space=pl.ANY)

LN1G, LN1B, QB, VB, OB, LN2G, LN2B, FB, IB = range(9)
VECS = 12
VROWS = 16


def dot(left, right):
    return jnp.dot(left, right, preferred_element_type=F32)


def dot_t(left, right):
    return lax.dot_general(left, right, (((1,), (1,)), ((), ())), preferred_element_type=F32)


def mean_rows(values):
    return jnp.mean(values, -1, keepdims=True)


def length_of(packed):
    numbers = packed[VECS : VECS + 2, 0:1].astype(F32)
    return (numbers[0:1] * 256.0 + numbers[1:2]).astype(jnp.int32)


def unit_of(values):
    centred = values - mean_rows(values)
    inverse = lax.rsqrt(mean_rows(centred * centred) + EPS)
    return centred * inverse, inverse


def split3(values):
    high = values.astype(BF)
    rest = values - high.astype(F32)
    mid = rest.astype(BF)
    low = (rest - mid.astype(F32)).astype(BF)
    return high, mid, low


class Place:
    def __init__(self):
        q = lax.axis_index("seq")
        s = lax.axis_index("shard")
        self.q, self.s = q, s
        self.core = core = lax.rem(s, 2)
        self.to = (2 * core + lax.rem(q, 2), s - core + q // 2)
        side = lax.rem(q, 2)
        self.quarter = side + 2 * core
        self.origin = (self.quarter, s - core + q // 2)
        self.stays = q // 2 == core
        self.sibling = (q, s + 1 - 2 * core)
        self.beside = (q + 1 - 2 * side, s)
        self.quarters = [side, side + 2, 1 - side, 3 - side]


def remote(src, dst, send, recv, device):
    return pltpu.make_async_remote_copy(
        src_ref=src, dst_ref=dst, send_sem=send, recv_sem=recv, device_id=device, device_id_type=MESH
    )


class Named:
    def __init__(self, specs, refs):
        refs = iter(refs)
        for name, spec in specs.items():
            setattr(self, name, [next(refs) for _ in spec] if isinstance(spec, list) else next(refs))


def flat(specs):
    return [one for spec in specs.values() for one in (spec if isinstance(spec, list) else [spec])]


def greet(here, devices, mover):
    barrier = pltpu.get_barrier_semaphore()
    for device in devices:
        pl.semaphore_signal(barrier, inc=1, device_id=device, device_id_type=MESH)

    @pl.when(jnp.logical_not(here.stays))
    def _():
        pl.semaphore_signal(barrier, inc=1, device_id=mover, device_id_type=MESH)
        pl.semaphore_wait(barrier, len(devices) + 1)

    @pl.when(here.stays)
    def _():
        pl.semaphore_wait(barrier, len(devices))


def forward_kernel(dims, *refs):
    shards, rows, width, heads, gather = dims
    n_more = 3 if gather else 0
    tok, cot, length_in, w_in, vec_in = refs[:5]
    shares = refs[5 : 5 + n_more]
    refs = refs[5 + n_more :]
    (ka_o, va_o, kt_o, qat_o, ctxt_o, ctx_o, h1_o, wf_o, xown_o, cot_o, len_o, vec_o, inb_o) = refs[:13]
    wholes = refs[13 : 13 + n_more]
    refs = refs[13 + n_more :]
    (
        xs, wf, vg, lens, h1, ka, va, kt, vt, qat, ctxt, ctx, exact,
        perm_s, perm_r, sib_s, sib_r, side_s, side_r, back_s, back_r,
        len_s, len_r, w_s, w_r, out_s, ctx_s, ctx_r, cot_s, cot_r, all_s, all_r, all_l,
    ) = refs
    here = Place()
    core, s = here.core, here.s
    half = width // 2
    share = width // shards
    chunks = 4
    step = rows // chunks
    x_bit, y_bit = lax.rem(s // 2, 2), lax.rem(s // 4, 2)
    shard_x, shard_y = s + 2 - 4 * x_bit, s + 4 - 8 * y_bit
    shard_d = shard_x + 4 - 8 * y_bit
    partner_x, partner_y = (here.q, shard_x), (here.q, shard_y)

    partners = [here.sibling, here.beside] + ([partner_x, partner_y] if gather else [])
    greet(here, partners, here.origin)

    to_core = here.q // 2

    def block(ref, j, i):
        return ref.at[pl.ds(pl.multiple_of(j * rows + i * step, step), step), :]

    def perm_copy(i):
        return remote(
            tok.at[pl.ds(i * step, step), :], block(xs, to_core, i), perm_s.at[i], perm_r.at[i], here.to
        )

    def len_copy():
        return remote(length_in, lens, len_s, len_r, here.to)

    @pl.when(jnp.logical_not(here.stays))
    def _():
        for i in range(chunks):
            perm_copy(i).start()
        len_copy().start()

    @pl.when(here.stays)
    def _():
        for i in range(chunks):
            pltpu.make_async_copy(
                tok.at[pl.ds(i * step, step), :], block(xs, to_core, i), perm_r.at[i]
            ).start()
        pltpu.make_async_copy(length_in, lens, len_r).start()

    w_copies = []
    if gather:
        def columns(j, which):
            return pl.ds(pl.multiple_of(j * width + which * half, 128), half)

        mine = pl.ds(pl.multiple_of(s * share, share), share)
        for j in range(3):
            copy = remote(
                w_in.at[:, columns(j, 1 - core)], wf.at[mine, pl.ds(j * half, half)],
                w_s.at[j], w_r.at[j], here.sibling,
            )
            copy.start()
            w_copies.append(copy)
            copy = pltpu.make_async_copy(
                w_in.at[:, columns(j, core)], wf.at[mine, pl.ds(j * half, half)], w_s.at[4 + j]
            )
            copy.start()
            w_copies.append(copy)
        copy = remote(vec_in, vg.at[s], w_s.at[3], w_r.at[3], here.sibling)
        copy.start()
        w_copies.append(copy)
        copy = pltpu.make_async_copy(vec_in, vg.at[s], w_s.at[7])
        copy.start()
        w_copies.append(copy)
    else:
        copy = pltpu.make_async_copy(w_in, wf, w_s.at[0])
        copy.start()
        w_copies.append(copy)

    def w_move(at):
        src, count, device = (
            (s - core, 2, partner_x),
            (s - core, 2, partner_y),
            (shard_x - core, 1, partner_y),
            (shard_y - core + 1, 1, partner_x),
        )[at]
        part = wf.at[pl.ds(pl.multiple_of(src * share, share), count * share), :]
        return remote(part, part, w_s.at[8 + at], w_r.at[8 + at], device)

    def v_move(at):
        src, device = ((s, partner_x), (s, partner_y), (shard_x, partner_y))[at]
        part = vg.at[pl.ds(src - core, 2)]
        return remote(part, part, w_s.at[12 + at], w_r.at[12 + at], device)

    def receive(i):
        pltpu.make_async_copy(tok.at[pl.ds(i * step, step), :], block(xs, core, i), perm_r.at[i]).wait()
        sib = remote(block(xs, core, i), block(xs, core, i), sib_s.at[i], sib_r.at[i], here.sibling)
        side = remote(block(xs, core, i), block(xs, 2 + core, i), side_s.at[i], side_r.at[i], here.beside)
        side.start()
        sib.start()
        return [sib, side]

    def relay(i):
        block_in = block(xs, 2 + core, i)
        remote(block_in, block_in, side_s.at[i], side_r.at[i], here.beside).wait_recv()
        copy = remote(block_in, block_in, back_s.at[i], back_r.at[i], here.sibling)
        copy.start()
        return copy

    def rows_of(k, shard):
        count = shares[k].shape[0]
        return pl.ds(pl.multiple_of(shard * count, count), count)

    def piece(k, shard, part=None):
        cut = shares[k].shape[1] // 2
        if part is None:
            return wholes[k].at[rows_of(k, shard), :]
        return wholes[k].at[rows_of(k, shard), part * cut : (part + 1) * cut]

    def pass_on(k, slot, src, dst, device):
        return remote(src, dst, all_s.at[k, slot], all_r.at[k, slot], device)

    def got(k, slot, ref):
        pass_on(k, slot, ref, ref, here.sibling).wait_recv()

    def move(k, slot):
        src, device = (
            (None, partner_x),
            (None, partner_y),
            (None, here.sibling),
            ((shard_x, 0), partner_y),
            ((shard_x,), here.sibling),
            ((shard_y, 1), partner_x),
            ((shard_y,), here.sibling),
            ((shard_d,), here.sibling),
        )[slot]
        if src is None:
            return pass_on(k, slot, shares[k], piece(k, s), device)
        return pass_on(k, slot, piece(k, *src), piece(k, *src), device)

    def share_out(k):
        for slot in range(3):
            move(k, slot).start()
        pltpu.make_async_copy(shares[k], piece(k, s), all_l.at[k]).start()

    def from_x(k):
        got(k, 0, piece(k, shard_x))
        move(k, 3).start()
        move(k, 4).start()

    def from_y(k):
        got(k, 1, piece(k, shard_y))
        move(k, 5).start()
        move(k, 6).start()

    def from_far(k):
        got(k, 3, piece(k, shard_d, 0))
        got(k, 5, piece(k, shard_d, 1))
        move(k, 7).start()

    def all_here(k):
        flip = 1 - 2 * core
        for slot, shard in ((2, s), (4, shard_x), (6, shard_y), (7, shard_d)):
            got(k, slot, piece(k, shard + flip))
        pltpu.make_async_copy(shares[k], piece(k, s), all_l.at[k]).wait()

    moved = []
    if gather:
        for copy in w_copies:
            copy.wait()
        for at in range(2):
            w_move(at).start()
            v_move(at).start()
        share_out(0)
        share_out(1)
    moved += receive(0)
    moved += receive(1)
    if gather:
        w_move(0).wait_recv()
        v_move(0).wait_recv()
        w_move(2).start()
        v_move(2).start()
        w_move(1).wait_recv()
        v_move(1).wait_recv()
        w_move(3).start()
    moved += receive(2)
    moved += receive(3)
    if gather:
        share_out(2)

    def cot_copy():
        return remote(cot, cot_o, cot_s, cot_r, here.to)

    @pl.when(jnp.logical_not(here.stays))
    def _():
        cot_copy().start()

    @pl.when(here.stays)
    def _():
        pltpu.make_async_copy(cot, cot_o, cot_r).start()

    def norm_one(first, count):
        def body(i, _):
            at = pl.ds(pl.multiple_of(first + i * 256, 256), 256)
            unit, _ = unit_of(xs[at, :].astype(F32))
            h1[at, :] = (unit * vec_o[LN1G : LN1G + 1, :] + vec_o[LN1B : LN1B + 1, :]).astype(BF)
            return 0

        lax.fori_loop(0, count // 256, body, 0)

    if gather:
        w_move(2).wait_recv()
        w_move(3).wait_recv()
        v_move(2).wait_recv()
        for i in range(shards):
            part = vg[i].astype(F32)
            vec_o[:, i * share : (i + 1) * share] = part[:, :share]
            for r in range(4):
                at = (4 * i + r) * share
                inb_o[:, at : at + share] = jnp.broadcast_to(
                    part[IB + r : IB + r + 1, :share], (8, share)
                )
    else:
        for copy in w_copies:
            copy.wait()
        vec_o[...] = vec_in[...].astype(F32)
        inb_o[...] = jnp.zeros_like(inb_o)

    pltpu.make_async_copy(length_in, lens, len_r).wait()
    length = length_of(lens)
    lane = lax.broadcasted_iota(jnp.int32, (rows, 128), 1)
    row_at = lax.broadcasted_iota(jnp.int32, (rows, 128), 0)
    lower = lane < HEAD_DIM
    ones_rows = (lax.broadcasted_iota(jnp.int32, (16, rows), 0) == 0).astype(BF)
    q_rest = (lax.broadcasted_iota(jnp.int32, (64, 2 * rows), 0) == 3).astype(BF)
    for h in range(heads):
        qat[h, HEAD_DIM:, :] = q_rest

    def bias_half(at):
        full = vec_o[at : at + 1, :]
        return jnp.where(core == 0, full[:, :half], full[:, half:])

    def project(j):
        at = slice(j * rows, (j + 1) * rows)
        norm = h1[at, :]
        dead = jnp.where(here.quarters[j] * rows + row_at < length, 0.0, MASKED)
        k_rest = jnp.where(lane == HEAD_DIM + 3, dead, jnp.where(lane < HEAD_DIM + 3, 1.0, 0.0))
        v_rest = jnp.where(lane < HEAD_DIM + 3, -1.0, 0.0)
        if j < 2:
            q = (dot(norm, wf[:, :half]) + bias_half(QB)).astype(BF) * BF(HEAD_DIM**-0.5)
        k = dot(norm, wf[:, half : 2 * half])
        v = dot(norm, wf[:, 2 * half :]) + bias_half(VB)
        for i in range(heads // 2):
            two = slice(i * 128, (i + 1) * 128)
            kp, vp = k[:, two], v[:, two]
            ka[2 * i, at, :] = jnp.where(lower, kp, k_rest).astype(BF)
            ka[2 * i + 1, at, :] = jnp.where(lower, pltpu.roll(kp, 64, 1), k_rest).astype(BF)
            va[2 * i, at, :] = jnp.where(lower, vp, v_rest).astype(BF)
            va[2 * i + 1, at, :] = jnp.where(lower, pltpu.roll(vp, 64, 1), v_rest).astype(BF)
            turned = kp.astype(BF).T
            kt[2 * i, :, at] = turned[:64]
            kt[2 * i + 1, :, at] = turned[64:]
            turned = vp.astype(BF).T
            vt[2 * i, :64, at] = turned[:64]
            vt[2 * i + 1, :64, at] = turned[64:]
            vt[2 * i, 64:, at] = ones_rows
            vt[2 * i + 1, 64:, at] = ones_rows
            if j < 2:
                turned = q[:, two].T
                qat[2 * i, :64, at] = turned[:64]
                qat[2 * i + 1, :64, at] = turned[64:]

    for i in range(chunks):
        remote(block(xs, core, i), block(xs, 1 - core, i), sib_s.at[i], sib_r.at[i], here.sibling).wait_recv()
    norm_one(0, 2 * rows)
    project(0)
    project(1)
    if gather:
        from_x(0)
        from_y(0)
    relays = [relay(i) for i in range(chunks)]
    for i in range(chunks):
        pl_block = block(xs, 3 - core, i)
        remote(pl_block, pl_block, back_s.at[i], back_r.at[i], here.sibling).wait_recv()
    norm_one(2 * rows, 2 * rows)
    project(2)
    project(3)
    if gather:
        from_x(1)
        from_y(1)

    saves = []
    own = pl.ds(pl.multiple_of(core * rows, rows), rows)
    for at, (src, dst) in enumerate(
        ((ka, ka_o), (va, va_o), (kt, kt_o), (h1, h1_o), (wf, wf_o), (xs.at[own, :], xown_o), (lens, len_o))
    ):
        copy = pltpu.make_async_copy(src, dst, out_s.at[at])
        copy.start()
        saves.append(copy)

    size = 512
    keys = 4 * rows

    def attend(h, _):
        for qb in range(2 * rows // size):
            at = slice(qb * size, (qb + 1) * size)
            query = qat[h, :, at]

            def scores(c):
                return dot(ka[h, c * size : (c + 1) * size, :], query)

            ahead = scores(0)
            highest = total = None
            for c in range(keys // size):
                now = ahead
                if c + 1 < keys // size:
                    ahead = scores(c + 1)
                top = jnp.max(now, axis=0, keepdims=True)
                top = top if highest is None else jnp.maximum(highest, top)
                weights = jnp.exp(now - top).astype(BF)
                part = dot(vt[h, :, c * size : (c + 1) * size], weights)
                total = part if total is None else total * jnp.exp(highest - top) + part
                highest = top
            mass = total[64:65]
            result = total[:64] / mass
            head = pl.ds(pl.multiple_of(h * 64, 64), 64)
            exact[head, at] = result
            ctxt[head, at] = result.astype(BF)
            high, mid, low = split3(-(highest + jnp.log(mass)))
            index = lax.broadcasted_iota(jnp.int32, (16, size), 0)
            rest = jnp.where(index == 3, 1.0, 0.0)
            for r, term in enumerate((high, mid, low)):
                rest = jnp.where(index == r, term.astype(F32), rest)
            qat[h, 64:80, at] = rest.astype(BF)

        if gather:
            @pl.when(h == 0)
            def _():
                from_far(0)

            @pl.when(h == heads // 2)
            def _():
                from_far(1)

        return 0

    lax.fori_loop(0, heads, attend, 0)

    mine = pl.ds(pl.multiple_of(core * half, 128), half)
    own = pl.ds(pl.multiple_of(core * rows, rows), rows)
    other = pl.ds(pl.multiple_of((1 - core) * rows, rows), rows)
    trade = remote(ctxt.at[:, other], ctx.at[mine, :], ctx_s, ctx_r, here.sibling)
    trade.start()
    local = pltpu.make_async_copy(ctxt.at[:, own], ctx.at[mine, :], out_s.at[7])
    local.start()
    for at, (src, dst) in enumerate(((qat, qat_o), (exact, ctxt_o))):
        copy = pltpu.make_async_copy(src, dst, out_s.at[8 + at])
        copy.start()
        saves.append(copy)
    local.wait()
    trade.wait()
    copy = pltpu.make_async_copy(ctx, ctx_o, out_s.at[10])
    copy.start()
    saves.append(copy)
    for copy in saves:
        copy.wait()

    @pl.when(jnp.logical_not(here.stays))
    def _():
        for i in range(chunks):
            perm_copy(i).wait_send()
        len_copy().wait_send()
        cot_copy().wait_send()

    pltpu.make_async_copy(cot, cot_o, cot_r).wait()
    for copy in moved + relays:
        copy.wait_send()
    if gather:
        for k in range(2):
            all_here(k)
            for slot in range(8):
                move(k, slot).wait_send()
        got(2, 0, piece(2, shard_x))
        got(2, 1, piece(2, shard_y))
        got(2, 2, piece(2, s + 1 - 2 * core))
        pltpu.make_async_copy(shares[2], piece(2, s), all_l.at[2]).wait()
        for slot in range(3):
            move(2, slot).wait_send()
        for at in range(4):
            w_move(at).wait_send()
        for at in range(3):
            v_move(at).wait_send()


def attention_forward(dims, tok, cot, length, w, vec, *shares):
    shards, rows, width, heads, gather = dims
    half = width // 2
    keys = 4 * rows
    out = [
        ((heads, keys, 128), BF),
        ((heads, keys, 128), BF),
        ((heads, 64, keys), BF),
        ((heads, 128, 2 * rows), BF),
        ((half, 2 * rows), F32),
        ((width, rows), BF),
        ((keys, width), BF),
        ((width, 3 * half), BF),
        ((rows, width), BF),
        ((rows, width), BF),
        ((VROWS, 128), BF),
        ((VROWS, width), F32),
        ((8, 4 * width), F32),
    ] + [((shards * share.shape[0], share.shape[1]), BF) for share in shares]
    sems = pltpu.SemaphoreType.DMA
    return pl.pallas_call(
        functools.partial(forward_kernel, dims),
        out_shape=tuple(jax.ShapeDtypeStruct(*o) for o in out),
        in_specs=[ANY, ANY, VMEM, ANY, VMEM] + [ANY] * len(shares),
        out_specs=tuple([ANY] * 11 + [VMEM] * 2 + [ANY] * len(shares)),
        scratch_shapes=[
            pltpu.VMEM((keys, width), BF),
            pltpu.VMEM((width, 3 * half), BF),
            pltpu.VMEM((shards, VROWS, 128), BF),
            pltpu.VMEM((VROWS, 128), BF),
            pltpu.VMEM((keys, width), BF),
            pltpu.VMEM((heads, keys, 128), BF),
            pltpu.VMEM((heads, keys, 128), BF),
            pltpu.VMEM((heads, 64, keys), BF),
            pltpu.VMEM((heads, 80, keys), BF),
            pltpu.VMEM((heads, 128, 2 * rows), BF),
            pltpu.VMEM((half, 2 * rows), BF),
            pltpu.VMEM((width, rows), BF),
            pltpu.VMEM((half, 2 * rows), F32),
            sems((4,)), sems((4,)), sems((4,)), sems((4,)), sems((4,)), sems((4,)), sems((4,)), sems((4,)),
            sems, sems, sems((16,)), sems((16,)), sems((12,)), sems, sems,
            sems, sems, sems((3, 8)), sems((3, 8)), sems((3,)),
        ],
        compiler_params=pltpu.CompilerParams(
            collective_id=0, has_side_effects=True, vmem_limit_bytes=56 * 2**20
        ),
        name=forward_kernel.__name__,
    )(tok, cot, length, w, vec, *shares)


IN_PARTS = ((2, ((0, 2),)),)
FAR_HEADS = (
    (0, ((0, 3),)),
    (1, ((2, 1),)),
    (2, ((1, 2),)),
    (3, ((2, 2),)),
    (5, ((0, 4), (1, 3), (2, 3))),
)
NEAR_HEADS = (
    (2, ((2, 4),)),
    (3, ((0, 5), (1, 4), (3, 2))),
    (4, ((3, 3),)),
    (5, ((2, 5), (4, 2))),
)
TAIL = (
    ((4, 3), (3, 4), (5, 2)),
    ((1, 5), (5, 3), (4, 4), (3, 5)),
    ((5, 4), (4, 5), (3, 6), (0, 6), (2, 6)),
    ((1, 6), (5, 5), (4, 6), (5, 6)),
)


class Links:
    def __init__(self, here):
        s, q = here.s, here.q
        self.x, self.y = lax.rem(s // 2, 2), lax.rem(s // 4, 2)
        self.to_x = (q, s + 2 - 4 * self.x)
        self.to_y = (q, s + 4 - 8 * self.y)
        self.inner = (q == 1) | (q == 2)
        self.to_inner = (3 - q, s)


class Reduction:
    def __init__(self, here, links, refs, mine, first_hops=None, core=None):
        self.got, self.last, self.seq_in, self.inner_in, self.done, self.send, self.recv = refs
        self.here, self.links, self.mine = here, links, mine
        self.first_hops, self.core = first_hops, core
        self.own = mine.at[links.y, links.x]

    @staticmethod
    def scratch(r, c):
        sems = pltpu.SemaphoreType.DMA
        return [pltpu.VMEM((2, 2, r, c), BF)] + [pltpu.VMEM((2, r, c), BF)] * 4 + [sems((11,)), sems((11,))]

    def copy(self, at):
        here, links, mine, own = self.here, self.links, self.mine, self.own
        x, y = links.x, links.y
        src, dst, device = (
            lambda: self.core + (here.sibling,),
            lambda: (mine.at[:, 1 - x, 0], self.got.at[0], links.to_x),
            lambda: (mine.at[1 - y, :, 1], self.got.at[1], links.to_y),
            lambda: (mine.at[1 - y, x, 0], self.last.at[0], links.to_y),
            lambda: (mine.at[y, 1 - x, 1], self.last.at[1], links.to_x),
        )[at]()
        return remote(src, dst, self.send.at[at], self.recv.at[at], device)

    def along(self, hop, ab):
        src, dst, device = (
            (self.own, self.seq_in, self.here.beside),
            (self.own, self.inner_in, self.links.to_inner),
            (self.done, self.done, self.here.beside),
        )[hop]
        at = 5 + 2 * hop + ab
        return remote(src.at[ab], dst.at[ab], self.send.at[at], self.recv.at[at], device)

    def add(self, left, right, out=None):
        r = left.shape[-2]
        step = 96 if left.shape[-1] > 512 else r
        out = left if out is None else out

        def body(n, _):
            at = pl.ds(pl.multiple_of(n * step, step), step)
            out[at, :] = left[at, :] + right[at, :]
            return 0

        lax.fori_loop(0, r // step, body, 0)

    def phase(self, number):
        links, mine = self.links, self.mine
        x, y, outer = links.x, links.y, jnp.logical_not(links.inner)
        if number == 1:
            if self.core is not None:
                self.copy(0).wait_recv()
                for j in range(2):
                    for i in range(2):
                        for ab in range(2):
                            self.add(mine.at[j, i, ab], self.core[1].at[j, i, ab])
            self.copy(1).start()
            self.copy(2).start()
        elif number == 2:
            for copy in self.first_hops or (self.copy(1), self.copy(2)):
                copy.wait_recv()
            for i in range(2):
                self.add(mine.at[i, x, 0], self.got.at[0, i])
                self.add(mine.at[y, i, 1], self.got.at[1, i])
            self.copy(3).start()
            self.copy(4).start()
        elif number == 3:
            self.copy(3).wait_recv()
            self.copy(4).wait_recv()
            for ab in range(2):
                self.add(self.own.at[ab], self.last.at[ab])
                pl.when(outer)(lambda: self.along(0, ab).start())
        elif number == 4:
            @pl.when(links.inner)
            def _():
                for ab in range(2):
                    self.along(0, ab).wait_recv()
                    self.add(self.own.at[ab], self.seq_in.at[ab])
                    self.along(1, ab).start()
        elif number == 5:
            @pl.when(links.inner)
            def _():
                for ab in range(2):
                    self.along(1, ab).wait_recv()
                    self.add(self.own.at[ab], self.inner_in.at[ab], self.done.at[ab])
                    self.along(2, ab).start()
        else:
            @pl.when(outer)
            def _():
                for ab in range(2):
                    self.along(2, ab).wait_recv()

    def finish(self):
        if self.core is not None:
            self.copy(0).wait_send()
        for copy in self.first_hops or (self.copy(1), self.copy(2)):
            copy.wait_send()
        self.copy(3).wait_send()
        self.copy(4).wait_send()

        @pl.when(jnp.logical_not(self.links.inner))
        def _():
            for ab in range(2):
                self.along(0, ab).wait_send()

        @pl.when(self.links.inner)
        def _():
            for ab in range(2):
                self.along(1, ab).wait_send()
                self.along(2, ab).wait_send()


class FirstHop:
    def __init__(self, make, sends=None, receives=None):
        self.make, self.sends, self.receives = make, sends, receives

    @staticmethod
    def on(condition, action):
        if condition is None:
            action()
        else:
            pl.when(condition)(action)

    def start(self):
        self.on(self.sends, lambda: self.make().start())

    def wait_send(self):
        self.on(self.sends, lambda: self.make().wait_send())

    def wait_recv(self):
        self.on(self.receives, lambda: self.make().wait_recv())


def grad_parts(dims):
    shards, rows, width, heads, _ = dims
    share, half = width // shards, width // 2
    return (half, 4 * share), (share, 2 * width), (share, half)


def middle_specs(dims):
    shards, rows, width, heads, _ = dims
    half, keys, share = width // 2, 4 * rows, width // shards
    groups = heads // 2
    sems = pltpu.SemaphoreType.DMA
    part_f, part_i, part_o = grad_parts(dims)
    ins = dict(ctx=VMEM, x=VMEM, cot=VMEM, lens=VMEM, vec=VMEM, inb=VMEM)
    ins |= dict(wo_h=ANY, wi_h=ANY, wf_h=ANY, ka_h=ANY, va_h=ANY, kt_h=ANY, qat_h=ANY, ctxt_h=ANY, h1_h=ANY, wq_h=ANY)
    outs = dict(
        gtok_o=((rows, width), BF, ANY),
        out_o=((rows, width), BF, ANY),
        vec_o=((VROWS, 128), F32, VMEM),
        sum_f=((2,) + part_f, BF, ANY),
        sum_i=((2,) + part_i, BF, ANY),
        sum_o=((2,) + part_o, BF, ANY),
        sum_w=((groups, 2, share, half), BF, ANY),
        far_f=((4 * width, width), BF, ANY),
    )
    scratch = dict(
        sum_refs=sum((Reduction.scratch(*part) for part in (part_f, part_i, part_o)), [])
        + Reduction.scratch(share, half) * groups,
        mine_w=[pltpu.VMEM((2, 2, 2, share, half), BF)] * groups,
        near_f=pltpu.VMEM((2, 2, 2) + part_f, BF),
        near_i=pltpu.VMEM((2, 2, 2) + part_i, BF),
        near_o=pltpu.VMEM((2, 2, 2) + part_o, BF),
        mine_f=pltpu.VMEM((2, 2, 2) + part_f, BF),
        mine_i=pltpu.VMEM((2, 2, 2) + part_i, BF),
        both_o=pltpu.VMEM((2, 2, 2, 2) + part_o, BF),
        gmid=pltpu.VMEM((rows, width), F32),
        vecs=pltpu.VMEM((VROWS, width), F32),
        gib=pltpu.VMEM((8, 4 * width), F32),
        gt=pltpu.VMEM((rows, width), BF),
        e_ctx=pltpu.VMEM((half, 2 * rows), BF),
        sib_in=pltpu.VMEM((2, width, rows), BF),
        side_in=pltpu.VMEM((width, rows), BF),
        vec_out=pltpu.VMEM((shards, VROWS, 128), F32),
        vec_in=pltpu.VMEM((shards, VROWS, 128), F32),
        vec_all=pltpu.VMEM((4, VROWS, 128), F32),
        w_in=pltpu.VMEM((groups, share, half), BF),
        core_sf=sems((4,)),
        core_rf=sems((4,)),
        core_si=sems((4,)),
        core_ri=sems((4,)),
        x_sf=sems((4,)),
        x_rf=sems((4,)),
        y_sf=sems((4,)),
        y_rf=sems((4,)),
        x_si=sems((4,)),
        x_ri=sems((4,)),
        y_si=sems((4,)),
        y_ri=sems((4,)),
        far_s=sems((8,)),
        far_r=sems((8,)),
        load_s=sems((9,)),
        head_s=sems((2, 4)),
        trade_s=sems((2,)),
        trade_r=sems,
        sib_s=sems((2,)),
        sib_r=sems((2,)),
        side_s=sems((4,)),
        side_r=sems((4,)),
        perm_s=sems((5,)),
        perm_r=sems((5,)),
        vec_s=sems((shards + 4,)),
        vec_r=sems((shards + 4,)),
        w_s=sems((groups,)),
        w_r=sems((groups,)),
        final_s=sems((3 + 2 * groups,)),
    )
    feed = dict(
        wo=pltpu.VMEM((width, width), BF),
        wi=pltpu.VMEM((2, width, width), BF),
        wf=pltpu.VMEM((2, width, width), BF),
        mid=pltpu.VMEM((rows, width), F32),
        h2=pltpu.VMEM((rows, width), BF),
        h2t=pltpu.VMEM((width + 16, rows), BF),
        eo=pltpu.VMEM((rows, width), BF),
        active=pltpu.VMEM((4, rows, width), BF),
        slope=pltpu.VMEM((4, rows, width), BF),
    )
    attend = dict(
        ka=pltpu.VMEM((2, 2 * rows, 128), BF),
        va=pltpu.VMEM((2, 2 * rows, 128), BF),
        kt=pltpu.VMEM((2, 64, 2 * rows), BF),
        qat=pltpu.VMEM((2, 128, 2 * rows), BF),
        h1=pltpu.VMEM((keys, width), BF),
        wq=pltpu.VMEM((width, 3 * half), BF),
        eat=pltpu.VMEM((heads, 128, 2 * rows), BF),
        grads=pltpu.VMEM((3 * half, keys), BF),
        sums=pltpu.VMEM((width, rows), F32),
        sib_out=pltpu.VMEM((2, width, rows), BF),
        side_out=pltpu.VMEM((width, rows), BF),
    )
    return ins, outs, scratch, feed, attend


def middle_kernel(dims, *refs):
    shards, rows, width, heads, _ = dims
    ins, outs, scratch, feed, attend = middle_specs(dims)
    at_ins, at_outs = len(ins), len(ins) + len(outs)
    i = Named(ins, refs[:at_ins])
    o = Named(outs, refs[at_ins:at_outs])
    v = Named(scratch, refs[at_outs:])
    here = Place()
    links = Links(here)
    core, x, y = here.core, links.x, links.y
    half, keys, share, size = width // 2, 4 * rows, width // shards, width
    groups, parts, chunks = heads // 2, 4, 4
    step = rows // chunks

    in_plane = [(here.q, lax.rem(here.s + n, shards)) for n in range(1, shards)]
    along = [(lax.rem(here.q + n, 4), here.s) for n in range(1, 4)]
    greet(here, in_plane + along, here.to)

    flip = 1 - 2 * core
    shard_x, shard_y = here.s + 2 - 4 * x, here.s + 4 - 8 * y
    shard_d = shard_x + 4 - 8 * y

    def share_of(ref, shard, part=None):
        count = 4 * share
        rows_of = pl.ds(pl.multiple_of(shard * count, count), count)
        return ref.at[rows_of, :] if part is None else ref.at[rows_of, part * half : (part + 1) * half]

    def far_move(at):
        shard, part, device = (
            (shard_x, 0, links.to_y),
            (shard_y, 1, links.to_x),
            (shard_x, None, here.sibling),
            (shard_y, None, here.sibling),
            (shard_d, None, here.sibling),
        )[at]
        src = share_of(o.far_f if at == 4 else i.wf_h, shard, part)
        return remote(src, share_of(o.far_f, shard, part), v.far_s.at[at], v.far_r.at[at], device)

    def far_came(at):
        shard, part = ((shard_d, 0), (shard_d, 1), (shard_x + flip, None), (shard_y + flip, None), (shard_d + flip, None))[at]
        ref = share_of(o.far_f, shard, part)
        remote(ref, ref, v.far_s.at[at], v.far_r.at[at], here.sibling).wait_recv()

    for at in range(4):
        far_move(at).start()

    def chip_of(k):
        return (1 - y if k // 2 else y), (1 - x if k % 2 else x)

    def columns(k):
        return pl.ds(pl.multiple_of(chip_of(k)[0] * size, size), size)

    def x_f(k):
        cy, cx = chip_of(k)
        return remote(v.mine_f.at[cy, cx, 0], v.got_f.at[0, cy], v.x_sf.at[k], v.x_rf.at[k], links.to_x)

    def y_f(k):
        cy, cx = chip_of(k)
        return remote(v.mine_f.at[cy, cx, 1], v.got_f.at[1, cx], v.y_sf.at[k], v.y_rf.at[k], links.to_y)

    def x_i(k):
        to = columns(k)
        return remote(
            v.mine_i.at[:, 1 - x, 0, :, to], v.got_i.at[0, :, :, to], v.x_si.at[k], v.x_ri.at[k], links.to_x
        )

    def y_i(k):
        to = columns(k)
        return remote(
            v.mine_i.at[1 - y, :, 1, :, to], v.got_i.at[1, :, :, to], v.y_si.at[k], v.y_ri.at[k], links.to_y
        )

    refs = [v.sum_refs[7 * n : 7 * n + 7] for n in range(3 + groups)]
    v.got_f, v.got_i = refs[0][0], refs[1][0]
    hops_f, hops_i = [], []
    for k in range(parts):
        cx = chip_of(k)[1]
        hops_f.append(([FirstHop(functools.partial(x_f, k))] if k % 2 else []) + ([FirstHop(functools.partial(y_f, k))] if k // 2 else []))
        hops_i.append(
            [FirstHop(functools.partial(x_i, k), cx == 0, cx == 1), FirstHop(functools.partial(y_i, k), cx == 1, cx == 1)]
        )
    sums = [
        Reduction(here, links, refs[0], v.mine_f, sum(hops_f, [])),
        Reduction(here, links, refs[1], v.mine_i, sum(hops_i, [])),
        Reduction(here, links, refs[2], v.both_o.at[core], None, (v.both_o.at[1 - core], v.near_o)),
    ]
    sums += [Reduction(here, links, refs[3 + g], v.mine_w[g]) for g in range(groups)]

    def run(*steps):
        for which, number in steps:
            sums[which].phase(number)

    def home(src, dst, at):
        return remote(src, dst, v.perm_s.at[at], v.perm_r.at[at], here.origin)

    def home_start(src, dst, at):
        @pl.when(jnp.logical_not(here.stays))
        def _():
            home(src, dst, at).start()

        @pl.when(here.stays)
        def _():
            pltpu.make_async_copy(src, dst, v.perm_s.at[at]).start()

    def home_sent(src, dst, at):
        @pl.when(jnp.logical_not(here.stays))
        def _():
            home(src, dst, at).wait_send()

        @pl.when(here.stays)
        def _():
            pltpu.make_async_copy(src, dst, v.perm_s.at[at]).wait()

    def home_came(src, dst, at):
        @pl.when(jnp.logical_not(here.stays))
        def _():
            home(src, dst, at).wait_recv()

    def vector(at):
        return i.vec[at : at + 1, :]

    def feed_part(*buffers):
        b = Named(feed, buffers)

        load_o = pltpu.make_async_copy(i.wo_h, b.wo, v.load_s.at[0])
        load_o.start()

        def load_i(k):
            cy, cx = chip_of(k)
            to = pl.ds(pl.multiple_of((2 * cy + cx) * size, size), size)
            return pltpu.make_async_copy(i.wi_h.at[:, to], b.wi.at[k % 2], v.load_s.at[1 + k % 2])

        def load_f(k):
            shard = (here.s, shard_x, shard_y, shard_d)[k]
            count = 4 * share
            return [
                pltpu.make_async_copy(
                    share_of(o.far_f if n or k == 3 else i.wf_h, each) if k else share_of(i.wf_h, each),
                    b.wf.at[k % 2, pl.ds(pl.multiple_of(lax.rem(each, 2) * count, count), count), :],
                    v.load_s.at[3 + 2 * (k % 2) + n],
                )
                for n, each in enumerate((shard, shard + flip))
            ]

        load_i(3).start()
        load_i(2).start()
        for copy in load_f(0):
            copy.start()

        row_at = lax.broadcasted_iota(jnp.int32, (rows, 1), 0) + here.quarter * rows
        live = row_at < length_of(i.lens)
        e_outer = jnp.where(live, i.cot[...].astype(F32), 0.0)
        b.eo[...] = e_outer.astype(BF)
        v.vecs[...] = jnp.zeros_like(v.vecs)
        v.vecs[FB : FB + 1, :] = jnp.sum(e_outer, 0, keepdims=True)

        load_o.wait()
        middle = i.x[...].astype(F32) + dot(i.ctx[...].T, b.wo[...]) + vector(OB)
        b.mid[...] = middle
        unit, _ = unit_of(middle)
        b.h2[...] = (unit * vector(LN2G) + vector(LN2B)).astype(BF)
        b.h2t[:width, :] = b.h2[...].T
        b.h2t[width:, :] = jnp.ones((16, rows), BF)

        def hidden_part(eot, both_f):
            def near_f(k):
                cy, cx = chip_of(k)
                return remote(
                    both_f.at[k % 2, 1 - core], v.near_f.at[cy, cx], v.core_sf.at[k], v.core_rf.at[k], here.sibling
                )

            def send_f(k):
                cy, cx = chip_of(k)
                near_f(k).wait_recv()
                for ab in range(2):
                    v.mine_f[cy, cx, ab] = both_f[k % 2, core, ab] + v.near_f[cy, cx, ab]
                for hop in hops_f[k]:
                    hop.start()

            eot[...] = b.eo[...].T
            order = (3, 2, 1, 0)
            for n, k in enumerate(order):
                cy, cx = chip_of(k)
                at = pl.ds(pl.multiple_of((2 * cy + cx) * size, size), size)
                load_i(k).wait()
                inner = dot(b.h2[...], b.wi[k % 2]) + i.inb[0:1, at]
                if n + 2 < parts:
                    load_i(order[n + 2]).start()
                square = inner * inner
                swing = jnp.tanh(GELU_C * inner * (1.0 + GELU_K * square))
                active = (0.5 * inner * (1.0 + swing)).astype(BF)
                b.active[k] = active
                b.slope[k] = (
                    0.5 * (1.0 + swing)
                    + 0.5 * inner * (1.0 - swing * swing) * (GELU_C * (1.0 + 3.0 * GELU_K * square))
                ).astype(BF)
                grad = dot(eot[...], active).astype(BF)
                if n >= 2:
                    near_f(order[n - 2]).wait_send()
                for c in range(2):
                    for ab in range(2):
                        both_f[k % 2, c, ab] = grad[ab * half : (ab + 1) * half, c * half : (c + 1) * half]
                near_f(k).start()
                if n > 0:
                    send_f(order[n - 1])
            load_i(0).start()
            load_i(1).start()
            send_f(order[-1])
            for k in order[-2:]:
                near_f(k).wait_send()

        part_f = grad_parts(dims)[0]
        pl.run_scoped(hidden_part, pltpu.VMEM((width, rows), BF), pltpu.VMEM((2, 2, 2) + part_f, BF))

        def back_part(gh2, acc, ect, both_i):
            def near_i(k):
                return remote(
                    both_i.at[k % 2, 1 - core], v.near_i.at[:, :, chip_of(k)[1], :, columns(k)], v.core_si.at[k],
                    v.core_ri.at[k], here.sibling,
                )

            def send_i(k):
                (cy, cx), to = chip_of(k), columns(k)
                near_i(k).wait_recv()
                for n in range(4):
                    v.mine_i[n // 2, n % 2, cx, :, to] = (
                        both_i[k % 2, core, n // 2, n % 2] + v.near_i[n // 2, n % 2, cx, :, to]
                    )
                for hop in hops_i[k]:
                    hop.start()

            acc[...] = b.mid[...] + vector(FB)
            for k in range(parts):
                cy, cx = chip_of(k)
                at = pl.ds(pl.multiple_of((2 * cy + cx) * size, size), size)
                load_i(k).wait()
                for copy in load_f(k):
                    copy.wait()
                if k == 0:
                    far_came(2)
                    far_came(3)
                if k == 1:
                    far_came(0)
                    far_came(1)
                    far_move(4).start()
                if k == 2:
                    far_came(4)
                if k + 1 < parts:
                    for copy in load_f(k + 1):
                        copy.start()
                wic, wfc = b.wi[k % 2], b.wf[k % 2]
                e_inner = (dot_t(b.eo[...], wfc) * b.slope[k].astype(F32)).astype(BF)
                grad = dot(b.h2t[...], e_inner)
                v.gib[:, at] = grad[width : width + 8]
                if k >= 2:
                    near_i(k - 2).wait_send()
                for c in range(2):
                    for n in range(4):
                        to = (2 * n + c) * share
                        both_i[k % 2, c, n // 2, n % 2] = grad[to : to + share].astype(BF)
                near_i(k).start()
                acc[...] += dot(b.active[k], wfc)
                part = dot_t(e_inner, wic)
                gh2[...] = part if k == 0 else gh2[...] + part
                if k + 2 < parts:
                    load_i(k + 2).start()
                if k > 0:
                    send_i(k - 1)
                for when, steps in IN_PARTS:
                    if when == k:
                        run(*steps)
            v.gt[...] = acc[...].astype(BF)
            home_start(v.gt, o.out_o, 4)
            unit, inverse = unit_of(b.mid[...])
            e_norm = gh2[...]
            v.vecs[LN2G : LN2G + 1, :] = jnp.sum(e_norm * unit, 0, keepdims=True)
            v.vecs[LN2B : LN2B + 1, :] = jnp.sum(e_norm, 0, keepdims=True)
            e_unit = e_norm * vector(LN2G)
            grad_mid = jnp.where(live, i.cot[...].astype(F32), 0.0) + inverse * (
                e_unit - mean_rows(e_unit) - unit * mean_rows(e_unit * unit)
            )
            v.gmid[...] = grad_mid
            e_branch = grad_mid.astype(BF)
            v.vecs[OB : OB + 1, :] = jnp.sum(e_branch.astype(F32), 0, keepdims=True)
            ect[...] = dot_t(b.wo[...], e_branch).astype(BF)
            mine = pl.ds(pl.multiple_of(core * half, 128), half)
            theirs = pl.ds(pl.multiple_of((1 - core) * half, 128), half)
            own = pl.ds(pl.multiple_of(core * rows, rows), rows)
            trade = remote(ect.at[theirs, :], v.e_ctx.at[:, own], v.trade_s.at[0], v.trade_r, here.sibling)
            trade.start()
            local = pltpu.make_async_copy(ect.at[mine, :], v.e_ctx.at[:, own], v.trade_s.at[1])
            local.start()
            send_i(parts - 1)
            grads = dot(i.ctx[...], e_branch).astype(BF)
            for n in range(shards):
                for ab in range(2):
                    v.both_o[n % 2, n // 4, n // 2 % 2, ab] = grads[
                        n * share : (n + 1) * share, ab * half : (ab + 1) * half
                    ]
            sums[2].copy(0).start()
            local.wait()
            trade.wait()
            for k in range(2, parts):
                near_i(k).wait_send()

        pl.run_scoped(
            back_part,
            pltpu.VMEM((rows, width), F32),
            pltpu.VMEM((rows, width), F32),
            pltpu.VMEM((width, rows), BF),
            pltpu.VMEM((2, 2, 2, 2, share, width), BF),
        )
        for at in range(5):
            far_move(at).wait_send()

    pl.run_scoped(feed_part, *flat(feed))

    def attend_part(*buffers):
        b = Named(attend, buffers)

        def fetch(far, h, slot):
            rows_of = slice(2 * rows, keys) if far else slice(0, 2 * rows)
            return [
                pltpu.make_async_copy(src, dst, v.head_s.at[slot, n])
                for n, (src, dst) in enumerate(
                    (
                        (i.qat_h.at[h], b.qat.at[slot]),
                        (i.ka_h.at[h, rows_of, :], b.ka.at[slot]),
                        (i.va_h.at[h, rows_of, :], b.va.at[slot]),
                        (i.kt_h.at[h, :, rows_of], b.kt.at[slot]),
                    )
                )
            ]

        for copy in fetch(True, 0, 0):
            copy.start()

        def with_delta(ctxt, sem):
            load = pltpu.make_async_copy(i.ctxt_h, ctxt, sem)
            load.start()
            load.wait()
            index = lax.broadcasted_iota(jnp.int32, (16, 2 * rows), 0)
            for h in range(heads):
                at = slice(h * 64, (h + 1) * 64)
                e_ctx = v.e_ctx[at, :]
                delta = jnp.sum(e_ctx.astype(F32) * ctxt[at, :], 0, keepdims=True)
                rest = jnp.zeros((16, 2 * rows), F32)
                for r, term in enumerate(split3(delta)):
                    rest = jnp.where(index == r, term.astype(F32), rest)
                b.eat[h, :64, :] = e_ctx
                b.eat[h, 64:80, :] = rest.astype(BF)
                b.eat[h, 80:, :] = jnp.zeros((48, 2 * rows), BF)

        pl.run_scoped(with_delta, pltpu.VMEM((half, 2 * rows), F32), pltpu.SemaphoreType.DMA)
        loads = [
            pltpu.make_async_copy(i.wq_h, b.wq, v.load_s.at[7]),
            pltpu.make_async_copy(i.h1_h, b.h1, v.load_s.at[8]),
        ]
        for copy in loads:
            copy.start()
        block = 256

        def attend_half(far, polls):
            first = 2 * rows if far else 0

            def body(h, _):
                slot = lax.rem(h, 2)
                for copy in fetch(far, h, slot):
                    copy.wait()

                @pl.when(h < heads - 1)
                def _():
                    for copy in fetch(far, h + 1, 1 - slot):
                        copy.start()

                if far:
                    @pl.when(h == heads - 1)
                    def _():
                        for copy in fetch(False, 0, 1 - slot):
                            copy.start()

                query, e_ctx = b.qat[slot], b.eat[h]
                e_query = None
                for c in range(2 * rows // block):
                    of = slice(c * block, (c + 1) * block)
                    to = slice(first + c * block, first + (c + 1) * block)
                    weights = jnp.exp(dot(b.ka[slot, of, :], query))
                    e_scores = (weights * dot(b.va[slot, of, :], e_ctx)).astype(BF)
                    e_value = dot_t(e_ctx[:64], weights.astype(BF))
                    e_key = dot_t(query[:64], e_scores)
                    part = dot(b.kt[slot, :, of], e_scores)
                    e_query = part if e_query is None else e_query + part
                    b.grads[pl.ds(pl.multiple_of(half + h * 64, 64), 64), to] = e_key.astype(BF)
                    b.grads[pl.ds(pl.multiple_of(2 * half + h * 64, 64), 64), to] = e_value.astype(BF)
                head = pl.ds(pl.multiple_of(h * 64, 64), 64)
                lower = pl.ds(pl.multiple_of(half + h * 64, 64), 64)
                if far:
                    b.sums[head, :] = e_query[:, :rows]
                    b.sums[lower, :] = e_query[:, rows:]
                else:
                    b.grads[head, :rows] = ((b.sums[head, :] + e_query[:, :rows]) * HEAD_DIM**-0.5).astype(BF)
                    b.grads[head, rows : 2 * rows] = (
                        (b.sums[lower, :] + e_query[:, rows:]) * HEAD_DIM**-0.5
                    ).astype(BF)
                for when, action in polls:
                    pl.when(h == when)(action)
                return 0

            lax.fori_loop(0, heads, body, 0)

        def steps_of(table):
            return [(when, functools.partial(run, *steps)) for when, steps in table]

        def partial_of(j, near):
            at = pl.ds(pl.multiple_of(j * rows, rows), rows)
            if near:
                return dot(b.wq[...], b.grads[:, at])
            return dot(b.wq[:, half:], b.grads[half:, at])

        def sib_copy(at):
            return remote(b.sib_out.at[at], v.sib_in.at[at], v.sib_s.at[at], v.sib_r.at[at], here.sibling)

        def side_copy(at):
            to = slice(at * step, (at + 1) * step)
            return remote(
                b.side_out.at[:, to], v.side_in.at[:, to], v.side_s.at[at], v.side_r.at[at], here.beside
            )

        def to_side():
            sib_copy(0).wait_recv()
            b.side_out[...] = (partial_of(2 + core, False) + v.sib_in[0].astype(F32)).astype(BF)
            for at in range(chunks):
                side_copy(at).start()

        def weight_grad(g):
            for part, count in ((0, 2 * rows), (1, keys), (2, keys)):
                at = part * half + g * 128
                result = dot(b.grads[at : at + 128, :count], b.h1[:count, :]).T.astype(BF)
                to = slice(part * 128, (part + 1) * 128)
                for j in range(shards):
                    sums[3 + g].mine[j // 4, j // 2 % 2, j % 2, :, to] = result[j * share : (j + 1) * share]
            run((3 + g, 1))

        attend_half(True, steps_of(FAR_HEADS))
        for copy in loads:
            copy.wait()
        b.sib_out[0] = partial_of(3 - core, False).astype(BF)
        sib_copy(0).start()
        attend_half(
            False,
            [(0, to_side)]
            + [(2 * g + 1, functools.partial(weight_grad, g)) for g in range(groups - 1)]
            + steps_of(NEAR_HEADS),
        )
        b.sib_out[1] = partial_of(1 - core, True).astype(BF)
        sib_copy(1).start()
        weight_grad(groups - 1)
        own_part = partial_of(core, True)
        home_sent(v.gt, o.out_o, 4)
        sib_copy(1).wait_recv()
        b.sums[...] = own_part + v.sib_in[1].astype(F32)
        run(*TAIL[0])

        gain = vector(LN1G)
        gain_sum = shift_sum = None
        for at in range(chunks):
            to = slice(at * step, (at + 1) * step)
            side_copy(at).wait_recv()
            e_norm = (b.sums[:, to] + v.side_in[:, to].astype(F32)).T
            unit, inverse = unit_of(i.x[to, :].astype(F32))
            e_unit = e_norm * gain
            result = v.gmid[to, :] + inverse * (
                e_unit - mean_rows(e_unit) - unit * mean_rows(e_unit * unit)
            )
            v.gt[to, :] = result.astype(BF)
            home_start(v.gt.at[to, :], o.gtok_o.at[to, :], at)
            gains = jnp.sum(e_norm * unit, 0, keepdims=True)
            shifts = jnp.sum(e_norm, 0, keepdims=True)
            gain_sum = gains if at == 0 else gain_sum + gains
            shift_sum = shifts if at == 0 else shift_sum + shifts
        v.vecs[LN1G : LN1G + 1, :] = gain_sum
        v.vecs[LN1B : LN1B + 1, :] = shift_sum

        def row_sums(values):
            folded = values[:, :128].astype(F32)
            for n in range(1, values.shape[1] // 128):
                folded += values[:, n * 128 : (n + 1) * 128].astype(F32)
            return jnp.sum(folded.T, 0, keepdims=True)

        for at, part in ((QB, b.grads[:half, : 2 * rows]), (VB, b.grads[2 * half :, :])):
            total = row_sums(part)
            for n in range(2):
                v.vecs[at : at + 1, n * half : (n + 1) * half] = jnp.where(core == n, total, 0.0)

        for n in range(shards):
            v.vec_out[n, :, :share] = v.vecs[:, n * share : (n + 1) * share]
            for r in range(4):
                to = (4 * n + r) * share
                v.vec_out[n, IB + r : IB + r + 1, :share] = v.gib[0:1, to : to + share]

        def vec_plane(n):
            to = lax.rem(here.s + n, shards)
            return remote(
                v.vec_out.at[to], v.vec_in.at[here.s], v.vec_s.at[n], v.vec_r.at[n], (here.q, to)
            )

        def vec_along(n):
            to, at = lax.rem(here.q + n, 4), shards + n
            return remote(
                v.vec_all.at[here.q], v.vec_all.at[here.q], v.vec_s.at[at], v.vec_r.at[at], (to, here.s)
            )

        for n in range(1, shards):
            vec_plane(n).start()
        v.vec_in[here.s] = v.vec_out[here.s]
        run(*TAIL[1])
        for n in range(1, shards):
            vec_plane(n).wait_recv()
        total = v.vec_in[0]
        for n in range(1, shards):
            total += v.vec_in[n]
        v.vec_all[here.q] = total
        for n in range(1, 4):
            vec_along(n).start()
        run(*TAIL[2])
        for n in range(1, 4):
            vec_along(n).wait_recv()
        o.vec_o[...] = (v.vec_all[0] + v.vec_all[1]) + (v.vec_all[2] + v.vec_all[3])
        run(*TAIL[3])
        finals = []

        def final(src, dst, at):
            copy = pltpu.make_async_copy(src, dst, v.final_s.at[at])
            copy.start()
            finals.append(copy)

        def w_trade(g):
            return remote(sums[3 + g].done.at[1 - core], v.w_in.at[g], v.w_s.at[g], v.w_r.at[g], here.sibling)

        for g in range(groups):
            w_trade(g).start()
        for n, dst in enumerate((o.sum_f, o.sum_i, o.sum_o)):
            final(sums[n].done, dst, n)
        for g in range(groups):
            final(sums[3 + g].done.at[core], o.sum_w.at[g, core], 3 + 2 * g)
            w_trade(g).wait()
            final(v.w_in.at[g], o.sum_w.at[g, 1 - core], 4 + 2 * g)
        for copy in finals:
            copy.wait()
        for each in sums:
            each.finish()
        for n in range(1, shards):
            vec_plane(n).wait_send()
        for n in range(1, 4):
            vec_along(n).wait_send()
        for at in range(2):
            sib_copy(at).wait_send()
        for at in range(chunks):
            side_copy(at).wait_send()
            to = slice(at * step, (at + 1) * step)
            home_sent(v.gt.at[to, :], o.gtok_o.at[to, :], at)
            home_came(v.gt.at[to, :], o.gtok_o.at[to, :], at)
        home_came(v.gt, o.out_o, 4)

    pl.run_scoped(attend_part, *flat(attend))


def call(kernel, dims, specs, args, **params):
    ins, outs, scratch = specs[:3]
    return pl.pallas_call(
        functools.partial(kernel, dims),
        out_shape=tuple(jax.ShapeDtypeStruct(*out[:2]) for out in outs.values()),
        in_specs=flat(ins),
        out_specs=tuple(out[2] for out in outs.values()),
        scratch_shapes=flat(scratch),
        compiler_params=pltpu.CompilerParams(**params),
        name=kernel.__name__,
    )(*args)


def middle(dims, *args):
    return call(
        middle_kernel, dims, middle_specs(dims), args, collective_id=1, has_side_effects=True,
        vmem_limit_bytes=62 * 2**20,
    )[:-1]


def feed_plain(ctx, x, cot, length, vec, in_bias, wo, wi, wf):
    here = Place()
    rows = x.shape[0]
    row_at = lax.broadcasted_iota(jnp.int32, (rows, 1), 0) + here.quarter * rows
    e_outer = jnp.where(row_at < length, cot.astype(F32), 0.0)
    mid = x.astype(F32) + dot(ctx.T, wo) + vec[OB]
    unit, inverse = unit_of(mid)
    h2 = (unit * vec[LN2G] + vec[LN2B]).astype(BF)
    inner = dot(h2, wi) + in_bias
    square = inner * inner
    swing = jnp.tanh(GELU_C * inner * (1.0 + GELU_K * square))
    active = (0.5 * inner * (1.0 + swing)).astype(BF)
    slope = 0.5 * (1.0 + swing) + 0.5 * inner * (1.0 - swing * swing) * (
        GELU_C * (1.0 + 3.0 * GELU_K * square)
    )
    out = (mid + dot(active, wf) + vec[FB]).astype(BF)
    e_low = e_outer.astype(BF)
    e_inner = (dot_t(e_low, wf) * slope).astype(BF)
    e_norm = dot_t(e_inner, wi)
    e_unit = e_norm * vec[LN2G]
    grad_mid = e_outer + inverse * (e_unit - mean_rows(e_unit) - unit * mean_rows(e_unit * unit))
    e_branch = grad_mid.astype(BF)
    grads = dot(active.T, e_low), dot(h2.T, e_inner), dot(ctx, e_branch)
    vectors = (
        jnp.sum(e_branch.astype(F32), 0),
        jnp.sum(e_norm * unit, 0),
        jnp.sum(e_norm, 0),
        jnp.sum(e_outer, 0),
    )
    in_sums = jnp.sum(e_inner.astype(F32), 0).reshape(4, -1)
    vectors = jnp.concatenate((jnp.stack(vectors), in_sums))
    return out, dot_t(wo, e_branch).astype(BF), grad_mid, vectors, [g.astype(BF) for g in grads]


def backward_specs(dims):
    shards, rows, width, heads, _ = dims
    half, keys = width // 2, 4 * rows
    sems = pltpu.SemaphoreType.DMA
    ins = dict(
        ect=VMEM, ka_h=ANY, va_h=ANY, kt_h=ANY, qat_h=ANY, ctxt_h=ANY, h1_h=ANY, wq_h=ANY, out_h=ANY, x=VMEM,
        gmid=VMEM, vec=VMEM,
    )
    outs = dict(
        gtok_o=((rows, width), BF, ANY),
        out_o=((rows, width), BF, ANY),
        vec_o=((VROWS, width), F32, VMEM),
        gw_o=((width, 3 * half), BF, VMEM),
    )
    scratch = dict(
        vecs=pltpu.VMEM((VROWS, width), F32),
        ka=pltpu.VMEM((heads, keys, 128), BF),
        va=pltpu.VMEM((heads, keys, 128), BF),
        kt=pltpu.VMEM((heads, 64, keys), BF),
        qat=pltpu.VMEM((heads, 128, 2 * rows), BF),
        h1=pltpu.VMEM((keys, width), BF),
        wq=pltpu.VMEM((width, 3 * half), BF),
        e_ctx=pltpu.VMEM((half, 2 * rows), BF),
        eat=pltpu.VMEM((heads, 128, 2 * rows), BF),
        grads=pltpu.VMEM((3 * half, keys), BF),
        sums=pltpu.VMEM((width, rows), F32),
        sib_out=pltpu.VMEM((2, width, rows), BF),
        sib_in=pltpu.VMEM((2, width, rows), BF),
        side_out=pltpu.VMEM((width, rows), BF),
        side_in=pltpu.VMEM((width, rows), BF),
        gt=pltpu.VMEM((rows, width), BF),
        load_s=sems((7,)),
        trade_s=sems((2,)),
        trade_r=sems,
        sib_s=sems((2,)),
        sib_r=sems((2,)),
        side_s=sems((4,)),
        side_r=sems((4,)),
        perm_s=sems((5,)),
        perm_r=sems((5,)),
    )
    return ins, outs, scratch


def backward_kernel(dims, *refs):
    shards, rows, width, heads, _ = dims
    ins, outs, scratch = backward_specs(dims)
    at_ins, at_outs = len(ins), len(ins) + len(outs)
    i = Named(ins, refs[:at_ins])
    o = Named(outs, refs[at_ins:at_outs])
    v = Named(scratch, refs[at_outs:])
    here = Place()
    core = here.core
    half, keys = width // 2, 4 * rows
    chunks = 4
    step = rows // chunks
    loads = []
    for at, (src, dst) in enumerate(
        ((i.qat_h, v.qat), (i.ka_h, v.ka), (i.va_h, v.va), (i.kt_h, v.kt), (i.wq_h, v.wq), (i.h1_h, v.h1))
    ):
        copy = pltpu.make_async_copy(src, dst, v.load_s.at[at])
        copy.start()
        loads.append(copy)

    greet(here, [here.sibling, here.beside], here.to)

    mine = pl.ds(pl.multiple_of(core * half, 128), half)
    theirs = pl.ds(pl.multiple_of((1 - core) * half, 128), half)
    own = pl.ds(pl.multiple_of(core * rows, rows), rows)
    trade = remote(i.ect.at[theirs, :], v.e_ctx.at[:, own], v.trade_s.at[0], v.trade_r, here.sibling)
    trade.start()
    local = pltpu.make_async_copy(i.ect.at[mine, :], v.e_ctx.at[:, own], v.trade_s.at[1])
    local.start()

    def home(src, dst, at):
        return remote(src, dst, v.perm_s.at[at], v.perm_r.at[at], here.origin)

    def home_start(src, dst, at):
        @pl.when(jnp.logical_not(here.stays))
        def _():
            home(src, dst, at).start()

        @pl.when(here.stays)
        def _():
            pltpu.make_async_copy(src, dst, v.perm_r.at[at]).start()

    def home_wait(src, dst, at):
        pltpu.make_async_copy(src, dst, v.perm_r.at[at]).wait()

        @pl.when(jnp.logical_not(here.stays))
        def _():
            home(src, dst, at).wait_send()

    home_start(i.out_h, o.out_o, 4)
    local.wait()
    trade.wait()

    def with_delta(ctxt, sem):
        load = pltpu.make_async_copy(i.ctxt_h, ctxt, sem)
        load.start()
        load.wait()
        index = lax.broadcasted_iota(jnp.int32, (16, 2 * rows), 0)
        for h in range(heads):
            at = slice(h * 64, (h + 1) * 64)
            e_ctx = v.e_ctx[at, :]
            delta = jnp.sum(e_ctx.astype(F32) * ctxt[at, :], 0, keepdims=True)
            rest = jnp.zeros((16, 2 * rows), F32)
            for r, term in enumerate(split3(delta)):
                rest = jnp.where(index == r, term.astype(F32), rest)
            v.eat[h, :64, :] = e_ctx
            v.eat[h, 64:80, :] = rest.astype(BF)
            v.eat[h, 80:, :] = jnp.zeros((48, 2 * rows), BF)

    pl.run_scoped(with_delta, pltpu.VMEM((half, 2 * rows), F32), pltpu.SemaphoreType.DMA)
    for copy in loads:
        copy.wait()

    size = 256

    def attend(far):
        first = 2 * rows if far else 0

        def body(h, _):
            query, e_ctx = v.qat[h], v.eat[h]
            e_query = None
            for c in range(2 * rows // size):
                to = slice(first + c * size, first + (c + 1) * size)
                weights = jnp.exp(dot(v.ka[h, to, :], query))
                e_scores = (weights * dot(v.va[h, to, :], e_ctx)).astype(BF)
                e_value = dot_t(e_ctx[:64], weights.astype(BF))
                e_key = dot_t(query[:64], e_scores)
                part = dot(v.kt[h, :, to], e_scores)
                e_query = part if e_query is None else e_query + part
                v.grads[pl.ds(pl.multiple_of(half + h * 64, 64), 64), to] = e_key.astype(BF)
                v.grads[pl.ds(pl.multiple_of(2 * half + h * 64, 64), 64), to] = e_value.astype(BF)
            head = pl.ds(pl.multiple_of(h * 64, 64), 64)
            lower = pl.ds(pl.multiple_of(half + h * 64, 64), 64)
            if far:
                v.sums[head, :] = e_query[:, :rows]
                v.sums[lower, :] = e_query[:, rows:]
            else:
                v.grads[head, :rows] = ((v.sums[head, :] + e_query[:, :rows]) * HEAD_DIM**-0.5).astype(BF)
                v.grads[head, rows : 2 * rows] = (
                    (v.sums[lower, :] + e_query[:, rows:]) * HEAD_DIM**-0.5
                ).astype(BF)
            return 0

        lax.fori_loop(0, heads, body, 0)

    def partial_of(j, near):
        at = pl.ds(pl.multiple_of(j * rows, rows), rows)
        if near:
            return dot(v.wq[...], v.grads[:, at])
        return dot(v.wq[:, half:], v.grads[half:, at])

    def sib_copy(at):
        return remote(v.sib_out.at[at], v.sib_in.at[at], v.sib_s.at[at], v.sib_r.at[at], here.sibling)

    def side_copy(at):
        to = slice(at * step, (at + 1) * step)
        return remote(
            v.side_out.at[:, to], v.side_in.at[:, to], v.side_s.at[at], v.side_r.at[at], here.beside
        )

    def to_side():
        sib_copy(0).wait_recv()
        v.side_out[...] = (partial_of(2 + core, False) + v.sib_in[0].astype(F32)).astype(BF)
        for at in range(chunks):
            side_copy(at).start()

    attend(True)
    v.sib_out[0] = partial_of(3 - core, False).astype(BF)
    sib_copy(0).start()
    attend(False)
    to_side()
    v.sib_out[1] = partial_of(1 - core, True).astype(BF)
    sib_copy(1).start()
    for part, count in ((0, 2 * rows), (1, keys), (2, keys)):
        at = slice(part * half, (part + 1) * half)
        o.gw_o[:, at] = dot(v.grads[at, :count], v.h1[:count, :]).T.astype(BF)
    own_part = partial_of(core, True)
    sib_copy(1).wait_recv()
    v.sums[...] = own_part + v.sib_in[1].astype(F32)

    def row_sums(values):
        folded = values[:, :128].astype(F32)
        for n in range(1, values.shape[1] // 128):
            folded += values[:, n * 128 : (n + 1) * 128].astype(F32)
        return jnp.sum(folded.T, 0, keepdims=True)

    v.vecs[...] = jnp.zeros_like(v.vecs)
    for at, part in ((QB, v.grads[:half, : 2 * rows]), (VB, v.grads[2 * half :, :])):
        total = row_sums(part)
        for n in range(2):
            v.vecs[at : at + 1, n * half : (n + 1) * half] = jnp.where(core == n, total, 0.0)

    gain = i.vec[LN1G : LN1G + 1, :]
    gain_sum = shift_sum = None
    for at in range(chunks):
        to = slice(at * step, (at + 1) * step)
        side_copy(at).wait_recv()
        e_norm = (v.sums[:, to] + v.side_in[:, to].astype(F32)).T
        unit, inverse = unit_of(i.x[to, :].astype(F32))
        e_unit = e_norm * gain
        result = i.gmid[to, :] + inverse * (
            e_unit - mean_rows(e_unit) - unit * mean_rows(e_unit * unit)
        )
        v.gt[to, :] = result.astype(BF)
        home_start(v.gt.at[to, :], o.gtok_o.at[to, :], at)
        gains = jnp.sum(e_norm * unit, 0, keepdims=True)
        shifts = jnp.sum(e_norm, 0, keepdims=True)
        gain_sum = gains if at == 0 else gain_sum + gains
        shift_sum = shifts if at == 0 else shift_sum + shifts
    v.vecs[LN1G : LN1G + 1, :] = gain_sum
    v.vecs[LN1B : LN1B + 1, :] = shift_sum
    o.vec_o[...] = v.vecs[...]

    for at in range(2):
        sib_copy(at).wait_send()
    for at in range(chunks):
        side_copy(at).wait_send()
        to = slice(at * step, (at + 1) * step)
        home_wait(v.gt.at[to, :], o.gtok_o.at[to, :], at)
    home_wait(i.out_h, o.out_o, 4)


def attention_backward(dims, *args):
    return call(
        backward_kernel, dims, backward_specs(dims), args, collective_id=2, has_side_effects=True,
        vmem_limit_bytes=60 * 2**20,
    )


def final_specs(dims):
    shards, rows, width, heads, _ = dims
    share, half = width // shards, width // 2
    ins = dict(vec=VMEM, sums=[ANY] * 4)
    outs = [(4 * share, width), (share, 4 * width), (share, width), (share, 3 * width)]
    outs += [(1, share)] * IB + [(1, 4 * share)]
    outs = {n: (shape, F32, VMEM) for n, shape in enumerate(outs)}
    shapes = [(2,) + part for part in grad_parts(dims)] + [(heads // 2, 2, share, half)]
    scratch = dict(held=[pltpu.VMEM(shape, BF) for shape in shapes], sem=pltpu.SemaphoreType.DMA((4,)))
    return ins, outs, scratch


def final_kernel(dims, *refs):
    vec, sums, out, held, sem = refs[0], refs[1:5], refs[5:-5], refs[-5:-1], refs[-1]
    copies = [pltpu.make_async_copy(src, dst, sem.at[n]) for n, (src, dst) in enumerate(zip(sums, held))]
    for copy in copies:
        copy.start()
    t_f, t_i, t_o, t_w, *vectors = out
    d_f, d_i, d_o, d_w = held
    half, share = d_f.shape[1], d_i.shape[1]
    width = 2 * half
    for n, result in enumerate(vectors[:-1]):
        result[...] = vec[n : n + 1, :share]
    for r in range(4):
        vectors[-1][:, r * share : (r + 1) * share] = vec[IB + r : IB + r + 1, :share]
    for copy in copies:
        copy.wait()
    for ab in range(2):
        t_f[:, ab * half : (ab + 1) * half] = d_f[ab].astype(F32).T
        t_o[:, ab * half : (ab + 1) * half] = d_o[ab].astype(F32)
        for sub in range(2):
            to = (2 * sub + ab) * width
            t_i[:, to : to + width] = d_i[ab, :, sub * width : (sub + 1) * width].astype(F32)
    for g in range(d_w.shape[0]):
        for core in range(2):
            for part in range(3):
                to = part * width + core * half + g * 128
                t_w[:, to : to + 128] = d_w[g, core, :, part * 128 : (part + 1) * 128].astype(F32)


def on_device(
    tokens, ln1_gain, ln1_shift, w_qkv, q_bias, v_bias, w_out, out_bias, ln2_gain, ln2_shift, w_in, in_bias,
    w_fin, fin_bias, cotangent, lengths, shards,
):
    _, rows, width = tokens.shape
    heads = width // HEAD_DIM // 2
    half = width // 2
    share = width // shards
    gather = shards == 8
    dims = (shards, rows, width, heads, gather)
    core = lax.rem(lax.axis_index("shard"), 2)

    vectors = (ln1_gain, ln1_shift, q_bias, v_bias, out_bias, ln2_gain, ln2_shift, fin_bias, in_bias)
    lanes = 128 if gather else max(128, share)
    packed = jnp.zeros((VROWS, lanes), BF)
    for at, one in enumerate(vectors):
        one = one.reshape(-1, share)
        packed += jnp.pad(one, ((at, VROWS - at - one.shape[0]), (0, lanes - share)))
    numbers = jnp.stack((lengths // 256, lengths % 256)).astype(BF)
    packed += jnp.pad(numbers, ((VECS, VROWS - VECS - 2), (0, lanes - 1)))
    if gather:
        vec, w_here, shares = packed, w_qkv, (w_out, w_in, w_fin)
    else:
        vec = lax.all_gather(packed[:, :share], "shard", axis=1, tiled=True)
        full_w = lax.all_gather(w_qkv, "shard", axis=0, tiled=True)
        w_here = lax.dynamic_index_in_dim(
            full_w.reshape(width, 3, 2, half), core, 2, keepdims=False
        ).reshape(width, 3 * half)
        shares = ()
    (ka, va, kt, qat, ctxt, ctx, h1, wq, x, cot, lens, vecs, inb, *wholes) = attention_forward(
        dims, tokens.reshape(rows, width), cotangent.reshape(rows, width), packed, w_here, vec, *shares
    )
    if gather:
        gtok, output, *sums = middle(
            dims, ctx, x, cot, lens, vecs, inb, *wholes, ka, va, kt, qat, ctxt, h1, wq
        )
        total_wf, total_wi, total_wo, total_w, *vectors = call(
            final_kernel, dims, final_specs(dims), sums, vmem_limit_bytes=60 * 2**20
        )
        vectors = [v.reshape(-1) for v in vectors]
    else:
        wholes = [lax.all_gather(w, "shard", axis=0, tiled=True) for w in (w_out, w_in, w_fin)]
        full_ib = lax.all_gather(in_bias, "shard", axis=0, tiled=True).astype(F32)
        out, ect, gmid, vec_two, grads = feed_plain(ctx, x, cot, length_of(lens), vecs, full_ib, *wholes)
        gtok, output, vec_one, gw = attention_backward(
            dims, ect, ka, va, kt, qat, ctxt, h1, wq, out, x, gmid, vecs
        )

        def total(grad):
            part = lax.psum_scatter(grad, "shard", scatter_dimension=0, tiled=True)
            return lax.psum(part, "seq").astype(F32)

        total_wf, total_wi, total_wo = [total(grad) for grad in grads]
        wide = jnp.zeros((width, 3, 2, half), BF)
        wide = lax.dynamic_update_index_in_dim(wide, gw.reshape(width, 3, half), core, 2)
        total_w = total(wide.reshape(width, 3 * width))
        sums = lax.psum(jnp.concatenate((vec_one[:OB], vec_two)), ("seq", "shard"))
        s = lax.axis_index("shard")
        mine = lax.dynamic_slice_in_dim(sums[:IB], s * share, share, 1)
        vectors = [mine[n] for n in range(IB)]
        vectors.append(lax.dynamic_slice_in_dim(sums[IB:].reshape(-1), s * 4 * share, 4 * share, 0))
    return (
        output.reshape(tokens.shape),
        gtok.reshape(tokens.shape),
        vectors[LN1G],
        vectors[LN1B],
        total_w,
        vectors[QB],
        vectors[VB],
        total_wo,
        vectors[OB],
        vectors[LN2G],
        vectors[LN2B],
        total_wi,
        vectors[IB],
        total_wf,
        vectors[FB],
    )


def solution(mesh):
    vector, matrix, rows = P("shard"), P("shard", None), P("shard", "seq", None)
    return jax.shard_map(
        functools.partial(on_device, shards=mesh.shape["shard"]),
        mesh=mesh,
        in_specs=(
            rows, vector, vector, matrix, vector, vector, matrix, vector, vector, vector, matrix, vector,
            matrix, vector, rows, vector,
        ),
        out_specs=(
            rows, rows, vector, vector, matrix, vector, vector, matrix, vector, vector, vector, matrix,
            vector, matrix, vector,
        ),
        check_vma=False,
    )
```
